128 devices in a mesh: dp: 64 (over x, y, z_hi, core), tensor: 2 (over z_lo).
Axes of the slice: x: 4, y: 4, z: 4 (z_hi: 2, z_lo: 2; z = z_hi * 2 + z_lo), core: 2. Of those that a mesh axis runs over, the one named last changes fastest.
Arguments:
- block_input: bfloat16 [16384, 2048], P(('dp', 'tensor')), may hold values from -24 to 24
- output_grad: bfloat16 [16384, 2048], P(('dp', 'tensor')), may hold values from -24 to 24
- segment_ids: int32 [64, 256], P('dp'), may hold values from 0 to 3, as said below
- norm_gains: float32 [4224], replicated, may hold values from 0.5 to 1.5
- gain_moment: float32 [4224], replicated, may hold values from -240.768 to 240.768
- gain_square: float32 [4224], replicated, may hold values from 5.91872 to 4258.5293
- query_weight: float32 [2048, 2048], P('dp', 'tensor'), may hold values from -0.125 to 0.125
- query_moment: float32 [2048, 2048], P('dp', 'tensor'), may hold values from -80 to 80
- query_square: float32 [2048, 2048], P('dp', 'tensor'), may hold values from 8.192 to 131.072
- key_weight: float32 [2048, 512], P('dp', 'tensor'), may hold values from -0.125 to 0.125
- key_moment: float32 [2048, 512], P('dp', 'tensor'), may hold values from -160 to 160
- key_square: float32 [2048, 512], P('dp', 'tensor'), may hold values from 32.768 to 524.288
- value_weight: float32 [2048, 512], P('dp', 'tensor'), may hold values from -0.125 to 0.125
- value_moment: float32 [2048, 512], P('dp', 'tensor'), may hold values from -256 to 256
- value_square: float32 [2048, 512], P('dp', 'tensor'), may hold values from 73.728 to 1179.648
- output_weight: float32 [2048, 2048], P('dp', 'tensor'), may hold values from -0.75 to 0.75
- output_moment: float32 [2048, 2048], P('dp', 'tensor'), may hold values from -16 to 16
- output_square: float32 [2048, 2048], P('dp', 'tensor'), may hold values from 0.32768 to 5.24288
- gate_weight: float32 [2048, 8192], P('dp', 'tensor'), may hold values from -0.125 to 0.125
- gate_moment: float32 [2048, 8192], P('dp', 'tensor'), may hold values from -24 to 24
- gate_square: float32 [2048, 8192], P('dp', 'tensor'), may hold values from 0.73728 to 11.79648
- up_weight: float32 [2048, 8192], P('dp', 'tensor'), may hold values from -0.125 to 0.125
- up_moment: float32 [2048, 8192], P('dp', 'tensor'), may hold values from -24 to 24
- up_square: float32 [2048, 8192], P('dp', 'tensor'), may hold values from 0.73728 to 11.79648
- down_weight: float32 [2048, 8192], P('dp', 'tensor'), may hold values from -0.0625 to 0.0625
- down_moment: float32 [2048, 8192], P('dp', 'tensor'), may hold values from -48 to 48
- down_square: float32 [2048, 8192], P('dp', 'tensor'), may hold values from 2.94912 to 47.5136
Outputs:
- block_output: float32 [16384, 2048], P(('dp', 'tensor'))
- input_grad: float32 [16384, 2048], P(('dp', 'tensor'))
- gains_updated: float32 [4224], replicated
- gain_momentum: float32 [4224], replicated
- gain_variance: float32 [4224], replicated
- query_updated: float32 [2048, 2048], P('dp', 'tensor')
- query_momentum: float32 [2048, 2048], P('dp', 'tensor')
- query_variance: float32 [2048, 2048], P('dp', 'tensor')
- key_updated: float32 [2048, 512], P('dp', 'tensor')
- key_momentum: float32 [2048, 512], P('dp', 'tensor')
- key_variance: float32 [2048, 512], P('dp', 'tensor')
- value_updated: float32 [2048, 512], P('dp', 'tensor')
- value_momentum: float32 [2048, 512], P('dp', 'tensor')
- value_variance: float32 [2048, 512], P('dp', 'tensor')
- output_updated: float32 [2048, 2048], P('dp', 'tensor')
- output_momentum: float32 [2048, 2048], P('dp', 'tensor')
- output_variance: float32 [2048, 2048], P('dp', 'tensor')
- gate_updated: float32 [2048, 8192], P('dp', 'tensor')
- gate_momentum: float32 [2048, 8192], P('dp', 'tensor')
- gate_variance: float32 [2048, 8192], P('dp', 'tensor')
- up_updated: float32 [2048, 8192], P('dp', 'tensor')
- up_momentum: float32 [2048, 8192], P('dp', 'tensor')
- up_variance: float32 [2048, 8192], P('dp', 'tensor')
- down_updated: float32 [2048, 8192], P('dp', 'tensor')
- down_momentum: float32 [2048, 8192], P('dp', 'tensor')
- down_variance: float32 [2048, 8192], P('dp', 'tensor')
The draws below stay inside these ranges and needn't reach their ends.
Inputs may be any that keep to these rules, and one draw needn't show every extreme that they name: `segment_ids`: ids never fall along a row; the document holding position 128 begins before 256 // 4 and ends at or after 3 * 64 - 1.
All inputs are finite; a program needn't handle non-finite values.
Results may differ from the reference program's by a relative error of at most 0.015.
Values may be sent and summed in bfloat16 or wider, within the bound.
A program may use at most 320 MiB of HBM per device.

```python
import math
import jax
import jax.numpy as jnp
from jax import lax

D = 2048
HEADS = 32
KV_HEADS = 8
HD = 64
FF = 8192
DOCS = 4
STEP = 10
SEQ = 256
TOKENS = 16384
QD = 2048
KVD = 512
GAINS = 4224
N_DP = 64


def gain_scales():
    places = jnp.arange(GAINS, dtype=jnp.int32)
    return jnp.where(places < D, 2.0, jnp.where(places < 2 * D, 0.85, 5.7)).astype(jnp.float32) * TOKENS ** 0.5


def draw_segment_ids(key, part):
    key = jax.random.fold_in(key, 11)
    cut_points = jax.random.randint(key, (TOKENS // SEQ, DOCS - 1), 1, SEQ // 2, dtype=jnp.int32)
    cut_points = jnp.where(cut_points < SEQ // 4, cut_points, cut_points + SEQ // 2)
    places = jnp.arange(SEQ, dtype=jnp.int32)
    return jnp.sum((cut_points[:, None, :] <= places[None, :, None]).astype(jnp.int32), axis=-1).astype(jnp.int32)


def draw_gain_moment(key, part):
    key = jax.random.fold_in(key, 23)
    normals = jax.random.truncated_normal(key, -3.0, 3.0, (GAINS,), jnp.float32)
    return (0.11 * gain_scales() * normals).astype(jnp.float32)


def draw_gain_square(key, part):
    key = jax.random.fold_in(key, 37)
    spread = jax.random.uniform(key, (GAINS,), jnp.float32, math.log(0.0005), math.log(0.008))
    return (jnp.exp(spread) * gain_scales() * gain_scales()).astype(jnp.float32)


def spiked(values, key, source, target, blocks, factor):
    owner, partner = [(jnp.arange(values.shape[axis_at]) // (values.shape[axis_at] // blocks)).reshape([-1 if axis == axis_at else 1 for axis in range(values.ndim)]) for axis_at in (source, target)]
    chosen = jax.random.permutation(key, blocks)[partner]
    strong = (owner == chosen) | (owner == (partner + blocks // 2) % blocks)
    return jnp.where(strong, factor * values, values)


def block_levels(own_key, dims, split, least, high):
    def one(axis_at, shards_of):
        heights = jax.random.uniform(jax.random.fold_in(jax.random.fold_in(own_key, 6), axis_at), (shards_of,), jnp.float32, least / len(split), high / len(split))
        return jnp.repeat(jnp.exp(heights), dims[axis_at] // shards_of).reshape((-1,) + (1,) * (len(dims) - axis_at - 1))

    loudness = one(*split[0])
    for cut in split[1:]:
        loudness = loudness * one(*cut)
    return loudness


def bell_draw(own_key, dims, deviation, reach, shards=(), held_as=jnp.bfloat16):
    values = jax.random.normal(own_key, dims, jnp.float32) * deviation
    if len(shards) > 0:
        values = block_levels(own_key, dims, shards, -0.22, 0.18) * values
    return jnp.clip(values, min=-reach, max=reach).astype(held_as)


def noise_with(key, shape, deviation, limit, cuts, heavy, kind=jnp.bfloat16):
    values = deviation * jax.random.normal(key, shape, jnp.float32)
    if cuts:
        values = values * block_levels(key, shape, cuts, -0.22, 0.18)
    return jnp.clip(spiked(values, jax.random.fold_in(key, 3), *heavy), -limit, limit).astype(kind)


def setup_inputs(seed: int = 0) -> dict:
    key_of = jax.random.split(jax.random.key(seed), 28)
    block_input = noise_with(key_of[0], (TOKENS, D), 1.0, 24.0, ((0, 128),), (0, 1, 128, 5.5))
    output_grad = noise_with(key_of[1], (TOKENS, D), 1.0, 24.0, ((0, 128),), (0, 1, 128, 5.5))
    segment_ids = draw_segment_ids(jax.random.fold_in(key_of[27], 71), 0)
    norm_gains = jnp.clip(1.0 + 0.1 * jax.random.normal(key_of[3], (GAINS,), jnp.float32), 0.5, 1.5)
    gain_moment = draw_gain_moment(jax.random.fold_in(key_of[27], 71), 0)
    gain_square = draw_gain_square(jax.random.fold_in(key_of[27], 71), 0)
    query_weight = bell_draw(key_of[6], (D, QD), D ** -0.5, 0.125, ((0, 64), (1, 2)), jnp.float32)
    query_moment = bell_draw(key_of[7], (D, QD), (0.11 * TOKENS ** 0.5), 80.0, ((0, 64), (1, 2)), jnp.float32)
    query_square = jnp.clip(jnp.exp(math.log(131.072) - 2.7725887 * jax.random.uniform(key_of[8], (D, QD), jnp.float32) ** block_levels(key_of[8], (D, QD), ((0, 64), (1, 2)), -0.2, 0.2)), 8.192, 131.072)
    key_weight = bell_draw(key_of[9], (D, KVD), D ** -0.5, 0.125, ((0, 64), (1, 2)), jnp.float32)
    key_moment = bell_draw(key_of[10], (D, KVD), (0.22 * TOKENS ** 0.5), 160.0, ((0, 64), (1, 2)), jnp.float32)
    key_square = jnp.clip(jnp.exp(math.log(524.288) - 2.7725887 * jax.random.uniform(key_of[11], (D, KVD), jnp.float32) ** block_levels(key_of[11], (D, KVD), ((0, 64), (1, 2)), -0.2, 0.2)), 32.768, 524.288)
    value_weight = bell_draw(key_of[12], (D, KVD), D ** -0.5, 0.125, ((0, 64), (1, 2)), jnp.float32)
    value_moment = bell_draw(key_of[13], (D, KVD), (0.33 * TOKENS ** 0.5), 256.0, ((0, 64), (1, 2)), jnp.float32)
    value_square = jnp.clip(jnp.exp(math.log(1179.648) - 2.7725887 * jax.random.uniform(key_of[14], (D, KVD), jnp.float32) ** block_levels(key_of[14], (D, KVD), ((0, 64), (1, 2)), -0.2, 0.2)), 73.728, 1179.648)
    output_weight = bell_draw(key_of[15], (D, QD), (max(D // 32, 16)) ** -0.5, 0.75, ((0, 64), (1, 2)), jnp.float32)
    output_moment = bell_draw(key_of[16], (D, QD), (0.022 * TOKENS ** 0.5), 16.0, ((0, 64), (1, 2)), jnp.float32)
    output_square = jnp.clip(jnp.exp(math.log(5.24288) - 2.7725887 * jax.random.uniform(key_of[17], (D, QD), jnp.float32) ** block_levels(key_of[17], (D, QD), ((0, 64), (1, 2)), -0.2, 0.2)), 0.32768, 5.24288)
    gate_weight = bell_draw(key_of[18], (D, FF), D ** -0.5, 0.125, ((0, 64), (1, 2)), jnp.float32)
    gate_moment = bell_draw(key_of[19], (D, FF), (0.033 * TOKENS ** 0.5), 24.0, ((0, 64), (1, 2)), jnp.float32)
    gate_square = jnp.clip(jnp.exp(math.log(11.79648) - 2.7725887 * jax.random.uniform(key_of[20], (D, FF), jnp.float32) ** block_levels(key_of[20], (D, FF), ((0, 64), (1, 2)), -0.2, 0.2)), 0.73728, 11.79648)
    up_weight = bell_draw(key_of[21], (D, FF), D ** -0.5, 0.125, ((0, 64), (1, 2)), jnp.float32)
    up_moment = bell_draw(key_of[22], (D, FF), (0.033 * TOKENS ** 0.5), 24.0, ((0, 64), (1, 2)), jnp.float32)
    up_square = jnp.clip(jnp.exp(math.log(11.79648) - 2.7725887 * jax.random.uniform(key_of[23], (D, FF), jnp.float32) ** block_levels(key_of[23], (D, FF), ((0, 64), (1, 2)), -0.2, 0.2)), 0.73728, 11.79648)
    down_weight = bell_draw(key_of[24], (D, FF), FF ** -0.5, 0.0625, ((0, 64), (1, 2)), jnp.float32)
    down_moment = bell_draw(key_of[25], (D, FF), (0.066 * TOKENS ** 0.5), 48.0, ((0, 64), (1, 2)), jnp.float32)
    down_square = jnp.clip(jnp.exp(math.log(47.5136) - 2.779509 * jax.random.uniform(key_of[26], (D, FF), jnp.float32) ** block_levels(key_of[26], (D, FF), ((0, 64), (1, 2)), -0.2, 0.2)), 2.94912, 47.5136)
    return {"block_input": block_input, "output_grad": output_grad, "segment_ids": segment_ids, "norm_gains": norm_gains, "gain_moment": gain_moment, "gain_square": gain_square, "query_weight": query_weight, "query_moment": query_moment, "query_square": query_square, "key_weight": key_weight, "key_moment": key_moment, "key_square": key_square, "value_weight": value_weight, "value_moment": value_moment, "value_square": value_square, "output_weight": output_weight, "output_moment": output_moment, "output_square": output_square, "gate_weight": gate_weight, "gate_moment": gate_moment, "gate_square": gate_square, "up_weight": up_weight, "up_moment": up_moment, "up_square": up_square, "down_weight": down_weight, "down_moment": down_moment, "down_square": down_square}


@jax.custom_vjp
def low(v):
    return lax.optimization_barrier(v.astype(jnp.bfloat16)).astype(jnp.float32)

@jax.custom_vjp
def low_back(v):
    return v

def low_keep(v):
    return (low(v), None)

def low_pass(kept, grad):
    return (grad,)

def back_keep(v):
    return (v, None)

def back_low(kept, grad):
    return (low(grad),)
low.defvjp(low_keep, low_pass)
low_back.defvjp(back_keep, back_low)
epsilon = 1e-06
rope_base = 1000000.0
beta_one = 0.9
beta_two = 0.999
adam_epsilon = 1e-08
weight_decay = 0.1
matrix_rates = (0.04, 0.04, 0.04, 0.15, 0.04, 0.04, 0.02)
gain_rate = 0.3
masked_score = -1000000000.0
highest = lax.Precision.HIGHEST

def matmul(left, right):
    return jnp.dot(left, right, precision=highest, preferred_element_type=jnp.float32)

def rms_scale(values, gain):
    return values * lax.rsqrt(lax.optimization_barrier(jnp.mean(values * values, axis=-1, keepdims=True)) + epsilon) * gain

def positions_of(segment_row):
    places = jnp.arange(segment_row.shape[0], dtype=jnp.int32)
    fresh = jnp.concatenate([jnp.ones((1,), dtype=jnp.bool_), segment_row[1:] != segment_row[:-1]])
    starts = jnp.where(fresh, places, jnp.zeros_like(places))
    return places - lax.cummax(starts, axis=0)

def rope_tables(positions):
    half_dim = HD // 2
    frequency = rope_base ** (-2.0 * jnp.arange(half_dim, dtype=jnp.float32) / HD)
    angles = positions.astype(jnp.float32)[:, None] * frequency[None, :]
    return (jnp.cos(angles), jnp.sin(angles))

def rotate(values, cosine, sine):
    half_dim = HD // 2
    front_half = values[..., :half_dim]
    back_half = values[..., half_dim:]
    cos_wide = cosine[:, None, :]
    sin_wide = sine[:, None, :]
    return jnp.concatenate([front_half * cos_wide - back_half * sin_wide, back_half * cos_wide + front_half * sin_wide], axis=-1)

def attend(pieces):
    query_rot, key_rot, value_rows, segment_row = pieces
    group_size = HEADS // KV_HEADS
    key_wide = jnp.repeat(key_rot, group_size, axis=1)
    value_wide = jnp.repeat(value_rows, group_size, axis=1)
    scores = low_back(jnp.einsum('qhd,khd->hqk', query_rot, key_wide, precision=highest) * HD ** (-0.5))
    places = jnp.arange(segment_row.shape[0], dtype=jnp.int32)
    allowed = (segment_row[:, None] == segment_row[None, :]) & (places[None, :] <= places[:, None])
    scores = jnp.where(allowed[None], scores, masked_score)
    top_score = lax.optimization_barrier(jnp.max(scores, axis=-1, keepdims=True))
    exps_now = jnp.exp(scores - top_score)
    probs = exps_now / lax.optimization_barrier(jnp.sum(exps_now, axis=-1, keepdims=True))
    return jnp.einsum('hqk,khd->qhd', low(probs), value_wide, precision=highest)

def block_forward(rows_in, segment_block, weight_set, gain_set):
    query_low, key_low, value_low, output_low, gate_low, up_low, down_low = [low(member) for member in weight_set]
    row_count = rows_in.shape[0]
    pack_count = segment_block.shape[0]
    normed_one = low(rms_scale(rows_in, gain_set[:D]))
    queries = low_back(matmul(normed_one, query_low)).reshape(row_count, HEADS, HD)
    key_rows = low_back(matmul(normed_one, key_low)).reshape(row_count, KV_HEADS, HD)
    value_rows = low(low_back(matmul(normed_one, value_low))).reshape(row_count, KV_HEADS, HD)
    positions = jax.vmap(positions_of)(segment_block).reshape(row_count)
    cosine, sine = rope_tables(positions)
    query_rot = low(rotate(rms_scale(queries, gain_set[2 * D:2 * D + HD]), cosine, sine))
    key_rot = low(rotate(rms_scale(key_rows, gain_set[2 * D + HD:]), cosine, sine))
    attended = lax.map(jax.checkpoint(attend), (query_rot.reshape(pack_count, SEQ, HEADS, HD), key_rot.reshape(pack_count, SEQ, KV_HEADS, HD), value_rows.reshape(pack_count, SEQ, KV_HEADS, HD), segment_block))
    mixed = low(low_back(attended.reshape(row_count, QD)))
    middle = rows_in + low_back(matmul(mixed, output_low.T))
    normed_two = low(rms_scale(middle, gain_set[D:2 * D]))
    gate_pre = low_back(matmul(normed_two, gate_low))
    up_pre = low_back(matmul(normed_two, up_low))
    hidden = low(gate_pre * jax.nn.sigmoid(gate_pre) * up_pre)
    return middle + low_back(matmul(hidden, down_low.T))

def adam_step(weights_now, moment_now, square_now, gradient, step_rate, decay_rate):
    momentum = beta_one * moment_now + (1.0 - beta_one) * gradient
    variance = beta_two * square_now + (1.0 - beta_two) * gradient * gradient
    ratio = momentum / (1.0 - beta_one ** STEP) / (jnp.sqrt(variance / (1.0 - beta_two ** STEP)) + adam_epsilon)
    return (weights_now - step_rate * (ratio + decay_rate * weights_now), momentum, variance)

def reference(block_input, output_grad, segment_ids, norm_gains, gain_moment, gain_square, query_weight, query_moment, query_square, key_weight, key_moment, key_square, value_weight, value_moment, value_square, output_weight, output_moment, output_square, gate_weight, gate_moment, gate_square, up_weight, up_moment, up_square, down_weight, down_moment, down_square):
    weight_set = (query_weight, key_weight, value_weight, output_weight, gate_weight, up_weight, down_weight)
    packs_step = 1
    while packs_step * 2 * SEQ <= 4096 and N_DP % (packs_step * 2) == 0:
        packs_step = packs_step * 2
    step_count = N_DP // packs_step
    rows_step = packs_step * SEQ
    inputs_all = block_input.astype(jnp.float32).reshape(step_count, rows_step, D)
    cotangent_all = output_grad.astype(jnp.float32).reshape(step_count, rows_step, D)
    segments_all = segment_ids.reshape(step_count, packs_step, SEQ)

    def one_step(totals, pieces):
        rows_in, cotangent_rows, segment_block = pieces

        def forward(rows_local, weights_local, gains_local):
            return block_forward(rows_local, segment_block, weights_local, gains_local)
        outputs, pullback = jax.vjp(forward, rows_in, weight_set, norm_gains)
        grad_rows, grad_weights, grad_gains = pullback(cotangent_rows)
        weight_totals = tuple((summed + addend for summed, addend in zip(totals[0], grad_weights)))
        return ((weight_totals, totals[1] + grad_gains), (outputs, grad_rows))
    start_totals = (tuple((jnp.zeros_like(member) for member in weight_set)), jnp.zeros_like(norm_gains))
    (weight_grads, gain_grads), (outputs, input_rows) = lax.scan(one_step, start_totals, (inputs_all, cotangent_all, segments_all))
    block_output = outputs.reshape(TOKENS, D)
    input_grad = input_rows.reshape(TOKENS, D)
    gains_updated, gain_momentum, gain_variance = adam_step(norm_gains, gain_moment, gain_square, gain_grads, gain_rate, 0.0)
    query_updated, query_momentum, query_variance = adam_step(query_weight, query_moment, query_square, weight_grads[0], matrix_rates[0], weight_decay)
    key_updated, key_momentum, key_variance = adam_step(key_weight, key_moment, key_square, weight_grads[1], matrix_rates[1], weight_decay)
    value_updated, value_momentum, value_variance = adam_step(value_weight, value_moment, value_square, weight_grads[2], matrix_rates[2], weight_decay)
    output_updated, output_momentum, output_variance = adam_step(output_weight, output_moment, output_square, weight_grads[3], matrix_rates[3], weight_decay)
    gate_updated, gate_momentum, gate_variance = adam_step(gate_weight, gate_moment, gate_square, weight_grads[4], matrix_rates[4], weight_decay)
    up_updated, up_momentum, up_variance = adam_step(up_weight, up_moment, up_square, weight_grads[5], matrix_rates[5], weight_decay)
    down_updated, down_momentum, down_variance = adam_step(down_weight, down_moment, down_square, weight_grads[6], matrix_rates[6], weight_decay)
    return (block_output, input_grad, gains_updated, gain_momentum, gain_variance, query_updated, query_momentum, query_variance, key_updated, key_momentum, key_variance, value_updated, value_momentum, value_variance, output_updated, output_momentum, output_variance, gate_updated, gate_momentum, gate_variance, up_updated, up_momentum, up_variance, down_updated, down_momentum, down_variance)
```

```python
import jax
import jax.numpy as jnp
from jax import lax
from jax.experimental import pallas as pl
from jax.experimental.pallas import tpu as pltpu

MESH = pl.DeviceIdType.MESH
VM = pltpu.VMEM
bf16 = jnp.bfloat16
f32 = jnp.float32


def m4(v):
    return lax.rem(v + 4, 4)


class Place:
    def __init__(self):
        dp = lax.axis_index("dp")
        self.l = lax.axis_index("tensor")
        self.x = lax.div(dp, 16)
        self.y = lax.rem(lax.div(dp, 4), 4)
        self.h = lax.rem(lax.div(dp, 2), 2)
        self.c = lax.rem(dp, 2)
        self.z = self.h * 2 + self.l

    def at(self, x=None, y=None, z=None, c=None):
        x = self.x if x is None else x
        y = self.y if y is None else y
        z = self.z if z is None else z
        c = self.c if c is None else c
        return (x * 16 + y * 4 + lax.div(z, 2) * 2 + c, lax.rem(z, 2))

    def pos(self, axis):
        return {"x": self.x, "y": self.y, "z": self.z}[axis]

    def step(self, axis, d):
        return self.at(**{axis: m4(self.pos(axis) + d)})

    def sibling(self):
        return self.at(c=1 - self.c)


class Wire:
    def __init__(self, send, recv):
        self.send, self.recv, self.n = send, recv, 0
        self.pending = []

    def go(self, src, dst, dev):
        i = self.n
        self.n += 1
        c = pltpu.make_async_remote_copy(
            src_ref=src, dst_ref=dst, send_sem=self.send.at[i], recv_sem=self.recv.at[i],
            device_id=dev, device_id_type=MESH)
        c.start()
        self.pending.append(c)
        return c

    def finish(self):
        for c in self.pending:
            c.wait_send()
        self.pending = []


def meet(devs):
    b = pltpu.get_barrier_semaphore()
    for d in devs:
        pl.semaphore_signal(b, inc=1, device_id=d, device_id_type=MESH)
    pl.semaphore_wait(b, len(devs))


def ring_gather(w, me, axis, whole, lo, hi, first=None, arrived=None):
    p = me.pos(axis)
    up, down = me.step(axis, 1), me.step(axis, -1)
    own = whole(p) if first is None else first
    a = w.go(own, whole(p), up)
    b = w.go(own, whole(p), down)
    yield
    a.wait_recv()
    fa = w.go(lo(m4(p - 1)), lo(m4(p - 1)), up)
    if arrived:
        arrived(whole(m4(p - 1)))
    b.wait_recv()
    fb = w.go(hi(m4(p + 1)), hi(m4(p + 1)), down)
    if arrived:
        arrived(whole(m4(p + 1)))
    yield
    fa.wait_recv()
    if arrived:
        arrived(lo(m4(p - 2)))
    fb.wait_recv()
    if arrived:
        arrived(hi(m4(p - 2)))


def ring_scatter(w, me, axis, lo, hi, tlo, thi, rup, rdown, add):
    p = me.pos(axis)
    up, down = me.step(axis, 1), me.step(axis, -1)
    far, nu, nd = m4(p + 2), m4(p + 1), m4(p - 1)
    ta = w.go(lo(far), tlo, up)
    tb = w.go(hi(far), thi, down)
    da = w.go(hi(nu), rup[1], up)
    db = w.go(lo(nd), rdown[0], down)
    yield
    ta.wait_recv()
    add(tlo, lo(nu))
    sa = w.go(tlo, rup[0], up)
    tb.wait_recv()
    add(thi, hi(nd))
    sb = w.go(thi, rdown[1], down)
    yield
    da.wait_recv()
    db.wait_recv()
    sa.wait_recv()
    sb.wait_recv()


def loop_add(dst, a, b=None, rows=16):
    n = dst.shape[0]

    def body(i, _):
        def inner(j, _):
            s = pl.ds(pl.multiple_of(j * rows, rows), rows)
            v = dst[i, s].astype(f32) + a[i, s].astype(f32)
            if b is not None:
                v = v + b[i, s].astype(f32)
            dst[i, s] = v.astype(dst.dtype)
            return 0
        return lax.fori_loop(0, dst.shape[1] // rows, inner, 0)
    lax.fori_loop(0, n, body, 0)


def run(gens):
    gens = list(gens)
    while gens:
        for g in list(gens):
            try:
                next(g)
            except StopIteration:
                gens.remove(g)


def params(cid, mb=56):
    return pltpu.CompilerParams(collective_id=cid, has_side_effects=True, vmem_limit_bytes=mb * 2**20)


def ag_xy_gens(w, me, src, out):
    H = 64
    x, y = me.x, me.y

    def half_a():
        yield from ring_gather(w, me, "x", lambda i: out.at[i, y, pl.ds(0, 64)], lambda i: out.at[i, y, pl.ds(0, 32)],
                               lambda i: out.at[i, y, pl.ds(32, 32)], first=src.at[pl.ds(0, 64)])
        yield
        yield from ring_gather(w, me, "y", lambda i: out.at[:, i, pl.ds(0, 64)], lambda i: out.at[:, i, pl.ds(0, 32)],
                               lambda i: out.at[:, i, pl.ds(32, 32)])

    def half_b():
        yield from ring_gather(w, me, "y", lambda i: out.at[x, i, pl.ds(64, 64)], lambda i: out.at[x, i, pl.ds(64, 32)],
                               lambda i: out.at[x, i, pl.ds(96, 32)], first=src.at[pl.ds(64, 64)])
        yield
        yield from ring_gather(w, me, "x", lambda i: out.at[i, :, pl.ds(64, 64)], lambda i: out.at[i, :, pl.ds(64, 32)],
                               lambda i: out.at[i, :, pl.ds(96, 32)])
    return [half_a(), half_b()]


def ag_xy(shard, cid, space=pl.ANY):
    C = shard.shape[1]

    def kernel(src, out, send, recv, lsem):
        me = Place()
        meet([me.step("x", 1), me.step("x", -1), me.step("y", 1), me.step("y", -1)])
        w = Wire(send, recv)
        lc = pltpu.make_async_copy(src, out.at[me.x, me.y], lsem)
        lc.start()
        lc.wait()
        run(ag_xy_gens(w, me, src, out))
        w.finish()

    return pl.pallas_call(
        kernel, out_shape=jax.ShapeDtypeStruct((4, 4, 128, C), shard.dtype),
        in_specs=[pl.BlockSpec(memory_space=space)], out_specs=pl.BlockSpec(memory_space=space),
        scratch_shapes=[pltpu.SemaphoreType.DMA((16,)), pltpu.SemaphoreType.DMA((16,)), pltpu.SemaphoreType.DMA],
        compiler_params=params(cid))(shard)


def rs_xy_scratch(C):
    return [VM((2, 2, 4, 32, C), bf16), VM((2, 2, 2, 4, 32, C), bf16),
            VM((2, 2, 32, C), bf16), VM((2, 2, 2, 32, C), bf16), VM((2, 4, 64, C), bf16)]


def rs_xy_gens(w, me, g, out, t1, r1, t2, r2, mid):
    x, y = me.x, me.y

    def half(k, first, second):
        base = k * 64
        if first == "y":
            pick = lambda i, o: g.at[:, i, pl.ds(base + o, 32)]
        else:
            pick = lambda i, o: g.at[i, :, pl.ds(base + o, 32)]
        yield from ring_scatter(w, me, first, lambda i: pick(i, 0), lambda i: pick(i, 32), t1.at[k, 0], t1.at[k, 1],
                                (r1.at[k, 0, 0], r1.at[k, 0, 1]), (r1.at[k, 1, 0], r1.at[k, 1, 1]), loop_add)
        p = me.pos(first)
        m = mid.at[k]
        for hh in range(2):
            own = pick(p, 32 * hh)

            def body(i, _):
                def inner(j, _):
                    s = pl.ds(pl.multiple_of(j * 16, 16), 16)
                    d = pl.ds(pl.multiple_of(j * 16 + 32 * hh, 16), 16)
                    v = own[i, s].astype(f32) + r1[k, 0, hh, i, s].astype(f32) + r1[k, 1, hh, i, s].astype(f32)
                    m[i, d] = v.astype(bf16)
                    return 0
                return lax.fori_loop(0, 2, inner, 0)
            lax.fori_loop(0, 4, body, 0)
        yield
        q = me.pos(second)
        add1 = lambda dst, a: loop_add(dst, a)
        pick2 = lambda i, o: mid.at[k, i, pl.ds(o, 32)]

        def add2(dst, a):
            def inner(j, _):
                s = pl.ds(pl.multiple_of(j * 16, 16), 16)
                dst[s] = (dst[s].astype(f32) + a[s].astype(f32)).astype(bf16)
                return 0
            lax.fori_loop(0, 2, inner, 0)
        yield from ring_scatter(w, me, second, lambda i: pick2(i, 0), lambda i: pick2(i, 32), t2.at[k, 0], t2.at[k, 1],
                                (r2.at[k, 0, 0], r2.at[k, 0, 1]), (r2.at[k, 1, 0], r2.at[k, 1, 1]), add2)
        for hh in range(2):
            def inner(j, _):
                s = pl.ds(pl.multiple_of(j * 16, 16), 16)
                d = pl.ds(pl.multiple_of(j * 16 + 32 * hh, 16), 16)
                dd = pl.ds(pl.multiple_of(j * 16 + 32 * hh + base, 16), 16)
                v = m[q, d].astype(f32) + r2[k, 0, hh, s].astype(f32) + r2[k, 1, hh, s].astype(f32)
                out[dd] = v.astype(out.dtype)
                return 0
            lax.fori_loop(0, 2, inner, 0)
    return [half(0, "y", "x"), half(1, "x", "y")]


def rs_xy(g, cid, out_dtype=f32):
    C = g.shape[-1]

    def kernel(gin, out, send, recv, *scr):
        me = Place()
        meet([me.step("x", 1), me.step("x", -1), me.step("y", 1), me.step("y", -1)])
        w = Wire(send, recv)
        run(rs_xy_gens(w, me, gin, out, *scr))
        w.finish()

    return pl.pallas_call(
        kernel, out_shape=jax.ShapeDtypeStruct((128, C), out_dtype),
        in_specs=[pl.BlockSpec(memory_space=VM)], out_specs=pl.BlockSpec(memory_space=VM),
        scratch_shapes=[pltpu.SemaphoreType.DMA((24,)), pltpu.SemaphoreType.DMA((24,))] + rs_xy_scratch(C),
        compiler_params=params(cid, 60))(g)


def ag_z_gen(w, me, src, out):
    sib = me.sibling()
    blk = lambda i, cc: out.at[lax.div(i, 2), cc, lax.rem(i, 2)]
    cs = []

    def to_sib(ref):
        cs.append(w.go(ref, ref, sib))
    whole = lambda i: blk(i, me.c)
    own = w.go(src, whole(me.z), sib)
    yield from ring_gather(w, me, "z", whole, lambda i: whole(i).at[pl.ds(0, 64)], lambda i: whole(i).at[pl.ds(64, 64)],
                           first=src, arrived=to_sib)
    own.wait_recv()
    for c in cs:
        c.wait_recv()


def ag_z(shard, cid, space=VM):
    C = shard.shape[1]

    def kernel(src, out, send, recv, lsem):
        me = Place()
        meet([me.step("z", 1), me.step("z", -1), me.sibling()])
        w = Wire(send, recv)
        lc = pltpu.make_async_copy(src, out.at[me.h, me.c, me.l], lsem)
        lc.start()
        lc.wait()
        run([ag_z_gen(w, me, src, out)])
        w.finish()

    return pl.pallas_call(
        kernel, out_shape=jax.ShapeDtypeStruct((2, 2, 2, 128, C), shard.dtype),
        in_specs=[pl.BlockSpec(memory_space=space)], out_specs=pl.BlockSpec(memory_space=space),
        scratch_shapes=[pltpu.SemaphoreType.DMA((16,)), pltpu.SemaphoreType.DMA((16,)), pltpu.SemaphoreType.DMA],
        compiler_params=params(cid))(shard)


def rs_z_scratch(C):
    return [VM((4, 128, C), bf16), VM((2, 64, C), bf16), VM((2, 2, 64, C), bf16)]


def rs_z_gen(w, me, g, out, sibs, t, r):
    sib = me.sibling()
    oc = 1 - me.c
    order = [2, 1, 3, 0]
    blk = lambda i, cc: g.at[lax.div(i, 2), cc, lax.rem(i, 2)]
    z = me.z
    sc = {}
    for o in order:
        i = m4(z + o)
        sc[o] = w.go(blk(i, oc), sibs.at[i], sib)
    yield

    def fold(o, s0, n):
        i = m4(z + o)
        b = blk(i, me.c)

        def inner(j, _):
            s = pl.ds(pl.multiple_of(j * 16 + s0, 16), 16)
            sibs[i, s] = (sibs[i, s].astype(f32) + b[s].astype(f32)).astype(bf16)
            return 0
        lax.fori_loop(0, n // 16, inner, 0)
    up, down = me.step("z", 1), me.step("z", -1)
    half = lambda o, k: sibs.at[m4(z + o), pl.ds(64 * k, 64)]
    sc[2].wait_recv()
    fold(2, 0, 64)
    ta = w.go(half(2, 0), t.at[0], up)
    fold(2, 64, 64)
    tb = w.go(half(2, 1), t.at[1], down)
    sc[1].wait_recv()
    fold(1, 64, 64)
    da = w.go(half(1, 1), r.at[0, 1], up)
    sc[3].wait_recv()
    fold(3, 0, 64)
    db = w.go(half(3, 0), r.at[1, 0], down)
    fold(1, 0, 64)
    fold(3, 64, 64)
    yield

    def add(dst, a):
        def inner(j, _):
            s = pl.ds(pl.multiple_of(j * 16, 16), 16)
            dst[s] = (dst[s].astype(f32) + a[s].astype(f32)).astype(bf16)
            return 0
        lax.fori_loop(0, 4, inner, 0)
    ta.wait_recv()
    add(t.at[0], half(1, 0))
    sa = w.go(t.at[0], r.at[0, 0], up)
    tb.wait_recv()
    add(t.at[1], half(3, 1))
    sb = w.go(t.at[1], r.at[1, 1], down)
    sc[0].wait_recv()
    own = blk(z, me.c)
    yield

    def last(hh):
        def inner(j, _):
            s = pl.ds(pl.multiple_of(j * 16, 16), 16)
            d = pl.ds(pl.multiple_of(j * 16 + 64 * hh, 16), 16)
            v = own[d].astype(f32) + sibs[z, d].astype(f32) + r[0, hh, s].astype(f32) + r[1, hh, s].astype(f32)
            out[d] = v.astype(out.dtype)
            return 0
        lax.fori_loop(0, 4, inner, 0)
    da.wait_recv()
    sa.wait_recv()
    db.wait_recv()
    sb.wait_recv()
    last(0)
    last(1)


def rs_z(g, cid, out_dtype=f32):
    C = g.shape[-1]

    def kernel(gin, out, send, recv, *scr):
        me = Place()
        meet([me.step("z", 1), me.step("z", -1), me.sibling()])
        w = Wire(send, recv)
        run([rs_z_gen(w, me, gin, out, *scr)])
        w.finish()

    return pl.pallas_call(
        kernel, out_shape=jax.ShapeDtypeStruct((128, C), out_dtype),
        in_specs=[pl.BlockSpec(memory_space=VM)], out_specs=pl.BlockSpec(memory_space=VM),
        scratch_shapes=[pltpu.SemaphoreType.DMA((16,)), pltpu.SemaphoreType.DMA((16,))] + rs_z_scratch(C),
        compiler_params=params(cid))(g)


def swap_devs(me):
    out = []
    for dh, dc in ((0, 1), (1, 0), (1, 1)):
        h = lax.rem(me.h + dh, 2)
        c = lax.rem(me.c + dc, 2)
        out.append((h * 2 + c, me.at(z=h * 2 + me.l, c=c)))
    return out


def swap_hc(parts, cid):
    n = len(parts)

    def kernel(*refs):
        ins, outs = refs[:n], refs[n:2 * n]
        send, recv, lsem = refs[2 * n:]
        me = Place()
        peers = swap_devs(me)
        meet([d for _, d in peers])
        w = Wire(send, recv)
        mine = me.h * 2 + me.c
        arrivals = []
        for j, d in reversed(peers):
            for a, b in zip(ins, outs):
                arrivals.append(w.go(a.at[j], b.at[mine], d))
        ls = []
        for k, (a, b) in enumerate(zip(ins, outs)):
            lc = pltpu.make_async_copy(a.at[mine], b.at[mine], lsem.at[k])
            lc.start()
            ls.append(lc)
        for lc in ls:
            lc.wait()
        for a in arrivals:
            a.wait_recv()
        w.finish()

    return pl.pallas_call(
        kernel, out_shape=[jax.ShapeDtypeStruct(p.shape, p.dtype) for p in parts],
        in_specs=[pl.BlockSpec(memory_space=VM)] * n, out_specs=[pl.BlockSpec(memory_space=VM)] * n,
        scratch_shapes=[pltpu.SemaphoreType.DMA((3 * n,)), pltpu.SemaphoreType.DMA((3 * n,)),
                        pltpu.SemaphoreType.DMA((n,))],
        compiler_params=params(cid))(*parts)


def sum_all(v, cid):
    R, C = v.shape

    def kernel(src, out, z_in, x_in, y_in, acc, send, recv):
        me = Place()
        zs = []
        for dz in range(4):
            for dc in range(2):
                if dz or dc:
                    z, c = m4(me.z + dz), lax.rem(me.c + dc, 2)
                    zs.append(me.at(z=z, c=c))
        xs = [me.step("x", d) for d in (1, 2, 3)]
        ys = [me.step("y", d) for d in (1, 2, 3)]
        meet(zs + xs + ys)
        w = Wire(send, recv)
        acc[...] = src[...]
        for buf, slot, devs, n in ((z_in, me.z * 2 + me.c, zs, 8), (x_in, me.x, xs, 4), (y_in, me.y, ys, 4)):
            buf[slot] = acc[...]
            cs = [w.go(buf.at[slot], buf.at[slot], d) for d in devs]
            for c in cs:
                c.wait_recv()
            total = buf[0]
            for k in range(1, n):
                total = total + buf[k]
            w.finish()
            acc[...] = total
        out[...] = acc[...]

    return pl.pallas_call(
        kernel, out_shape=jax.ShapeDtypeStruct((R, C), f32),
        in_specs=[pl.BlockSpec(memory_space=VM)], out_specs=pl.BlockSpec(memory_space=VM),
        scratch_shapes=[VM((8, R, C), f32), VM((4, R, C), f32), VM((4, R, C), f32), VM((R, C), f32),
                        pltpu.SemaphoreType.DMA((13,)), pltpu.SemaphoreType.DMA((13,))],
        compiler_params=params(cid))(v)


from jax.sharding import PartitionSpec as P

D = 2048
HD = 64
STEP = 10
SEQ = 256
PACKS = 4
ROWS = 1024
epsilon = 1e-06
rope_base = 1000000.0
beta_one = 0.9
beta_two = 0.999
adam_epsilon = 1e-08
weight_decay = 0.1
gain_rate = 0.3
masked_score = -1000000000.0
PLANE = [[x * 16 + y * 4 + k for x in range(4) for y in range(4)] for k in range(4)]


def rows_product(left, right):
    return lax.dot_general(left, right, (((0,), (0,)), ((), ())), preferred_element_type=f32)


def column_product(left, right):
    return lax.dot_general(left, right, (((1,), (1,)), ((), ())), preferred_element_type=f32)


def product(left, right):
    return jnp.dot(left, right, preferred_element_type=f32)


def norm_forward(values, gain):
    inverse = lax.rsqrt(jnp.mean(values * values, axis=-1, keepdims=True) + epsilon)
    return (values * inverse * gain, inverse)


def norm_backward(values, inverse, gain, upstream):
    scaled = upstream * gain
    inner = jnp.mean(values * scaled, axis=-1, keepdims=True)
    return (inverse * (scaled - values * inverse * inverse * inner), upstream * values * inverse)


def positions_of(rows):
    places = jnp.arange(SEQ, dtype=jnp.int32)[None, :]
    fresh = jnp.concatenate([jnp.ones((rows.shape[0], 1), jnp.bool_), rows[:, 1:] != rows[:, :-1]], axis=1)
    starts = jnp.where(fresh, places, 0)
    return places - lax.cummax(starts, axis=1)


def rope_tables(positions):
    half_dim = HD // 2
    frequency = rope_base ** (-2.0 * jnp.arange(half_dim, dtype=f32) / HD)
    angles = positions.astype(f32)[..., None] * frequency
    return (jnp.cos(angles), jnp.sin(angles))


def rotate(values, cosine, sine):
    front, back = values[..., : HD // 2], values[..., HD // 2 :]
    return jnp.concatenate([front * cosine - back * sine, back * cosine + front * sine], axis=-1)


def adam_step(weights_now, moment_now, square_now, gradient, step_rate, decay_rate):
    momentum = beta_one * moment_now + (1.0 - beta_one) * gradient
    variance = beta_two * square_now + (1.0 - beta_two) * gradient * gradient
    ratio = momentum / (1.0 - beta_one**STEP) / (jnp.sqrt(variance / (1.0 - beta_two**STEP)) + adam_epsilon)
    return (weights_now - step_rate * (ratio + decay_rate * weights_now), momentum, variance)


def split_out(parts):
    return jnp.concatenate([p.reshape(32, 4, -1) for p in parts], axis=2).transpose(1, 0, 2)


def join_back(whole, widths):
    out, at = [], 0
    for n in widths:
        out.append(whole[:, :, at : at + n].transpose(1, 0, 2).reshape(32, 4 * n))
        at += n
    return out


def gather_plane(shard):
    return lax.all_gather(shard, "dp", axis_index_groups=PLANE, axis=0, tiled=True)


def scatter_plane(whole):
    return lax.psum_scatter(whole, "dp", axis_index_groups=PLANE, scatter_dimension=0, tiled=True)


def gather_tokens(shard):
    return ag_z(shard, 3).reshape(ROWS, D)


def scatter_tokens(whole):
    return rs_z(whole.astype(bf16).reshape(2, 2, 2, 128, D), 4)


def local(
    block_input, output_grad, segment_ids, norm_gains, gain_moment, gain_square,
    query_weight, query_moment, query_square, key_weight, key_moment, key_square,
    value_weight, value_moment, value_square, output_weight, output_moment, output_square,
    gate_weight, gate_moment, gate_square, up_weight, up_moment, up_square,
    down_weight, down_moment, down_square,
):
    gain_one = norm_gains[:D]
    gain_two = norm_gains[D : 2 * D]
    gain_query = norm_gains[2 * D : 2 * D + HD]
    gain_key = norm_gains[2 * D + HD :]
    low = lambda w: w.astype(bf16)
    front_out = split_out([low(query_weight), low(key_weight), low(value_weight), low(output_weight)])
    rest_out = split_out([low(gate_weight), low(up_weight), low(down_weight)])
    segment_out = jnp.broadcast_to(segment_ids[None], (4, 8, SEQ))
    front_shard, rest_shard, segments = swap_hc([front_out, rest_out, segment_out], 1)
    front_full = gather_plane(front_shard.reshape(128, 640))
    rest_full = gather_plane(rest_shard.reshape(128, 3072))
    qkv_full, output_full = front_full[:, :384], front_full[:, 384:]
    gate_up_full, down_full = rest_full[:, :2048], rest_full[:, 2048:]

    rows_in = block_input.astype(f32)
    normed_one, inverse_one = norm_forward(rows_in, gain_one)
    gathered_one = gather_tokens(normed_one.astype(bf16))
    gathered_cot = gather_tokens(output_grad)

    packs = segments[:, 0, :]
    cosine, sine = rope_tables(positions_of(packs))
    places = jnp.arange(SEQ, dtype=jnp.int32)
    allowed = (packs[:, :, None] == packs[:, None, :]) & (places[None, None, :] <= places[None, :, None])
    score_scale = HD ** (-0.5)

    qkv = product(gathered_one, qkv_full)
    query_pre = qkv[:, :256].reshape(PACKS, SEQ, 4, HD)
    key_pre = qkv[:, 256:320].reshape(PACKS, SEQ, HD)
    value_low = qkv[:, 320:].astype(bf16).reshape(PACKS, SEQ, HD)
    query_normed, query_inverse = norm_forward(query_pre, gain_query)
    key_normed, key_inverse = norm_forward(key_pre, gain_key)
    query_rot = rotate(query_normed, cosine[:, :, None, :], sine[:, :, None, :]).astype(bf16)
    key_rot = rotate(key_normed, cosine, sine).astype(bf16)
    scores = jnp.einsum("pqjd,pkd->pjqk", query_rot, key_rot, preferred_element_type=f32) * score_scale
    scores = jnp.where(allowed[:, None], scores, masked_score)
    exps = jnp.exp(scores - jnp.max(scores, axis=-1, keepdims=True))
    probs = exps / jnp.sum(exps, axis=-1, keepdims=True)
    probs_low = probs.astype(bf16)
    mixed = jnp.einsum("pjqk,pkd->pqjd", probs_low, value_low, preferred_element_type=f32)
    mixed_low = mixed.astype(bf16).reshape(ROWS, 256)

    middle = rows_in + scatter_tokens(column_product(mixed_low, output_full))
    normed_two, inverse_two = norm_forward(middle, gain_two)
    gathered_two = gather_tokens(normed_two.astype(bf16))
    gate_up = product(gathered_two, gate_up_full)
    gate_pre, up_pre = gate_up[:, :1024], gate_up[:, 1024:]
    sigmoid_gate = jax.nn.sigmoid(gate_pre)
    silu_gate = gate_pre * sigmoid_gate
    hidden_low = (silu_gate * up_pre).astype(bf16)

    hidden_grad = product(gathered_cot, down_full)
    up_low = (hidden_grad * silu_gate).astype(bf16)
    gate_low = (hidden_grad * up_pre * (sigmoid_gate + silu_gate * (1.0 - sigmoid_gate))).astype(bf16)
    gate_up_low = jnp.concatenate([gate_low, up_low], axis=1)
    gate_up_grad = rows_product(gathered_two, gate_up_low)
    down_grad = rows_product(gathered_cot, hidden_low)
    rest_grad = jnp.concatenate([gate_up_grad.astype(bf16), down_grad.astype(bf16)], axis=1)
    rest_mine = scatter_plane(rest_grad)

    normed_two_grad = scatter_tokens(column_product(gate_up_low, gate_up_full))
    block_output = middle + scatter_tokens(column_product(hidden_low, down_full))
    middle_back, gain_two_terms = norm_backward(middle, inverse_two, gain_two, normed_two_grad)
    middle_grad = output_grad.astype(f32) + middle_back
    gathered_attn = gather_tokens(middle_grad.astype(bf16))
    mixed_grad = product(gathered_attn, output_full).astype(bf16).reshape(PACKS, SEQ, 4, HD)
    output_weight_grad = rows_product(gathered_attn, mixed_low)

    prob_grad = jnp.einsum("pqjd,pkd->pjqk", mixed_grad, value_low, preferred_element_type=f32)
    inner_term = jnp.sum(probs * prob_grad, axis=-1, keepdims=True)
    score_grad = (probs * (prob_grad - inner_term)).astype(bf16)
    query_rot_grad = jnp.einsum("pjqk,pkd->pqjd", score_grad, key_rot, preferred_element_type=f32) * score_scale
    key_rot_grad = jnp.einsum("pjqk,pqjd->pkd", score_grad, query_rot, preferred_element_type=f32) * score_scale
    value_grad = jnp.einsum("pjqk,pqjd->pkd", probs_low, mixed_grad, preferred_element_type=f32).astype(bf16)
    query_pre_grad, gain_query_terms = norm_backward(
        query_pre, query_inverse, gain_query, rotate(query_rot_grad, cosine[:, :, None, :], -sine[:, :, None, :])
    )
    key_pre_grad, gain_key_terms = norm_backward(key_pre, key_inverse, gain_key, rotate(key_rot_grad, cosine, -sine))
    qkv_low = jnp.concatenate(
        [query_pre_grad.astype(bf16).reshape(ROWS, 256), key_pre_grad.astype(bf16).reshape(ROWS, HD),
         value_grad.reshape(ROWS, HD)], axis=1
    )
    qkv_grad = rows_product(gathered_one, qkv_low)
    front_grad = jnp.concatenate([qkv_grad.astype(bf16), output_weight_grad.astype(bf16)], axis=1)
    front_mine = scatter_plane(front_grad)
    normed_one_grad = scatter_tokens(column_product(qkv_low, qkv_full))
    input_back, gain_one_terms = norm_backward(rows_in, inverse_one, gain_one, normed_one_grad)
    input_grad = middle_grad + input_back

    gain_local = jnp.concatenate(
        [jnp.sum(gain_one_terms, axis=0), jnp.sum(gain_two_terms, axis=0),
         jnp.sum(gain_query_terms, axis=(0, 1, 2)), jnp.sum(gain_key_terms, axis=(0, 1))]
    )
    gain_grads = sum_all(gain_local.reshape(33, 128), 5).reshape(-1)

    front_back, rest_back = swap_hc([front_mine.reshape(4, 32, 640), rest_mine.reshape(4, 32, 3072)], 2)
    sums = join_back(front_back.astype(f32), (256, 64, 64, 256)) + join_back(rest_back.astype(f32), (1024, 1024, 1024))
    results = [block_output, input_grad]
    results += adam_step(norm_gains, gain_moment, gain_square, gain_grads, gain_rate, 0.0)
    states = (
        (query_weight, query_moment, query_square, 0.04), (key_weight, key_moment, key_square, 0.04),
        (value_weight, value_moment, value_square, 0.04), (output_weight, output_moment, output_square, 0.15),
        (gate_weight, gate_moment, gate_square, 0.04), (up_weight, up_moment, up_square, 0.04),
        (down_weight, down_moment, down_square, 0.02),
    )
    for (w, m, v, rate), grad in zip(states, sums):
        results += adam_step(w, m, v, grad, rate, weight_decay)
    return tuple(results)


def solution(mesh):
    tokens, weight = P(("dp", "tensor"), None), P("dp", "tensor")
    in_specs = (tokens, tokens, P("dp", None), P(), P(), P()) + (weight,) * 21
    out_specs = (tokens, tokens, P(), P(), P()) + (weight,) * 21
    return jax.shard_map(local, mesh=mesh, in_specs=in_specs, out_specs=out_specs, check_vma=False)
```

```python
import jax
import jax.numpy as jnp
import numpy as np
from jax import lax
from jax.experimental import pallas as pl
from jax.experimental.pallas import tpu as pltpu

MESH = pl.DeviceIdType.MESH
VM = pltpu.VMEM
bf16 = jnp.bfloat16
f32 = jnp.float32


def m4(v):
    return lax.rem(v + 4, 4)


class Place:
    def __init__(self):
        dp = lax.axis_index("dp")
        self.l = lax.axis_index("tensor")
        self.x = lax.div(dp, 16)
        self.y = lax.rem(lax.div(dp, 4), 4)
        self.h = lax.rem(lax.div(dp, 2), 2)
        self.c = lax.rem(dp, 2)
        self.z = self.h * 2 + self.l

    def at(self, x=None, y=None, z=None, c=None):
        x = self.x if x is None else x
        y = self.y if y is None else y
        z = self.z if z is None else z
        c = self.c if c is None else c
        return (x * 16 + y * 4 + lax.div(z, 2) * 2 + c, lax.rem(z, 2))

    def pos(self, axis):
        return {"x": self.x, "y": self.y, "z": self.z}[axis]

    def step(self, axis, d):
        return self.at(**{axis: m4(self.pos(axis) + d)})

    def sibling(self):
        return self.at(c=1 - self.c)


class Wire:
    def __init__(self, send, recv):
        self.send, self.recv, self.n = send, recv, 0
        self.pending = []

    def go(self, src, dst, dev):
        i = self.n
        self.n += 1
        c = pltpu.make_async_remote_copy(
            src_ref=src, dst_ref=dst, send_sem=self.send.at[i], recv_sem=self.recv.at[i],
            device_id=dev, device_id_type=MESH)
        c.start()
        self.pending.append(c)
        return c

    def finish(self):
        for c in self.pending:
            c.wait_send()
        self.pending = []


def meet(devs):
    b = pltpu.get_barrier_semaphore()
    for d in devs:
        pl.semaphore_signal(b, inc=1, device_id=d, device_id_type=MESH)
    pl.semaphore_wait(b, len(devs))


def ring_gather(w, me, axis, whole, lo, hi, first=None, arrived=None):
    p = me.pos(axis)
    up, down = me.step(axis, 1), me.step(axis, -1)
    own = whole(p) if first is None else first
    a = w.go(own, whole(p), up)
    b = w.go(own, whole(p), down)
    yield
    a.wait_recv()
    fa = w.go(lo(m4(p - 1)), lo(m4(p - 1)), up)
    if arrived:
        arrived(whole(m4(p - 1)))
    b.wait_recv()
    fb = w.go(hi(m4(p + 1)), hi(m4(p + 1)), down)
    if arrived:
        arrived(whole(m4(p + 1)))
    yield
    fa.wait_recv()
    if arrived:
        arrived(lo(m4(p - 2)))
    fb.wait_recv()
    if arrived:
        arrived(hi(m4(p - 2)))


def ring_scatter(w, me, axis, lo, hi, tlo, thi, rup, rdown, add):
    p = me.pos(axis)
    up, down = me.step(axis, 1), me.step(axis, -1)
    far, nu, nd = m4(p + 2), m4(p + 1), m4(p - 1)
    ta = w.go(lo(far), tlo, up)
    tb = w.go(hi(far), thi, down)
    da = w.go(hi(nu), rup[1], up)
    db = w.go(lo(nd), rdown[0], down)
    yield
    ta.wait_recv()
    add(tlo, lo(nu))
    sa = w.go(tlo, rup[0], up)
    tb.wait_recv()
    add(thi, hi(nd))
    sb = w.go(thi, rdown[1], down)
    yield
    da.wait_recv()
    db.wait_recv()
    sa.wait_recv()
    sb.wait_recv()


def loop_add(dst, a, b=None, rows=16):
    n = dst.shape[0]

    def body(i, _):
        def inner(j, _):
            s = pl.ds(pl.multiple_of(j * rows, rows), rows)
            v = dst[i, s].astype(f32) + a[i, s].astype(f32)
            if b is not None:
                v = v + b[i, s].astype(f32)
            dst[i, s] = v.astype(dst.dtype)
            return 0
        return lax.fori_loop(0, dst.shape[1] // rows, inner, 0)
    lax.fori_loop(0, n, body, 0)


def run(gens):
    gens = list(gens)
    while gens:
        for g in list(gens):
            try:
                next(g)
            except StopIteration:
                gens.remove(g)


def params(cid, mb=56):
    return pltpu.CompilerParams(collective_id=cid, has_side_effects=True, vmem_limit_bytes=mb * 2**20)


def ag_xy_gens(w, me, src, out):
    H = 64
    x, y = me.x, me.y

    def half_a():
        yield from ring_gather(w, me, "x", lambda i: out.at[i, y, pl.ds(0, 64)], lambda i: out.at[i, y, pl.ds(0, 32)],
                               lambda i: out.at[i, y, pl.ds(32, 32)], first=src.at[pl.ds(0, 64)])
        yield
        yield from ring_gather(w, me, "y", lambda i: out.at[:, i, pl.ds(0, 64)], lambda i: out.at[:, i, pl.ds(0, 32)],
                               lambda i: out.at[:, i, pl.ds(32, 32)])

    def half_b():
        yield from ring_gather(w, me, "y", lambda i: out.at[x, i, pl.ds(64, 64)], lambda i: out.at[x, i, pl.ds(64, 32)],
                               lambda i: out.at[x, i, pl.ds(96, 32)], first=src.at[pl.ds(64, 64)])
        yield
        yield from ring_gather(w, me, "x", lambda i: out.at[i, :, pl.ds(64, 64)], lambda i: out.at[i, :, pl.ds(64, 32)],
                               lambda i: out.at[i, :, pl.ds(96, 32)])
    return [half_a(), half_b()]


def ag_xy(shard, cid, space=pl.ANY):
    C = shard.shape[1]

    def kernel(src, out, send, recv, lsem):
        me = Place()
        meet([me.step("x", 1), me.step("x", -1), me.step("y", 1), me.step("y", -1)])
        w = Wire(send, recv)
        lc = pltpu.make_async_copy(src, out.at[me.x, me.y], lsem)
        lc.start()
        lc.wait()
        run(ag_xy_gens(w, me, src, out))
        w.finish()

    return pl.pallas_call(
        kernel, out_shape=jax.ShapeDtypeStruct((4, 4, 128, C), shard.dtype),
        in_specs=[pl.BlockSpec(memory_space=space)], out_specs=pl.BlockSpec(memory_space=space),
        scratch_shapes=[pltpu.SemaphoreType.DMA((16,)), pltpu.SemaphoreType.DMA((16,)), pltpu.SemaphoreType.DMA],
        compiler_params=params(cid))(shard)


def rs_xy_scratch(C):
    return [VM((2, 2, 4, 32, C), bf16), VM((2, 2, 2, 4, 32, C), bf16),
            VM((2, 2, 32, C), bf16), VM((2, 2, 2, 32, C), bf16), VM((2, 4, 64, C), bf16)]


def rs_xy_gens(w, me, g, out, t1, r1, t2, r2, mid):
    x, y = me.x, me.y

    def half(k, first, second):
        base = k * 64
        if first == "y":
            pick = lambda i, o: g.at[:, i, pl.ds(base + o, 32)]
        else:
            pick = lambda i, o: g.at[i, :, pl.ds(base + o, 32)]
        yield from ring_scatter(w, me, first, lambda i: pick(i, 0), lambda i: pick(i, 32), t1.at[k, 0], t1.at[k, 1],
                                (r1.at[k, 0, 0], r1.at[k, 0, 1]), (r1.at[k, 1, 0], r1.at[k, 1, 1]), loop_add)
        p = me.pos(first)
        m = mid.at[k]
        for hh in range(2):
            own = pick(p, 32 * hh)

            def body(i, _):
                def inner(j, _):
                    s = pl.ds(pl.multiple_of(j * 16, 16), 16)
                    d = pl.ds(pl.multiple_of(j * 16 + 32 * hh, 16), 16)
                    v = own[i, s].astype(f32) + r1[k, 0, hh, i, s].astype(f32) + r1[k, 1, hh, i, s].astype(f32)
                    m[i, d] = v.astype(bf16)
                    return 0
                return lax.fori_loop(0, 2, inner, 0)
            lax.fori_loop(0, 4, body, 0)
        yield
        q = me.pos(second)
        add1 = lambda dst, a: loop_add(dst, a)
        pick2 = lambda i, o: mid.at[k, i, pl.ds(o, 32)]

        def add2(dst, a):
            def inner(j, _):
                s = pl.ds(pl.multiple_of(j * 16, 16), 16)
                dst[s] = (dst[s].astype(f32) + a[s].astype(f32)).astype(bf16)
                return 0
            lax.fori_loop(0, 2, inner, 0)
        yield from ring_scatter(w, me, second, lambda i: pick2(i, 0), lambda i: pick2(i, 32), t2.at[k, 0], t2.at[k, 1],
                                (r2.at[k, 0, 0], r2.at[k, 0, 1]), (r2.at[k, 1, 0], r2.at[k, 1, 1]), add2)
        for hh in range(2):
            def inner(j, _):
                s = pl.ds(pl.multiple_of(j * 16, 16), 16)
                d = pl.ds(pl.multiple_of(j * 16 + 32 * hh, 16), 16)
                dd = pl.ds(pl.multiple_of(j * 16 + 32 * hh + base, 16), 16)
                v = m[q, d].astype(f32) + r2[k, 0, hh, s].astype(f32) + r2[k, 1, hh, s].astype(f32)
                out[dd] = v.astype(out.dtype)
                return 0
            lax.fori_loop(0, 2, inner, 0)
    return [half(0, "y", "x"), half(1, "x", "y")]


def rs_xy(g, cid, out_dtype=f32):
    C = g.shape[-1]

    def kernel(gin, out, send, recv, *scr):
        me = Place()
        meet([me.step("x", 1), me.step("x", -1), me.step("y", 1), me.step("y", -1)])
        w = Wire(send, recv)
        run(rs_xy_gens(w, me, gin, out, *scr))
        w.finish()

    return pl.pallas_call(
        kernel, out_shape=jax.ShapeDtypeStruct((128, C), out_dtype),
        in_specs=[pl.BlockSpec(memory_space=VM)], out_specs=pl.BlockSpec(memory_space=VM),
        scratch_shapes=[pltpu.SemaphoreType.DMA((24,)), pltpu.SemaphoreType.DMA((24,))] + rs_xy_scratch(C),
        compiler_params=params(cid, 60))(g)


def ag_z_gen(w, me, src, out):
    sib = me.sibling()
    blk = lambda i, cc: out.at[lax.div(i, 2), cc, lax.rem(i, 2)]
    cs = []

    def to_sib(ref):
        cs.append(w.go(ref, ref, sib))
    whole = lambda i: blk(i, me.c)
    own = w.go(src, whole(me.z), sib)
    yield from ring_gather(w, me, "z", whole, lambda i: whole(i).at[pl.ds(0, 64)], lambda i: whole(i).at[pl.ds(64, 64)],
                           first=src, arrived=to_sib)
    own.wait_recv()
    for c in cs:
        c.wait_recv()


def ag_z(shard, cid, space=VM):
    C = shard.shape[1]

    def kernel(src, out, send, recv, lsem):
        me = Place()
        meet([me.step("z", 1), me.step("z", -1), me.sibling()])
        w = Wire(send, recv)
        lc = pltpu.make_async_copy(src, out.at[me.h, me.c, me.l], lsem)
        lc.start()
        lc.wait()
        run([ag_z_gen(w, me, src, out)])
        w.finish()

    return pl.pallas_call(
        kernel, out_shape=jax.ShapeDtypeStruct((2, 2, 2, 128, C), shard.dtype),
        in_specs=[pl.BlockSpec(memory_space=space)], out_specs=pl.BlockSpec(memory_space=space),
        scratch_shapes=[pltpu.SemaphoreType.DMA((16,)), pltpu.SemaphoreType.DMA((16,)), pltpu.SemaphoreType.DMA],
        compiler_params=params(cid))(shard)


def rs_z_scratch(C):
    return [VM((4, 128, C), bf16), VM((2, 64, C), bf16), VM((2, 2, 64, C), bf16)]


def rs_z_gen(w, me, g, out, sibs, t, r):
    sib = me.sibling()
    oc = 1 - me.c
    order = [2, 1, 3, 0]
    blk = lambda i, cc: g.at[lax.div(i, 2), cc, lax.rem(i, 2)]
    z = me.z
    sc = {}
    for o in order:
        i = m4(z + o)
        sc[o] = w.go(blk(i, oc), sibs.at[i], sib)
    yield

    def fold(o, s0, n):
        i = m4(z + o)
        b = blk(i, me.c)

        def inner(j, _):
            s = pl.ds(pl.multiple_of(j * 16 + s0, 16), 16)
            sibs[i, s] = (sibs[i, s].astype(f32) + b[s].astype(f32)).astype(bf16)
            return 0
        lax.fori_loop(0, n // 16, inner, 0)
    up, down = me.step("z", 1), me.step("z", -1)
    half = lambda o, k: sibs.at[m4(z + o), pl.ds(64 * k, 64)]
    sc[2].wait_recv()
    fold(2, 0, 64)
    ta = w.go(half(2, 0), t.at[0], up)
    fold(2, 64, 64)
    tb = w.go(half(2, 1), t.at[1], down)
    sc[1].wait_recv()
    fold(1, 64, 64)
    da = w.go(half(1, 1), r.at[0, 1], up)
    sc[3].wait_recv()
    fold(3, 0, 64)
    db = w.go(half(3, 0), r.at[1, 0], down)
    fold(1, 0, 64)
    fold(3, 64, 64)
    yield

    def add(dst, a):
        def inner(j, _):
            s = pl.ds(pl.multiple_of(j * 16, 16), 16)
            dst[s] = (dst[s].astype(f32) + a[s].astype(f32)).astype(bf16)
            return 0
        lax.fori_loop(0, 4, inner, 0)
    ta.wait_recv()
    add(t.at[0], half(1, 0))
    sa = w.go(t.at[0], r.at[0, 0], up)
    tb.wait_recv()
    add(t.at[1], half(3, 1))
    sb = w.go(t.at[1], r.at[1, 1], down)
    sc[0].wait_recv()
    own = blk(z, me.c)
    yield

    def last(hh):
        def inner(j, _):
            s = pl.ds(pl.multiple_of(j * 16, 16), 16)
            d = pl.ds(pl.multiple_of(j * 16 + 64 * hh, 16), 16)
            v = own[d].astype(f32) + sibs[z, d].astype(f32) + r[0, hh, s].astype(f32) + r[1, hh, s].astype(f32)
            out(d, v)
            return 0
        lax.fori_loop(0, 4, inner, 0)
    da.wait_recv()
    sa.wait_recv()
    db.wait_recv()
    sb.wait_recv()
    last(0)
    last(1)


def rs_z(g, cid, out_dtype=f32):
    C = g.shape[-1]

    def kernel(gin, out, send, recv, *scr):
        me = Place()
        meet([me.step("z", 1), me.step("z", -1), me.sibling()])
        w = Wire(send, recv)

        def put(s, v):
            out[s] = v.astype(out.dtype)
        run([rs_z_gen(w, me, gin, put, *scr)])
        w.finish()

    return pl.pallas_call(
        kernel, out_shape=jax.ShapeDtypeStruct((128, C), out_dtype),
        in_specs=[pl.BlockSpec(memory_space=VM)], out_specs=pl.BlockSpec(memory_space=VM),
        scratch_shapes=[pltpu.SemaphoreType.DMA((16,)), pltpu.SemaphoreType.DMA((16,))] + rs_z_scratch(C),
        compiler_params=params(cid))(g)


def swap_devs(me):
    out = []
    for dh, dc in ((0, 1), (1, 0), (1, 1)):
        h = lax.rem(me.h + dh, 2)
        c = lax.rem(me.c + dc, 2)
        out.append((h * 2 + c, me.at(z=h * 2 + me.l, c=c)))
    return out


def swap_hc(parts, cid):
    n = len(parts)

    def kernel(*refs):
        ins, outs = refs[:n], refs[n:2 * n]
        send, recv, lsem = refs[2 * n:]
        me = Place()
        peers = swap_devs(me)
        meet([d for _, d in peers])
        w = Wire(send, recv)
        mine = me.h * 2 + me.c
        arrivals = []
        for j, d in reversed(peers):
            for a, b in zip(ins, outs):
                arrivals.append(w.go(a.at[j], b.at[mine], d))
        ls = []
        for k, (a, b) in enumerate(zip(ins, outs)):
            lc = pltpu.make_async_copy(a.at[mine], b.at[mine], lsem.at[k])
            lc.start()
            ls.append(lc)
        for lc in ls:
            lc.wait()
        for a in arrivals:
            a.wait_recv()
        w.finish()

    return pl.pallas_call(
        kernel, out_shape=[jax.ShapeDtypeStruct(p.shape, p.dtype) for p in parts],
        in_specs=[pl.BlockSpec(memory_space=VM)] * n, out_specs=[pl.BlockSpec(memory_space=VM)] * n,
        scratch_shapes=[pltpu.SemaphoreType.DMA((3 * n,)), pltpu.SemaphoreType.DMA((3 * n,)),
                        pltpu.SemaphoreType.DMA((n,))],
        compiler_params=params(cid))(*parts)


def sum_all(v, cid):
    R, C = v.shape

    def kernel(src, out, z_in, x_in, y_in, acc, send, recv):
        me = Place()
        zs = []
        for dz in range(4):
            for dc in range(2):
                if dz or dc:
                    z, c = m4(me.z + dz), lax.rem(me.c + dc, 2)
                    zs.append(me.at(z=z, c=c))
        xs = [me.step("x", d) for d in (1, 2, 3)]
        ys = [me.step("y", d) for d in (1, 2, 3)]
        meet(zs + xs + ys)
        w = Wire(send, recv)
        acc[...] = src[...]
        for buf, slot, devs, n in ((z_in, me.z * 2 + me.c, zs, 8), (x_in, me.x, xs, 4), (y_in, me.y, ys, 4)):
            buf[slot] = acc[...]
            cs = [w.go(buf.at[slot], buf.at[slot], d) for d in devs]
            for c in cs:
                c.wait_recv()
            total = buf[0]
            for k in range(1, n):
                total = total + buf[k]
            w.finish()
            acc[...] = total
        out[...] = acc[...]

    return pl.pallas_call(
        kernel, out_shape=jax.ShapeDtypeStruct((R, C), f32),
        in_specs=[pl.BlockSpec(memory_space=VM)], out_specs=pl.BlockSpec(memory_space=VM),
        scratch_shapes=[VM((8, R, C), f32), VM((4, R, C), f32), VM((4, R, C), f32), VM((R, C), f32),
                        pltpu.SemaphoreType.DMA((13,)), pltpu.SemaphoreType.DMA((13,))],
        compiler_params=params(cid))(v)


D = 2048
HD = 64
STEP = 10
SEQ = 256
PACKS = 4
ROWS = 1024
epsilon = 1e-06
rope_base = 1000000.0
beta_one = 0.9
beta_two = 0.999
adam_epsilon = 1e-08
weight_decay = 0.1
gain_rate = 0.3
masked_score = -1000000000.0
score_scale = HD ** (-0.5)
exact = lax.Precision.HIGHEST


def dot(a, b, ca=1, cb=0, precision=None):
    return lax.dot_general(a, b, (((ca,), (cb,)), ((), ())), precision=precision, preferred_element_type=f32)


def chunks(n, body, rows=16):
    def one(j, _):
        body(pl.ds(pl.multiple_of(j * rows, rows), rows))
        return 0
    lax.fori_loop(0, n // rows, one, 0)


def dma_sems(n):
    return [pltpu.SemaphoreType.DMA((n,)), pltpu.SemaphoreType.DMA((n,))]


def vm_specs(n):
    return [pl.BlockSpec(memory_space=VM)] * n


def any_specs(n):
    return [pl.BlockSpec(memory_space=pl.ANY)] * n


def spread_weights(weights, segments, cid):
    def kernel(q, k, v, o, g, u, d, seg, front, rest, segs, fbuf, rbuf, sbuf, send, recv):
        me = Place()
        peers = swap_devs(me)
        mine = me.h * 2 + me.c
        for j in range(4):
            fbuf[j, :, 0:256] = q[:, 256 * j:256 * j + 256].astype(bf16)
            fbuf[j, :, 256:384] = jnp.concatenate(
                [k[:, 64 * j:64 * j + 64], v[:, 64 * j:64 * j + 64]], axis=1).astype(bf16)
            fbuf[j, :, 384:640] = o[:, 256 * j:256 * j + 256].astype(bf16)
            for i, w in enumerate((g, u, d)):
                rbuf[j, :, 1024 * i:1024 * i + 1024] = w[:, 1024 * j:1024 * j + 1024].astype(bf16)
        sbuf[...] = jnp.broadcast_to(seg[...], (8, SEQ))
        meet([dev for _, dev in peers])
        w = Wire(send, recv)
        arrivals = []
        for j, dev in reversed(peers):
            arrivals.append(w.go(rbuf.at[j], rest.at[mine], dev))
            arrivals.append(w.go(fbuf.at[j], front.at[mine], dev))
            arrivals.append(w.go(sbuf, segs.at[mine], dev))
        front[mine] = fbuf[mine]
        rest[mine] = rbuf[mine]
        segs[mine] = sbuf[...]
        for a in arrivals:
            a.wait_recv()
        w.finish()

    return pl.pallas_call(
        kernel,
        out_shape=[jax.ShapeDtypeStruct((4, 32, 640), bf16), jax.ShapeDtypeStruct((4, 32, 3072), bf16),
                   jax.ShapeDtypeStruct((4, 8, SEQ), jnp.int32)],
        in_specs=vm_specs(8), out_specs=vm_specs(3),
        scratch_shapes=[VM((4, 32, 640), bf16), VM((4, 32, 3072), bf16), VM((8, SEQ), jnp.int32)] + dma_sems(9),
        compiler_params=params(cid))(*weights, segments)


def rope_constants():
    frequency = np.float32(rope_base) ** (np.float32(-2.0) * np.arange(HD // 2, dtype=np.float32) / np.float32(HD))
    angles = (np.arange(SEQ, dtype=np.float32)[None, :] * frequency[:, None].astype(np.float32)).astype(np.float64)
    return np.concatenate([np.cos(angles), np.sin(angles)], axis=0).astype(np.float32)


def pack_tables(segs, p, table):
    row = segs[p].astype(f32)[0:1, :]
    column = jnp.broadcast_to(row, (128, SEQ)).T[:, 0:1]
    key_at = lax.broadcasted_iota(jnp.int32, (SEQ, SEQ), 0)
    query_at = lax.broadcasted_iota(jnp.int32, (SEQ, SEQ), 1)
    allowed = (column == row) & (key_at <= query_at)
    start = jnp.sum(jnp.where(column < row, 1.0, 0.0), axis=0, keepdims=True)
    where = query_at.astype(f32) - start
    hot = jnp.where(key_at.astype(f32) == where, 1.0, 0.0)
    both = dot(table[...], hot, precision=exact)
    return allowed, both[0:32], both[32:64]


def head_norm(z, gain):
    inverse = lax.rsqrt(jnp.mean(z * z, axis=0, keepdims=True) + epsilon)
    return z * inverse * gain, inverse


def head_norm_back(z, inverse, gain, up):
    scaled = up * gain
    inner = jnp.mean(z * scaled, axis=0, keepdims=True)
    return inverse * (scaled - z * inverse * inverse * inner), up * z * inverse


def turn(u, cosine, sine):
    a, b = u[0:32], u[32:64]
    return jnp.concatenate([a * cosine - b * sine, b * cosine + a * sine], axis=0)


def turn_back(u, cosine, sine):
    a, b = u[0:32], u[32:64]
    return jnp.concatenate([a * cosine + b * sine, b * cosine - a * sine], axis=0)


def pack_probs(key_rows, query_rot, allowed):
    scores = jnp.where(allowed, dot(key_rows, query_rot) * score_scale, masked_score)
    exps = jnp.exp(scores - jnp.max(scores, axis=0, keepdims=True))
    return exps / jnp.sum(exps, axis=0, keepdims=True)


def pack_of(ref, p):
    v = ref[lax.div(p, 2), lax.rem(p, 2)]
    return v.reshape(SEQ, v.shape[-1])


def attention_forward(x, cot, front, segs, gain_one, gain_two, gain_query, gain_key, table, cid):
    def kernel(x, cot, front, segs, gain_one, gain_two, gain_query, gain_key, table,
               a_full, cot_full, n_full, front_full, qk_pre, v_rows, mixed, middle,
               shard, shard_two, a_buf, part, sibs, t, r, send, recv, lsem):
        me = Place()

        def norm_one(s):
            v = x[s].astype(f32)
            inverse = lax.rsqrt(jnp.mean(v * v, axis=-1, keepdims=True) + epsilon)
            shard[s] = (v * inverse * gain_one[...]).astype(bf16)
        chunks(128, norm_one)
        meet([me.step("x", 1), me.step("x", -1), me.step("y", 1), me.step("y", -1),
              me.step("z", 1), me.step("z", -1), me.sibling()])
        w = Wire(send, recv)
        locals_ = [pltpu.make_async_copy(front, front_full.at[me.x, me.y], lsem.at[0]),
                   pltpu.make_async_copy(shard, a_buf.at[me.h, me.c, me.l], lsem.at[1]),
                   pltpu.make_async_copy(cot, cot_full.at[me.h, me.c, me.l], lsem.at[2])]
        gens = ag_xy_gens(w, me, front, front_full) + [ag_z_gen(w, me, shard, a_buf)]
        for g in gens:
            next(g)
        for c in locals_:
            c.start()
        for c in locals_:
            c.wait()
        run(gens)
        cot_gen = ag_z_gen(w, me, cot, cot_full)
        next(cot_gen)
        keep = pltpu.make_async_copy(a_buf, a_full, lsem.at[4])
        keep.start()

        def one_pack(p, _):
            allowed, cosine, sine = pack_tables(segs, p, table)
            weights = front_full[...].reshape(D, 640)
            qkv = dot(pack_of(a_buf, p), weights[:, 0:384]).T
            qk_pre[p] = qkv[0:320]
            value = qkv[320:384].astype(bf16)
            v_rows[p] = value
            kn, _i = head_norm(qkv[256:320], gain_key[...])
            key_rows = turn(kn, cosine, sine).T.astype(bf16)
            heads = []
            for j in range(4):
                qn, _i = head_norm(qkv[64 * j:64 * j + 64], gain_query[...])
                probs = pack_probs(key_rows, turn(qn, cosine, sine).astype(bf16), allowed)
                heads.append(dot(value, probs.astype(bf16)))
            o = jnp.concatenate(heads, axis=0).T.astype(bf16)
            mixed[p] = o
            out = dot(o, weights[:, 384:640], 1, 1).astype(bf16)
            part[lax.div(p, 2), lax.rem(p, 2)] = out.reshape(2, 128, D)
            return 0
        lax.fori_loop(0, PACKS, one_pack, 0)
        next(cot_gen)

        def residual(s, v):
            middle[s] = x[s].astype(f32) + v
        run([rs_z_gen(w, me, part, residual, sibs, t, r)])

        def norm_two(s):
            v = middle[s]
            inverse = lax.rsqrt(jnp.mean(v * v, axis=-1, keepdims=True) + epsilon)
            shard_two[s] = (v * inverse * gain_two[...]).astype(bf16)
        chunks(128, norm_two)
        n_gen = ag_z_gen(w, me, shard_two, n_full)
        next(n_gen)
        own = pltpu.make_async_copy(shard_two, n_full.at[me.h, me.c, me.l], lsem.at[3])
        own.start()
        run([cot_gen])
        run([n_gen])
        own.wait()
        keep.wait()
        w.finish()

    full = jax.ShapeDtypeStruct((2, 2, 2, 128, D), bf16)
    return pl.pallas_call(
        kernel,
        out_shape=[full, full, full, jax.ShapeDtypeStruct((4, 4, 128, 640), bf16),
                   jax.ShapeDtypeStruct((PACKS, 320, SEQ), f32), jax.ShapeDtypeStruct((PACKS, HD, SEQ), bf16),
                   jax.ShapeDtypeStruct((PACKS, SEQ, 256), bf16), jax.ShapeDtypeStruct((128, D), f32)],
        in_specs=vm_specs(9), out_specs=any_specs(3) + vm_specs(5),
        scratch_shapes=[VM((128, D), bf16)] * 2 + [VM((2, 2, 2, 128, D), bf16)] * 2 + rs_z_scratch(D)
        + dma_sems(64) + [pltpu.SemaphoreType.DMA((5,))],
        compiler_params=params(cid))(x, cot, front, segs, gain_one, gain_two, gain_query, gain_key, table)


def sigmoid(v):
    return 1.0 / (1.0 + jnp.exp(-v))


def feed_forward(n_full, cot_full, weights, cid):
    def kernel(n_hbm, cot_hbm, w_hbm, grad_hbm, out_part, db_sum,
               n, cot, w, hidden, gate_up, part, grad, sibs, t, r, send, recv, lsem, gsem):
        me = Place()
        loads = [pltpu.make_async_copy(n_hbm, n, lsem.at[0])]
        loads += [pltpu.make_async_copy(w_hbm.at[:, pl.ds(1024 * i, 1024)], w.at[:, pl.ds(1024 * i, 1024)],
                                        lsem.at[1 + i]) for i in range(3)]
        loads.append(pltpu.make_async_copy(cot_hbm, cot, lsem.at[4]))
        for c in loads:
            c.start()
        meet([me.step("z", 1), me.step("z", -1), me.sibling()])
        for c in loads:
            c.wait()

        def hidden_block(i, _):
            at = pl.multiple_of(i * 256, 256)
            rows = n[...].reshape(ROWS, D)
            g = dot(rows, w[:, pl.ds(at, 256)])
            u = dot(rows, w[:, pl.ds(at + 1024, 256)])
            dh = dot(cot[...].reshape(ROWS, D), w[:, pl.ds(at + 2048, 256)])
            s = sigmoid(g)
            silu = g * s
            hidden[:, pl.ds(at, 256)] = (silu * u).astype(bf16)
            gate_up[:, pl.ds(at, 256)] = (dh * u * (s + silu * (1.0 - s))).astype(bf16)
            gate_up[:, pl.ds(at + 1024, 256)] = (dh * silu).astype(bf16)
            return 0
        lax.fori_loop(0, 4, hidden_block, 0)

        def back_block(i, _):
            at = pl.multiple_of(i * 256, 256)
            v = dot(gate_up[...], w[pl.ds(at, 256), 0:2048], 1, 1).astype(bf16)
            part[:, :, :, :, pl.ds(at, 256)] = v.reshape(2, 2, 2, 128, 256)
            return 0
        lax.fori_loop(0, 8, back_block, 0)
        wire = Wire(send, recv)

        def put(s, v):
            db_sum[s] = v
        gen = rs_z_gen(wire, me, part, put, sibs, t, r)
        next(gen)
        stores = []
        for i in range(4):
            at = 512 * i
            slot = i % 2
            if i >= 2:
                stores[i - 2].wait()
            grad[slot, :, 0:2048] = dot(n[:, :, :, :, at:at + 512].reshape(ROWS, 512), gate_up[...], 0, 0).astype(bf16)
            grad[slot, :, 2048:3072] = dot(cot[:, :, :, :, at:at + 512].reshape(ROWS, 512), hidden[...], 0, 0).astype(bf16)
            c = pltpu.make_async_copy(grad.at[slot], grad_hbm.at[pl.ds(at, 512)], gsem.at[i])
            c.start()
            stores.append(c)
            if i == 0 or i == 2:
                next(gen)

        def out_block(i, _):
            at = pl.multiple_of(i * 256, 256)
            v = dot(hidden[...], w[pl.ds(at, 256), 2048:3072], 1, 1).astype(bf16)
            out_part[:, :, :, :, pl.ds(at, 256)] = v.reshape(2, 2, 2, 128, 256)
            return 0
        lax.fori_loop(0, 8, out_block, 0)
        run([gen])
        stores[2].wait()
        stores[3].wait()
        wire.finish()

    full = (2, 2, 2, 128, D)
    return pl.pallas_call(
        kernel,
        out_shape=[jax.ShapeDtypeStruct((D, 3072), bf16), jax.ShapeDtypeStruct(full, bf16),
                   jax.ShapeDtypeStruct((128, D), f32)],
        in_specs=any_specs(3), out_specs=any_specs(1) + vm_specs(2),
        scratch_shapes=[VM(full, bf16), VM(full, bf16), VM((D, 3072), bf16), VM((ROWS, 1024), bf16),
                        VM((ROWS, 2048), bf16), VM(full, bf16), VM((2, 512, 3072), bf16)]
        + rs_z_scratch(D) + dma_sems(16) + [pltpu.SemaphoreType.DMA((5,)), pltpu.SemaphoreType.DMA((4,))],
        compiler_params=params(cid, 60))(n_full, cot_full, weights)


def attention_backward(x, cot, middle, db_sum, out_part, a_full, front_full, qk_pre, v_rows, mixed, segs,
                       gain_one, gain_two, gain_query, gain_key, table, cid):
    def kernel(x, cot, middle, db_sum, out_part, a_full, front_full, qk_pre, v_rows, mixed, segs,
               gain_one, gain_two, gain_query, gain_key, table,
               input_grad, block_output, front_mine, gains,
               shard, dm_full, mid_grad, dqkv, part, front_grad, q_acc, k_acc, one_acc, two_acc,
               sibs_a, t_a, r_a, sibs_b, t_b, r_b, t1, r1, t2, r2, mid, send, recv, lsem):
        me = Place()
        two_acc[...] = jnp.zeros_like(two_acc)
        one_acc[...] = jnp.zeros_like(one_acc)
        q_acc[...] = jnp.zeros_like(q_acc)
        k_acc[...] = jnp.zeros_like(k_acc)

        def back(z, gain, up):
            inverse = lax.rsqrt(jnp.mean(z * z, axis=-1, keepdims=True) + epsilon)
            scaled = up * gain
            inner = jnp.mean(z * scaled, axis=-1, keepdims=True)
            return inverse * (scaled - z * inverse * inverse * inner), up * z * inverse

        def norm_two(s):
            dz, terms = back(middle[s], gain_two[...], db_sum[s])
            v = cot[s].astype(f32) + dz
            mid_grad[s] = v
            shard[s] = v.astype(bf16)
            two_acc[...] += terms
        chunks(128, norm_two)
        meet([me.step("x", 1), me.step("x", -1), me.step("y", 1), me.step("y", -1),
              me.step("z", 1), me.step("z", -1), me.sibling()])
        w = Wire(send, recv)
        gen = ag_z_gen(w, me, shard, dm_full)
        next(gen)
        own = pltpu.make_async_copy(shard, dm_full.at[me.h, me.c, me.l], lsem.at[0])
        own.start()
        run([gen])
        own.wait()

        def put_out(s, v):
            block_output[s] = middle[s] + v
        out_gen = rs_z_gen(w, me, out_part, put_out, sibs_a, t_a, r_a)
        next(out_gen)

        def one_pack(p, _):
            allowed, cosine, sine = pack_tables(segs, p, table)
            weights = front_full[...].reshape(D, 640)
            mixed_grad = dot(pack_of(dm_full, p), weights[:, 384:640]).T.astype(bf16)
            value_rows = v_rows[p].astype(f32).T.astype(bf16)
            key_pre = qk_pre[p, 256:320]
            kn, k_inverse = head_norm(key_pre, gain_key[...])
            kr = turn(kn, cosine, sine)
            key_rows = kr.T.astype(bf16)
            kr = kr.astype(bf16)
            dk = jnp.zeros((HD, SEQ), f32)
            dv = jnp.zeros((HD, SEQ), f32)
            heads = []
            terms_q = jnp.zeros((HD, SEQ), f32)
            for j in range(4):
                query_pre = qk_pre[p, 64 * j:64 * j + 64]
                qn, q_inverse = head_norm(query_pre, gain_query[...])
                qr = turn(qn, cosine, sine).astype(bf16)
                probs = pack_probs(key_rows, qr, allowed)
                do = mixed_grad[64 * j:64 * j + 64]
                dp = dot(value_rows, do)
                inner = jnp.sum(probs * dp, axis=0, keepdims=True)
                ds = (probs * (dp - inner)).astype(bf16)
                dqr = dot(kr, ds) * score_scale
                dk += dot(qr, ds, 1, 1)
                dv += dot(do, probs.astype(bf16), 1, 1)
                dq, terms = head_norm_back(query_pre, q_inverse, gain_query[...], turn_back(dqr, cosine, sine))
                terms_q += terms
                heads.append(dq)
            dk, terms_k = head_norm_back(key_pre, k_inverse, gain_key[...], turn_back(dk * score_scale, cosine, sine))
            q_acc[...] += terms_q
            k_acc[...] += terms_k
            grads = jnp.concatenate(heads + [dk, dv], axis=0).T.astype(bf16)
            dqkv[p] = grads
            out = dot(grads, weights[:, 0:384], 1, 1).astype(bf16)
            part[lax.div(p, 2), lax.rem(p, 2)] = out.reshape(2, 128, D)
            return 0
        lax.fori_loop(0, 2, one_pack, 0)
        next(out_gen)
        lax.fori_loop(2, PACKS, one_pack, 0)
        next(out_gen)
        for i in range(4):
            at = 512 * i
            a_rows = a_full[:, :, :, :, at:at + 512].reshape(ROWS, 512)
            dm_rows = dm_full[:, :, :, :, at:at + 512].reshape(ROWS, 512)
            g = jnp.concatenate([dot(a_rows, dqkv[...].reshape(ROWS, 384), 0, 0),
                                 dot(dm_rows, mixed[...].reshape(ROWS, 256), 0, 0)], axis=1)
            front_grad[i] = g.astype(bf16).reshape(4, 128, 640)

        def put_in(s, v):
            dz, terms = back(x[s].astype(f32), gain_one[...], v)
            input_grad[s] = mid_grad[s] + dz
            one_acc[...] += terms
        run([out_gen])
        in_gen = rs_z_gen(w, me, part, put_in, sibs_b, t_b, r_b)
        run([in_gen] + rs_xy_gens(w, me, front_grad, front_mine, t1, r1, t2, r2, mid))
        w.finish()
        one = jnp.sum(one_acc[...], axis=0, keepdims=True)
        two = jnp.sum(two_acc[...], axis=0, keepdims=True)
        for i in range(16):
            gains[i:i + 1, :] = one[:, 128 * i:128 * i + 128]
            gains[16 + i:17 + i, :] = two[:, 128 * i:128 * i + 128]
        small = jnp.concatenate([q_acc[...], k_acc[...]], axis=0).T
        gains[32:33, :] = jnp.sum(small, axis=0, keepdims=True)

    full = (2, 2, 2, 128, D)
    rows = jax.ShapeDtypeStruct((128, D), f32)
    return pl.pallas_call(
        kernel,
        out_shape=[rows, rows, jax.ShapeDtypeStruct((128, 640), bf16), jax.ShapeDtypeStruct((33, 128), f32)],
        in_specs=vm_specs(16), out_specs=vm_specs(4),
        scratch_shapes=[VM((128, D), bf16), VM(full, bf16), VM((128, D), f32), VM((PACKS, SEQ, 384), bf16),
                        VM(full, bf16), VM((4, 4, 128, 640), bf16), VM((HD, SEQ), f32), VM((HD, SEQ), f32),
                        VM((16, D), f32), VM((16, D), f32)]
        + rs_z_scratch(D) * 2 + rs_xy_scratch(640) + dma_sems(64) + [pltpu.SemaphoreType.DMA((2,))],
        compiler_params=params(cid, 60))(
            x, cot, middle, db_sum, out_part, a_full, front_full, qk_pre, v_rows, mixed, segs,
            gain_one, gain_two, gain_query, gain_key, table)


def adam(weight, moment, square, gradient, rate, decay):
    momentum = beta_one * moment + (1.0 - beta_one) * gradient
    variance = beta_two * square + (1.0 - beta_two) * gradient * gradient
    ratio = momentum / (1.0 - beta_one**STEP) / (jnp.sqrt(variance / (1.0 - beta_two**STEP)) + adam_epsilon)
    return weight - rate * (ratio + decay * weight), momentum, variance


RATES = (0.04, 0.04, 0.04, 0.15, 0.04, 0.04, 0.02)
SPANS = (256, 64, 64, 256, 1024, 1024, 1024)


def update(front, rest, gain_terms, gain_states, states, cid):
    def kernel(*refs):
        front, rest, terms, g_w, g_m, g_v = refs[:6]
        ins, g_out, outs = refs[6:27], refs[27:30], refs[30:51]
        fbuf, rbuf, z_in, x_in, y_in = refs[51:56]
        held, made = refs[56:77], refs[77:98]
        send, recv, lsem, osem = refs[98:]
        me = Place()
        loads = [pltpu.make_async_copy(a, b, lsem.at[i]) for i, (a, b) in enumerate(zip(ins, held))]
        for c in loads:
            c.start()
        peers = swap_devs(me)
        mine = me.h * 2 + me.c
        zs = [me.at(z=m4(me.z + dz), c=lax.rem(me.c + dc, 2)) for dz in range(4) for dc in range(2) if dz or dc]
        xs = [me.step("x", d) for d in (1, 2, 3)]
        ys = [me.step("y", d) for d in (1, 2, 3)]
        meet(zs + xs + ys)
        w = Wire(send, recv)

        def total(buf, n):
            v = buf[0]
            for k in range(1, n):
                v = v + buf[k]
            return v

        def share(value, buf, slot, devs):
            buf[slot] = value
            return [w.go(buf.at[slot], buf.at[slot], d) for d in devs]
        gs = share(terms[...], z_in, me.z * 2 + me.c, zs)
        arrivals = []
        for j, dev in reversed(peers):
            arrivals.append(w.go(front.at[j], fbuf.at[mine], dev))
            arrivals.append(w.go(rest.at[j], rbuf.at[mine], dev))
        fbuf[mine] = front[mine]
        rbuf[mine] = rest[mine]
        for c in gs:
            c.wait_recv()
        gs = share(total(z_in, 8), x_in, me.x, xs)
        for c in gs:
            c.wait_recv()
        gs = share(total(x_in, 4), y_in, me.y, ys)
        for c in gs:
            c.wait_recv()
        new = adam(g_w[...], g_m[...], g_v[...], total(y_in, 4), gain_rate, 0.0)
        for ref, v in zip(g_out, new):
            ref[...] = v
        for c in loads:
            c.wait()
        for a in arrivals:
            a.wait_recv()
        stores = []
        at = {False: 0, True: 0}
        for i, (n, rate) in enumerate(zip(SPANS, RATES)):
            late = i >= 4
            buf = rbuf if late else fbuf
            for j in range(4):
                here = pl.ds(n * j, n)
                grad = buf[j, :, at[late]:at[late] + n].astype(f32)
                new = adam(held[3 * i][:, here], held[3 * i + 1][:, here], held[3 * i + 2][:, here], grad, rate,
                           weight_decay)
                for k in range(3):
                    made[3 * i + k][:, here] = new[k]
            at[late] += n
            for k in range(3):
                c = pltpu.make_async_copy(made[3 * i + k], outs[3 * i + k], osem.at[3 * i + k])
                c.start()
                stores.append(c)
        for c in stores:
            c.wait()
        w.finish()

    shapes = [jax.ShapeDtypeStruct(s.shape, f32) for s in states]
    gain_shape = jax.ShapeDtypeStruct((33, 128), f32)
    return pl.pallas_call(
        kernel, out_shape=[gain_shape] * 3 + shapes,
        in_specs=vm_specs(6) + any_specs(21), out_specs=vm_specs(3) + any_specs(21),
        scratch_shapes=[VM((4, 32, 640), bf16), VM((4, 32, 3072), bf16), VM((8, 33, 128), f32), VM((4, 33, 128), f32),
                        VM((4, 33, 128), f32)] + [VM(s.shape, f32) for s in states] * 2
        + dma_sems(19) + [pltpu.SemaphoreType.DMA((21,)), pltpu.SemaphoreType.DMA((21,))],
        compiler_params=params(cid))(front, rest, gain_terms, *gain_states, *states)


from jax.sharding import PartitionSpec as P

PLANE = [[x * 16 + y * 4 + k for x in range(4) for y in range(4)] for k in range(4)]


def gather_plane(shard):
    return lax.all_gather(shard, "dp", axis_index_groups=PLANE, axis=0, tiled=True)


def scatter_plane(whole):
    return lax.psum_scatter(whole, "dp", axis_index_groups=PLANE, scatter_dimension=0, tiled=True)


def local(block_input, output_grad, segment_ids, norm_gains, gain_moment, gain_square, *states):
    gain_one = norm_gains[:D][None]
    gain_two = norm_gains[D : 2 * D][None]
    gain_query = norm_gains[2 * D : 2 * D + HD][:, None]
    gain_key = norm_gains[2 * D + HD :][:, None]
    table = jnp.asarray(rope_constants())
    front_shard, rest_shard, segments = spread_weights(states[::3], segment_ids, 1)
    rest_full = gather_plane(rest_shard.reshape(128, 3072))
    one_full, cot_full, two_full, front_full, qk_pre, v_rows, mixed, middle = attention_forward(
        block_input, output_grad, front_shard.reshape(128, 640), segments, gain_one, gain_two, gain_query, gain_key,
        table, 2)
    rest_grad, out_part, db_sum = feed_forward(two_full, cot_full, rest_full, 3)
    rest_mine = scatter_plane(rest_grad)
    input_grad, block_output, front_mine, gain_terms = attention_backward(
        block_input, output_grad, middle, db_sum, out_part, one_full, front_full, qk_pre, v_rows, mixed, segments,
        gain_one, gain_two, gain_query, gain_key, table, 4)
    square = lambda v: v.reshape(33, 128)
    news = update(front_mine.reshape(4, 32, 640), rest_mine.reshape(4, 32, 3072), gain_terms,
                  [square(norm_gains), square(gain_moment), square(gain_square)], states, 5)
    return (block_output, input_grad) + tuple(v.reshape(-1) for v in news[:3]) + tuple(news[3:])


def solution(mesh):
    tokens, weight = P(("dp", "tensor"), None), P("dp", "tensor")
    in_specs = (tokens, tokens, P("dp", None), P(), P(), P()) + (weight,) * 21
    out_specs = (tokens, tokens, P(), P(), P()) + (weight,) * 21
    return jax.shard_map(local, mesh=mesh, in_specs=in_specs, out_specs=out_specs, check_vma=False)
```

```python
import jax
import jax.numpy as jnp
import numpy as np
from jax import lax
from jax.experimental import pallas as pl
from jax.experimental.pallas import tpu as pltpu

MESH = pl.DeviceIdType.MESH
VM = pltpu.VMEM
bf16 = jnp.bfloat16
f32 = jnp.float32


def m4(v):
    return lax.rem(v + 4, 4)


class Place:
    def __init__(self):
        dp = lax.axis_index("dp")
        self.l = lax.axis_index("tensor")
        self.x = lax.div(dp, 16)
        self.y = lax.rem(lax.div(dp, 4), 4)
        self.h = lax.rem(lax.div(dp, 2), 2)
        self.c = lax.rem(dp, 2)
        self.z = self.h * 2 + self.l

    def at(self, x=None, y=None, z=None, c=None):
        x = self.x if x is None else x
        y = self.y if y is None else y
        z = self.z if z is None else z
        c = self.c if c is None else c
        return (x * 16 + y * 4 + lax.div(z, 2) * 2 + c, lax.rem(z, 2))

    def pos(self, axis):
        return {"x": self.x, "y": self.y, "z": self.z}[axis]

    def step(self, axis, d):
        return self.at(**{axis: m4(self.pos(axis) + d)})

    def sibling(self):
        return self.at(c=1 - self.c)


class Wire:
    def __init__(self, send, recv):
        self.send, self.recv, self.n = send, recv, 0
        self.pending = []

    def go(self, src, dst, dev):
        i = self.n
        self.n += 1
        c = pltpu.make_async_remote_copy(
            src_ref=src, dst_ref=dst, send_sem=self.send.at[i], recv_sem=self.recv.at[i],
            device_id=dev, device_id_type=MESH)
        c.start()
        self.pending.append(c)
        return c

    def finish(self):
        for c in self.pending:
            c.wait_send()
        self.pending = []


def meet(devs):
    b = pltpu.get_barrier_semaphore()
    for d in devs:
        pl.semaphore_signal(b, inc=1, device_id=d, device_id_type=MESH)
    pl.semaphore_wait(b, len(devs))


def ring_gather(w, me, axis, whole, lo, hi, first=None, arrived=None):
    p = me.pos(axis)
    up, down = me.step(axis, 1), me.step(axis, -1)
    own = whole(p) if first is None else first
    a = w.go(own, whole(p), up)
    b = w.go(own, whole(p), down)
    yield
    a.wait_recv()
    fa = w.go(lo(m4(p - 1)), lo(m4(p - 1)), up)
    if arrived:
        arrived(whole(m4(p - 1)))
    b.wait_recv()
    fb = w.go(hi(m4(p + 1)), hi(m4(p + 1)), down)
    if arrived:
        arrived(whole(m4(p + 1)))
    yield
    fa.wait_recv()
    if arrived:
        arrived(lo(m4(p - 2)))
    fb.wait_recv()
    if arrived:
        arrived(hi(m4(p - 2)))


def ring_scatter(w, me, axis, lo, hi, tlo, thi, rup, rdown, add):
    p = me.pos(axis)
    up, down = me.step(axis, 1), me.step(axis, -1)
    far, nu, nd = m4(p + 2), m4(p + 1), m4(p - 1)
    ta = w.go(lo(far), tlo, up)
    tb = w.go(hi(far), thi, down)
    da = w.go(hi(nu), rup[1], up)
    db = w.go(lo(nd), rdown[0], down)
    yield
    ta.wait_recv()
    add(tlo, lo(nu))
    sa = w.go(tlo, rup[0], up)
    tb.wait_recv()
    add(thi, hi(nd))
    sb = w.go(thi, rdown[1], down)
    yield
    da.wait_recv()
    db.wait_recv()
    sa.wait_recv()
    sb.wait_recv()


def loop_add(dst, a, b=None, rows=16):
    n = dst.shape[0]

    def body(i, _):
        def inner(j, _):
            s = pl.ds(pl.multiple_of(j * rows, rows), rows)
            v = dst[i, s].astype(f32) + a[i, s].astype(f32)
            if b is not None:
                v = v + b[i, s].astype(f32)
            dst[i, s] = v.astype(dst.dtype)
            return 0
        return lax.fori_loop(0, dst.shape[1] // rows, inner, 0)
    lax.fori_loop(0, n, body, 0)


def run(gens):
    gens = list(gens)
    while gens:
        for g in list(gens):
            try:
                next(g)
            except StopIteration:
                gens.remove(g)


def params(cid, mb=56):
    return pltpu.CompilerParams(collective_id=cid, has_side_effects=True, vmem_limit_bytes=mb * 2**20)


def ag_xy_gens(w, me, src, out):
    H = 64
    x, y = me.x, me.y

    def half_a():
        yield from ring_gather(w, me, "x", lambda i: out.at[i, y, pl.ds(0, 64)], lambda i: out.at[i, y, pl.ds(0, 32)],
                               lambda i: out.at[i, y, pl.ds(32, 32)], first=src.at[pl.ds(0, 64)])
        yield
        yield from ring_gather(w, me, "y", lambda i: out.at[:, i, pl.ds(0, 64)], lambda i: out.at[:, i, pl.ds(0, 32)],
                               lambda i: out.at[:, i, pl.ds(32, 32)])

    def half_b():
        yield from ring_gather(w, me, "y", lambda i: out.at[x, i, pl.ds(64, 64)], lambda i: out.at[x, i, pl.ds(64, 32)],
                               lambda i: out.at[x, i, pl.ds(96, 32)], first=src.at[pl.ds(64, 64)])
        yield
        yield from ring_gather(w, me, "x", lambda i: out.at[i, :, pl.ds(64, 64)], lambda i: out.at[i, :, pl.ds(64, 32)],
                               lambda i: out.at[i, :, pl.ds(96, 32)])
    return [half_a(), half_b()]


def ag_xy(shard, cid, space=pl.ANY):
    C = shard.shape[1]

    def kernel(src, out, send, recv, lsem):
        me = Place()
        meet([me.step("x", 1), me.step("x", -1), me.step("y", 1), me.step("y", -1)])
        w = Wire(send, recv)
        lc = pltpu.make_async_copy(src, out.at[me.x, me.y], lsem)
        lc.start()
        lc.wait()
        run(ag_xy_gens(w, me, src, out))
        w.finish()

    return pl.pallas_call(
        kernel, out_shape=jax.ShapeDtypeStruct((4, 4, 128, C), shard.dtype),
        in_specs=[pl.BlockSpec(memory_space=space)], out_specs=pl.BlockSpec(memory_space=space),
        scratch_shapes=[pltpu.SemaphoreType.DMA((16,)), pltpu.SemaphoreType.DMA((16,)), pltpu.SemaphoreType.DMA],
        compiler_params=params(cid))(shard)


def rs_xy_scratch(C):
    return [VM((2, 2, 4, 32, C), bf16), VM((2, 2, 2, 4, 32, C), bf16),
            VM((2, 2, 32, C), bf16), VM((2, 2, 2, 32, C), bf16), VM((2, 4, 64, C), bf16)]


def rs_xy_gens(w, me, g, out, t1, r1, t2, r2, mid):
    x, y = me.x, me.y

    def half(k, first, second):
        base = k * 64
        if first == "y":
            pick = lambda i, o: g.at[:, i, pl.ds(base + o, 32)]
        else:
            pick = lambda i, o: g.at[i, :, pl.ds(base + o, 32)]
        yield from ring_scatter(w, me, first, lambda i: pick(i, 0), lambda i: pick(i, 32), t1.at[k, 0], t1.at[k, 1],
                                (r1.at[k, 0, 0], r1.at[k, 0, 1]), (r1.at[k, 1, 0], r1.at[k, 1, 1]), loop_add)
        p = me.pos(first)
        m = mid.at[k]
        for hh in range(2):
            own = pick(p, 32 * hh)

            def body(i, _):
                def inner(j, _):
                    s = pl.ds(pl.multiple_of(j * 16, 16), 16)
                    d = pl.ds(pl.multiple_of(j * 16 + 32 * hh, 16), 16)
                    v = own[i, s].astype(f32) + r1[k, 0, hh, i, s].astype(f32) + r1[k, 1, hh, i, s].astype(f32)
                    m[i, d] = v.astype(bf16)
                    return 0
                return lax.fori_loop(0, 2, inner, 0)
            lax.fori_loop(0, 4, body, 0)
        yield
        q = me.pos(second)
        add1 = lambda dst, a: loop_add(dst, a)
        pick2 = lambda i, o: mid.at[k, i, pl.ds(o, 32)]

        def add2(dst, a):
            def inner(j, _):
                s = pl.ds(pl.multiple_of(j * 16, 16), 16)
                dst[s] = (dst[s].astype(f32) + a[s].astype(f32)).astype(bf16)
                return 0
            lax.fori_loop(0, 2, inner, 0)
        yield from ring_scatter(w, me, second, lambda i: pick2(i, 0), lambda i: pick2(i, 32), t2.at[k, 0], t2.at[k, 1],
                                (r2.at[k, 0, 0], r2.at[k, 0, 1]), (r2.at[k, 1, 0], r2.at[k, 1, 1]), add2)
        for hh in range(2):
            def inner(j, _):
                s = pl.ds(pl.multiple_of(j * 16, 16), 16)
                d = pl.ds(pl.multiple_of(j * 16 + 32 * hh, 16), 16)
                dd = pl.ds(pl.multiple_of(j * 16 + 32 * hh + base, 16), 16)
                v = m[q, d].astype(f32) + r2[k, 0, hh, s].astype(f32) + r2[k, 1, hh, s].astype(f32)
                out[dd] = v.astype(out.dtype)
                return 0
            lax.fori_loop(0, 2, inner, 0)
    return [half(0, "y", "x"), half(1, "x", "y")]


def rs_xy(g, cid, out_dtype=f32):
    C = g.shape[-1]

    def kernel(gin, out, send, recv, *scr):
        me = Place()
        meet([me.step("x", 1), me.step("x", -1), me.step("y", 1), me.step("y", -1)])
        w = Wire(send, recv)
        run(rs_xy_gens(w, me, gin, out, *scr))
        w.finish()

    return pl.pallas_call(
        kernel, out_shape=jax.ShapeDtypeStruct((128, C), out_dtype),
        in_specs=[pl.BlockSpec(memory_space=VM)], out_specs=pl.BlockSpec(memory_space=VM),
        scratch_shapes=[pltpu.SemaphoreType.DMA((24,)), pltpu.SemaphoreType.DMA((24,))] + rs_xy_scratch(C),
        compiler_params=params(cid, 60))(g)


def ag_z_gen(w, me, src, out):
    sib = me.sibling()
    blk = lambda i, cc: out.at[lax.div(i, 2), cc, lax.rem(i, 2)]
    cs = []

    def to_sib(ref):
        cs.append(w.go(ref, ref, sib))
    whole = lambda i: blk(i, me.c)
    own = w.go(src, whole(me.z), sib)
    yield from ring_gather(w, me, "z", whole, lambda i: whole(i).at[pl.ds(0, 64)], lambda i: whole(i).at[pl.ds(64, 64)],
                           first=src, arrived=to_sib)
    own.wait_recv()
    for c in cs:
        c.wait_recv()


def ag_z(shard, cid, space=VM):
    C = shard.shape[1]

    def kernel(src, out, send, recv, lsem):
        me = Place()
        meet([me.step("z", 1), me.step("z", -1), me.sibling()])
        w = Wire(send, recv)
        lc = pltpu.make_async_copy(src, out.at[me.h, me.c, me.l], lsem)
        lc.start()
        lc.wait()
        run([ag_z_gen(w, me, src, out)])
        w.finish()

    return pl.pallas_call(
        kernel, out_shape=jax.ShapeDtypeStruct((2, 2, 2, 128, C), shard.dtype),
        in_specs=[pl.BlockSpec(memory_space=space)], out_specs=pl.BlockSpec(memory_space=space),
        scratch_shapes=[pltpu.SemaphoreType.DMA((16,)), pltpu.SemaphoreType.DMA((16,)), pltpu.SemaphoreType.DMA],
        compiler_params=params(cid))(shard)


def rs_z_scratch(C):
    return [VM((4, 128, C), bf16), VM((2, 64, C), bf16), VM((2, 2, 64, C), bf16)]


def rs_z_gen(w, me, g, out, sibs, t, r):
    sib = me.sibling()
    oc = 1 - me.c
    order = [2, 1, 3, 0]
    blk = lambda i, cc: g.at[lax.div(i, 2), cc, lax.rem(i, 2)]
    z = me.z
    sc = {}
    for o in order:
        i = m4(z + o)
        sc[o] = w.go(blk(i, oc), sibs.at[i], sib)
    yield

    def fold(o, s0, n):
        i = m4(z + o)
        b = blk(i, me.c)

        def inner(j, _):
            s = pl.ds(pl.multiple_of(j * 16 + s0, 16), 16)
            sibs[i, s] = (sibs[i, s].astype(f32) + b[s].astype(f32)).astype(bf16)
            return 0
        lax.fori_loop(0, n // 16, inner, 0)
    up, down = me.step("z", 1), me.step("z", -1)
    half = lambda o, k: sibs.at[m4(z + o), pl.ds(64 * k, 64)]
    sc[2].wait_recv()
    fold(2, 0, 64)
    ta = w.go(half(2, 0), t.at[0], up)
    fold(2, 64, 64)
    tb = w.go(half(2, 1), t.at[1], down)
    sc[1].wait_recv()
    fold(1, 64, 64)
    da = w.go(half(1, 1), r.at[0, 1], up)
    sc[3].wait_recv()
    fold(3, 0, 64)
    db = w.go(half(3, 0), r.at[1, 0], down)
    fold(1, 0, 64)
    fold(3, 64, 64)
    yield

    def add(dst, a):
        def inner(j, _):
            s = pl.ds(pl.multiple_of(j * 16, 16), 16)
            dst[s] = (dst[s].astype(f32) + a[s].astype(f32)).astype(bf16)
            return 0
        lax.fori_loop(0, 4, inner, 0)
    ta.wait_recv()
    add(t.at[0], half(1, 0))
    sa = w.go(t.at[0], r.at[0, 0], up)
    tb.wait_recv()
    add(t.at[1], half(3, 1))
    sb = w.go(t.at[1], r.at[1, 1], down)
    sc[0].wait_recv()
    own = blk(z, me.c)
    yield

    def last(hh):
        def inner(j, _):
            s = pl.ds(pl.multiple_of(j * 16, 16), 16)
            d = pl.ds(pl.multiple_of(j * 16 + 64 * hh, 16), 16)
            v = own[d].astype(f32) + sibs[z, d].astype(f32) + r[0, hh, s].astype(f32) + r[1, hh, s].astype(f32)
            out(d, v)
            return 0
        lax.fori_loop(0, 4, inner, 0)
    da.wait_recv()
    sa.wait_recv()
    db.wait_recv()
    sb.wait_recv()
    last(0)
    last(1)


def rs_z(g, cid, out_dtype=f32):
    C = g.shape[-1]

    def kernel(gin, out, send, recv, *scr):
        me = Place()
        meet([me.step("z", 1), me.step("z", -1), me.sibling()])
        w = Wire(send, recv)

        def put(s, v):
            out[s] = v.astype(out.dtype)
        run([rs_z_gen(w, me, gin, put, *scr)])
        w.finish()

    return pl.pallas_call(
        kernel, out_shape=jax.ShapeDtypeStruct((128, C), out_dtype),
        in_specs=[pl.BlockSpec(memory_space=VM)], out_specs=pl.BlockSpec(memory_space=VM),
        scratch_shapes=[pltpu.SemaphoreType.DMA((16,)), pltpu.SemaphoreType.DMA((16,))] + rs_z_scratch(C),
        compiler_params=params(cid))(g)


def swap_devs(me):
    out = []
    for dh, dc in ((0, 1), (1, 0), (1, 1)):
        h = lax.rem(me.h + dh, 2)
        c = lax.rem(me.c + dc, 2)
        out.append((h * 2 + c, me.at(z=h * 2 + me.l, c=c)))
    return out


def swap_hc(parts, cid):
    n = len(parts)

    def kernel(*refs):
        ins, outs = refs[:n], refs[n:2 * n]
        send, recv, lsem = refs[2 * n:]
        me = Place()
        peers = swap_devs(me)
        meet([d for _, d in peers])
        w = Wire(send, recv)
        mine = me.h * 2 + me.c
        arrivals = []
        for j, d in reversed(peers):
            for a, b in zip(ins, outs):
                arrivals.append(w.go(a.at[j], b.at[mine], d))
        ls = []
        for k, (a, b) in enumerate(zip(ins, outs)):
            lc = pltpu.make_async_copy(a.at[mine], b.at[mine], lsem.at[k])
            lc.start()
            ls.append(lc)
        for lc in ls:
            lc.wait()
        for a in arrivals:
            a.wait_recv()
        w.finish()

    return pl.pallas_call(
        kernel, out_shape=[jax.ShapeDtypeStruct(p.shape, p.dtype) for p in parts],
        in_specs=[pl.BlockSpec(memory_space=VM)] * n, out_specs=[pl.BlockSpec(memory_space=VM)] * n,
        scratch_shapes=[pltpu.SemaphoreType.DMA((3 * n,)), pltpu.SemaphoreType.DMA((3 * n,)),
                        pltpu.SemaphoreType.DMA((n,))],
        compiler_params=params(cid))(*parts)


def sum_all(v, cid):
    R, C = v.shape

    def kernel(src, out, z_in, x_in, y_in, acc, send, recv):
        me = Place()
        zs = []
        for dz in range(4):
            for dc in range(2):
                if dz or dc:
                    z, c = m4(me.z + dz), lax.rem(me.c + dc, 2)
                    zs.append(me.at(z=z, c=c))
        xs = [me.step("x", d) for d in (1, 2, 3)]
        ys = [me.step("y", d) for d in (1, 2, 3)]
        meet(zs + xs + ys)
        w = Wire(send, recv)
        acc[...] = src[...]
        for buf, slot, devs, n in ((z_in, me.z * 2 + me.c, zs, 8), (x_in, me.x, xs, 4), (y_in, me.y, ys, 4)):
            buf[slot] = acc[...]
            cs = [w.go(buf.at[slot], buf.at[slot], d) for d in devs]
            for c in cs:
                c.wait_recv()
            total = buf[0]
            for k in range(1, n):
                total = total + buf[k]
            w.finish()
            acc[...] = total
        out[...] = acc[...]

    return pl.pallas_call(
        kernel, out_shape=jax.ShapeDtypeStruct((R, C), f32),
        in_specs=[pl.BlockSpec(memory_space=VM)], out_specs=pl.BlockSpec(memory_space=VM),
        scratch_shapes=[VM((8, R, C), f32), VM((4, R, C), f32), VM((4, R, C), f32), VM((R, C), f32),
                        pltpu.SemaphoreType.DMA((13,)), pltpu.SemaphoreType.DMA((13,))],
        compiler_params=params(cid))(v)


D = 2048
HD = 64
STEP = 10
SEQ = 256
PACKS = 4
ROWS = 1024
epsilon = 1e-06
rope_base = 1000000.0
beta_one = 0.9
beta_two = 0.999
adam_epsilon = 1e-08
weight_decay = 0.1
gain_rate = 0.3
masked_score = -1000000000.0
score_scale = HD ** (-0.5)
exact = lax.Precision.HIGHEST


def dot(a, b, ca=1, cb=0, precision=None):
    return lax.dot_general(a, b, (((ca,), (cb,)), ((), ())), precision=precision, preferred_element_type=f32)


def chunks(n, body, rows=16):
    def one(j, _):
        body(pl.ds(pl.multiple_of(j * rows, rows), rows))
        return 0
    lax.fori_loop(0, n // rows, one, 0)


def dma_sems(n):
    return [pltpu.SemaphoreType.DMA((n,)), pltpu.SemaphoreType.DMA((n,))]


def vm_specs(n):
    return [pl.BlockSpec(memory_space=VM)] * n


def any_specs(n):
    return [pl.BlockSpec(memory_space=pl.ANY)] * n


class Columns:
    def __init__(self, ref, n):
        self.ref, self.n = ref, n

    def __getitem__(self, j):
        return self.ref[:, pl.ds(pl.multiple_of(j * self.n, self.n), self.n)]


def spread_weights(weights, segments, cid):
    def kernel(q_, k_, v_, o_, g_, u_, d_, seg, front, rest, segs, fbuf, rbuf, sbuf, kv, send, recv):
        me = Place()
        peers = swap_devs(me)
        mine = me.h * 2 + me.c
        q, o = Columns(q_, 256), Columns(o_, 256)
        g, u, d = Columns(g_, 1024), Columns(u_, 1024), Columns(d_, 1024)
        for j in range(4):
            kv[j] = jnp.concatenate([k_[:, 64 * j:64 * j + 64], v_[:, 64 * j:64 * j + 64]], axis=1)
        sbuf[...] = jnp.broadcast_to(seg[...], (8, SEQ))

        def rounded(j, fdst, rdst):
            fdst[:, 0:256] = q[j].astype(bf16)
            fdst[:, 256:384] = kv[j].astype(bf16)
            fdst[:, 384:640] = o[j].astype(bf16)
            for i, w in enumerate((g, u, d)):
                rdst[:, 1024 * i:1024 * i + 1024] = w[j].astype(bf16)
        meet([dev for _, dev in peers])
        w = Wire(send, recv)
        arrivals = []
        for j, dev in reversed(peers):
            rounded(j, fbuf.at[j], rbuf.at[j])
            arrivals.append(w.go(rbuf.at[j], rest.at[mine], dev))
            arrivals.append(w.go(fbuf.at[j], front.at[mine], dev))
            arrivals.append(w.go(sbuf, segs.at[mine], dev))
        rounded(mine, front.at[mine], rest.at[mine])
        segs[mine] = sbuf[...]
        for a in arrivals:
            a.wait_recv()
        w.finish()

    return pl.pallas_call(
        kernel,
        out_shape=[jax.ShapeDtypeStruct((4, 32, 640), bf16), jax.ShapeDtypeStruct((4, 32, 3072), bf16),
                   jax.ShapeDtypeStruct((4, 8, SEQ), jnp.int32)],
        in_specs=vm_specs(8), out_specs=vm_specs(3),
        scratch_shapes=[VM((4, 32, 640), bf16), VM((4, 32, 3072), bf16), VM((8, SEQ), jnp.int32),
                        VM((4, 32, 128), f32)] + dma_sems(9),
        compiler_params=params(cid))(*weights, segments)


def gain_rows(gains):
    one = jnp.concatenate([gains[i:i + 1, :] for i in range(16)], axis=1)
    two = jnp.concatenate([gains[16 + i:17 + i, :] for i in range(16)], axis=1)
    small = jnp.broadcast_to(gains[32:33, :], (128, 128)).T
    return one, two, small[0:64, 0:1], small[64:128, 0:1]


def rope_constants():
    frequency = np.float32(rope_base) ** (np.float32(-2.0) * np.arange(HD // 2, dtype=np.float32) / np.float32(HD))
    angles = (np.arange(SEQ, dtype=np.float32)[None, :] * frequency[:, None].astype(np.float32)).astype(np.float64)
    return np.concatenate([np.cos(angles), np.sin(angles)], axis=0).astype(np.float32)


def pack_tables(segs, p, table):
    row = segs[p].astype(f32)[0:1, :]
    column = jnp.broadcast_to(row, (128, SEQ)).T[:, 0:1]
    key_at = lax.broadcasted_iota(jnp.int32, (SEQ, SEQ), 0)
    query_at = lax.broadcasted_iota(jnp.int32, (SEQ, SEQ), 1)
    allowed = (column == row) & (key_at <= query_at)
    start = jnp.sum(jnp.where(column < row, 1.0, 0.0), axis=0, keepdims=True)
    where = query_at.astype(f32) - start
    hot = jnp.where(key_at.astype(f32) == where, 1.0, 0.0)
    both = dot(table[...], hot, precision=exact)
    return allowed, both[0:32], both[32:64]


def head_norm(z, gain):
    inverse = lax.rsqrt(jnp.mean(z * z, axis=0, keepdims=True) + epsilon)
    return z * inverse * gain, inverse


def head_norm_back(z, inverse, gain, up):
    scaled = up * gain
    inner = jnp.mean(z * scaled, axis=0, keepdims=True)
    return inverse * (scaled - z * inverse * inverse * inner), up * z * inverse


def turn(u, cosine, sine):
    a, b = u[0:32], u[32:64]
    return jnp.concatenate([a * cosine - b * sine, b * cosine + a * sine], axis=0)


def turn_back(u, cosine, sine):
    a, b = u[0:32], u[32:64]
    return jnp.concatenate([a * cosine + b * sine, b * cosine - a * sine], axis=0)


def pack_probs(key_rows, query_rot, allowed):
    scores = jnp.where(allowed, dot(key_rows, query_rot) * score_scale, masked_score)
    exps = jnp.exp(scores - jnp.max(scores, axis=0, keepdims=True))
    return exps / jnp.sum(exps, axis=0, keepdims=True)


def pack_of(ref, p):
    v = ref[lax.div(p, 2), lax.rem(p, 2)]
    return v.reshape(SEQ, v.shape[-1])


def attention_forward(x, cot, front, segs, gains, table, cid):
    def kernel(x, cot, front, segs, gains, table,
               a_full, cot_full, n_full, front_full, qk_pre, v_rows, mixed, middle,
               shard, shard_two, a_buf, part, sibs, t, r, send, recv, lsem):
        me = Place()
        gain_one, gain_two, gain_query, gain_key = gain_rows(gains)

        def norm_one(s):
            v = x[s].astype(f32)
            inverse = lax.rsqrt(jnp.mean(v * v, axis=-1, keepdims=True) + epsilon)
            shard[s] = (v * inverse * gain_one).astype(bf16)
        chunks(128, norm_one)
        meet([me.step("x", 1), me.step("x", -1), me.step("y", 1), me.step("y", -1),
              me.step("z", 1), me.step("z", -1), me.sibling()])
        w = Wire(send, recv)
        locals_ = [pltpu.make_async_copy(front, front_full.at[me.x, me.y], lsem.at[0]),
                   pltpu.make_async_copy(shard, a_buf.at[me.h, me.c, me.l], lsem.at[1]),
                   pltpu.make_async_copy(cot, cot_full.at[me.h, me.c, me.l], lsem.at[2])]
        gens = ag_xy_gens(w, me, front, front_full) + [ag_z_gen(w, me, shard, a_buf)]
        ga, gb, gz = gens
        for g in gens:
            next(g)
        for c in locals_:
            c.start()
        for c in locals_:
            c.wait()
        for g in (ga, gb, ga, gb, ga, gb, gz, ga, gb):
            next(g)
        run([ga, gb])
        run([gz])
        cot_gen = ag_z_gen(w, me, cot, cot_full)
        next(cot_gen)
        keep = pltpu.make_async_copy(a_buf, a_full, lsem.at[4])
        keep.start()

        def one_pack(p, _):
            allowed, cosine, sine = pack_tables(segs, p, table)
            qkv = dot(pack_of(a_buf, p), front_full[:, :, :, 0:384].reshape(D, 384)).T
            qk_pre[p] = qkv[0:320]
            value = qkv[320:384].astype(bf16)
            v_rows[p] = value
            kn, _i = head_norm(qkv[256:320], gain_key)
            key_rows = turn(kn, cosine, sine).T.astype(bf16)
            heads = []
            for j in range(4):
                qn, _i = head_norm(qkv[64 * j:64 * j + 64], gain_query)
                probs = pack_probs(key_rows, turn(qn, cosine, sine).astype(bf16), allowed)
                heads.append(dot(value, probs.astype(bf16)))
            o = jnp.concatenate(heads, axis=0).T.astype(bf16)
            mixed[p] = o
            out = dot(o, front_full[:, :, :, 384:640].reshape(D, 256), 1, 1).astype(bf16)
            part[lax.div(p, 2), lax.rem(p, 2)] = out.reshape(2, 128, D)
            return 0
        lax.fori_loop(0, 3, one_pack, 0)
        next(cot_gen)
        lax.fori_loop(3, PACKS, one_pack, 0)

        def residual(s, v):
            middle[s] = x[s].astype(f32) + v
        run([rs_z_gen(w, me, part, residual, sibs, t, r)])

        def norm_two(s):
            v = middle[s]
            inverse = lax.rsqrt(jnp.mean(v * v, axis=-1, keepdims=True) + epsilon)
            shard_two[s] = (v * inverse * gain_two).astype(bf16)
        chunks(128, norm_two)
        n_gen = ag_z_gen(w, me, shard_two, n_full)
        next(n_gen)
        own = pltpu.make_async_copy(shard_two, n_full.at[me.h, me.c, me.l], lsem.at[3])
        own.start()
        run([cot_gen])
        run([n_gen])
        own.wait()
        keep.wait()
        w.finish()

    full = jax.ShapeDtypeStruct((2, 2, 2, 128, D), bf16)
    return pl.pallas_call(
        kernel,
        out_shape=[full, full, full, jax.ShapeDtypeStruct((4, 4, 128, 640), bf16),
                   jax.ShapeDtypeStruct((PACKS, 320, SEQ), f32), jax.ShapeDtypeStruct((PACKS, HD, SEQ), bf16),
                   jax.ShapeDtypeStruct((PACKS, SEQ, 256), bf16), jax.ShapeDtypeStruct((128, D), f32)],
        in_specs=vm_specs(6), out_specs=any_specs(3) + vm_specs(5),
        scratch_shapes=[VM((128, D), bf16)] * 2 + [VM((2, 2, 2, 128, D), bf16)] * 2 + rs_z_scratch(D)
        + dma_sems(64) + [pltpu.SemaphoreType.DMA((5,))],
        compiler_params=params(cid))(x, cot, front, segs, gains, table)


def sigmoid(v):
    return 1.0 / (1.0 + jnp.exp(-v))


def feed_forward(n_full, cot_full, weights):
    def kernel(n_hbm, cot_hbm, w_hbm, grad_hbm, hidden_hbm, gate_up_hbm,
               n, cot, w, hidden, gate_up, grad, lsem, wsem, gsem):
        loads = [pltpu.make_async_copy(n_hbm, n, lsem.at[0]), pltpu.make_async_copy(cot_hbm, cot, lsem.at[1])]
        loads[0].start()

        def piece(i, k):
            here = pl.ds(pl.multiple_of(i * 256 + 1024 * k, 256), 256)
            return pltpu.make_async_copy(w_hbm.at[:, here], w.at[:, here], wsem.at[i, k])
        for i in range(4):
            for k in range(3):
                piece(i, k).start()
            if i == 0:
                loads[1].start()
        for c in loads:
            c.wait()

        def hidden_block(i, _):
            at = pl.multiple_of(i * 256, 256)
            for k in range(3):
                piece(i, k).wait()
            rows = n[...].reshape(ROWS, D)
            g = dot(rows, w[:, pl.ds(at, 256)])
            u = dot(rows, w[:, pl.ds(at + 1024, 256)])
            dh = dot(cot[...].reshape(ROWS, D), w[:, pl.ds(at + 2048, 256)])
            s = sigmoid(g)
            silu = g * s
            hidden[:, pl.ds(at, 256)] = (silu * u).astype(bf16)
            gate_up[:, pl.ds(at, 256)] = (dh * u * (s + silu * (1.0 - s))).astype(bf16)
            gate_up[:, pl.ds(at + 1024, 256)] = (dh * silu).astype(bf16)
            return 0
        lax.fori_loop(0, 4, hidden_block, 0)
        keep = [pltpu.make_async_copy(hidden, hidden_hbm, lsem.at[2]),
                pltpu.make_async_copy(gate_up, gate_up_hbm, lsem.at[3])]
        for c in keep:
            c.start()
        stores = []
        for i in range(4):
            at = 512 * i
            slot = i % 2
            if i >= 2:
                stores[i - 2].wait()
            grad[slot, :, 0:2048] = dot(n[:, :, :, :, at:at + 512].reshape(ROWS, 512), gate_up[...], 0, 0).astype(bf16)
            grad[slot, :, 2048:3072] = dot(cot[:, :, :, :, at:at + 512].reshape(ROWS, 512), hidden[...], 0, 0).astype(bf16)
            c = pltpu.make_async_copy(grad.at[slot], grad_hbm.at[pl.ds(at, 512)], gsem.at[i])
            c.start()
            stores.append(c)
        for c in stores[2:] + keep:
            c.wait()

    full = (2, 2, 2, 128, D)
    return pl.pallas_call(
        kernel,
        out_shape=[jax.ShapeDtypeStruct((D, 3072), bf16), jax.ShapeDtypeStruct((ROWS, 1024), bf16),
                   jax.ShapeDtypeStruct((ROWS, 2048), bf16)],
        in_specs=any_specs(3), out_specs=any_specs(3),
        scratch_shapes=[VM(full, bf16), VM(full, bf16), VM((D, 3072), bf16), VM((ROWS, 1024), bf16),
                        VM((ROWS, 2048), bf16), VM((2, 512, 3072), bf16), pltpu.SemaphoreType.DMA((4,)),
                        pltpu.SemaphoreType.DMA((4, 3)), pltpu.SemaphoreType.DMA((4,))],
        compiler_params=pltpu.CompilerParams(has_side_effects=True, vmem_limit_bytes=60 * 2**20))(
            n_full, cot_full, weights)


def feed_back(hidden, gate_up, weights, cid):
    def kernel(hidden_hbm, gate_up_hbm, w_hbm, out_part, db_sum, hidden, gate_up, w, part, sibs, t, r, send, recv, lsem, wsem):
        me = Place()
        loads = [pltpu.make_async_copy(gate_up_hbm, gate_up, lsem.at[0]),
                 pltpu.make_async_copy(hidden_hbm, hidden, lsem.at[1])]
        loads[0].start()

        def piece(i):
            here = pl.ds(pl.multiple_of(i * 256, 256), 256)
            return pltpu.make_async_copy(w_hbm.at[here], w.at[here], wsem.at[i])
        for i in range(8):
            piece(i).start()
        loads[1].start()
        meet([me.step("z", 1), me.step("z", -1), me.sibling()])
        loads[0].wait()

        def back_block(i, _):
            at = pl.multiple_of(i * 256, 256)
            piece(i).wait()
            v = dot(gate_up[...], w[pl.ds(at, 256), 0:2048], 1, 1).astype(bf16)
            part[:, :, :, :, pl.ds(at, 256)] = v.reshape(2, 2, 2, 128, 256)
            return 0
        lax.fori_loop(0, 8, back_block, 0)
        wire = Wire(send, recv)

        def put(s, v):
            db_sum[s] = v
        gen = rs_z_gen(wire, me, part, put, sibs, t, r)
        next(gen)
        loads[1].wait()

        def out_block(i, _):
            at = pl.multiple_of(i * 256, 256)
            v = dot(hidden[...], w[pl.ds(at, 256), 2048:3072], 1, 1).astype(bf16)
            out_part[:, :, :, :, pl.ds(at, 256)] = v.reshape(2, 2, 2, 128, 256)
            return 0
        lax.fori_loop(0, 2, out_block, 0)
        next(gen)
        lax.fori_loop(2, 8, out_block, 0)
        run([gen])
        wire.finish()

    full = (2, 2, 2, 128, D)
    return pl.pallas_call(
        kernel,
        out_shape=[jax.ShapeDtypeStruct(full, bf16), jax.ShapeDtypeStruct((128, D), f32)],
        in_specs=any_specs(3), out_specs=vm_specs(2),
        scratch_shapes=[VM((ROWS, 1024), bf16), VM((ROWS, 2048), bf16), VM((D, 3072), bf16), VM(full, bf16)]
        + rs_z_scratch(D) + dma_sems(16) + [pltpu.SemaphoreType.DMA((2,)), pltpu.SemaphoreType.DMA((8,))],
        compiler_params=params(cid, 60))(hidden, gate_up, weights)


def attention_backward(x, cot, middle, db_sum, out_part, a_full, front_full, qk_pre, v_rows, mixed, segs,
                       gains, table, cid):
    def kernel(x, cot, middle, db_sum, out_part, a_full, front_full, qk_pre, v_rows, mixed, segs,
               gains, table, input_grad, block_output, front_mine, gain_terms,
               shard, dm_full, mid_grad, dqkv, part, front_grad, q_acc, k_acc, one_acc, two_acc,
               sibs_a, t_a, r_a, sibs_b, t_b, r_b, t1, r1, t2, r2, mid, send, recv, lsem):
        me = Place()
        gain_one, gain_two, gain_query, gain_key = gain_rows(gains)
        two_acc[...] = jnp.zeros_like(two_acc)
        one_acc[...] = jnp.zeros_like(one_acc)
        q_acc[...] = jnp.zeros_like(q_acc)
        k_acc[...] = jnp.zeros_like(k_acc)

        def back(z, gain, up):
            inverse = lax.rsqrt(jnp.mean(z * z, axis=-1, keepdims=True) + epsilon)
            scaled = up * gain
            inner = jnp.mean(z * scaled, axis=-1, keepdims=True)
            return inverse * (scaled - z * inverse * inverse * inner), up * z * inverse

        def norm_two(s):
            dz, terms = back(middle[s], gain_two, db_sum[s])
            v = cot[s].astype(f32) + dz
            mid_grad[s] = v
            shard[s] = v.astype(bf16)
            two_acc[...] += terms
        chunks(128, norm_two)
        meet([me.step("x", 1), me.step("x", -1), me.step("y", 1), me.step("y", -1),
              me.step("z", 1), me.step("z", -1), me.sibling()])
        w = Wire(send, recv)
        gen = ag_z_gen(w, me, shard, dm_full)
        next(gen)
        own = pltpu.make_async_copy(shard, dm_full.at[me.h, me.c, me.l], lsem.at[0])
        own.start()
        run([gen])
        own.wait()

        def put_out(s, v):
            block_output[s] = middle[s] + v
        out_gen = rs_z_gen(w, me, out_part, put_out, sibs_a, t_a, r_a)
        next(out_gen)

        def one_pack(p, _):
            allowed, cosine, sine = pack_tables(segs, p, table)
            mixed_grad = dot(pack_of(dm_full, p), front_full[:, :, :, 384:640].reshape(D, 256)).T.astype(bf16)
            value_rows = v_rows[p].astype(f32).T.astype(bf16)
            key_pre = qk_pre[p, 256:320]
            kn, k_inverse = head_norm(key_pre, gain_key)
            kr = turn(kn, cosine, sine)
            key_rows = kr.T.astype(bf16)
            kr = kr.astype(bf16)
            dk = jnp.zeros((HD, SEQ), f32)
            dv = jnp.zeros((HD, SEQ), f32)
            heads = []
            terms_q = jnp.zeros((HD, SEQ), f32)
            for j in range(4):
                query_pre = qk_pre[p, 64 * j:64 * j + 64]
                qn, q_inverse = head_norm(query_pre, gain_query)
                qr = turn(qn, cosine, sine).astype(bf16)
                probs = pack_probs(key_rows, qr, allowed)
                do = mixed_grad[64 * j:64 * j + 64]
                dp = dot(value_rows, do)
                inner = jnp.sum(probs * dp, axis=0, keepdims=True)
                ds = (probs * (dp - inner)).astype(bf16)
                dqr = dot(kr, ds) * score_scale
                dk += dot(qr, ds, 1, 1)
                dv += dot(do, probs.astype(bf16), 1, 1)
                dq, terms = head_norm_back(query_pre, q_inverse, gain_query, turn_back(dqr, cosine, sine))
                terms_q += terms
                heads.append(dq)
            dk, terms_k = head_norm_back(key_pre, k_inverse, gain_key, turn_back(dk * score_scale, cosine, sine))
            q_acc[...] += terms_q
            k_acc[...] += terms_k
            grads = jnp.concatenate(heads + [dk, dv], axis=0).T.astype(bf16)
            dqkv[p] = grads
            out = dot(grads, front_full[:, :, :, 0:384].reshape(D, 384), 1, 1).astype(bf16)
            part[lax.div(p, 2), lax.rem(p, 2)] = out.reshape(2, 128, D)
            return 0
        lax.fori_loop(0, 2, one_pack, 0)
        next(out_gen)
        lax.fori_loop(2, PACKS, one_pack, 0)
        next(out_gen)
        def grad_block(i):
            at = 512 * i
            a_rows = a_full[:, :, :, :, at:at + 512].reshape(ROWS, 512)
            dm_rows = dm_full[:, :, :, :, at:at + 512].reshape(ROWS, 512)
            g = jnp.concatenate([dot(a_rows, dqkv[...].reshape(ROWS, 384), 0, 0),
                                 dot(dm_rows, mixed[...].reshape(ROWS, 256), 0, 0)], axis=1)
            front_grad[i] = g.astype(bf16).reshape(4, 128, 640)

        def put_in(s, v):
            dz, terms = back(x[s].astype(f32), gain_one, v)
            input_grad[s] = mid_grad[s] + dz
            one_acc[...] += terms
        in_gen = rs_z_gen(w, me, part, put_in, sibs_b, t_b, r_b)
        next(in_gen)
        grad_block(0)
        run([out_gen])
        next(in_gen)
        for i in range(1, 4):
            grad_block(i)
        ga, gb = rs_xy_gens(w, me, front_grad, front_mine, t1, r1, t2, r2, mid)
        for g in (ga, gb, ga, gb, in_gen, ga, gb, ga, gb, ga, gb):
            next(g)
        run([ga, gb])
        run([in_gen])
        w.finish()
        one = jnp.sum(one_acc[...], axis=0, keepdims=True)
        two = jnp.sum(two_acc[...], axis=0, keepdims=True)
        for i in range(16):
            gain_terms[i:i + 1, :] = one[:, 128 * i:128 * i + 128]
            gain_terms[16 + i:17 + i, :] = two[:, 128 * i:128 * i + 128]
        small = jnp.concatenate([q_acc[...], k_acc[...]], axis=0).T
        gain_terms[32:33, :] = jnp.sum(small, axis=0, keepdims=True)

    full = (2, 2, 2, 128, D)
    rows = jax.ShapeDtypeStruct((128, D), f32)
    return pl.pallas_call(
        kernel,
        out_shape=[rows, rows, jax.ShapeDtypeStruct((128, 640), bf16), jax.ShapeDtypeStruct((33, 128), f32)],
        in_specs=vm_specs(13), out_specs=vm_specs(4),
        scratch_shapes=[VM((128, D), bf16), VM(full, bf16), VM((128, D), f32), VM((PACKS, SEQ, 384), bf16),
                        VM(full, bf16), VM((4, 4, 128, 640), bf16), VM((HD, SEQ), f32), VM((HD, SEQ), f32),
                        VM((16, D), f32), VM((16, D), f32)]
        + rs_z_scratch(D) * 2 + rs_xy_scratch(640) + dma_sems(64) + [pltpu.SemaphoreType.DMA((2,))],
        compiler_params=params(cid, 60))(
            x, cot, middle, db_sum, out_part, a_full, front_full, qk_pre, v_rows, mixed, segs,
            gains, table)


def adam(weight, moment, square, gradient, rate, decay):
    momentum = beta_one * moment + (1.0 - beta_one) * gradient
    variance = beta_two * square + (1.0 - beta_two) * gradient * gradient
    ratio = momentum / (1.0 - beta_one**STEP) / (jnp.sqrt(variance / (1.0 - beta_two**STEP)) + adam_epsilon)
    return weight - rate * (ratio + decay * weight), momentum, variance


RATES = (0.04, 0.04, 0.04, 0.15, 0.04, 0.04, 0.02)
SPANS = (256, 64, 64, 256, 1024, 1024, 1024)


def return_gradients(front, rest, gain_terms, cid):
    def kernel(front, rest, terms, fbuf, rbuf, gain_sum, z_in, x_in, y_in, send, recv):
        me = Place()
        peers = swap_devs(me)
        mine = me.h * 2 + me.c
        zs = [me.at(z=m4(me.z + dz), c=lax.rem(me.c + dc, 2)) for dz in range(4) for dc in range(2) if dz or dc]
        xs = [me.step("x", d) for d in (1, 2, 3)]
        ys = [me.step("y", d) for d in (1, 2, 3)]
        meet(zs + xs + ys)
        w = Wire(send, recv)

        def total(buf, n):
            v = buf[0]
            for k in range(1, n):
                v = v + buf[k]
            return v

        def share(value, buf, slot, devs):
            buf[slot] = value
            return [w.go(buf.at[slot], buf.at[slot], d) for d in devs]
        gs = share(terms[...], z_in, me.z * 2 + me.c, zs)
        arrivals = []
        for j, dev in reversed(peers):
            arrivals.append(w.go(front.at[j], fbuf.at[mine], dev))
            arrivals.append(w.go(rest.at[j], rbuf.at[mine], dev))
        fbuf[mine] = front[mine]
        rbuf[mine] = rest[mine]
        for c in gs:
            c.wait_recv()
        gs = share(total(z_in, 8), x_in, me.x, xs)
        for c in gs:
            c.wait_recv()
        gs = share(total(x_in, 4), y_in, me.y, ys)
        for c in gs:
            c.wait_recv()
        gain_sum[...] = total(y_in, 4)
        for a in arrivals:
            a.wait_recv()
        w.finish()

    return pl.pallas_call(
        kernel, out_shape=[jax.ShapeDtypeStruct((4, 32, 640), bf16), jax.ShapeDtypeStruct((4, 32, 3072), bf16),
                           jax.ShapeDtypeStruct((33, 128), f32)],
        in_specs=vm_specs(3), out_specs=vm_specs(3),
        scratch_shapes=[VM((8, 33, 128), f32), VM((4, 33, 128), f32), VM((4, 33, 128), f32)] + dma_sems(19),
        compiler_params=params(cid))(front, rest, gain_terms)


def update(front, rest, gain_sum, gain_states, states, tokens):
    def kernel(*refs):
        front, rest, g_sum, g_w, g_m, g_v = refs[:6]
        ins, t_in, g_out, outs, t_out = refs[6:27], refs[27:29], refs[29:32], refs[32:53], refs[53:55]
        held, made = refs[55:76], refs[76:97]
        lsem, osem, tsem = refs[97:]
        loads = [pltpu.make_async_copy(a, b, lsem.at[i]) for i, (a, b) in enumerate(zip(ins, held))]
        passing = [pltpu.make_async_copy(a, b, tsem.at[i]) for i, (a, b) in enumerate(zip(t_in, t_out))]
        for c in loads + passing:
            c.start()
        new = adam(g_w[...], g_m[...], g_v[...], g_sum[...], gain_rate, 0.0)
        for ref, v in zip(g_out, new):
            ref[...] = v
        stores = []
        at = {False: 0, True: 0}
        for i, (n, rate) in enumerate(zip(SPANS, RATES)):
            late = i >= 4
            buf = rest if late else front
            for k in range(3):
                loads[3 * i + k].wait()
            for j in range(4):
                here = pl.ds(n * j, n)
                grad = buf[j, :, at[late]:at[late] + n].astype(f32)
                new = adam(held[3 * i][:, here], held[3 * i + 1][:, here], held[3 * i + 2][:, here], grad, rate,
                           weight_decay)
                for k in range(3):
                    made[3 * i + k][:, here] = new[k]
            at[late] += n
            for k in range(3):
                c = pltpu.make_async_copy(made[3 * i + k], outs[3 * i + k], osem.at[3 * i + k])
                c.start()
                stores.append(c)
        for c in stores + passing:
            c.wait()

    shapes = [jax.ShapeDtypeStruct(s.shape, f32) for s in states]
    gain_shape = jax.ShapeDtypeStruct((33, 128), f32)
    return pl.pallas_call(
        kernel, out_shape=[gain_shape] * 3 + shapes + [jax.ShapeDtypeStruct(t.shape, f32) for t in tokens],
        in_specs=vm_specs(6) + any_specs(23), out_specs=vm_specs(3) + any_specs(23),
        scratch_shapes=[VM(s.shape, f32) for s in states] * 2
        + [pltpu.SemaphoreType.DMA((21,)), pltpu.SemaphoreType.DMA((21,)), pltpu.SemaphoreType.DMA((2,))],
        compiler_params=pltpu.CompilerParams(has_side_effects=True, vmem_limit_bytes=56 * 2**20))(
            front, rest, gain_sum, *gain_states, *states, *tokens)


from jax.sharding import PartitionSpec as P

PLANE = [[x * 16 + y * 4 + k for x in range(4) for y in range(4)] for k in range(4)]


def gather_plane(shard):
    return lax.all_gather(shard, "dp", axis_index_groups=PLANE, axis=0, tiled=True)


def scatter_plane(whole):
    return lax.psum_scatter(whole, "dp", axis_index_groups=PLANE, scatter_dimension=0, tiled=True)


def local(block_input, output_grad, segment_ids, norm_gains, gain_moment, gain_square, *states):
    square = lambda v: v.reshape(33, 128)
    gains = square(norm_gains)
    table = jnp.asarray(rope_constants())
    front_shard, rest_shard, segments = spread_weights(states[::3], segment_ids, 1)
    rest_full = gather_plane(rest_shard.reshape(128, 3072))
    one_full, cot_full, two_full, front_full, qk_pre, v_rows, mixed, middle = attention_forward(
        block_input, output_grad, front_shard.reshape(128, 640), segments, gains, table, 2)
    rest_grad, hidden, gate_up = feed_forward(two_full, cot_full, rest_full)
    rest_mine = scatter_plane(rest_grad)
    out_part, db_sum = feed_back(hidden, gate_up, rest_full, 3)
    input_grad, block_output, front_mine, gain_terms = attention_backward(
        block_input, output_grad, middle, db_sum, out_part, one_full, front_full, qk_pre, v_rows, mixed, segments,
        gains, table, 4)
    front_back, rest_back, gain_sum = return_gradients(
        front_mine.reshape(4, 32, 640), rest_mine.reshape(4, 32, 3072), gain_terms, 5)
    news = update(front_back, rest_back, gain_sum, [gains, square(gain_moment), square(gain_square)], states,
                  (block_output, input_grad))
    return tuple(news[-2:]) + tuple(v.reshape(-1) for v in news[:3]) + tuple(news[3:-2])


def solution(mesh):
    tokens, weight = P(("dp", "tensor"), None), P("dp", "tensor")
    in_specs = (tokens, tokens, P("dp", None), P(), P(), P()) + (weight,) * 21
    out_specs = (tokens, tokens, P(), P(), P()) + (weight,) * 21
    return jax.shard_map(local, mesh=mesh, in_specs=in_specs, out_specs=out_specs, check_vma=False)
```

```python
import jax
import jax.numpy as jnp
import numpy as np
from jax import lax
from jax.experimental import pallas as pl
from jax.experimental.pallas import tpu as pltpu

MESH = pl.DeviceIdType.MESH
VM = pltpu.VMEM
bf16 = jnp.bfloat16
f32 = jnp.float32


def m4(v):
    return lax.rem(v + 4, 4)


class Place:
    def __init__(self):
        dp = lax.axis_index("dp")
        self.l = lax.axis_index("tensor")
        self.x = lax.div(dp, 16)
        self.y = lax.rem(lax.div(dp, 4), 4)
        self.h = lax.rem(lax.div(dp, 2), 2)
        self.c = lax.rem(dp, 2)
        self.z = self.h * 2 + self.l

    def at(self, x=None, y=None, z=None, c=None):
        x = self.x if x is None else x
        y = self.y if y is None else y
        z = self.z if z is None else z
        c = self.c if c is None else c
        return (x * 16 + y * 4 + lax.div(z, 2) * 2 + c, lax.rem(z, 2))

    def pos(self, axis):
        return {"x": self.x, "y": self.y, "z": self.z}[axis]

    def step(self, axis, d):
        return self.at(**{axis: m4(self.pos(axis) + d)})

    def sibling(self):
        return self.at(c=1 - self.c)


class Wire:
    def __init__(self, send, recv):
        self.send, self.recv, self.n = send, recv, 0
        self.pending = []

    def go(self, src, dst, dev):
        i = self.n
        self.n += 1
        c = pltpu.make_async_remote_copy(
            src_ref=src, dst_ref=dst, send_sem=self.send.at[i], recv_sem=self.recv.at[i],
            device_id=dev, device_id_type=MESH)
        c.start()
        self.pending.append(c)
        return c

    def finish(self):
        for c in self.pending:
            c.wait_send()
        self.pending = []


def meet(devs):
    b = pltpu.get_barrier_semaphore()
    for d in devs:
        pl.semaphore_signal(b, inc=1, device_id=d, device_id_type=MESH)
    pl.semaphore_wait(b, len(devs))


def ring_gather(w, me, axis, whole, lo, hi, first=None, arrived=None):
    p = me.pos(axis)
    up, down = me.step(axis, 1), me.step(axis, -1)
    own = whole(p) if first is None else first
    a = w.go(own, whole(p), up)
    b = w.go(own, whole(p), down)
    yield
    a.wait_recv()
    fa = w.go(lo(m4(p - 1)), lo(m4(p - 1)), up)
    if arrived:
        arrived(whole(m4(p - 1)))
    b.wait_recv()
    fb = w.go(hi(m4(p + 1)), hi(m4(p + 1)), down)
    if arrived:
        arrived(whole(m4(p + 1)))
    yield
    fa.wait_recv()
    if arrived:
        arrived(lo(m4(p - 2)))
    fb.wait_recv()
    if arrived:
        arrived(hi(m4(p - 2)))


def ring_scatter(w, me, axis, lo, hi, tlo, thi, rup, rdown, add):
    p = me.pos(axis)
    up, down = me.step(axis, 1), me.step(axis, -1)
    far, nu, nd = m4(p + 2), m4(p + 1), m4(p - 1)
    ta = w.go(lo(far), tlo, up)
    tb = w.go(hi(far), thi, down)
    da = w.go(hi(nu), rup[1], up)
    db = w.go(lo(nd), rdown[0], down)
    yield
    ta.wait_recv()
    add(tlo, lo(nu))
    sa = w.go(tlo, rup[0], up)
    tb.wait_recv()
    add(thi, hi(nd))
    sb = w.go(thi, rdown[1], down)
    yield
    da.wait_recv()
    db.wait_recv()
    sa.wait_recv()
    sb.wait_recv()


def loop_add(dst, a, b=None, rows=16):
    n = dst.shape[0]

    def body(i, _):
        def inner(j, _):
            s = pl.ds(pl.multiple_of(j * rows, rows), rows)
            v = dst[i, s].astype(f32) + a[i, s].astype(f32)
            if b is not None:
                v = v + b[i, s].astype(f32)
            dst[i, s] = v.astype(dst.dtype)
            return 0
        return lax.fori_loop(0, dst.shape[1] // rows, inner, 0)
    lax.fori_loop(0, n, body, 0)


def run(gens):
    gens = list(gens)
    while gens:
        for g in list(gens):
            try:
                next(g)
            except StopIteration:
                gens.remove(g)


def params(cid, mb=56):
    return pltpu.CompilerParams(collective_id=cid, has_side_effects=True, vmem_limit_bytes=mb * 2**20)


def ag_xy_gens(w, me, src, out):
    H = 64
    x, y = me.x, me.y

    def half_a():
        yield from ring_gather(w, me, "x", lambda i: out.at[i, y, pl.ds(0, 64)], lambda i: out.at[i, y, pl.ds(0, 32)],
                               lambda i: out.at[i, y, pl.ds(32, 32)], first=src.at[pl.ds(0, 64)])
        yield
        yield from ring_gather(w, me, "y", lambda i: out.at[:, i, pl.ds(0, 64)], lambda i: out.at[:, i, pl.ds(0, 32)],
                               lambda i: out.at[:, i, pl.ds(32, 32)])

    def half_b():
        yield from ring_gather(w, me, "y", lambda i: out.at[x, i, pl.ds(64, 64)], lambda i: out.at[x, i, pl.ds(64, 32)],
                               lambda i: out.at[x, i, pl.ds(96, 32)], first=src.at[pl.ds(64, 64)])
        yield
        yield from ring_gather(w, me, "x", lambda i: out.at[i, :, pl.ds(64, 64)], lambda i: out.at[i, :, pl.ds(64, 32)],
                               lambda i: out.at[i, :, pl.ds(96, 32)])
    return [half_a(), half_b()]


def ag_xy(shard, cid, space=pl.ANY):
    C = shard.shape[1]

    def kernel(src, out, send, recv, lsem):
        me = Place()
        meet([me.step("x", 1), me.step("x", -1), me.step("y", 1), me.step("y", -1)])
        w = Wire(send, recv)
        lc = pltpu.make_async_copy(src, out.at[me.x, me.y], lsem)
        lc.start()
        lc.wait()
        run(ag_xy_gens(w, me, src, out))
        w.finish()

    return pl.pallas_call(
        kernel, out_shape=jax.ShapeDtypeStruct((4, 4, 128, C), shard.dtype),
        in_specs=[pl.BlockSpec(memory_space=space)], out_specs=pl.BlockSpec(memory_space=space),
        scratch_shapes=[pltpu.SemaphoreType.DMA((16,)), pltpu.SemaphoreType.DMA((16,)), pltpu.SemaphoreType.DMA],
        compiler_params=params(cid))(shard)


def rs_xy_scratch(C):
    return [VM((2, 2, 4, 32, C), bf16), VM((2, 2, 2, 4, 32, C), bf16),
            VM((2, 2, 32, C), bf16), VM((2, 2, 2, 32, C), bf16), VM((2, 4, 64, C), bf16)]


def rs_xy_gens(w, me, g, out, t1, r1, t2, r2, mid):
    x, y = me.x, me.y

    def half(k, first, second):
        base = k * 64
        if first == "y":
            pick = lambda i, o: g.at[:, i, pl.ds(base + o, 32)]
        else:
            pick = lambda i, o: g.at[i, :, pl.ds(base + o, 32)]
        yield from ring_scatter(w, me, first, lambda i: pick(i, 0), lambda i: pick(i, 32), t1.at[k, 0], t1.at[k, 1],
                                (r1.at[k, 0, 0], r1.at[k, 0, 1]), (r1.at[k, 1, 0], r1.at[k, 1, 1]), loop_add)
        p = me.pos(first)
        m = mid.at[k]
        for hh in range(2):
            own = pick(p, 32 * hh)

            def body(i, _):
                def inner(j, _):
                    s = pl.ds(pl.multiple_of(j * 16, 16), 16)
                    d = pl.ds(pl.multiple_of(j * 16 + 32 * hh, 16), 16)
                    v = own[i, s].astype(f32) + r1[k, 0, hh, i, s].astype(f32) + r1[k, 1, hh, i, s].astype(f32)
                    m[i, d] = v.astype(bf16)
                    return 0
                return lax.fori_loop(0, 2, inner, 0)
            lax.fori_loop(0, 4, body, 0)
        yield
        q = me.pos(second)
        add1 = lambda dst, a: loop_add(dst, a)
        pick2 = lambda i, o: mid.at[k, i, pl.ds(o, 32)]

        def add2(dst, a):
            def inner(j, _):
                s = pl.ds(pl.multiple_of(j * 16, 16), 16)
                dst[s] = (dst[s].astype(f32) + a[s].astype(f32)).astype(bf16)
                return 0
            lax.fori_loop(0, 2, inner, 0)
        yield from ring_scatter(w, me, second, lambda i: pick2(i, 0), lambda i: pick2(i, 32), t2.at[k, 0], t2.at[k, 1],
                                (r2.at[k, 0, 0], r2.at[k, 0, 1]), (r2.at[k, 1, 0], r2.at[k, 1, 1]), add2)
        for hh in range(2):
            def inner(j, _):
                s = pl.ds(pl.multiple_of(j * 16, 16), 16)
                d = pl.ds(pl.multiple_of(j * 16 + 32 * hh, 16), 16)
                dd = pl.ds(pl.multiple_of(j * 16 + 32 * hh + base, 16), 16)
                v = m[q, d].astype(f32) + r2[k, 0, hh, s].astype(f32) + r2[k, 1, hh, s].astype(f32)
                out[dd] = v.astype(out.dtype)
                return 0
            lax.fori_loop(0, 2, inner, 0)
    return [half(0, "y", "x"), half(1, "x", "y")]


def rs_xy(g, cid, out_dtype=f32):
    C = g.shape[-1]

    def kernel(gin, out, send, recv, *scr):
        me = Place()
        meet([me.step("x", 1), me.step("x", -1), me.step("y", 1), me.step("y", -1)])
        w = Wire(send, recv)
        run(rs_xy_gens(w, me, gin, out, *scr))
        w.finish()

    return pl.pallas_call(
        kernel, out_shape=jax.ShapeDtypeStruct((128, C), out_dtype),
        in_specs=[pl.BlockSpec(memory_space=VM)], out_specs=pl.BlockSpec(memory_space=VM),
        scratch_shapes=[pltpu.SemaphoreType.DMA((24,)), pltpu.SemaphoreType.DMA((24,))] + rs_xy_scratch(C),
        compiler_params=params(cid, 60))(g)


def ag_z_gen(w, me, src, out):
    sib = me.sibling()
    blk = lambda i, cc: out.at[lax.div(i, 2), cc, lax.rem(i, 2)]
    cs = []

    def to_sib(ref):
        cs.append(w.go(ref, ref, sib))
    whole = lambda i: blk(i, me.c)
    own = w.go(src, whole(me.z), sib)
    yield from ring_gather(w, me, "z", whole, lambda i: whole(i).at[pl.ds(0, 64)], lambda i: whole(i).at[pl.ds(64, 64)],
                           first=src, arrived=to_sib)
    own.wait_recv()
    for c in cs:
        c.wait_recv()


def ag_z(shard, cid, space=VM):
    C = shard.shape[1]

    def kernel(src, out, send, recv, lsem):
        me = Place()
        meet([me.step("z", 1), me.step("z", -1), me.sibling()])
        w = Wire(send, recv)
        lc = pltpu.make_async_copy(src, out.at[me.h, me.c, me.l], lsem)
        lc.start()
        lc.wait()
        run([ag_z_gen(w, me, src, out)])
        w.finish()

    return pl.pallas_call(
        kernel, out_shape=jax.ShapeDtypeStruct((2, 2, 2, 128, C), shard.dtype),
        in_specs=[pl.BlockSpec(memory_space=space)], out_specs=pl.BlockSpec(memory_space=space),
        scratch_shapes=[pltpu.SemaphoreType.DMA((16,)), pltpu.SemaphoreType.DMA((16,)), pltpu.SemaphoreType.DMA],
        compiler_params=params(cid))(shard)


def rs_z_scratch(C):
    return [VM((4, 128, C), bf16), VM((2, 64, C), bf16), VM((2, 2, 64, C), bf16)]


def rs_z_gen(w, me, g, out, sibs, t, r):
    sib = me.sibling()
    oc = 1 - me.c
    order = [2, 1, 3, 0]
    blk = lambda i, cc: g.at[lax.div(i, 2), cc, lax.rem(i, 2)]
    z = me.z
    sc = {}
    for o in order:
        i = m4(z + o)
        sc[o] = w.go(blk(i, oc), sibs.at[i], sib)
    yield

    def fold(o, s0, n):
        i = m4(z + o)
        b = blk(i, me.c)

        def inner(j, _):
            s = pl.ds(pl.multiple_of(j * 16 + s0, 16), 16)
            sibs[i, s] = (sibs[i, s].astype(f32) + b[s].astype(f32)).astype(bf16)
            return 0
        lax.fori_loop(0, n // 16, inner, 0)
    up, down = me.step("z", 1), me.step("z", -1)
    half = lambda o, k: sibs.at[m4(z + o), pl.ds(64 * k, 64)]
    sc[2].wait_recv()
    fold(2, 0, 64)
    ta = w.go(half(2, 0), t.at[0], up)
    fold(2, 64, 64)
    tb = w.go(half(2, 1), t.at[1], down)
    sc[1].wait_recv()
    fold(1, 64, 64)
    da = w.go(half(1, 1), r.at[0, 1], up)
    sc[3].wait_recv()
    fold(3, 0, 64)
    db = w.go(half(3, 0), r.at[1, 0], down)
    fold(1, 0, 64)
    fold(3, 64, 64)
    yield

    def add(dst, a):
        def inner(j, _):
            s = pl.ds(pl.multiple_of(j * 16, 16), 16)
            dst[s] = (dst[s].astype(f32) + a[s].astype(f32)).astype(bf16)
            return 0
        lax.fori_loop(0, 4, inner, 0)
    ta.wait_recv()
    add(t.at[0], half(1, 0))
    sa = w.go(t.at[0], r.at[0, 0], up)
    tb.wait_recv()
    add(t.at[1], half(3, 1))
    sb = w.go(t.at[1], r.at[1, 1], down)
    sc[0].wait_recv()
    own = blk(z, me.c)
    yield

    def last(hh):
        def inner(j, _):
            s = pl.ds(pl.multiple_of(j * 16, 16), 16)
            d = pl.ds(pl.multiple_of(j * 16 + 64 * hh, 16), 16)
            v = own[d].astype(f32) + sibs[z, d].astype(f32) + r[0, hh, s].astype(f32) + r[1, hh, s].astype(f32)
            out(d, v)
            return 0
        lax.fori_loop(0, 4, inner, 0)
    da.wait_recv()
    sa.wait_recv()
    db.wait_recv()
    sb.wait_recv()
    last(0)
    last(1)


def rs_z(g, cid, out_dtype=f32):
    C = g.shape[-1]

    def kernel(gin, out, send, recv, *scr):
        me = Place()
        meet([me.step("z", 1), me.step("z", -1), me.sibling()])
        w = Wire(send, recv)

        def put(s, v):
            out[s] = v.astype(out.dtype)
        run([rs_z_gen(w, me, gin, put, *scr)])
        w.finish()

    return pl.pallas_call(
        kernel, out_shape=jax.ShapeDtypeStruct((128, C), out_dtype),
        in_specs=[pl.BlockSpec(memory_space=VM)], out_specs=pl.BlockSpec(memory_space=VM),
        scratch_shapes=[pltpu.SemaphoreType.DMA((16,)), pltpu.SemaphoreType.DMA((16,))] + rs_z_scratch(C),
        compiler_params=params(cid))(g)


def swap_devs(me):
    out = []
    for dh, dc in ((0, 1), (1, 0), (1, 1)):
        h = lax.rem(me.h + dh, 2)
        c = lax.rem(me.c + dc, 2)
        out.append((h * 2 + c, me.at(z=h * 2 + me.l, c=c)))
    return out


def swap_hc(parts, cid):
    n = len(parts)

    def kernel(*refs):
        ins, outs = refs[:n], refs[n:2 * n]
        send, recv, lsem = refs[2 * n:]
        me = Place()
        peers = swap_devs(me)
        meet([d for _, d in peers])
        w = Wire(send, recv)
        mine = me.h * 2 + me.c
        arrivals = []
        for j, d in reversed(peers):
            for a, b in zip(ins, outs):
                arrivals.append(w.go(a.at[j], b.at[mine], d))
        ls = []
        for k, (a, b) in enumerate(zip(ins, outs)):
            lc = pltpu.make_async_copy(a.at[mine], b.at[mine], lsem.at[k])
            lc.start()
            ls.append(lc)
        for lc in ls:
            lc.wait()
        for a in arrivals:
            a.wait_recv()
        w.finish()

    return pl.pallas_call(
        kernel, out_shape=[jax.ShapeDtypeStruct(p.shape, p.dtype) for p in parts],
        in_specs=[pl.BlockSpec(memory_space=VM)] * n, out_specs=[pl.BlockSpec(memory_space=VM)] * n,
        scratch_shapes=[pltpu.SemaphoreType.DMA((3 * n,)), pltpu.SemaphoreType.DMA((3 * n,)),
                        pltpu.SemaphoreType.DMA((n,))],
        compiler_params=params(cid))(*parts)


def sum_all(v, cid):
    R, C = v.shape

    def kernel(src, out, z_in, x_in, y_in, acc, send, recv):
        me = Place()
        zs = []
        for dz in range(4):
            for dc in range(2):
                if dz or dc:
                    z, c = m4(me.z + dz), lax.rem(me.c + dc, 2)
                    zs.append(me.at(z=z, c=c))
        xs = [me.step("x", d) for d in (1, 2, 3)]
        ys = [me.step("y", d) for d in (1, 2, 3)]
        meet(zs + xs + ys)
        w = Wire(send, recv)
        acc[...] = src[...]
        for buf, slot, devs, n in ((z_in, me.z * 2 + me.c, zs, 8), (x_in, me.x, xs, 4), (y_in, me.y, ys, 4)):
            buf[slot] = acc[...]
            cs = [w.go(buf.at[slot], buf.at[slot], d) for d in devs]
            for c in cs:
                c.wait_recv()
            total = buf[0]
            for k in range(1, n):
                total = total + buf[k]
            w.finish()
            acc[...] = total
        out[...] = acc[...]

    return pl.pallas_call(
        kernel, out_shape=jax.ShapeDtypeStruct((R, C), f32),
        in_specs=[pl.BlockSpec(memory_space=VM)], out_specs=pl.BlockSpec(memory_space=VM),
        scratch_shapes=[VM((8, R, C), f32), VM((4, R, C), f32), VM((4, R, C), f32), VM((R, C), f32),
                        pltpu.SemaphoreType.DMA((13,)), pltpu.SemaphoreType.DMA((13,))],
        compiler_params=params(cid))(v)


def rs_z_packs(w, me, g, put, sibs, t, r):
    sib, oc, z = me.sibling(), 1 - me.c, me.z
    blk = lambda i, cc: g.at[lax.div(i, 2), cc, lax.rem(i, 2)]
    far = m4(z + 2)
    flip = lambda i: i + 1 - 2 * lax.rem(i, 2)
    beside, partner = flip(far), flip(z)
    up, down = me.step("z", 1), me.step("z", -1)
    half = lambda i, k: sibs.at[i, pl.ds(64 * k, 64)]

    def fold(i, s0, n):
        b = blk(i, me.c)

        def inner(j, _):
            s = pl.ds(pl.multiple_of(j * 16 + s0, 16), 16)
            sibs[i, s] = (sibs[i, s].astype(f32) + b[s].astype(f32)).astype(bf16)
            return 0
        lax.fori_loop(0, n // 16, inner, 0)

    def add(dst, a):
        def inner(j, _):
            s = pl.ds(pl.multiple_of(j * 16, 16), 16)
            dst[s] = (dst[s].astype(f32) + a[s].astype(f32)).astype(bf16)
            return 0
        lax.fori_loop(0, 4, inner, 0)
    s_far = w.go(blk(far, oc), sibs.at[far], sib)
    s_beside = w.go(blk(beside, oc), sibs.at[beside], sib)
    yield
    s_far.wait_recv()
    fold(far, 0, 64)
    ta = w.go(half(far, 0), t.at[0], up)
    fold(far, 64, 64)
    tb = w.go(half(far, 1), t.at[1], down)
    s_beside.wait_recv()
    fold(beside, 0, 128)
    yield
    s_partner = w.go(blk(partner, oc), sibs.at[partner], sib)
    s_own = w.go(blk(z, oc), sibs.at[z], sib)
    yield
    s_partner.wait_recv()
    fold(partner, 0, 128)
    nu, nd = m4(z + 1), m4(z - 1)
    da = w.go(half(nu, 1), r.at[0, 1], up)
    db = w.go(half(nd, 0), r.at[1, 0], down)
    ta.wait_recv()
    add(t.at[0], half(nu, 0))
    sa = w.go(t.at[0], r.at[0, 0], up)
    tb.wait_recv()
    add(t.at[1], half(nd, 1))
    sb = w.go(t.at[1], r.at[1, 1], down)
    s_own.wait_recv()
    own = blk(z, me.c)
    yield

    def last(hh):
        def inner(j, _):
            s = pl.ds(pl.multiple_of(j * 16, 16), 16)
            d = pl.ds(pl.multiple_of(j * 16 + 64 * hh, 16), 16)
            put(d, own[d].astype(f32) + sibs[z, d].astype(f32) + r[0, hh, s].astype(f32) + r[1, hh, s].astype(f32))
            return 0
        lax.fori_loop(0, 4, inner, 0)
    da.wait_recv()
    sa.wait_recv()
    db.wait_recv()
    sb.wait_recv()
    last(0)
    last(1)


D = 2048
HD = 64
STEP = 10
SEQ = 256
PACKS = 4
ROWS = 1024
epsilon = 1e-06
rope_base = 1000000.0
beta_one = 0.9
beta_two = 0.999
adam_epsilon = 1e-08
weight_decay = 0.1
gain_rate = 0.3
masked_score = -1000000000.0
score_scale = HD ** (-0.5)
exact = lax.Precision.HIGHEST


def dot(a, b, ca=1, cb=0, precision=None):
    return lax.dot_general(a, b, (((ca,), (cb,)), ((), ())), precision=precision, preferred_element_type=f32)


def chunks(n, body, rows=16):
    def one(j, _):
        body(pl.ds(pl.multiple_of(j * rows, rows), rows))
        return 0
    lax.fori_loop(0, n // rows, one, 0)


def dma_sems(n):
    return [pltpu.SemaphoreType.DMA((n,)), pltpu.SemaphoreType.DMA((n,))]


def vm_specs(n):
    return [pl.BlockSpec(memory_space=VM)] * n


def any_specs(n):
    return [pl.BlockSpec(memory_space=pl.ANY)] * n


class Columns:
    def __init__(self, ref, n):
        self.ref, self.n = ref, n

    def __getitem__(self, j):
        return self.ref[:, pl.ds(pl.multiple_of(j * self.n, self.n), self.n)]


def spread_weights(weights, segments, cid):
    def kernel(q_, k_, v_, o_, g_, u_, d_, seg, front, rest, segs, fbuf, rbuf, sbuf, kv, send, recv):
        me = Place()
        peers = swap_devs(me)
        mine = me.h * 2 + me.c
        q, o = Columns(q_, 256), Columns(o_, 256)
        g, u, d = Columns(g_, 1024), Columns(u_, 1024), Columns(d_, 1024)
        for j in range(4):
            kv[j] = jnp.concatenate([k_[:, 64 * j:64 * j + 64], v_[:, 64 * j:64 * j + 64]], axis=1)
        sbuf[...] = jnp.broadcast_to(seg[...], (8, SEQ))

        def rounded(j, fdst, rdst):
            fdst[:, 0:256] = q[j].astype(bf16)
            fdst[:, 256:384] = kv[j].astype(bf16)
            fdst[:, 384:640] = o[j].astype(bf16)
            for i, w in enumerate((g, u, d)):
                rdst[:, 1024 * i:1024 * i + 1024] = w[j].astype(bf16)
        meet([dev for _, dev in peers])
        w = Wire(send, recv)
        arrivals = []
        for j, dev in reversed(peers):
            rounded(j, fbuf.at[j], rbuf.at[j])
            arrivals.append(w.go(rbuf.at[j], rest.at[mine], dev))
            arrivals.append(w.go(fbuf.at[j], front.at[mine], dev))
            arrivals.append(w.go(sbuf, segs.at[mine], dev))
        rounded(mine, front.at[mine], rest.at[mine])
        segs[mine] = sbuf[...]
        for a in arrivals:
            a.wait_recv()
        w.finish()

    return pl.pallas_call(
        kernel,
        out_shape=[jax.ShapeDtypeStruct((4, 32, 640), bf16), jax.ShapeDtypeStruct((4, 32, 3072), bf16),
                   jax.ShapeDtypeStruct((4, 8, SEQ), jnp.int32)],
        in_specs=vm_specs(8), out_specs=vm_specs(3),
        scratch_shapes=[VM((4, 32, 640), bf16), VM((4, 32, 3072), bf16), VM((8, SEQ), jnp.int32),
                        VM((4, 32, 128), f32)] + dma_sems(9),
        compiler_params=params(cid))(*weights, segments)


def gain_rows(gains):
    one = jnp.concatenate([gains[i:i + 1, :] for i in range(16)], axis=1)
    two = jnp.concatenate([gains[16 + i:17 + i, :] for i in range(16)], axis=1)
    small = jnp.broadcast_to(gains[32:33, :], (128, 128)).T
    return one, two, small[0:64, 0:1], small[64:128, 0:1]


def rope_constants():
    frequency = np.float32(rope_base) ** (np.float32(-2.0) * np.arange(HD // 2, dtype=np.float32) / np.float32(HD))
    angles = (np.arange(SEQ, dtype=np.float32)[None, :] * frequency[:, None].astype(np.float32)).astype(np.float64)
    return np.concatenate([np.cos(angles), np.sin(angles)], axis=0).astype(np.float32)


def pack_tables(segs, p, table):
    row = segs[p].astype(f32)[0:1, :]
    column = jnp.broadcast_to(row, (128, SEQ)).T[:, 0:1]
    key_at = lax.broadcasted_iota(jnp.int32, (SEQ, SEQ), 0)
    query_at = lax.broadcasted_iota(jnp.int32, (SEQ, SEQ), 1)
    allowed = (column == row) & (key_at <= query_at)
    start = jnp.sum(jnp.where(column < row, 1.0, 0.0), axis=0, keepdims=True)
    where = query_at.astype(f32) - start
    hot = jnp.where(key_at.astype(f32) == where, 1.0, 0.0)
    both = dot(table[...], hot, precision=exact)
    return allowed, both[0:32], both[32:64]


def head_norm(z, gain):
    inverse = lax.rsqrt(jnp.mean(z * z, axis=0, keepdims=True) + epsilon)
    return z * inverse * gain, inverse


def head_norm_back(z, inverse, gain, up):
    scaled = up * gain
    inner = jnp.mean(z * scaled, axis=0, keepdims=True)
    return inverse * (scaled - z * inverse * inverse * inner), up * z * inverse


def turn(u, cosine, sine):
    a, b = u[0:32], u[32:64]
    return jnp.concatenate([a * cosine - b * sine, b * cosine + a * sine], axis=0)


def turn_back(u, cosine, sine):
    a, b = u[0:32], u[32:64]
    return jnp.concatenate([a * cosine + b * sine, b * cosine - a * sine], axis=0)


def pack_probs(key_rows, query_rot, allowed):
    scores = jnp.where(allowed, dot(key_rows, query_rot) * score_scale, masked_score)
    exps = jnp.exp(scores - jnp.max(scores, axis=0, keepdims=True))
    return exps / jnp.sum(exps, axis=0, keepdims=True)


def pack_of(ref, p):
    v = ref[lax.div(p, 2), lax.rem(p, 2)]
    return v.reshape(SEQ, v.shape[-1])


def pack_turn(me, i):
    h = me.h if i >= 2 else 1 - me.h
    c = me.c if i % 2 else 1 - me.c
    return h * 2 + c


def attention_forward(x, cot, front, segs, gains, table, cid):
    def kernel(x, cot, front, segs, gains, table,
               a_full, cot_full, n_full, front_full, qk_pre, v_rows, mixed, middle,
               shard, shard_two, a_buf, part, sibs, t, r, send, recv, lsem):
        me = Place()
        gain_one, gain_two, gain_query, gain_key = gain_rows(gains)

        def norm_one(s):
            v = x[s].astype(f32)
            inverse = lax.rsqrt(jnp.mean(v * v, axis=-1, keepdims=True) + epsilon)
            shard[s] = (v * inverse * gain_one).astype(bf16)
        chunks(128, norm_one)
        meet([me.step("x", 1), me.step("x", -1), me.step("y", 1), me.step("y", -1),
              me.step("z", 1), me.step("z", -1), me.sibling()])
        w = Wire(send, recv)
        locals_ = [pltpu.make_async_copy(front, front_full.at[me.x, me.y], lsem.at[0]),
                   pltpu.make_async_copy(shard, a_buf.at[me.h, me.c, me.l], lsem.at[1]),
                   pltpu.make_async_copy(cot, cot_full.at[me.h, me.c, me.l], lsem.at[2])]
        gens = ag_xy_gens(w, me, front, front_full) + [ag_z_gen(w, me, shard, a_buf)]
        ga, gb, gz = gens
        for g in gens:
            next(g)
        for c in locals_:
            c.start()
        for c in locals_:
            c.wait()
        for g in (ga, gb, ga, gb, ga, gb, gz, ga, gb):
            next(g)
        run([ga, gb])
        run([gz])
        cot_gen = ag_z_gen(w, me, cot, cot_full)
        next(cot_gen)
        keep = pltpu.make_async_copy(a_buf, a_full, lsem.at[4])
        keep.start()

        def one_pack(p, _):
            allowed, cosine, sine = pack_tables(segs, p, table)
            qkv = dot(pack_of(a_buf, p), front_full[:, :, :, 0:384].reshape(D, 384)).T
            qk_pre[p] = qkv[0:320]
            value = qkv[320:384].astype(bf16)
            v_rows[p] = value
            kn, _i = head_norm(qkv[256:320], gain_key)
            key_rows = turn(kn, cosine, sine).T.astype(bf16)
            heads = []
            for j in range(4):
                qn, _i = head_norm(qkv[64 * j:64 * j + 64], gain_query)
                probs = pack_probs(key_rows, turn(qn, cosine, sine).astype(bf16), allowed)
                heads.append(dot(value, probs.astype(bf16)))
            o = jnp.concatenate(heads, axis=0).T.astype(bf16)
            mixed[p] = o
            out = dot(o, front_full[:, :, :, 384:640].reshape(D, 256), 1, 1).astype(bf16)
            part[lax.div(p, 2), lax.rem(p, 2)] = out.reshape(2, 128, D)
            return 0
        lax.fori_loop(0, 3, one_pack, 0)
        next(cot_gen)
        lax.fori_loop(3, PACKS, one_pack, 0)

        def residual(s, v):
            middle[s] = x[s].astype(f32) + v
        run([rs_z_gen(w, me, part, residual, sibs, t, r)])

        def norm_two(s):
            v = middle[s]
            inverse = lax.rsqrt(jnp.mean(v * v, axis=-1, keepdims=True) + epsilon)
            shard_two[s] = (v * inverse * gain_two).astype(bf16)
        chunks(128, norm_two)
        n_gen = ag_z_gen(w, me, shard_two, n_full)
        next(n_gen)
        own = pltpu.make_async_copy(shard_two, n_full.at[me.h, me.c, me.l], lsem.at[3])
        own.start()
        run([cot_gen])
        run([n_gen])
        own.wait()
        keep.wait()
        w.finish()

    full = jax.ShapeDtypeStruct((2, 2, 2, 128, D), bf16)
    return pl.pallas_call(
        kernel,
        out_shape=[full, full, full, jax.ShapeDtypeStruct((4, 4, 128, 640), bf16),
                   jax.ShapeDtypeStruct((PACKS, 320, SEQ), f32), jax.ShapeDtypeStruct((PACKS, HD, SEQ), bf16),
                   jax.ShapeDtypeStruct((PACKS, SEQ, 256), bf16), jax.ShapeDtypeStruct((128, D), f32)],
        in_specs=vm_specs(6), out_specs=any_specs(3) + vm_specs(5),
        scratch_shapes=[VM((128, D), bf16)] * 2 + [VM((2, 2, 2, 128, D), bf16)] * 2 + rs_z_scratch(D)
        + dma_sems(64) + [pltpu.SemaphoreType.DMA((5,))],
        compiler_params=params(cid))(x, cot, front, segs, gains, table)


def sigmoid(v):
    return 1.0 / (1.0 + jnp.exp(-v))


def feed_forward(n_full, cot_full, weights, cid):
    def kernel(n_hbm, cot_hbm, w_hbm, grad_hbm, hidden_hbm, db_sum,
               n, cot, w, hidden, gate_up, part, grad, sibs_a, t_a, r_a, sibs_b, t_b, r_b, send, recv, lsem, wsem, gsem):
        me = Place()
        loads = [pltpu.make_async_copy(n_hbm, n, lsem.at[0]), pltpu.make_async_copy(cot_hbm, cot, lsem.at[1])]
        loads[0].start()

        def piece(i, k):
            here = pl.ds(pl.multiple_of(i * 256 + 1024 * k, 256), 256)
            return pltpu.make_async_copy(w_hbm.at[:, here], w.at[:, here], wsem.at[i, k])
        for i in range(4):
            for k in range(3):
                piece(i, k).start()
            if i == 0:
                loads[1].start()
        meet([me.step("z", 1), me.step("z", -1), me.sibling()])
        for c in loads:
            c.wait()

        def hidden_block(i, _):
            at = pl.multiple_of(i * 256, 256)
            for k in range(3):
                piece(i, k).wait()
            rows = n[...].reshape(ROWS, D)
            g = dot(rows, w[:, pl.ds(at, 256)])
            u = dot(rows, w[:, pl.ds(at + 1024, 256)])
            dh = dot(cot[...].reshape(ROWS, D), w[:, pl.ds(at + 2048, 256)])
            s = sigmoid(g)
            silu = g * s
            hidden[:, pl.ds(at, 256)] = (silu * u).astype(bf16)
            gate_up[:, pl.ds(at, 256)] = (dh * u * (s + silu * (1.0 - s))).astype(bf16)
            gate_up[:, pl.ds(at + 1024, 256)] = (dh * silu).astype(bf16)
            return 0
        lax.fori_loop(0, 4, hidden_block, 0)
        keep = pltpu.make_async_copy(hidden, hidden_hbm, lsem.at[2])
        keep.start()

        def back_block(i, _):
            at = pl.multiple_of(i * 256, 256)
            v = dot(gate_up[...], w[pl.ds(at, 256), 0:2048], 1, 1).astype(bf16)
            part[:, :, :, :, pl.ds(at, 256)] = v.reshape(2, 2, 2, 128, 256)
            return 0
        wire = Wire(send, recv)

        def put_a(s, v):
            db_sum[s, 0:1024] = v

        def put_b(s, v):
            db_sum[s, 1024:2048] = v
        stores = []

        def grad_block(i):
            at = 512 * i
            slot = i % 2
            if i >= 2:
                stores[i - 2].wait()
            grad[slot, :, 0:2048] = dot(n[:, :, :, :, at:at + 512].reshape(ROWS, 512), gate_up[...], 0, 0).astype(bf16)
            grad[slot, :, 2048:3072] = dot(cot[:, :, :, :, at:at + 512].reshape(ROWS, 512), hidden[...], 0, 0).astype(bf16)
            c = pltpu.make_async_copy(grad.at[slot], grad_hbm.at[pl.ds(at, 512)], gsem.at[i])
            c.start()
            stores.append(c)
        lax.fori_loop(0, 4, back_block, 0)
        gen_a = rs_z_gen(wire, me, part.at[:, :, :, :, pl.ds(0, 1024)], put_a, sibs_a, t_a, r_a)
        gen_b = rs_z_gen(wire, me, part.at[:, :, :, :, pl.ds(1024, 1024)], put_b, sibs_b, t_b, r_b)
        next(gen_a)
        lax.fori_loop(4, 8, back_block, 0)
        next(gen_b)
        next(gen_a)
        grad_block(0)
        next(gen_b)
        grad_block(1)
        next(gen_a)
        grad_block(2)
        next(gen_b)
        grad_block(3)
        run([gen_a])
        run([gen_b])
        for c in stores[2:] + [keep]:
            c.wait()
        wire.finish()

    full = (2, 2, 2, 128, D)
    return pl.pallas_call(
        kernel,
        out_shape=[jax.ShapeDtypeStruct((D, 3072), bf16), jax.ShapeDtypeStruct((ROWS, 1024), bf16),
                   jax.ShapeDtypeStruct((128, D), f32)],
        in_specs=any_specs(3), out_specs=any_specs(2) + vm_specs(1),
        scratch_shapes=[VM(full, bf16), VM(full, bf16), VM((D, 3072), bf16), VM((ROWS, 1024), bf16),
                        VM((ROWS, 2048), bf16), VM(full, bf16), VM((2, 512, 3072), bf16)]
        + rs_z_scratch(1024) * 2 + dma_sems(32) + [pltpu.SemaphoreType.DMA((3,)), pltpu.SemaphoreType.DMA((4, 3)),
                                                   pltpu.SemaphoreType.DMA((4,))],
        compiler_params=params(cid, 60))(n_full, cot_full, weights)


def attention_backward(x, cot, middle, db_sum, hidden, weights, a_full, front_full, qk_pre, v_rows, mixed, segs,
                       gains, table, cid):
    def kernel(x, cot, middle, db_sum, hidden_hbm, w_hbm, a_full, front_full, qk_pre, v_rows, mixed, segs,
               gains, table, input_grad, block_output, front_mine, gain_terms,
               shard, hidden, wd, out_part, dm_full, mid_grad, dqkv, part, front_grad, q_acc, k_acc, one_acc, two_acc,
               sibs_a, t_a, r_a, sibs_b, t_b, r_b, t1, r1, t2, r2, mid, send, recv, lsem):
        me = Place()
        gain_one, gain_two, gain_query, gain_key = gain_rows(gains)
        loads = [pltpu.make_async_copy(hidden_hbm, hidden, lsem.at[1]),
                 pltpu.make_async_copy(w_hbm.at[:, pl.ds(2048, 1024)], wd, lsem.at[2])]
        for c in loads:
            c.start()
        two_acc[...] = jnp.zeros_like(two_acc)
        one_acc[...] = jnp.zeros_like(one_acc)
        q_acc[...] = jnp.zeros_like(q_acc)
        k_acc[...] = jnp.zeros_like(k_acc)

        def back(z, gain, up):
            inverse = lax.rsqrt(jnp.mean(z * z, axis=-1, keepdims=True) + epsilon)
            scaled = up * gain
            inner = jnp.mean(z * scaled, axis=-1, keepdims=True)
            return inverse * (scaled - z * inverse * inverse * inner), up * z * inverse

        def norm_two(s):
            dz, terms = back(middle[s], gain_two, db_sum[s])
            v = cot[s].astype(f32) + dz
            mid_grad[s] = v
            shard[s] = v.astype(bf16)
            two_acc[...] += terms
        chunks(128, norm_two)
        meet([me.step("x", 1), me.step("x", -1), me.step("y", 1), me.step("y", -1),
              me.step("z", 1), me.step("z", -1), me.sibling()])
        w = Wire(send, recv)
        gen = ag_z_gen(w, me, shard, dm_full)
        next(gen)
        own = pltpu.make_async_copy(shard, dm_full.at[me.h, me.c, me.l], lsem.at[0])
        own.start()
        for c in loads:
            c.wait()

        def out_block(i, _):
            at = pl.multiple_of(i * 256, 256)
            v = dot(hidden[...], wd[pl.ds(at, 256)], 1, 1).astype(bf16)
            out_part[:, :, :, :, pl.ds(at, 256)] = v.reshape(2, 2, 2, 128, 256)
            return 0
        lax.fori_loop(0, 8, out_block, 0)

        def put_out(s, v):
            block_output[s] = middle[s] + v
        out_gen = rs_z_gen(w, me, out_part, put_out, sibs_a, t_a, r_a)
        next(gen)
        next(out_gen)
        run([gen])
        own.wait()

        def one_pack(p, _):
            allowed, cosine, sine = pack_tables(segs, p, table)
            mixed_grad = dot(pack_of(dm_full, p), front_full[:, :, :, 384:640].reshape(D, 256)).T.astype(bf16)
            value_rows = v_rows[p].astype(f32).T.astype(bf16)
            key_pre = qk_pre[p, 256:320]
            kn, k_inverse = head_norm(key_pre, gain_key)
            kr = turn(kn, cosine, sine)
            key_rows = kr.T.astype(bf16)
            kr = kr.astype(bf16)
            dk = jnp.zeros((HD, SEQ), f32)
            dv = jnp.zeros((HD, SEQ), f32)
            heads = []
            terms_q = jnp.zeros((HD, SEQ), f32)
            for j in range(4):
                query_pre = qk_pre[p, 64 * j:64 * j + 64]
                qn, q_inverse = head_norm(query_pre, gain_query)
                qr = turn(qn, cosine, sine).astype(bf16)
                probs = pack_probs(key_rows, qr, allowed)
                do = mixed_grad[64 * j:64 * j + 64]
                dp = dot(value_rows, do)
                inner = jnp.sum(probs * dp, axis=0, keepdims=True)
                ds = (probs * (dp - inner)).astype(bf16)
                dqr = dot(kr, ds) * score_scale
                dk += dot(qr, ds, 1, 1)
                dv += dot(do, probs.astype(bf16), 1, 1)
                dq, terms = head_norm_back(query_pre, q_inverse, gain_query, turn_back(dqr, cosine, sine))
                terms_q += terms
                heads.append(dq)
            dk, terms_k = head_norm_back(key_pre, k_inverse, gain_key, turn_back(dk * score_scale, cosine, sine))
            q_acc[...] += terms_q
            k_acc[...] += terms_k
            grads = jnp.concatenate(heads + [dk, dv], axis=0).T.astype(bf16)
            dqkv[p] = grads
            out = dot(grads, front_full[:, :, :, 0:384].reshape(D, 384), 1, 1).astype(bf16)
            part[lax.div(p, 2), lax.rem(p, 2)] = out.reshape(2, 128, D)
            return 0
        def grad_block(i):
            at = 512 * i
            a_rows = a_full[:, :, :, :, at:at + 512].reshape(ROWS, 512)
            dm_rows = dm_full[:, :, :, :, at:at + 512].reshape(ROWS, 512)
            g = jnp.concatenate([dot(a_rows, dqkv[...].reshape(ROWS, 384), 0, 0),
                                 dot(dm_rows, mixed[...].reshape(ROWS, 256), 0, 0)], axis=1)
            front_grad[i] = g.astype(bf16).reshape(4, 128, 640)

        def put_in(s, v):
            dz, terms = back(x[s].astype(f32), gain_one, v)
            input_grad[s] = mid_grad[s] + dz
            one_acc[...] += terms
        in_gen = rs_z_packs(w, me, part, put_in, sibs_b, t_b, r_b)
        next(out_gen)
        one_pack(pack_turn(me, 0), 0)
        next(in_gen)
        next(out_gen)
        one_pack(pack_turn(me, 1), 0)
        run([out_gen])
        next(in_gen)
        one_pack(pack_turn(me, 2), 0)
        next(in_gen)
        one_pack(pack_turn(me, 3), 0)
        next(in_gen)
        for i in range(4):
            grad_block(i)
        ga, gb = rs_xy_gens(w, me, front_grad, front_mine, t1, r1, t2, r2, mid)
        for g in (ga, gb, ga, gb, ga, gb, ga, gb):
            next(g)
        run([in_gen])
        run([ga, gb])
        w.finish()
        one = jnp.sum(one_acc[...], axis=0, keepdims=True)
        two = jnp.sum(two_acc[...], axis=0, keepdims=True)
        for i in range(16):
            gain_terms[i:i + 1, :] = one[:, 128 * i:128 * i + 128]
            gain_terms[16 + i:17 + i, :] = two[:, 128 * i:128 * i + 128]
        small = jnp.concatenate([q_acc[...], k_acc[...]], axis=0).T
        gain_terms[32:33, :] = jnp.sum(small, axis=0, keepdims=True)

    full = (2, 2, 2, 128, D)
    rows = jax.ShapeDtypeStruct((128, D), f32)
    return pl.pallas_call(
        kernel,
        out_shape=[rows, rows, jax.ShapeDtypeStruct((128, 640), bf16), jax.ShapeDtypeStruct((33, 128), f32)],
        in_specs=vm_specs(4) + any_specs(2) + vm_specs(8), out_specs=vm_specs(4),
        scratch_shapes=[VM((128, D), bf16), VM((ROWS, 1024), bf16), VM((D, 1024), bf16), VM(full, bf16),
                        VM(full, bf16), VM((128, D), f32), VM((PACKS, SEQ, 384), bf16),
                        VM(full, bf16), VM((4, 4, 128, 640), bf16), VM((HD, SEQ), f32), VM((HD, SEQ), f32),
                        VM((16, D), f32), VM((16, D), f32)]
        + rs_z_scratch(D) * 2 + rs_xy_scratch(640) + dma_sems(64) + [pltpu.SemaphoreType.DMA((3,))],
        compiler_params=params(cid, 60))(
            x, cot, middle, db_sum, hidden, weights, a_full, front_full, qk_pre, v_rows, mixed, segs,
            gains, table)


def adam(weight, moment, square, gradient, rate, decay):
    momentum = beta_one * moment + (1.0 - beta_one) * gradient
    variance = beta_two * square + (1.0 - beta_two) * gradient * gradient
    ratio = momentum / (1.0 - beta_one**STEP) / (jnp.sqrt(variance / (1.0 - beta_two**STEP)) + adam_epsilon)
    return weight - rate * (ratio + decay * weight), momentum, variance


RATES = (0.04, 0.04, 0.04, 0.15, 0.04, 0.04, 0.02)
SPANS = (256, 64, 64, 256, 1024, 1024, 1024)


def return_gradients(front, rest, gain_terms, cid):
    def kernel(front, rest, terms, fbuf, rbuf, gain_sum, z_in, x_in, y_in, send, recv):
        me = Place()
        peers = swap_devs(me)
        mine = me.h * 2 + me.c
        zs = [me.at(z=m4(me.z + dz), c=lax.rem(me.c + dc, 2)) for dz in range(4) for dc in range(2) if dz or dc]
        xs = [me.step("x", d) for d in (1, 2, 3)]
        ys = [me.step("y", d) for d in (1, 2, 3)]
        meet(zs + xs + ys)
        w = Wire(send, recv)

        def total(buf, n):
            v = buf[0]
            for k in range(1, n):
                v = v + buf[k]
            return v

        def share(value, buf, slot, devs):
            buf[slot] = value
            return [w.go(buf.at[slot], buf.at[slot], d) for d in devs]
        gs = share(terms[...], z_in, me.z * 2 + me.c, zs)
        arrivals = []
        for j, dev in reversed(peers):
            arrivals.append(w.go(front.at[j], fbuf.at[mine], dev))
            arrivals.append(w.go(rest.at[j], rbuf.at[mine], dev))
        fbuf[mine] = front[mine]
        rbuf[mine] = rest[mine]
        for c in gs:
            c.wait_recv()
        gs = share(total(z_in, 8), x_in, me.x, xs)
        for c in gs:
            c.wait_recv()
        gs = share(total(x_in, 4), y_in, me.y, ys)
        for c in gs:
            c.wait_recv()
        gain_sum[...] = total(y_in, 4)
        for a in arrivals:
            a.wait_recv()
        w.finish()

    return pl.pallas_call(
        kernel, out_shape=[jax.ShapeDtypeStruct((4, 32, 640), bf16), jax.ShapeDtypeStruct((4, 32, 3072), bf16),
                           jax.ShapeDtypeStruct((33, 128), f32)],
        in_specs=vm_specs(3), out_specs=vm_specs(3),
        scratch_shapes=[VM((8, 33, 128), f32), VM((4, 33, 128), f32), VM((4, 33, 128), f32)] + dma_sems(19),
        compiler_params=params(cid))(front, rest, gain_terms)


def update(front, rest, gain_sum, gain_states, states, tokens):
    def kernel(*refs):
        front, rest, g_sum, g_w, g_m, g_v = refs[:6]
        ins, t_in, g_out, outs, t_out = refs[6:27], refs[27:29], refs[29:32], refs[32:53], refs[53:55]
        held, made, kept = refs[55:76], refs[76:97], refs[97:99]
        lsem, osem, tsem = refs[99:]
        loads = [pltpu.make_async_copy(a, b, lsem.at[i]) for i, (a, b) in enumerate(zip(ins, held))]
        coming = [pltpu.make_async_copy(a, b, tsem.at[i]) for i, (a, b) in enumerate(zip(t_in, kept))]
        for c in loads + coming:
            c.start()
        new = adam(g_w[...], g_m[...], g_v[...], g_sum[...], gain_rate, 0.0)
        for ref, v in zip(g_out, new):
            ref[...] = v
        stores = []
        at = {False: 0, True: 0}
        for i, (n, rate) in enumerate(zip(SPANS, RATES)):
            late = i >= 4
            buf = rest if late else front
            for k in range(3):
                loads[3 * i + k].wait()
            for j in range(4):
                here = pl.ds(n * j, n)
                grad = buf[j, :, at[late]:at[late] + n].astype(f32)
                new = adam(held[3 * i][:, here], held[3 * i + 1][:, here], held[3 * i + 2][:, here], grad, rate,
                           weight_decay)
                for k in range(3):
                    made[3 * i + k][:, here] = new[k]
            at[late] += n
            for k in range(3):
                c = pltpu.make_async_copy(made[3 * i + k], outs[3 * i + k], osem.at[3 * i + k])
                c.start()
                stores.append(c)
        for i in range(2):
            coming[i].wait()
            c = pltpu.make_async_copy(kept[i], t_out[i], tsem.at[2 + i])
            c.start()
            stores.append(c)
        for c in stores:
            c.wait()

    shapes = [jax.ShapeDtypeStruct(s.shape, f32) for s in states]
    gain_shape = jax.ShapeDtypeStruct((33, 128), f32)
    return pl.pallas_call(
        kernel, out_shape=[gain_shape] * 3 + shapes + [jax.ShapeDtypeStruct(t.shape, f32) for t in tokens],
        in_specs=vm_specs(6) + any_specs(23), out_specs=vm_specs(3) + any_specs(23),
        scratch_shapes=[VM(s.shape, f32) for s in states] * 2 + [VM(t.shape, f32) for t in tokens]
        + [pltpu.SemaphoreType.DMA((21,)), pltpu.SemaphoreType.DMA((21,)), pltpu.SemaphoreType.DMA((4,))],
        compiler_params=pltpu.CompilerParams(has_side_effects=True, vmem_limit_bytes=56 * 2**20))(
            front, rest, gain_sum, *gain_states, *states, *tokens)


from jax.sharding import PartitionSpec as P

PLANE = [[x * 16 + y * 4 + k for x in range(4) for y in range(4)] for k in range(4)]


def gather_plane(shard):
    return lax.all_gather(shard, "dp", axis_index_groups=PLANE, axis=0, tiled=True)


def scatter_plane(whole):
    return lax.psum_scatter(whole, "dp", axis_index_groups=PLANE, scatter_dimension=0, tiled=True)


def local(block_input, output_grad, segment_ids, norm_gains, gain_moment, gain_square, *states):
    square = lambda v: v.reshape(33, 128)
    gains = square(norm_gains)
    table = jnp.asarray(rope_constants())
    front_shard, rest_shard, segments = spread_weights(states[::3], segment_ids, 1)
    rest_full = gather_plane(rest_shard.reshape(128, 3072))
    one_full, cot_full, two_full, front_full, qk_pre, v_rows, mixed, middle = attention_forward(
        block_input, output_grad, front_shard.reshape(128, 640), segments, gains, table, 2)
    rest_grad, hidden, db_sum = feed_forward(two_full, cot_full, rest_full, 3)
    rest_mine = scatter_plane(rest_grad)
    input_grad, block_output, front_mine, gain_terms = attention_backward(
        block_input, output_grad, middle, db_sum, hidden, rest_full, one_full, front_full, qk_pre, v_rows, mixed, segments,
        gains, table, 4)
    front_back, rest_back, gain_sum = return_gradients(
        front_mine.reshape(4, 32, 640), rest_mine.reshape(4, 32, 3072), gain_terms, 5)
    news = update(front_back, rest_back, gain_sum, [gains, square(gain_moment), square(gain_square)], states,
                  (block_output, input_grad))
    return tuple(news[-2:]) + tuple(v.reshape(-1) for v in news[:3]) + tuple(news[3:-2])


def solution(mesh):
    tokens, weight = P(("dp", "tensor"), None), P("dp", "tensor")
    in_specs = (tokens, tokens, P("dp", None), P(), P(), P()) + (weight,) * 21
    out_specs = (tokens, tokens, P(), P(), P()) + (weight,) * 21
    return jax.shard_map(local, mesh=mesh, in_specs=in_specs, out_specs=out_specs, check_vma=False)
```

```python
import jax
import jax.numpy as jnp
import numpy as np
from jax import lax
from jax.experimental import pallas as pl
from jax.experimental.pallas import tpu as pltpu

MESH = pl.DeviceIdType.MESH
VM = pltpu.VMEM
bf16 = jnp.bfloat16
f32 = jnp.float32


def m4(v):
    return lax.rem(v + 4, 4)


class Place:
    def __init__(self):
        dp = lax.axis_index("dp")
        self.l = lax.axis_index("tensor")
        self.x = lax.div(dp, 16)
        self.y = lax.rem(lax.div(dp, 4), 4)
        self.h = lax.rem(lax.div(dp, 2), 2)
        self.c = lax.rem(dp, 2)
        self.z = self.h * 2 + self.l

    def at(self, x=None, y=None, z=None, c=None):
        x = self.x if x is None else x
        y = self.y if y is None else y
        z = self.z if z is None else z
        c = self.c if c is None else c
        return (x * 16 + y * 4 + lax.div(z, 2) * 2 + c, lax.rem(z, 2))

    def pos(self, axis):
        return {"x": self.x, "y": self.y, "z": self.z}[axis]

    def step(self, axis, d):
        return self.at(**{axis: m4(self.pos(axis) + d)})

    def sibling(self):
        return self.at(c=1 - self.c)


class Wire:
    def __init__(self, send, recv):
        self.send, self.recv, self.n = send, recv, 0
        self.pending = []

    def go(self, src, dst, dev):
        i = self.n
        self.n += 1
        c = pltpu.make_async_remote_copy(
            src_ref=src, dst_ref=dst, send_sem=self.send.at[i], recv_sem=self.recv.at[i],
            device_id=dev, device_id_type=MESH)
        c.start()
        self.pending.append(c)
        return c

    def finish(self):
        for c in self.pending:
            c.wait_send()
        self.pending = []


def meet(devs):
    b = pltpu.get_barrier_semaphore()
    for d in devs:
        pl.semaphore_signal(b, inc=1, device_id=d, device_id_type=MESH)
    pl.semaphore_wait(b, len(devs))


def ring_gather(w, me, axis, whole, lo, hi, first=None, arrived=None):
    p = me.pos(axis)
    up, down = me.step(axis, 1), me.step(axis, -1)
    own = whole(p) if first is None else first
    a = w.go(own, whole(p), up)
    b = w.go(own, whole(p), down)
    yield
    a.wait_recv()
    fa = w.go(lo(m4(p - 1)), lo(m4(p - 1)), up)
    if arrived:
        arrived(whole(m4(p - 1)))
    b.wait_recv()
    fb = w.go(hi(m4(p + 1)), hi(m4(p + 1)), down)
    if arrived:
        arrived(whole(m4(p + 1)))
    yield
    fa.wait_recv()
    if arrived:
        arrived(lo(m4(p - 2)))
    fb.wait_recv()
    if arrived:
        arrived(hi(m4(p - 2)))


def ring_scatter(w, me, axis, lo, hi, tlo, thi, rup, rdown, add):
    p = me.pos(axis)
    up, down = me.step(axis, 1), me.step(axis, -1)
    far, nu, nd = m4(p + 2), m4(p + 1), m4(p - 1)
    ta = w.go(lo(far), tlo, up)
    tb = w.go(hi(far), thi, down)
    da = w.go(hi(nu), rup[1], up)
    db = w.go(lo(nd), rdown[0], down)
    yield
    ta.wait_recv()
    add(tlo, lo(nu))
    sa = w.go(tlo, rup[0], up)
    tb.wait_recv()
    add(thi, hi(nd))
    sb = w.go(thi, rdown[1], down)
    yield
    da.wait_recv()
    db.wait_recv()
    sa.wait_recv()
    sb.wait_recv()


def loop_add(dst, a, b=None, rows=16):
    n = dst.shape[0]

    def body(i, _):
        def inner(j, _):
            s = pl.ds(pl.multiple_of(j * rows, rows), rows)
            v = dst[i, s].astype(f32) + a[i, s].astype(f32)
            if b is not None:
                v = v + b[i, s].astype(f32)
            dst[i, s] = v.astype(dst.dtype)
            return 0
        return lax.fori_loop(0, dst.shape[1] // rows, inner, 0)
    lax.fori_loop(0, n, body, 0)


def run(gens):
    gens = list(gens)
    while gens:
        for g in list(gens):
            try:
                next(g)
            except StopIteration:
                gens.remove(g)


def params(cid, mb=56):
    return pltpu.CompilerParams(collective_id=cid, has_side_effects=True, vmem_limit_bytes=mb * 2**20)


def ag_xy_gens(w, me, src, out):
    H = 64
    x, y = me.x, me.y

    def half_a():
        yield from ring_gather(w, me, "x", lambda i: out.at[i, y, pl.ds(0, 64)], lambda i: out.at[i, y, pl.ds(0, 32)],
                               lambda i: out.at[i, y, pl.ds(32, 32)], first=src.at[pl.ds(0, 64)])
        yield
        yield from ring_gather(w, me, "y", lambda i: out.at[:, i, pl.ds(0, 64)], lambda i: out.at[:, i, pl.ds(0, 32)],
                               lambda i: out.at[:, i, pl.ds(32, 32)])

    def half_b():
        yield from ring_gather(w, me, "y", lambda i: out.at[x, i, pl.ds(64, 64)], lambda i: out.at[x, i, pl.ds(64, 32)],
                               lambda i: out.at[x, i, pl.ds(96, 32)], first=src.at[pl.ds(64, 64)])
        yield
        yield from ring_gather(w, me, "x", lambda i: out.at[i, :, pl.ds(64, 64)], lambda i: out.at[i, :, pl.ds(64, 32)],
                               lambda i: out.at[i, :, pl.ds(96, 32)])
    return [half_a(), half_b()]


def ag_xy(shard, cid, space=pl.ANY):
    C = shard.shape[1]

    def kernel(src, out, send, recv, lsem):
        me = Place()
        meet([me.step("x", 1), me.step("x", -1), me.step("y", 1), me.step("y", -1)])
        w = Wire(send, recv)
        lc = pltpu.make_async_copy(src, out.at[me.x, me.y], lsem)
        lc.start()
        lc.wait()
        run(ag_xy_gens(w, me, src, out))
        w.finish()

    return pl.pallas_call(
        kernel, out_shape=jax.ShapeDtypeStruct((4, 4, 128, C), shard.dtype),
        in_specs=[pl.BlockSpec(memory_space=space)], out_specs=pl.BlockSpec(memory_space=space),
        scratch_shapes=[pltpu.SemaphoreType.DMA((16,)), pltpu.SemaphoreType.DMA((16,)), pltpu.SemaphoreType.DMA],
        compiler_params=params(cid))(shard)


def rs_xy_scratch(C):
    return [VM((2, 2, 4, 32, C), bf16), VM((2, 2, 2, 4, 32, C), bf16),
            VM((2, 2, 32, C), bf16), VM((2, 2, 2, 32, C), bf16), VM((2, 4, 64, C), bf16)]


def rs_xy_gens(w, me, g, out, t1, r1, t2, r2, mid):
    x, y = me.x, me.y

    def half(k, first, second):
        base = k * 64
        if first == "y":
            pick = lambda i, o: g.at[:, i, pl.ds(base + o, 32)]
        else:
            pick = lambda i, o: g.at[i, :, pl.ds(base + o, 32)]
        yield from ring_scatter(w, me, first, lambda i: pick(i, 0), lambda i: pick(i, 32), t1.at[k, 0], t1.at[k, 1],
                                (r1.at[k, 0, 0], r1.at[k, 0, 1]), (r1.at[k, 1, 0], r1.at[k, 1, 1]), loop_add)
        p = me.pos(first)
        m = mid.at[k]
        for hh in range(2):
            own = pick(p, 32 * hh)

            def body(i, _):
                def inner(j, _):
                    s = pl.ds(pl.multiple_of(j * 16, 16), 16)
                    d = pl.ds(pl.multiple_of(j * 16 + 32 * hh, 16), 16)
                    v = own[i, s].astype(f32) + r1[k, 0, hh, i, s].astype(f32) + r1[k, 1, hh, i, s].astype(f32)
                    m[i, d] = v.astype(bf16)
                    return 0
                return lax.fori_loop(0, 2, inner, 0)
            lax.fori_loop(0, 4, body, 0)
        yield
        q = me.pos(second)
        add1 = lambda dst, a: loop_add(dst, a)
        pick2 = lambda i, o: mid.at[k, i, pl.ds(o, 32)]

        def add2(dst, a):
            def inner(j, _):
                s = pl.ds(pl.multiple_of(j * 16, 16), 16)
                dst[s] = (dst[s].astype(f32) + a[s].astype(f32)).astype(bf16)
                return 0
            lax.fori_loop(0, 2, inner, 0)
        yield from ring_scatter(w, me, second, lambda i: pick2(i, 0), lambda i: pick2(i, 32), t2.at[k, 0], t2.at[k, 1],
                                (r2.at[k, 0, 0], r2.at[k, 0, 1]), (r2.at[k, 1, 0], r2.at[k, 1, 1]), add2)
        for hh in range(2):
            def inner(j, _):
                s = pl.ds(pl.multiple_of(j * 16, 16), 16)
                d = pl.ds(pl.multiple_of(j * 16 + 32 * hh, 16), 16)
                dd = pl.ds(pl.multiple_of(j * 16 + 32 * hh + base, 16), 16)
                v = m[q, d].astype(f32) + r2[k, 0, hh, s].astype(f32) + r2[k, 1, hh, s].astype(f32)
                out[dd] = v.astype(out.dtype)
                return 0
            lax.fori_loop(0, 2, inner, 0)
    return [half(0, "y", "x"), half(1, "x", "y")]


def rs_xy(g, cid, out_dtype=f32):
    C = g.shape[-1]

    def kernel(gin, out, send, recv, *scr):
        me = Place()
        meet([me.step("x", 1), me.step("x", -1), me.step("y", 1), me.step("y", -1)])
        w = Wire(send, recv)
        run(rs_xy_gens(w, me, gin, out, *scr))
        w.finish()

    return pl.pallas_call(
        kernel, out_shape=jax.ShapeDtypeStruct((128, C), out_dtype),
        in_specs=[pl.BlockSpec(memory_space=VM)], out_specs=pl.BlockSpec(memory_space=VM),
        scratch_shapes=[pltpu.SemaphoreType.DMA((24,)), pltpu.SemaphoreType.DMA((24,))] + rs_xy_scratch(C),
        compiler_params=params(cid, 60))(g)


def ag_z_gen(w, me, src, out, r0=0, n=128):
    sib = me.sibling()
    blk = lambda i, cc: out.at[lax.div(i, 2), cc, lax.rem(i, 2)]
    cs = []

    def to_sib(ref):
        cs.append(w.go(ref, ref, sib))
    whole = lambda i: blk(i, me.c).at[pl.ds(r0, n)]
    lo = lambda i: blk(i, me.c).at[pl.ds(r0, n // 2)]
    hi = lambda i: blk(i, me.c).at[pl.ds(r0 + n // 2, n // 2)]
    own = w.go(src, whole(me.z), sib)
    yield from ring_gather(w, me, "z", whole, lo, hi, first=src, arrived=to_sib)
    own.wait_recv()
    for c in cs:
        c.wait_recv()


def ag_z(shard, cid, space=VM):
    C = shard.shape[1]

    def kernel(src, out, send, recv, lsem):
        me = Place()
        meet([me.step("z", 1), me.step("z", -1), me.sibling()])
        w = Wire(send, recv)
        lc = pltpu.make_async_copy(src, out.at[me.h, me.c, me.l], lsem)
        lc.start()
        lc.wait()
        run([ag_z_gen(w, me, src, out)])
        w.finish()

    return pl.pallas_call(
        kernel, out_shape=jax.ShapeDtypeStruct((2, 2, 2, 128, C), shard.dtype),
        in_specs=[pl.BlockSpec(memory_space=space)], out_specs=pl.BlockSpec(memory_space=space),
        scratch_shapes=[pltpu.SemaphoreType.DMA((16,)), pltpu.SemaphoreType.DMA((16,)), pltpu.SemaphoreType.DMA],
        compiler_params=params(cid))(shard)


def rs_z_scratch(C):
    return [VM((4, 128, C), bf16), VM((2, 64, C), bf16), VM((2, 2, 64, C), bf16)]


def rs_z_gen(w, me, g, out, sibs, t, r):
    sib = me.sibling()
    oc = 1 - me.c
    order = [2, 1, 3, 0]
    blk = lambda i, cc: g.at[lax.div(i, 2), cc, lax.rem(i, 2)]
    z = me.z
    sc = {}
    for o in order:
        i = m4(z + o)
        sc[o] = w.go(blk(i, oc), sibs.at[i], sib)
    yield

    def fold(o, s0, n):
        i = m4(z + o)
        b = blk(i, me.c)

        def inner(j, _):
            s = pl.ds(pl.multiple_of(j * 16 + s0, 16), 16)
            sibs[i, s] = (sibs[i, s].astype(f32) + b[s].astype(f32)).astype(bf16)
            return 0
        lax.fori_loop(0, n // 16, inner, 0)
    up, down = me.step("z", 1), me.step("z", -1)
    half = lambda o, k: sibs.at[m4(z + o), pl.ds(64 * k, 64)]
    sc[2].wait_recv()
    fold(2, 0, 64)
    ta = w.go(half(2, 0), t.at[0], up)
    fold(2, 64, 64)
    tb = w.go(half(2, 1), t.at[1], down)
    sc[1].wait_recv()
    fold(1, 64, 64)
    da = w.go(half(1, 1), r.at[0, 1], up)
    sc[3].wait_recv()
    fold(3, 0, 64)
    db = w.go(half(3, 0), r.at[1, 0], down)
    fold(1, 0, 64)
    fold(3, 64, 64)
    yield

    def add(dst, a):
        def inner(j, _):
            s = pl.ds(pl.multiple_of(j * 16, 16), 16)
            dst[s] = (dst[s].astype(f32) + a[s].astype(f32)).astype(bf16)
            return 0
        lax.fori_loop(0, 4, inner, 0)
    ta.wait_recv()
    add(t.at[0], half(1, 0))
    sa = w.go(t.at[0], r.at[0, 0], up)
    tb.wait_recv()
    add(t.at[1], half(3, 1))
    sb = w.go(t.at[1], r.at[1, 1], down)
    sc[0].wait_recv()
    own = blk(z, me.c)
    yield

    def last(hh):
        def inner(j, _):
            s = pl.ds(pl.multiple_of(j * 16, 16), 16)
            d = pl.ds(pl.multiple_of(j * 16 + 64 * hh, 16), 16)
            v = own[d].astype(f32) + sibs[z, d].astype(f32) + r[0, hh, s].astype(f32) + r[1, hh, s].astype(f32)
            out(d, v)
            return 0
        lax.fori_loop(0, 4, inner, 0)
    da.wait_recv()
    sa.wait_recv()
    db.wait_recv()
    sb.wait_recv()
    last(0)
    last(1)


def rs_z(g, cid, out_dtype=f32):
    C = g.shape[-1]

    def kernel(gin, out, send, recv, *scr):
        me = Place()
        meet([me.step("z", 1), me.step("z", -1), me.sibling()])
        w = Wire(send, recv)

        def put(s, v):
            out[s] = v.astype(out.dtype)
        run([rs_z_gen(w, me, gin, put, *scr)])
        w.finish()

    return pl.pallas_call(
        kernel, out_shape=jax.ShapeDtypeStruct((128, C), out_dtype),
        in_specs=[pl.BlockSpec(memory_space=VM)], out_specs=pl.BlockSpec(memory_space=VM),
        scratch_shapes=[pltpu.SemaphoreType.DMA((16,)), pltpu.SemaphoreType.DMA((16,))] + rs_z_scratch(C),
        compiler_params=params(cid))(g)


def swap_devs(me):
    out = []
    for dh, dc in ((0, 1), (1, 0), (1, 1)):
        h = lax.rem(me.h + dh, 2)
        c = lax.rem(me.c + dc, 2)
        out.append((h * 2 + c, me.at(z=h * 2 + me.l, c=c)))
    return out


def swap_hc(parts, cid):
    n = len(parts)

    def kernel(*refs):
        ins, outs = refs[:n], refs[n:2 * n]
        send, recv, lsem = refs[2 * n:]
        me = Place()
        peers = swap_devs(me)
        meet([d for _, d in peers])
        w = Wire(send, recv)
        mine = me.h * 2 + me.c
        arrivals = []
        for j, d in reversed(peers):
            for a, b in zip(ins, outs):
                arrivals.append(w.go(a.at[j], b.at[mine], d))
        ls = []
        for k, (a, b) in enumerate(zip(ins, outs)):
            lc = pltpu.make_async_copy(a.at[mine], b.at[mine], lsem.at[k])
            lc.start()
            ls.append(lc)
        for lc in ls:
            lc.wait()
        for a in arrivals:
            a.wait_recv()
        w.finish()

    return pl.pallas_call(
        kernel, out_shape=[jax.ShapeDtypeStruct(p.shape, p.dtype) for p in parts],
        in_specs=[pl.BlockSpec(memory_space=VM)] * n, out_specs=[pl.BlockSpec(memory_space=VM)] * n,
        scratch_shapes=[pltpu.SemaphoreType.DMA((3 * n,)), pltpu.SemaphoreType.DMA((3 * n,)),
                        pltpu.SemaphoreType.DMA((n,))],
        compiler_params=params(cid))(*parts)


def sum_all(v, cid):
    R, C = v.shape

    def kernel(src, out, z_in, x_in, y_in, acc, send, recv):
        me = Place()
        zs = []
        for dz in range(4):
            for dc in range(2):
                if dz or dc:
                    z, c = m4(me.z + dz), lax.rem(me.c + dc, 2)
                    zs.append(me.at(z=z, c=c))
        xs = [me.step("x", d) for d in (1, 2, 3)]
        ys = [me.step("y", d) for d in (1, 2, 3)]
        meet(zs + xs + ys)
        w = Wire(send, recv)
        acc[...] = src[...]
        for buf, slot, devs, n in ((z_in, me.z * 2 + me.c, zs, 8), (x_in, me.x, xs, 4), (y_in, me.y, ys, 4)):
            buf[slot] = acc[...]
            cs = [w.go(buf.at[slot], buf.at[slot], d) for d in devs]
            for c in cs:
                c.wait_recv()
            total = buf[0]
            for k in range(1, n):
                total = total + buf[k]
            w.finish()
            acc[...] = total
        out[...] = acc[...]

    return pl.pallas_call(
        kernel, out_shape=jax.ShapeDtypeStruct((R, C), f32),
        in_specs=[pl.BlockSpec(memory_space=VM)], out_specs=pl.BlockSpec(memory_space=VM),
        scratch_shapes=[VM((8, R, C), f32), VM((4, R, C), f32), VM((4, R, C), f32), VM((R, C), f32),
                        pltpu.SemaphoreType.DMA((13,)), pltpu.SemaphoreType.DMA((13,))],
        compiler_params=params(cid))(v)


def rs_z_packs(w, me, g, put, sibs, t, r):
    sib, oc, z = me.sibling(), 1 - me.c, me.z
    blk = lambda i, cc: g.at[lax.div(i, 2), cc, lax.rem(i, 2)]
    far = m4(z + 2)
    flip = lambda i: i + 1 - 2 * lax.rem(i, 2)
    beside, partner = flip(far), flip(z)
    up, down = me.step("z", 1), me.step("z", -1)
    half = lambda i, k: sibs.at[i, pl.ds(64 * k, 64)]

    def fold(i, s0, n):
        b = blk(i, me.c)

        def inner(j, _):
            s = pl.ds(pl.multiple_of(j * 16 + s0, 16), 16)
            sibs[i, s] = (sibs[i, s].astype(f32) + b[s].astype(f32)).astype(bf16)
            return 0
        lax.fori_loop(0, n // 16, inner, 0)

    def add(dst, a):
        def inner(j, _):
            s = pl.ds(pl.multiple_of(j * 16, 16), 16)
            dst[s] = (dst[s].astype(f32) + a[s].astype(f32)).astype(bf16)
            return 0
        lax.fori_loop(0, 4, inner, 0)
    s_far = w.go(blk(far, oc), sibs.at[far], sib)
    s_beside = w.go(blk(beside, oc), sibs.at[beside], sib)
    yield
    s_far.wait_recv()
    fold(far, 0, 64)
    ta = w.go(half(far, 0), t.at[0], up)
    fold(far, 64, 64)
    tb = w.go(half(far, 1), t.at[1], down)
    s_beside.wait_recv()
    fold(beside, 0, 128)
    yield
    s_partner = w.go(blk(partner, oc), sibs.at[partner], sib)
    s_own = w.go(blk(z, oc), sibs.at[z], sib)
    yield
    s_partner.wait_recv()
    fold(partner, 0, 128)
    nu, nd = m4(z + 1), m4(z - 1)
    da = w.go(half(nu, 1), r.at[0, 1], up)
    db = w.go(half(nd, 0), r.at[1, 0], down)
    ta.wait_recv()
    add(t.at[0], half(nu, 0))
    sa = w.go(t.at[0], r.at[0, 0], up)
    tb.wait_recv()
    add(t.at[1], half(nd, 1))
    sb = w.go(t.at[1], r.at[1, 1], down)
    s_own.wait_recv()
    own = blk(z, me.c)
    yield

    def last(hh):
        def inner(j, _):
            s = pl.ds(pl.multiple_of(j * 16, 16), 16)
            d = pl.ds(pl.multiple_of(j * 16 + 64 * hh, 16), 16)
            put(d, own[d].astype(f32) + sibs[z, d].astype(f32) + r[0, hh, s].astype(f32) + r[1, hh, s].astype(f32))
            return 0
        lax.fori_loop(0, 4, inner, 0)
    da.wait_recv()
    sa.wait_recv()
    db.wait_recv()
    sb.wait_recv()
    last(0)
    last(1)


D = 2048
HD = 64
STEP = 10
SEQ = 256
PACKS = 4
ROWS = 1024
epsilon = 1e-06
rope_base = 1000000.0
beta_one = 0.9
beta_two = 0.999
adam_epsilon = 1e-08
weight_decay = 0.1
gain_rate = 0.3
masked_score = -1000000000.0
score_scale = HD ** (-0.5)
exact = lax.Precision.HIGHEST


def dot(a, b, ca=1, cb=0, precision=None):
    return lax.dot_general(a, b, (((ca,), (cb,)), ((), ())), precision=precision, preferred_element_type=f32)


def chunks(n, body, rows=16):
    def one(j, _):
        body(pl.ds(pl.multiple_of(j * rows, rows), rows))
        return 0
    lax.fori_loop(0, n // rows, one, 0)


def dma_sems(n):
    return [pltpu.SemaphoreType.DMA((n,)), pltpu.SemaphoreType.DMA((n,))]


def vm_specs(n):
    return [pl.BlockSpec(memory_space=VM)] * n


def any_specs(n):
    return [pl.BlockSpec(memory_space=pl.ANY)] * n


class Columns:
    def __init__(self, ref, n):
        self.ref, self.n = ref, n

    def __getitem__(self, j):
        return self.ref[:, pl.ds(pl.multiple_of(j * self.n, self.n), self.n)]


def gain_rows(gains):
    one = jnp.concatenate([gains[i:i + 1, :] for i in range(16)], axis=1)
    two = jnp.concatenate([gains[16 + i:17 + i, :] for i in range(16)], axis=1)
    small = jnp.broadcast_to(gains[32:33, :], (128, 128)).T
    return one, two, small[0:64, 0:1], small[64:128, 0:1]


def rope_constants():
    frequency = np.float32(rope_base) ** (np.float32(-2.0) * np.arange(HD // 2, dtype=np.float32) / np.float32(HD))
    angles = (np.arange(SEQ, dtype=np.float32)[None, :] * frequency[:, None].astype(np.float32)).astype(np.float64)
    return np.concatenate([np.cos(angles), np.sin(angles)], axis=0).astype(np.float32)


def pack_tables(segs, p, table):
    row = segs[p].astype(f32)[0:1, :]
    column = jnp.broadcast_to(row, (128, SEQ)).T[:, 0:1]
    key_at = lax.broadcasted_iota(jnp.int32, (SEQ, SEQ), 0)
    query_at = lax.broadcasted_iota(jnp.int32, (SEQ, SEQ), 1)
    allowed = (column == row) & (key_at <= query_at)
    start = jnp.sum(jnp.where(column < row, 1.0, 0.0), axis=0, keepdims=True)
    where = query_at.astype(f32) - start
    hot = jnp.where(key_at.astype(f32) == where, 1.0, 0.0)
    both = dot(table[...], hot, precision=exact)
    return allowed, both[0:32], both[32:64]


def head_norm(z, gain):
    inverse = lax.rsqrt(jnp.mean(z * z, axis=0, keepdims=True) + epsilon)
    return z * inverse * gain, inverse


def head_norm_back(z, inverse, gain, up):
    scaled = up * gain
    inner = jnp.mean(z * scaled, axis=0, keepdims=True)
    return inverse * (scaled - z * inverse * inverse * inner), up * z * inverse


def turn(u, cosine, sine):
    a, b = u[0:32], u[32:64]
    return jnp.concatenate([a * cosine - b * sine, b * cosine + a * sine], axis=0)


def turn_back(u, cosine, sine):
    a, b = u[0:32], u[32:64]
    return jnp.concatenate([a * cosine + b * sine, b * cosine - a * sine], axis=0)


def pack_probs(key_rows, query_rot, allowed):
    scores = jnp.where(allowed, dot(key_rows, query_rot) * score_scale, masked_score)
    exps = jnp.exp(scores - jnp.max(scores, axis=0, keepdims=True))
    return exps / jnp.sum(exps, axis=0, keepdims=True)


def pack_of(ref, p):
    v = ref[lax.div(p, 2), lax.rem(p, 2)]
    return v.reshape(SEQ, v.shape[-1])


def pack_turn(me, i):
    h = me.h if i >= 2 else 1 - me.h
    c = me.c if i % 2 else 1 - me.c
    return h * 2 + c


def attention_forward(x, cot, weights, seg, gains, table, cid):
    def kernel(x, cot, q_, k_, v_, o_, g_, u_, d_, seg, gains, table,
               a_full, cot_full, n_full, rest_full, front_full, segs, qk_pre, v_rows, mixed, middle,
               fbuf, rbuf, sbuf, kv, fshard, rshard, rest, shard, shard_two, a_buf, part, sibs, t, r,
               send, recv, lsem, ksem):
        me = Place()
        gain_one, gain_two, gain_query, gain_key = gain_rows(gains)
        peers = swap_devs(me)
        mine = me.h * 2 + me.c
        q, o = Columns(q_, 256), Columns(o_, 256)
        g, u, d = Columns(g_, 1024), Columns(u_, 1024), Columns(d_, 1024)
        for j in range(4):
            kv[j] = jnp.concatenate([k_[:, 64 * j:64 * j + 64], v_[:, 64 * j:64 * j + 64]], axis=1)
        sbuf[...] = jnp.broadcast_to(seg[...], (8, SEQ))
        here = pl.ds(pl.multiple_of(mine * 32, 32), 32)

        def round_front(j, dst):
            dst[:, 0:256] = q[j].astype(bf16)
            dst[:, 256:384] = kv[j].astype(bf16)
            dst[:, 384:640] = o[j].astype(bf16)

        def round_rest(j, dst):
            for i, w in enumerate((g, u, d)):
                dst[:, 1024 * i:1024 * i + 1024] = w[j].astype(bf16)
        meet([me.step("x", 1), me.step("x", -1), me.step("y", 1), me.step("y", -1),
              me.step("z", 1), me.step("z", -1)] + [dev for _, dev in peers])
        w = Wire(send, recv)
        first, second = [], []
        for j, dev in reversed(peers):
            round_front(j, fbuf.at[j])
            first.append(w.go(fbuf.at[j], fshard.at[here], dev))
            second.append(w.go(sbuf, segs.at[mine], dev))
        for j, dev in reversed(peers):
            round_rest(j, rbuf.at[j])
            second.append(w.go(rbuf.at[j], rshard.at[here], dev))
        round_front(mine, fshard.at[here])
        round_rest(mine, rshard.at[here])
        segs[mine] = sbuf[...]

        def norm_one(s):
            v = x[s].astype(f32)
            inverse = lax.rsqrt(jnp.mean(v * v, axis=-1, keepdims=True) + epsilon)
            shard[s] = (v * inverse * gain_one).astype(bf16)
        chunks(128, norm_one)
        for c in first:
            c.wait_recv()

        def both(gens):
            for g in gens:
                next(g)
        front_gens = ag_xy_gens(w, me, fshard, front_full)
        both(front_gens)
        gz = ag_z_gen(w, me, shard, a_buf)
        next(gz)
        locals_ = [pltpu.make_async_copy(fshard, front_full.at[me.x, me.y], lsem.at[0]),
                   pltpu.make_async_copy(shard, a_buf.at[me.h, me.c, me.l], lsem.at[1]),
                   pltpu.make_async_copy(cot, cot_full.at[me.h, me.c, me.l], lsem.at[2])]
        for c in locals_:
            c.start()
        both(front_gens)
        for c in locals_:
            c.wait()
        both(front_gens)
        both(front_gens)
        for c in second:
            c.wait_recv()
        rest_gens = ag_xy_gens(w, me, rshard, rest)
        both(rest_gens)
        own = pltpu.make_async_copy(rshard, rest.at[me.x, me.y], lsem.at[3])
        own.start()
        both(front_gens)
        both(rest_gens)
        own.wait()
        run(front_gens)
        both(rest_gens)
        both(rest_gens)
        next(gz)
        run([gz])
        cot_gen = ag_z_gen(w, me, cot.at[pl.ds(0, 64)], cot_full, 0, 64)
        next(cot_gen)
        keep = pltpu.make_async_copy(a_buf, a_full, lsem.at[4])
        keep.start()

        def one_pack(p):
            allowed, cosine, sine = pack_tables(segs, p, table)
            qkv = dot(pack_of(a_buf, p), front_full[:, :, :, 0:384].reshape(D, 384)).T
            qk_pre[p] = qkv[0:320]
            value = qkv[320:384].astype(bf16)
            v_rows[p] = value
            kn, _i = head_norm(qkv[256:320], gain_key)
            key_rows = turn(kn, cosine, sine).T.astype(bf16)
            heads = []
            for j in range(4):
                qn, _i = head_norm(qkv[64 * j:64 * j + 64], gain_query)
                probs = pack_probs(key_rows, turn(qn, cosine, sine).astype(bf16), allowed)
                heads.append(dot(value, probs.astype(bf16)))
            o = jnp.concatenate(heads, axis=0).T.astype(bf16)
            mixed[p] = o
            out = dot(o, front_full[:, :, :, 384:640].reshape(D, 256), 1, 1).astype(bf16)
            part[lax.div(p, 2), lax.rem(p, 2)] = out.reshape(2, 128, D)

        def residual(s, v):
            middle[s] = x[s].astype(f32) + v
        sum_gen = rs_z_packs(w, me, part, residual, sibs, t, r)
        for i in range(4):
            one_pack(pack_turn(me, i))
            next(sum_gen)
            if i == 2:
                next(cot_gen)
        run([sum_gen])

        def norm_two(s):
            v = middle[s]
            inverse = lax.rsqrt(jnp.mean(v * v, axis=-1, keepdims=True) + epsilon)
            shard_two[s] = (v * inverse * gain_two).astype(bf16)
        chunks(128, norm_two)
        n_gen = ag_z_gen(w, me, shard_two, n_full)
        next(n_gen)
        own = pltpu.make_async_copy(shard_two, n_full.at[me.h, me.c, me.l], lsem.at[3])
        own.start()
        run([cot_gen])
        both(rest_gens)
        stores = []

        def store(k, a, b, at):
            here = pl.ds(at, 64)
            c = pltpu.make_async_copy(rest.at[a, b, here], rest_full.at[a, b, here], ksem.at[k])
            c.start()
            stores.append(c)
        every = slice(None)
        for k in (0, 1, 3):
            store(k, every, m4(me.y + k), 0)
            store(4 + k, m4(me.x + k), every, 64)
        next(n_gen)
        cot_gen = ag_z_gen(w, me, cot.at[pl.ds(64, 64)], cot_full, 64, 64)
        next(cot_gen)
        run([n_gen])
        run(rest_gens)
        store(2, every, m4(me.y + 2), 0)
        store(6, m4(me.x + 2), every, 64)
        run([cot_gen])
        own.wait()
        keep.wait()
        for c in stores:
            c.wait()
        w.finish()

    full = jax.ShapeDtypeStruct((2, 2, 2, 128, D), bf16)
    return pl.pallas_call(
        kernel,
        out_shape=[full, full, full, jax.ShapeDtypeStruct((4, 4, 128, 3072), bf16),
                   jax.ShapeDtypeStruct((4, 4, 128, 640), bf16), jax.ShapeDtypeStruct((4, 8, SEQ), jnp.int32),
                   jax.ShapeDtypeStruct((PACKS, 320, SEQ), f32), jax.ShapeDtypeStruct((PACKS, HD, SEQ), bf16),
                   jax.ShapeDtypeStruct((PACKS, SEQ, 256), bf16), jax.ShapeDtypeStruct((128, D), f32)],
        in_specs=vm_specs(12), out_specs=any_specs(4) + vm_specs(6),
        scratch_shapes=[VM((4, 32, 640), bf16), VM((4, 32, 3072), bf16), VM((8, SEQ), jnp.int32), VM((4, 32, 128), f32),
                        VM((128, 640), bf16), VM((128, 3072), bf16), VM((4, 4, 128, 3072), bf16)]
        + [VM((128, D), bf16)] * 2 + [VM((2, 2, 2, 128, D), bf16)] * 2 + rs_z_scratch(D)
        + dma_sems(96) + [pltpu.SemaphoreType.DMA((5,)), pltpu.SemaphoreType.DMA((8,))],
        compiler_params=params(cid, 58))(x, cot, *weights, seg, gains, table)


def sigmoid(v):
    return 1.0 / (1.0 + jnp.exp(-v))


def feed_forward(n_full, cot_full, weights, cid):
    def kernel(n_hbm, cot_hbm, w_hbm, grad_hbm, hidden_hbm, db_sum,
               n, cot, w, hidden, gate_up, part, grad, sibs_a, t_a, r_a, sibs_b, t_b, r_b, send, recv, lsem, wsem, gsem):
        me = Place()
        loads = [pltpu.make_async_copy(n_hbm, n, lsem.at[0]), pltpu.make_async_copy(cot_hbm, cot, lsem.at[1])]
        loads[0].start()

        def piece(i, k):
            here = pl.ds(pl.multiple_of(i * 256 + 1024 * k, 256), 256)
            return pltpu.make_async_copy(w_hbm.at[:, here], w.at[:, here], wsem.at[i, k])
        for i in range(4):
            for k in range(3):
                piece(i, k).start()
            if i == 0:
                loads[1].start()
        meet([me.step("z", 1), me.step("z", -1), me.sibling()])
        for c in loads:
            c.wait()

        def hidden_block(i, _):
            at = pl.multiple_of(i * 256, 256)
            for k in range(3):
                piece(i, k).wait()
            rows = n[...].reshape(ROWS, D)
            g = dot(rows, w[:, pl.ds(at, 256)])
            u = dot(rows, w[:, pl.ds(at + 1024, 256)])
            dh = dot(cot[...].reshape(ROWS, D), w[:, pl.ds(at + 2048, 256)])
            s = sigmoid(g)
            silu = g * s
            hidden[:, pl.ds(at, 256)] = (silu * u).astype(bf16)
            gate_up[:, pl.ds(at, 256)] = (dh * u * (s + silu * (1.0 - s))).astype(bf16)
            gate_up[:, pl.ds(at + 1024, 256)] = (dh * silu).astype(bf16)
            return 0
        lax.fori_loop(0, 4, hidden_block, 0)
        keep = pltpu.make_async_copy(hidden, hidden_hbm, lsem.at[2])
        keep.start()

        def back_block(i, _):
            at = pl.multiple_of(i * 256, 256)
            v = dot(gate_up[...], w[pl.ds(at, 256), 0:2048], 1, 1).astype(bf16)
            part[:, :, :, :, pl.ds(at, 256)] = v.reshape(2, 2, 2, 128, 256)
            return 0
        wire = Wire(send, recv)

        def put_a(s, v):
            db_sum[s, 0:1024] = v

        def put_b(s, v):
            db_sum[s, 1024:2048] = v
        stores = []

        def grad_block(i):
            at = 512 * i
            slot = i % 2
            if i >= 2:
                stores[i - 2].wait()
            grad[slot, :, 0:2048] = dot(n[:, :, :, :, at:at + 512].reshape(ROWS, 512), gate_up[...], 0, 0).astype(bf16)
            grad[slot, :, 2048:3072] = dot(cot[:, :, :, :, at:at + 512].reshape(ROWS, 512), hidden[...], 0, 0).astype(bf16)
            c = pltpu.make_async_copy(grad.at[slot], grad_hbm.at[pl.ds(at, 512)], gsem.at[i])
            c.start()
            stores.append(c)
        lax.fori_loop(0, 4, back_block, 0)
        gen_a = rs_z_gen(wire, me, part.at[:, :, :, :, pl.ds(0, 1024)], put_a, sibs_a, t_a, r_a)
        gen_b = rs_z_gen(wire, me, part.at[:, :, :, :, pl.ds(1024, 1024)], put_b, sibs_b, t_b, r_b)
        next(gen_a)
        lax.fori_loop(4, 8, back_block, 0)
        next(gen_b)
        next(gen_a)
        grad_block(0)
        next(gen_b)
        grad_block(1)
        next(gen_a)
        grad_block(2)
        next(gen_b)
        grad_block(3)
        run([gen_a])
        run([gen_b])
        for c in stores[2:] + [keep]:
            c.wait()
        wire.finish()

    full = (2, 2, 2, 128, D)
    return pl.pallas_call(
        kernel,
        out_shape=[jax.ShapeDtypeStruct((D, 3072), bf16), jax.ShapeDtypeStruct((ROWS, 1024), bf16),
                   jax.ShapeDtypeStruct((128, D), f32)],
        in_specs=any_specs(3), out_specs=any_specs(2) + vm_specs(1),
        scratch_shapes=[VM(full, bf16), VM(full, bf16), VM((D, 3072), bf16), VM((ROWS, 1024), bf16),
                        VM((ROWS, 2048), bf16), VM(full, bf16), VM((2, 512, 3072), bf16)]
        + rs_z_scratch(1024) * 2 + dma_sems(32) + [pltpu.SemaphoreType.DMA((3,)), pltpu.SemaphoreType.DMA((4, 3)),
                                                   pltpu.SemaphoreType.DMA((4,))],
        compiler_params=params(cid, 60))(n_full, cot_full, weights)


def attention_backward(x, cot, middle, db_sum, hidden, weights, a_full, front_full, qk_pre, v_rows, mixed, segs,
                       gains, table, cid):
    def kernel(x, cot, middle, db_sum, hidden_hbm, w_hbm, a_full, front_full, qk_pre, v_rows, mixed, segs,
               gains, table, input_grad, block_output, front_mine, gain_terms,
               shard, hidden, wd, out_part, dm_full, mid_grad, dqkv, part, front_grad, q_acc, k_acc, one_acc, two_acc,
               sibs_a, t_a, r_a, sibs_b, t_b, r_b, t1, r1, t2, r2, mid, send, recv, lsem):
        me = Place()
        gain_one, gain_two, gain_query, gain_key = gain_rows(gains)
        loads = [pltpu.make_async_copy(hidden_hbm, hidden, lsem.at[1]),
                 pltpu.make_async_copy(w_hbm.at[:, pl.ds(2048, 1024)], wd, lsem.at[2])]
        for c in loads:
            c.start()
        two_acc[...] = jnp.zeros_like(two_acc)
        one_acc[...] = jnp.zeros_like(one_acc)
        q_acc[...] = jnp.zeros_like(q_acc)
        k_acc[...] = jnp.zeros_like(k_acc)

        def back(z, gain, up):
            inverse = lax.rsqrt(jnp.mean(z * z, axis=-1, keepdims=True) + epsilon)
            scaled = up * gain
            inner = jnp.mean(z * scaled, axis=-1, keepdims=True)
            return inverse * (scaled - z * inverse * inverse * inner), up * z * inverse

        def norm_two(s):
            dz, terms = back(middle[s], gain_two, db_sum[s])
            v = cot[s].astype(f32) + dz
            mid_grad[s] = v
            shard[s] = v.astype(bf16)
            two_acc[...] += terms
        chunks(128, norm_two)
        meet([me.step("x", 1), me.step("x", -1), me.step("y", 1), me.step("y", -1),
              me.step("z", 1), me.step("z", -1), me.sibling()])
        w = Wire(send, recv)
        gen = ag_z_gen(w, me, shard, dm_full)
        next(gen)
        own = pltpu.make_async_copy(shard, dm_full.at[me.h, me.c, me.l], lsem.at[0])
        own.start()
        for c in loads:
            c.wait()

        def out_block(i, _):
            at = pl.multiple_of(i * 256, 256)
            v = dot(hidden[...], wd[pl.ds(at, 256)], 1, 1).astype(bf16)
            out_part[:, :, :, :, pl.ds(at, 256)] = v.reshape(2, 2, 2, 128, 256)
            return 0
        lax.fori_loop(0, 8, out_block, 0)

        def put_out(s, v):
            block_output[s] = middle[s] + v
        out_gen = rs_z_gen(w, me, out_part, put_out, sibs_a, t_a, r_a)
        next(gen)
        next(out_gen)
        run([gen])
        own.wait()

        def one_pack(p, _):
            allowed, cosine, sine = pack_tables(segs, p, table)
            mixed_grad = dot(pack_of(dm_full, p), front_full[:, :, :, 384:640].reshape(D, 256)).T.astype(bf16)
            value_rows = v_rows[p].astype(f32).T.astype(bf16)
            key_pre = qk_pre[p, 256:320]
            kn, k_inverse = head_norm(key_pre, gain_key)
            kr = turn(kn, cosine, sine)
            key_rows = kr.T.astype(bf16)
            kr = kr.astype(bf16)
            dk = jnp.zeros((HD, SEQ), f32)
            dv = jnp.zeros((HD, SEQ), f32)
            heads = []
            terms_q = jnp.zeros((HD, SEQ), f32)
            for j in range(4):
                query_pre = qk_pre[p, 64 * j:64 * j + 64]
                qn, q_inverse = head_norm(query_pre, gain_query)
                qr = turn(qn, cosine, sine).astype(bf16)
                probs = pack_probs(key_rows, qr, allowed)
                do = mixed_grad[64 * j:64 * j + 64]
                dp = dot(value_rows, do)
                inner = jnp.sum(probs * dp, axis=0, keepdims=True)
                ds = (probs * (dp - inner)).astype(bf16)
                dqr = dot(kr, ds) * score_scale
                dk += dot(qr, ds, 1, 1)
                dv += dot(do, probs.astype(bf16), 1, 1)
                dq, terms = head_norm_back(query_pre, q_inverse, gain_query, turn_back(dqr, cosine, sine))
                terms_q += terms
                heads.append(dq)
            dk, terms_k = head_norm_back(key_pre, k_inverse, gain_key, turn_back(dk * score_scale, cosine, sine))
            q_acc[...] += terms_q
            k_acc[...] += terms_k
            grads = jnp.concatenate(heads + [dk, dv], axis=0).T.astype(bf16)
            dqkv[p] = grads
            out = dot(grads, front_full[:, :, :, 0:384].reshape(D, 384), 1, 1).astype(bf16)
            part[lax.div(p, 2), lax.rem(p, 2)] = out.reshape(2, 128, D)
            return 0
        def grad_block(i):
            at = 512 * i
            a_rows = a_full[:, :, :, :, at:at + 512].reshape(ROWS, 512)
            dm_rows = dm_full[:, :, :, :, at:at + 512].reshape(ROWS, 512)
            g = jnp.concatenate([dot(a_rows, dqkv[...].reshape(ROWS, 384), 0, 0),
                                 dot(dm_rows, mixed[...].reshape(ROWS, 256), 0, 0)], axis=1)
            front_grad[i] = g.astype(bf16).reshape(4, 128, 640)

        def put_in(s, v):
            dz, terms = back(x[s].astype(f32), gain_one, v)
            input_grad[s] = mid_grad[s] + dz
            one_acc[...] += terms
        in_gen = rs_z_packs(w, me, part, put_in, sibs_b, t_b, r_b)
        next(out_gen)
        one_pack(pack_turn(me, 0), 0)
        next(in_gen)
        next(out_gen)
        one_pack(pack_turn(me, 1), 0)
        run([out_gen])
        next(in_gen)
        one_pack(pack_turn(me, 2), 0)
        next(in_gen)
        one_pack(pack_turn(me, 3), 0)
        next(in_gen)
        for i in range(4):
            grad_block(i)
        ga, gb = rs_xy_gens(w, me, front_grad, front_mine, t1, r1, t2, r2, mid)
        for g in (ga, gb, ga, gb, ga, gb, ga, gb):
            next(g)
        run([in_gen])
        run([ga, gb])
        w.finish()
        one = jnp.sum(one_acc[...], axis=0, keepdims=True)
        two = jnp.sum(two_acc[...], axis=0, keepdims=True)
        for i in range(16):
            gain_terms[i:i + 1, :] = one[:, 128 * i:128 * i + 128]
            gain_terms[16 + i:17 + i, :] = two[:, 128 * i:128 * i + 128]
        small = jnp.concatenate([q_acc[...], k_acc[...]], axis=0).T
        gain_terms[32:33, :] = jnp.sum(small, axis=0, keepdims=True)

    full = (2, 2, 2, 128, D)
    rows = jax.ShapeDtypeStruct((128, D), f32)
    return pl.pallas_call(
        kernel,
        out_shape=[rows, rows, jax.ShapeDtypeStruct((128, 640), bf16), jax.ShapeDtypeStruct((33, 128), f32)],
        in_specs=vm_specs(4) + any_specs(2) + vm_specs(8), out_specs=vm_specs(4),
        scratch_shapes=[VM((128, D), bf16), VM((ROWS, 1024), bf16), VM((D, 1024), bf16), VM(full, bf16),
                        VM(full, bf16), VM((128, D), f32), VM((PACKS, SEQ, 384), bf16),
                        VM(full, bf16), VM((4, 4, 128, 640), bf16), VM((HD, SEQ), f32), VM((HD, SEQ), f32),
                        VM((16, D), f32), VM((16, D), f32)]
        + rs_z_scratch(D) * 2 + rs_xy_scratch(640) + dma_sems(64) + [pltpu.SemaphoreType.DMA((3,))],
        compiler_params=params(cid, 60))(
            x, cot, middle, db_sum, hidden, weights, a_full, front_full, qk_pre, v_rows, mixed, segs,
            gains, table)


def adam(weight, moment, square, gradient, rate, decay):
    momentum = beta_one * moment + (1.0 - beta_one) * gradient
    variance = beta_two * square + (1.0 - beta_two) * gradient * gradient
    ratio = momentum / (1.0 - beta_one**STEP) / (jnp.sqrt(variance / (1.0 - beta_two**STEP)) + adam_epsilon)
    return weight - rate * (ratio + decay * weight), momentum, variance


RATES = (0.04, 0.04, 0.04, 0.15, 0.04, 0.04, 0.02)
SPANS = (256, 64, 64, 256, 1024, 1024, 1024)


def return_gradients(front, rest, gain_terms, cid):
    def kernel(front, rest, terms, fbuf, rbuf, gain_sum, z_in, x_in, y_in, send, recv):
        me = Place()
        peers = swap_devs(me)
        mine = me.h * 2 + me.c
        zs = [me.at(z=m4(me.z + dz), c=lax.rem(me.c + dc, 2)) for dz in range(4) for dc in range(2) if dz or dc]
        xs = [me.step("x", d) for d in (1, 2, 3)]
        ys = [me.step("y", d) for d in (1, 2, 3)]
        meet(zs + xs + ys)
        w = Wire(send, recv)

        def total(buf, n):
            v = buf[0]
            for k in range(1, n):
                v = v + buf[k]
            return v

        def share(value, buf, slot, devs):
            buf[slot] = value
            return [w.go(buf.at[slot], buf.at[slot], d) for d in devs]
        gs = share(terms[...], z_in, me.z * 2 + me.c, zs)
        arrivals = []
        for j, dev in reversed(peers):
            arrivals.append(w.go(front.at[j], fbuf.at[mine], dev))
            arrivals.append(w.go(rest.at[j], rbuf.at[mine], dev))
        fbuf[mine] = front[mine]
        rbuf[mine] = rest[mine]
        for c in gs:
            c.wait_recv()
        gs = share(total(z_in, 8), x_in, me.x, xs)
        for c in gs:
            c.wait_recv()
        gs = share(total(x_in, 4), y_in, me.y, ys)
        for c in gs:
            c.wait_recv()
        gain_sum[...] = total(y_in, 4)
        for a in arrivals:
            a.wait_recv()
        w.finish()

    return pl.pallas_call(
        kernel, out_shape=[jax.ShapeDtypeStruct((4, 32, 640), bf16), jax.ShapeDtypeStruct((4, 32, 3072), bf16),
                           jax.ShapeDtypeStruct((33, 128), f32)],
        in_specs=vm_specs(3), out_specs=vm_specs(3),
        scratch_shapes=[VM((8, 33, 128), f32), VM((4, 33, 128), f32), VM((4, 33, 128), f32)] + dma_sems(19),
        compiler_params=params(cid))(front, rest, gain_terms)


def update(front, rest, gain_sum, gain_states, states, tokens):
    def kernel(*refs):
        front, rest, g_sum, g_w, g_m, g_v = refs[:6]
        ins, t_in, g_out, outs, t_out = refs[6:27], refs[27:29], refs[29:32], refs[32:53], refs[53:55]
        held, made, kept = refs[55:76], refs[76:97], refs[97:99]
        lsem, osem, tsem = refs[99:]
        loads = [pltpu.make_async_copy(a, b, lsem.at[i]) for i, (a, b) in enumerate(zip(ins, held))]
        coming = [pltpu.make_async_copy(a, b, tsem.at[i]) for i, (a, b) in enumerate(zip(t_in, kept))]
        for c in loads + coming:
            c.start()
        new = adam(g_w[...], g_m[...], g_v[...], g_sum[...], gain_rate, 0.0)
        for ref, v in zip(g_out, new):
            ref[...] = v
        stores = []
        at = {False: 0, True: 0}
        for i, (n, rate) in enumerate(zip(SPANS, RATES)):
            late = i >= 4
            buf = rest if late else front
            for k in range(3):
                loads[3 * i + k].wait()
            for j in range(4):
                here = pl.ds(n * j, n)
                grad = buf[j, :, at[late]:at[late] + n].astype(f32)
                new = adam(held[3 * i][:, here], held[3 * i + 1][:, here], held[3 * i + 2][:, here], grad, rate,
                           weight_decay)
                for k in range(3):
                    made[3 * i + k][:, here] = new[k]
            at[late] += n
            for k in range(3):
                c = pltpu.make_async_copy(made[3 * i + k], outs[3 * i + k], osem.at[3 * i + k])
                c.start()
                stores.append(c)
        for i in range(2):
            coming[i].wait()
            c = pltpu.make_async_copy(kept[i], t_out[i], tsem.at[2 + i])
            c.start()
            stores.append(c)
        for c in stores:
            c.wait()

    shapes = [jax.ShapeDtypeStruct(s.shape, f32) for s in states]
    gain_shape = jax.ShapeDtypeStruct((33, 128), f32)
    return pl.pallas_call(
        kernel, out_shape=[gain_shape] * 3 + shapes + [jax.ShapeDtypeStruct(t.shape, f32) for t in tokens],
        in_specs=vm_specs(6) + any_specs(23), out_specs=vm_specs(3) + any_specs(23),
        scratch_shapes=[VM(s.shape, f32) for s in states] * 2 + [VM(t.shape, f32) for t in tokens]
        + [pltpu.SemaphoreType.DMA((21,)), pltpu.SemaphoreType.DMA((21,)), pltpu.SemaphoreType.DMA((4,))],
        compiler_params=pltpu.CompilerParams(has_side_effects=True, vmem_limit_bytes=56 * 2**20))(
            front, rest, gain_sum, *gain_states, *states, *tokens)


from jax.sharding import PartitionSpec as P

PLANE = [[x * 16 + y * 4 + k for x in range(4) for y in range(4)] for k in range(4)]


def scatter_plane(whole):
    return lax.psum_scatter(whole, "dp", axis_index_groups=PLANE, scatter_dimension=0, tiled=True)


def local(block_input, output_grad, segment_ids, norm_gains, gain_moment, gain_square, *states):
    square = lambda v: v.reshape(33, 128)
    gains = square(norm_gains)
    table = jnp.asarray(rope_constants())
    one_full, cot_full, two_full, rest_full, front_full, segments, qk_pre, v_rows, mixed, middle = attention_forward(
        block_input, output_grad, states[::3], segment_ids, gains, table, 2)
    rest_full = rest_full.reshape(D, 3072)
    rest_grad, hidden, db_sum = feed_forward(two_full, cot_full, rest_full, 3)
    rest_mine = scatter_plane(rest_grad)
    input_grad, block_output, front_mine, gain_terms = attention_backward(
        block_input, output_grad, middle, db_sum, hidden, rest_full, one_full, front_full, qk_pre, v_rows, mixed, segments,
        gains, table, 4)
    front_back, rest_back, gain_sum = return_gradients(
        front_mine.reshape(4, 32, 640), rest_mine.reshape(4, 32, 3072), gain_terms, 5)
    news = update(front_back, rest_back, gain_sum, [gains, square(gain_moment), square(gain_square)], states,
                  (block_output, input_grad))
    return tuple(news[-2:]) + tuple(v.reshape(-1) for v in news[:3]) + tuple(news[3:-2])


def solution(mesh):
    tokens, weight = P(("dp", "tensor"), None), P("dp", "tensor")
    in_specs = (tokens, tokens, P("dp", None), P(), P(), P()) + (weight,) * 21
    out_specs = (tokens, tokens, P(), P(), P()) + (weight,) * 21
    return jax.shard_map(local, mesh=mesh, in_specs=in_specs, out_specs=out_specs, check_vma=False)
```

```python
import jax
import jax.numpy as jnp
import numpy as np
from jax import lax
from jax.experimental import pallas as pl
from jax.experimental.pallas import tpu as pltpu

MESH = pl.DeviceIdType.MESH
VM = pltpu.VMEM
bf16 = jnp.bfloat16
f32 = jnp.float32


def m4(v):
    return lax.rem(v + 4, 4)


class Place:
    def __init__(self):
        dp = lax.axis_index("dp")
        self.l = lax.axis_index("tensor")
        self.x = lax.div(dp, 16)
        self.y = lax.rem(lax.div(dp, 4), 4)
        self.h = lax.rem(lax.div(dp, 2), 2)
        self.c = lax.rem(dp, 2)
        self.z = self.h * 2 + self.l

    def at(self, x=None, y=None, z=None, c=None):
        x = self.x if x is None else x
        y = self.y if y is None else y
        z = self.z if z is None else z
        c = self.c if c is None else c
        return (x * 16 + y * 4 + lax.div(z, 2) * 2 + c, lax.rem(z, 2))

    def pos(self, axis):
        return {"x": self.x, "y": self.y, "z": self.z}[axis]

    def step(self, axis, d):
        return self.at(**{axis: m4(self.pos(axis) + d)})

    def sibling(self):
        return self.at(c=1 - self.c)


class Wire:
    def __init__(self, send, recv):
        self.send, self.recv, self.n = send, recv, 0
        self.pending = []

    def go(self, src, dst, dev):
        i = self.n
        self.n += 1
        c = pltpu.make_async_remote_copy(
            src_ref=src, dst_ref=dst, send_sem=self.send.at[i], recv_sem=self.recv.at[i],
            device_id=dev, device_id_type=MESH)
        c.start()
        self.pending.append(c)
        return c

    def finish(self):
        for c in self.pending:
            c.wait_send()
        self.pending = []


def meet(devs):
    b = pltpu.get_barrier_semaphore()
    for d in devs:
        pl.semaphore_signal(b, inc=1, device_id=d, device_id_type=MESH)
    pl.semaphore_wait(b, len(devs))


def ring_gather(w, me, axis, whole, lo, hi, first=None, arrived=None):
    p = me.pos(axis)
    up, down = me.step(axis, 1), me.step(axis, -1)
    own = whole(p) if first is None else first
    a = w.go(own, whole(p), up)
    b = w.go(own, whole(p), down)
    yield
    a.wait_recv()
    fa = w.go(lo(m4(p - 1)), lo(m4(p - 1)), up)
    if arrived:
        arrived(whole(m4(p - 1)))
    b.wait_recv()
    fb = w.go(hi(m4(p + 1)), hi(m4(p + 1)), down)
    if arrived:
        arrived(whole(m4(p + 1)))
    yield
    fa.wait_recv()
    if arrived:
        arrived(lo(m4(p - 2)))
    fb.wait_recv()
    if arrived:
        arrived(hi(m4(p - 2)))


def ring_scatter(w, me, axis, lo, hi, tlo, thi, rup, rdown, add):
    p = me.pos(axis)
    up, down = me.step(axis, 1), me.step(axis, -1)
    far, nu, nd = m4(p + 2), m4(p + 1), m4(p - 1)
    ta = w.go(lo(far), tlo, up)
    tb = w.go(hi(far), thi, down)
    da = w.go(hi(nu), rup[1], up)
    db = w.go(lo(nd), rdown[0], down)
    yield
    ta.wait_recv()
    add(tlo, lo(nu))
    sa = w.go(tlo, rup[0], up)
    tb.wait_recv()
    add(thi, hi(nd))
    sb = w.go(thi, rdown[1], down)
    yield
    da.wait_recv()
    db.wait_recv()
    sa.wait_recv()
    sb.wait_recv()


def loop_add(dst, a, b=None, rows=16):
    n = dst.shape[0]

    def body(i, _):
        def inner(j, _):
            s = pl.ds(pl.multiple_of(j * rows, rows), rows)
            v = dst[i, s].astype(f32) + a[i, s].astype(f32)
            if b is not None:
                v = v + b[i, s].astype(f32)
            dst[i, s] = v.astype(dst.dtype)
            return 0
        return lax.fori_loop(0, dst.shape[1] // rows, inner, 0)
    lax.fori_loop(0, n, body, 0)


def run(gens):
    gens = list(gens)
    while gens:
        for g in list(gens):
            try:
                next(g)
            except StopIteration:
                gens.remove(g)


def params(cid, mb=56):
    return pltpu.CompilerParams(collective_id=cid, has_side_effects=True, vmem_limit_bytes=mb * 2**20)


def ag_xy_gens(w, me, src, out):
    H = 64
    x, y = me.x, me.y

    def half_a():
        yield from ring_gather(w, me, "x", lambda i: out.at[i, y, pl.ds(0, 64)], lambda i: out.at[i, y, pl.ds(0, 32)],
                               lambda i: out.at[i, y, pl.ds(32, 32)], first=src.at[pl.ds(0, 64)])
        yield
        yield from ring_gather(w, me, "y", lambda i: out.at[:, i, pl.ds(0, 64)], lambda i: out.at[:, i, pl.ds(0, 32)],
                               lambda i: out.at[:, i, pl.ds(32, 32)])

    def half_b():
        yield from ring_gather(w, me, "y", lambda i: out.at[x, i, pl.ds(64, 64)], lambda i: out.at[x, i, pl.ds(64, 32)],
                               lambda i: out.at[x, i, pl.ds(96, 32)], first=src.at[pl.ds(64, 64)])
        yield
        yield from ring_gather(w, me, "x", lambda i: out.at[i, :, pl.ds(64, 64)], lambda i: out.at[i, :, pl.ds(64, 32)],
                               lambda i: out.at[i, :, pl.ds(96, 32)])
    return [half_a(), half_b()]


def ag_xy(shard, cid, space=pl.ANY):
    C = shard.shape[1]

    def kernel(src, out, send, recv, lsem):
        me = Place()
        meet([me.step("x", 1), me.step("x", -1), me.step("y", 1), me.step("y", -1)])
        w = Wire(send, recv)
        lc = pltpu.make_async_copy(src, out.at[me.x, me.y], lsem)
        lc.start()
        lc.wait()
        run(ag_xy_gens(w, me, src, out))
        w.finish()

    return pl.pallas_call(
        kernel, out_shape=jax.ShapeDtypeStruct((4, 4, 128, C), shard.dtype),
        in_specs=[pl.BlockSpec(memory_space=space)], out_specs=pl.BlockSpec(memory_space=space),
        scratch_shapes=[pltpu.SemaphoreType.DMA((16,)), pltpu.SemaphoreType.DMA((16,)), pltpu.SemaphoreType.DMA],
        compiler_params=params(cid))(shard)


def rs_xy_scratch(C):
    return [VM((2, 2, 4, 32, C), bf16), VM((2, 2, 2, 4, 32, C), bf16),
            VM((2, 2, 32, C), bf16), VM((2, 2, 2, 32, C), bf16), VM((2, 4, 64, C), bf16)]


def rs_xy_gens(w, me, g, out, t1, r1, t2, r2, mid):
    x, y = me.x, me.y

    def half(k, first, second):
        base = k * 64
        if first == "y":
            pick = lambda i, o: g.at[:, i, pl.ds(base + o, 32)]
        else:
            pick = lambda i, o: g.at[i, :, pl.ds(base + o, 32)]
        yield from ring_scatter(w, me, first, lambda i: pick(i, 0), lambda i: pick(i, 32), t1.at[k, 0], t1.at[k, 1],
                                (r1.at[k, 0, 0], r1.at[k, 0, 1]), (r1.at[k, 1, 0], r1.at[k, 1, 1]), loop_add)
        p = me.pos(first)
        m = mid.at[k]
        for hh in range(2):
            own = pick(p, 32 * hh)

            def body(i, _):
                def inner(j, _):
                    s = pl.ds(pl.multiple_of(j * 16, 16), 16)
                    d = pl.ds(pl.multiple_of(j * 16 + 32 * hh, 16), 16)
                    v = own[i, s].astype(f32) + r1[k, 0, hh, i, s].astype(f32) + r1[k, 1, hh, i, s].astype(f32)
                    m[i, d] = v.astype(bf16)
                    return 0
                return lax.fori_loop(0, 2, inner, 0)
            lax.fori_loop(0, 4, body, 0)
        yield
        q = me.pos(second)
        add1 = lambda dst, a: loop_add(dst, a)
        pick2 = lambda i, o: mid.at[k, i, pl.ds(o, 32)]

        def add2(dst, a):
            def inner(j, _):
                s = pl.ds(pl.multiple_of(j * 16, 16), 16)
                dst[s] = (dst[s].astype(f32) + a[s].astype(f32)).astype(bf16)
                return 0
            lax.fori_loop(0, 2, inner, 0)
        yield from ring_scatter(w, me, second, lambda i: pick2(i, 0), lambda i: pick2(i, 32), t2.at[k, 0], t2.at[k, 1],
                                (r2.at[k, 0, 0], r2.at[k, 0, 1]), (r2.at[k, 1, 0], r2.at[k, 1, 1]), add2)
        for hh in range(2):
            def inner(j, _):
                s = pl.ds(pl.multiple_of(j * 16, 16), 16)
                d = pl.ds(pl.multiple_of(j * 16 + 32 * hh, 16), 16)
                dd = pl.ds(pl.multiple_of(j * 16 + 32 * hh + base, 16), 16)
                v = m[q, d].astype(f32) + r2[k, 0, hh, s].astype(f32) + r2[k, 1, hh, s].astype(f32)
                out[dd] = v.astype(out.dtype)
                return 0
            lax.fori_loop(0, 2, inner, 0)
    return [half(0, "y", "x"), half(1, "x", "y")]


def rs_xy(g, cid, out_dtype=f32):
    C = g.shape[-1]

    def kernel(gin, out, send, recv, *scr):
        me = Place()
        meet([me.step("x", 1), me.step("x", -1), me.step("y", 1), me.step("y", -1)])
        w = Wire(send, recv)
        run(rs_xy_gens(w, me, gin, out, *scr))
        w.finish()

    return pl.pallas_call(
        kernel, out_shape=jax.ShapeDtypeStruct((128, C), out_dtype),
        in_specs=[pl.BlockSpec(memory_space=VM)], out_specs=pl.BlockSpec(memory_space=VM),
        scratch_shapes=[pltpu.SemaphoreType.DMA((24,)), pltpu.SemaphoreType.DMA((24,))] + rs_xy_scratch(C),
        compiler_params=params(cid, 60))(g)


def ag_z_gen(w, me, src, out, r0=0, n=128):
    sib = me.sibling()
    blk = lambda i, cc: out.at[lax.div(i, 2), cc, lax.rem(i, 2)]
    cs = []

    def to_sib(ref):
        cs.append(w.go(ref, ref, sib))
    whole = lambda i: blk(i, me.c).at[pl.ds(r0, n)]
    lo = lambda i: blk(i, me.c).at[pl.ds(r0, n // 2)]
    hi = lambda i: blk(i, me.c).at[pl.ds(r0 + n // 2, n // 2)]
    own = w.go(src, whole(me.z), sib)
    yield from ring_gather(w, me, "z", whole, lo, hi, first=src, arrived=to_sib)
    own.wait_recv()
    for c in cs:
        c.wait_recv()


def ag_z(shard, cid, space=VM):
    C = shard.shape[1]

    def kernel(src, out, send, recv, lsem):
        me = Place()
        meet([me.step("z", 1), me.step("z", -1), me.sibling()])
        w = Wire(send, recv)
        lc = pltpu.make_async_copy(src, out.at[me.h, me.c, me.l], lsem)
        lc.start()
        lc.wait()
        run([ag_z_gen(w, me, src, out)])
        w.finish()

    return pl.pallas_call(
        kernel, out_shape=jax.ShapeDtypeStruct((2, 2, 2, 128, C), shard.dtype),
        in_specs=[pl.BlockSpec(memory_space=space)], out_specs=pl.BlockSpec(memory_space=space),
        scratch_shapes=[pltpu.SemaphoreType.DMA((16,)), pltpu.SemaphoreType.DMA((16,)), pltpu.SemaphoreType.DMA],
        compiler_params=params(cid))(shard)


def rs_z_scratch(C):
    return [VM((4, 128, C), bf16), VM((2, 64, C), bf16), VM((2, 2, 64, C), bf16)]


def rs_z_gen(w, me, g, out, sibs, t, r):
    sib = me.sibling()
    oc = 1 - me.c
    order = [2, 1, 3, 0]
    blk = lambda i, cc: g.at[lax.div(i, 2), cc, lax.rem(i, 2)]
    z = me.z
    sc = {}
    for o in order:
        i = m4(z + o)
        sc[o] = w.go(blk(i, oc), sibs.at[i], sib)
    yield

    def fold(o, s0, n):
        i = m4(z + o)
        b = blk(i, me.c)

        def inner(j, _):
            s = pl.ds(pl.multiple_of(j * 16 + s0, 16), 16)
            sibs[i, s] = (sibs[i, s].astype(f32) + b[s].astype(f32)).astype(bf16)
            return 0
        lax.fori_loop(0, n // 16, inner, 0)
    up, down = me.step("z", 1), me.step("z", -1)
    half = lambda o, k: sibs.at[m4(z + o), pl.ds(64 * k, 64)]
    sc[2].wait_recv()
    fold(2, 0, 64)
    ta = w.go(half(2, 0), t.at[0], up)
    fold(2, 64, 64)
    tb = w.go(half(2, 1), t.at[1], down)
    sc[1].wait_recv()
    fold(1, 64, 64)
    da = w.go(half(1, 1), r.at[0, 1], up)
    sc[3].wait_recv()
    fold(3, 0, 64)
    db = w.go(half(3, 0), r.at[1, 0], down)
    fold(1, 0, 64)
    fold(3, 64, 64)
    yield

    def add(dst, a):
        def inner(j, _):
            s = pl.ds(pl.multiple_of(j * 16, 16), 16)
            dst[s] = (dst[s].astype(f32) + a[s].astype(f32)).astype(bf16)
            return 0
        lax.fori_loop(0, 4, inner, 0)
    ta.wait_recv()
    add(t.at[0], half(1, 0))
    sa = w.go(t.at[0], r.at[0, 0], up)
    tb.wait_recv()
    add(t.at[1], half(3, 1))
    sb = w.go(t.at[1], r.at[1, 1], down)
    sc[0].wait_recv()
    own = blk(z, me.c)
    yield

    def last(hh):
        def inner(j, _):
            s = pl.ds(pl.multiple_of(j * 16, 16), 16)
            d = pl.ds(pl.multiple_of(j * 16 + 64 * hh, 16), 16)
            v = own[d].astype(f32) + sibs[z, d].astype(f32) + r[0, hh, s].astype(f32) + r[1, hh, s].astype(f32)
            out(d, v)
            return 0
        lax.fori_loop(0, 4, inner, 0)
    da.wait_recv()
    sa.wait_recv()
    db.wait_recv()
    sb.wait_recv()
    last(0)
    last(1)


def rs_z(g, cid, out_dtype=f32):
    C = g.shape[-1]

    def kernel(gin, out, send, recv, *scr):
        me = Place()
        meet([me.step("z", 1), me.step("z", -1), me.sibling()])
        w = Wire(send, recv)

        def put(s, v):
            out[s] = v.astype(out.dtype)
        run([rs_z_gen(w, me, gin, put, *scr)])
        w.finish()

    return pl.pallas_call(
        kernel, out_shape=jax.ShapeDtypeStruct((128, C), out_dtype),
        in_specs=[pl.BlockSpec(memory_space=VM)], out_specs=pl.BlockSpec(memory_space=VM),
        scratch_shapes=[pltpu.SemaphoreType.DMA((16,)), pltpu.SemaphoreType.DMA((16,))] + rs_z_scratch(C),
        compiler_params=params(cid))(g)


def swap_devs(me):
    out = []
    for dh, dc in ((0, 1), (1, 0), (1, 1)):
        h = lax.rem(me.h + dh, 2)
        c = lax.rem(me.c + dc, 2)
        out.append((h * 2 + c, me.at(z=h * 2 + me.l, c=c)))
    return out


def swap_hc(parts, cid):
    n = len(parts)

    def kernel(*refs):
        ins, outs = refs[:n], refs[n:2 * n]
        send, recv, lsem = refs[2 * n:]
        me = Place()
        peers = swap_devs(me)
        meet([d for _, d in peers])
        w = Wire(send, recv)
        mine = me.h * 2 + me.c
        arrivals = []
        for j, d in reversed(peers):
            for a, b in zip(ins, outs):
                arrivals.append(w.go(a.at[j], b.at[mine], d))
        ls = []
        for k, (a, b) in enumerate(zip(ins, outs)):
            lc = pltpu.make_async_copy(a.at[mine], b.at[mine], lsem.at[k])
            lc.start()
            ls.append(lc)
        for lc in ls:
            lc.wait()
        for a in arrivals:
            a.wait_recv()
        w.finish()

    return pl.pallas_call(
        kernel, out_shape=[jax.ShapeDtypeStruct(p.shape, p.dtype) for p in parts],
        in_specs=[pl.BlockSpec(memory_space=VM)] * n, out_specs=[pl.BlockSpec(memory_space=VM)] * n,
        scratch_shapes=[pltpu.SemaphoreType.DMA((3 * n,)), pltpu.SemaphoreType.DMA((3 * n,)),
                        pltpu.SemaphoreType.DMA((n,))],
        compiler_params=params(cid))(*parts)


def sum_all(v, cid):
    R, C = v.shape

    def kernel(src, out, z_in, x_in, y_in, acc, send, recv):
        me = Place()
        zs = []
        for dz in range(4):
            for dc in range(2):
                if dz or dc:
                    z, c = m4(me.z + dz), lax.rem(me.c + dc, 2)
                    zs.append(me.at(z=z, c=c))
        xs = [me.step("x", d) for d in (1, 2, 3)]
        ys = [me.step("y", d) for d in (1, 2, 3)]
        meet(zs + xs + ys)
        w = Wire(send, recv)
        acc[...] = src[...]
        for buf, slot, devs, n in ((z_in, me.z * 2 + me.c, zs, 8), (x_in, me.x, xs, 4), (y_in, me.y, ys, 4)):
            buf[slot] = acc[...]
            cs = [w.go(buf.at[slot], buf.at[slot], d) for d in devs]
            for c in cs:
                c.wait_recv()
            total = buf[0]
            for k in range(1, n):
                total = total + buf[k]
            w.finish()
            acc[...] = total
        out[...] = acc[...]

    return pl.pallas_call(
        kernel, out_shape=jax.ShapeDtypeStruct((R, C), f32),
        in_specs=[pl.BlockSpec(memory_space=VM)], out_specs=pl.BlockSpec(memory_space=VM),
        scratch_shapes=[VM((8, R, C), f32), VM((4, R, C), f32), VM((4, R, C), f32), VM((R, C), f32),
                        pltpu.SemaphoreType.DMA((13,)), pltpu.SemaphoreType.DMA((13,))],
        compiler_params=params(cid))(v)


def rs_z_packs(w, me, g, put, sibs, t, r):
    sib, oc, z = me.sibling(), 1 - me.c, me.z
    blk = lambda i, cc: g.at[lax.div(i, 2), cc, lax.rem(i, 2)]
    far = m4(z + 2)
    flip = lambda i: i + 1 - 2 * lax.rem(i, 2)
    beside, partner = flip(far), flip(z)
    up, down = me.step("z", 1), me.step("z", -1)
    half = lambda i, k: sibs.at[i, pl.ds(64 * k, 64)]

    def fold(i, s0, n):
        b = blk(i, me.c)

        def inner(j, _):
            s = pl.ds(pl.multiple_of(j * 16 + s0, 16), 16)
            sibs[i, s] = (sibs[i, s].astype(f32) + b[s].astype(f32)).astype(bf16)
            return 0
        lax.fori_loop(0, n // 16, inner, 0)

    def add(dst, a):
        def inner(j, _):
            s = pl.ds(pl.multiple_of(j * 16, 16), 16)
            dst[s] = (dst[s].astype(f32) + a[s].astype(f32)).astype(bf16)
            return 0
        lax.fori_loop(0, 4, inner, 0)
    s_far = w.go(blk(far, oc), sibs.at[far], sib)
    s_beside = w.go(blk(beside, oc), sibs.at[beside], sib)
    yield
    s_far.wait_recv()
    fold(far, 0, 64)
    ta = w.go(half(far, 0), t.at[0], up)
    fold(far, 64, 64)
    tb = w.go(half(far, 1), t.at[1], down)
    s_beside.wait_recv()
    fold(beside, 0, 128)
    yield
    s_partner = w.go(blk(partner, oc), sibs.at[partner], sib)
    s_own = w.go(blk(z, oc), sibs.at[z], sib)
    yield
    s_partner.wait_recv()
    fold(partner, 0, 128)
    nu, nd = m4(z + 1), m4(z - 1)
    da = w.go(half(nu, 1), r.at[0, 1], up)
    db = w.go(half(nd, 0), r.at[1, 0], down)
    ta.wait_recv()
    add(t.at[0], half(nu, 0))
    sa = w.go(t.at[0], r.at[0, 0], up)
    tb.wait_recv()
    add(t.at[1], half(nd, 1))
    sb = w.go(t.at[1], r.at[1, 1], down)
    s_own.wait_recv()
    own = blk(z, me.c)
    yield

    def last(hh):
        def inner(j, _):
            s = pl.ds(pl.multiple_of(j * 16, 16), 16)
            d = pl.ds(pl.multiple_of(j * 16 + 64 * hh, 16), 16)
            put(d, own[d].astype(f32) + sibs[z, d].astype(f32) + r[0, hh, s].astype(f32) + r[1, hh, s].astype(f32))
            return 0
        lax.fori_loop(0, 4, inner, 0)
    da.wait_recv()
    sa.wait_recv()
    db.wait_recv()
    sb.wait_recv()
    last(0)
    last(1)


D = 2048
HD = 64
STEP = 10
SEQ = 256
PACKS = 4
ROWS = 1024
epsilon = 1e-06
rope_base = 1000000.0
beta_one = 0.9
beta_two = 0.999
adam_epsilon = 1e-08
weight_decay = 0.1
gain_rate = 0.3
masked_score = -1000000000.0
score_scale = HD ** (-0.5)
exact = lax.Precision.HIGHEST


def dot(a, b, ca=1, cb=0, precision=None):
    return lax.dot_general(a, b, (((ca,), (cb,)), ((), ())), precision=precision, preferred_element_type=f32)


def chunks(n, body, rows=16):
    def one(j, _):
        body(pl.ds(pl.multiple_of(j * rows, rows), rows))
        return 0
    lax.fori_loop(0, n // rows, one, 0)


def dma_sems(n):
    return [pltpu.SemaphoreType.DMA((n,)), pltpu.SemaphoreType.DMA((n,))]


def vm_specs(n):
    return [pl.BlockSpec(memory_space=VM)] * n


def any_specs(n):
    return [pl.BlockSpec(memory_space=pl.ANY)] * n


class Columns:
    def __init__(self, ref, n):
        self.ref, self.n = ref, n

    def __getitem__(self, j):
        return self.ref[:, pl.ds(pl.multiple_of(j * self.n, self.n), self.n)]


def gain_rows(gains):
    one = jnp.concatenate([gains[i:i + 1, :] for i in range(16)], axis=1)
    two = jnp.concatenate([gains[16 + i:17 + i, :] for i in range(16)], axis=1)
    small = jnp.broadcast_to(gains[32:33, :], (128, 128)).T
    return one, two, small[0:64, 0:1], small[64:128, 0:1]


def rope_constants():
    frequency = np.float32(rope_base) ** (np.float32(-2.0) * np.arange(HD // 2, dtype=np.float32) / np.float32(HD))
    angles = (np.arange(SEQ, dtype=np.float32)[None, :] * frequency[:, None].astype(np.float32)).astype(np.float64)
    return np.concatenate([np.cos(angles), np.sin(angles)], axis=0).astype(np.float32)


def pack_tables(segs, p, table):
    row = segs[p].astype(f32)[0:1, :]
    column = jnp.broadcast_to(row, (128, SEQ)).T[:, 0:1]
    key_at = lax.broadcasted_iota(jnp.int32, (SEQ, SEQ), 0)
    query_at = lax.broadcasted_iota(jnp.int32, (SEQ, SEQ), 1)
    allowed = (column == row) & (key_at <= query_at)
    start = jnp.sum(jnp.where(column < row, 1.0, 0.0), axis=0, keepdims=True)
    where = query_at.astype(f32) - start
    hot = jnp.where(key_at.astype(f32) == where, 1.0, 0.0)
    both = dot(table[...], hot, precision=exact)
    return allowed, both[0:32], both[32:64]


def head_norm(z, gain):
    inverse = lax.rsqrt(jnp.mean(z * z, axis=0, keepdims=True) + epsilon)
    return z * inverse * gain, inverse


def head_norm_back(z, inverse, gain, up):
    scaled = up * gain
    inner = jnp.mean(z * scaled, axis=0, keepdims=True)
    return inverse * (scaled - z * inverse * inverse * inner), up * z * inverse


def turn(u, cosine, sine):
    a, b = u[0:32], u[32:64]
    return jnp.concatenate([a * cosine - b * sine, b * cosine + a * sine], axis=0)


def turn_back(u, cosine, sine):
    a, b = u[0:32], u[32:64]
    return jnp.concatenate([a * cosine + b * sine, b * cosine - a * sine], axis=0)


def pack_probs(key_rows, query_rot, allowed):
    scores = jnp.where(allowed, dot(key_rows, query_rot) * score_scale, masked_score)
    exps = jnp.exp(scores - jnp.max(scores, axis=0, keepdims=True))
    return exps / jnp.sum(exps, axis=0, keepdims=True)


def pack_of(ref, p):
    v = ref[lax.div(p, 2), lax.rem(p, 2)]
    return v.reshape(SEQ, v.shape[-1])


def pack_turn(me, i):
    h = me.h if i >= 2 else 1 - me.h
    c = me.c if i % 2 else 1 - me.c
    return h * 2 + c


def attention_forward(x, cot, weights, seg, gains, table, cid):
    def kernel(x, cot, q_, k_, v_, o_, g_, u_, d_, seg, gains, table,
               a_full, cot_full, n_full, rest_full, front_full, segs, qk_pre, v_rows, mixed, middle,
               fbuf, rbuf, sbuf, kv, fshard, rshard, rest, shard, shard_two, a_buf, part, sibs, t, r,
               send, recv, lsem, ksem):
        me = Place()
        gain_one, gain_two, gain_query, gain_key = gain_rows(gains)
        peers = swap_devs(me)
        mine = me.h * 2 + me.c
        q, o = Columns(q_, 256), Columns(o_, 256)
        g, u, d = Columns(g_, 1024), Columns(u_, 1024), Columns(d_, 1024)
        for j in range(4):
            kv[j] = jnp.concatenate([k_[:, 64 * j:64 * j + 64], v_[:, 64 * j:64 * j + 64]], axis=1)
        sbuf[...] = jnp.broadcast_to(seg[...], (8, SEQ))
        here = pl.ds(pl.multiple_of(mine * 32, 32), 32)

        def round_front(j, dst):
            dst[:, 0:256] = q[j].astype(bf16)
            dst[:, 256:384] = kv[j].astype(bf16)
            dst[:, 384:640] = o[j].astype(bf16)

        def round_rest(j, dst):
            for i, w in enumerate((g, u, d)):
                dst[:, 1024 * i:1024 * i + 1024] = w[j].astype(bf16)
        meet([me.step("x", 1), me.step("x", -1), me.step("y", 1), me.step("y", -1),
              me.step("z", 1), me.step("z", -1)] + [dev for _, dev in peers])
        w = Wire(send, recv)
        first, second = [], []
        for j, dev in reversed(peers):
            round_front(j, fbuf.at[j])
            first.append(w.go(fbuf.at[j], fshard.at[here], dev))
            second.append(w.go(sbuf, segs.at[mine], dev))
        for j, dev in reversed(peers):
            round_rest(j, rbuf.at[j])
            second.append(w.go(rbuf.at[j], rshard.at[here], dev))
        round_front(mine, fshard.at[here])
        round_rest(mine, rshard.at[here])
        segs[mine] = sbuf[...]

        def norm_one(s):
            v = x[s].astype(f32)
            inverse = lax.rsqrt(jnp.mean(v * v, axis=-1, keepdims=True) + epsilon)
            shard[s] = (v * inverse * gain_one).astype(bf16)
        chunks(128, norm_one)
        for c in first:
            c.wait_recv()

        def both(gens):
            for g in gens:
                next(g)
        front_gens = ag_xy_gens(w, me, fshard, front_full)
        both(front_gens)
        gz = ag_z_gen(w, me, shard, a_buf)
        next(gz)
        locals_ = [pltpu.make_async_copy(fshard, front_full.at[me.x, me.y], lsem.at[0]),
                   pltpu.make_async_copy(shard, a_buf.at[me.h, me.c, me.l], lsem.at[1]),
                   pltpu.make_async_copy(cot, cot_full.at[me.h, me.c, me.l], lsem.at[2])]
        for c in locals_:
            c.start()
        both(front_gens)
        for c in locals_:
            c.wait()
        both(front_gens)
        both(front_gens)
        for c in second:
            c.wait_recv()
        rest_gens = ag_xy_gens(w, me, rshard, rest)
        both(rest_gens)
        own = pltpu.make_async_copy(rshard, rest.at[me.x, me.y], lsem.at[3])
        own.start()
        both(front_gens)
        both(rest_gens)
        own.wait()
        run(front_gens)
        both(rest_gens)
        both(rest_gens)
        next(gz)
        run([gz])
        cot_gen = ag_z_gen(w, me, cot.at[pl.ds(0, 64)], cot_full, 0, 64)
        next(cot_gen)
        keep = pltpu.make_async_copy(a_buf, a_full, lsem.at[4])
        keep.start()

        def one_pack(p):
            allowed, cosine, sine = pack_tables(segs, p, table)
            qkv = dot(pack_of(a_buf, p), front_full[:, :, :, 0:384].reshape(D, 384)).T
            qk_pre[p] = qkv[0:320]
            value = qkv[320:384].astype(bf16)
            v_rows[p] = value
            kn, _i = head_norm(qkv[256:320], gain_key)
            key_rows = turn(kn, cosine, sine).T.astype(bf16)
            heads = []
            for j in range(4):
                qn, _i = head_norm(qkv[64 * j:64 * j + 64], gain_query)
                probs = pack_probs(key_rows, turn(qn, cosine, sine).astype(bf16), allowed)
                heads.append(dot(value, probs.astype(bf16)))
            o = jnp.concatenate(heads, axis=0).T.astype(bf16)
            mixed[p] = o
            out = dot(o, front_full[:, :, :, 384:640].reshape(D, 256), 1, 1).astype(bf16)
            part[lax.div(p, 2), lax.rem(p, 2)] = out.reshape(2, 128, D)

        def residual(s, v):
            middle[s] = x[s].astype(f32) + v
        sum_gen = rs_z_packs(w, me, part, residual, sibs, t, r)
        for i in range(4):
            one_pack(pack_turn(me, i))
            next(sum_gen)
            if i == 2:
                next(cot_gen)
        both(rest_gens)
        run([sum_gen])

        def norm_two(s):
            v = middle[s]
            inverse = lax.rsqrt(jnp.mean(v * v, axis=-1, keepdims=True) + epsilon)
            shard_two[s] = (v * inverse * gain_two).astype(bf16)
        chunks(128, norm_two)
        n_gen = ag_z_gen(w, me, shard_two, n_full)
        next(n_gen)
        own = pltpu.make_async_copy(shard_two, n_full.at[me.h, me.c, me.l], lsem.at[3])
        own.start()
        run([cot_gen])
        stores = []

        def store(k, a, b, at):
            here = pl.ds(at, 64)
            c = pltpu.make_async_copy(rest.at[a, b, here], rest_full.at[a, b, here], ksem.at[k])
            c.start()
            stores.append(c)
        every = slice(None)
        for k in (0, 1, 3):
            store(k, every, m4(me.y + k), 0)
            store(4 + k, m4(me.x + k), every, 64)
        next(n_gen)
        run([n_gen])
        run(rest_gens)
        store(2, every, m4(me.y + 2), 0)
        store(6, m4(me.x + 2), every, 64)
        own.wait()
        keep.wait()
        for c in stores:
            c.wait()
        w.finish()

    full = jax.ShapeDtypeStruct((2, 2, 2, 128, D), bf16)
    return pl.pallas_call(
        kernel,
        out_shape=[full, full, full, jax.ShapeDtypeStruct((4, 4, 128, 3072), bf16),
                   jax.ShapeDtypeStruct((4, 4, 128, 640), bf16), jax.ShapeDtypeStruct((4, 8, SEQ), jnp.int32),
                   jax.ShapeDtypeStruct((PACKS, 320, SEQ), f32), jax.ShapeDtypeStruct((PACKS, HD, SEQ), bf16),
                   jax.ShapeDtypeStruct((PACKS, SEQ, 256), bf16), jax.ShapeDtypeStruct((128, D), f32)],
        in_specs=vm_specs(12), out_specs=any_specs(4) + vm_specs(6),
        scratch_shapes=[VM((4, 32, 640), bf16), VM((4, 32, 3072), bf16), VM((8, SEQ), jnp.int32), VM((4, 32, 128), f32),
                        VM((128, 640), bf16), VM((128, 3072), bf16), VM((4, 4, 128, 3072), bf16)]
        + [VM((128, D), bf16)] * 2 + [VM((2, 2, 2, 128, D), bf16)] * 2 + rs_z_scratch(D)
        + dma_sems(96) + [pltpu.SemaphoreType.DMA((5,)), pltpu.SemaphoreType.DMA((8,))],
        compiler_params=params(cid, 58))(x, cot, *weights, seg, gains, table)


def sigmoid(v):
    return 1.0 / (1.0 + jnp.exp(-v))


def feed_forward(n_full, cot_full, cot, weights, cid):
    def kernel(n_hbm, cot_hbm, mine, w_hbm, grad_hbm, hidden_hbm, part_hbm,
               n, cot, w, hidden, gate_up, silus, slopes, part, grad, send, recv, lsem, wsem, gsem):
        me = Place()
        early = pl.ds(0, 64)
        loads = [pltpu.make_async_copy(n_hbm, n, lsem.at[0]),
                 pltpu.make_async_copy(cot_hbm.at[:, :, :, early], cot.at[:, :, :, early], lsem.at[1])]
        loads[0].start()

        def piece(i, k):
            here = pl.ds(pl.multiple_of(i * 256 + 1024 * k, 256), 256)
            return pltpu.make_async_copy(w_hbm.at[:, here], w.at[:, here], wsem.at[i, k])
        for i in range(4):
            piece(i, 0).start()
            piece(i, 1).start()
        loads[1].start()
        for i in range(4):
            piece(i, 2).start()
        meet([me.step("z", 1), me.step("z", -1), me.sibling()])
        wire = Wire(send, recv)
        gen = ag_z_gen(wire, me, mine.at[pl.ds(64, 64)], cot, 64, 64)
        next(gen)
        own = pltpu.make_async_copy(mine.at[pl.ds(64, 64)], cot.at[me.h, me.c, me.l, pl.ds(64, 64)], lsem.at[2])
        own.start()
        for c in loads + [own]:
            c.wait()

        def hidden_block(i, _):
            at = pl.multiple_of(i * 256, 256)
            piece(i, 0).wait()
            piece(i, 1).wait()
            rows = n[...].reshape(ROWS, D)
            g = dot(rows, w[:, pl.ds(at, 256)])
            u = dot(rows, w[:, pl.ds(at + 1024, 256)])
            s = sigmoid(g)
            silu = g * s
            hidden[:, pl.ds(at, 256)] = (silu * u).astype(bf16)
            silus[:, pl.ds(at, 256)] = silu
            slopes[:, pl.ds(at, 256)] = u * (s + silu * (1.0 - s))
            return 0
        lax.fori_loop(0, 2, hidden_block, 0)
        next(gen)
        lax.fori_loop(2, 4, hidden_block, 0)
        run([gen])
        keep = [pltpu.make_async_copy(hidden, hidden_hbm, lsem.at[3])]
        keep[0].start()

        def slope_block(i, _):
            at = pl.multiple_of(i * 256, 256)
            piece(i, 2).wait()
            dh = dot(cot[...].reshape(ROWS, D), w[:, pl.ds(at + 2048, 256)])
            gate_up[:, pl.ds(at, 256)] = (dh * slopes[:, pl.ds(at, 256)]).astype(bf16)
            gate_up[:, pl.ds(at + 1024, 256)] = (dh * silus[:, pl.ds(at, 256)]).astype(bf16)
            return 0
        lax.fori_loop(0, 4, slope_block, 0)

        def back_block(i, _):
            at = pl.multiple_of(i * 256, 256)
            v = dot(gate_up[...], w[pl.ds(at, 256), 0:2048], 1, 1).astype(bf16)
            part[:, :, :, :, pl.ds(at, 256)] = v.reshape(2, 2, 2, 128, 256)
            return 0
        lax.fori_loop(0, 8, back_block, 0)
        keep.append(pltpu.make_async_copy(part, part_hbm, lsem.at[4]))
        keep[1].start()
        stores = []
        for i in range(4):
            at = 512 * i
            slot = i % 2
            if i >= 2:
                stores[i - 2].wait()
            grad[slot, :, 0:2048] = dot(n[:, :, :, :, at:at + 512].reshape(ROWS, 512), gate_up[...], 0, 0).astype(bf16)
            grad[slot, :, 2048:3072] = dot(cot[:, :, :, :, at:at + 512].reshape(ROWS, 512), hidden[...], 0, 0).astype(bf16)
            c = pltpu.make_async_copy(grad.at[slot], grad_hbm.at[pl.ds(at, 512)], gsem.at[i])
            c.start()
            stores.append(c)
        for c in stores[2:] + keep:
            c.wait()
        wire.finish()

    full = (2, 2, 2, 128, D)
    return pl.pallas_call(
        kernel,
        out_shape=[jax.ShapeDtypeStruct((D, 3072), bf16), jax.ShapeDtypeStruct((ROWS, 1024), bf16),
                   jax.ShapeDtypeStruct(full, bf16)],
        in_specs=any_specs(2) + vm_specs(1) + any_specs(1), out_specs=any_specs(3),
        scratch_shapes=[VM(full, bf16), VM(full, bf16), VM((D, 3072), bf16), VM((ROWS, 1024), bf16),
                        VM((ROWS, 2048), bf16), VM((ROWS, 1024), f32), VM((ROWS, 1024), f32), VM(full, bf16),
                        VM((2, 512, 3072), bf16)]
        + dma_sems(16) + [pltpu.SemaphoreType.DMA((5,)), pltpu.SemaphoreType.DMA((4, 3)),
                          pltpu.SemaphoreType.DMA((4,))],
        compiler_params=params(cid, 60))(n_full, cot_full, cot, weights)


def attention_backward(x, cot, middle, db_part, hidden, weights, a_full, front_full, qk_pre, v_rows, mixed, segs,
                       gains, table, cid):
    def kernel(x, cot, middle, db_hbm, hidden_hbm, w_hbm, a_full, front_full, qk_pre, v_rows, mixed, segs,
               gains, table, input_grad, block_output, front_mine, gain_terms,
               shard, hidden, wd, out_part, dm_full, mid_grad, dqkv, part, front_grad, q_acc, k_acc, one_acc, two_acc,
               probs_at, turned, waves, sibs_c, t_c, r_c,
               sibs_a, t_a, r_a, sibs_b, t_b, r_b, t1, r1, t2, r2, mid, send, recv, lsem):
        me = Place()
        gain_one, gain_two, gain_query, gain_key = gain_rows(gains)
        loads = [pltpu.make_async_copy(hidden_hbm, hidden, lsem.at[1]),
                 pltpu.make_async_copy(w_hbm.at[:, pl.ds(2048, 1024)], wd, lsem.at[2])]
        term_load = pltpu.make_async_copy(db_hbm, part, lsem.at[3])
        for c in [term_load] + loads:
            c.start()
        two_acc[...] = jnp.zeros_like(two_acc)
        one_acc[...] = jnp.zeros_like(one_acc)
        q_acc[...] = jnp.zeros_like(q_acc)
        k_acc[...] = jnp.zeros_like(k_acc)

        def back(z, gain, up):
            inverse = lax.rsqrt(jnp.mean(z * z, axis=-1, keepdims=True) + epsilon)
            scaled = up * gain
            inner = jnp.mean(z * scaled, axis=-1, keepdims=True)
            return inverse * (scaled - z * inverse * inverse * inner), up * z * inverse

        meet([me.step("x", 1), me.step("x", -1), me.step("y", 1), me.step("y", -1),
              me.step("z", 1), me.step("z", -1), me.sibling()])
        w = Wire(send, recv)

        def put_two(s, v):
            dz, terms = back(middle[s], gain_two, v)
            v = cot[s].astype(f32) + dz
            mid_grad[s] = v
            shard[s] = v.astype(bf16)
            two_acc[...] += terms
        term_load.wait()
        two_gen = rs_z_gen(w, me, part, put_two, sibs_c, t_c, r_c)
        next(two_gen)

        def again(p, _):
            allowed, cosine, sine = pack_tables(segs, p, table)
            waves[p, 0:32] = cosine
            waves[p, 32:64] = sine
            kn, _i = head_norm(qk_pre[p, 256:320], gain_key)
            kr = turn(kn, cosine, sine)
            key_rows = kr.T.astype(bf16)
            turned[p, 256:320] = kr.astype(bf16)
            for j in range(4):
                qn, _i = head_norm(qk_pre[p, 64 * j:64 * j + 64], gain_query)
                qr = turn(qn, cosine, sine).astype(bf16)
                turned[p, 64 * j:64 * j + 64] = qr
                probs_at[p, j] = pack_probs(key_rows, qr, allowed)
            return 0

        def out_block(i, _):
            at = pl.multiple_of(i * 256, 256)
            v = dot(hidden[...], wd[pl.ds(at, 256)], 1, 1).astype(bf16)
            out_part[:, :, :, :, pl.ds(at, 256)] = v.reshape(2, 2, 2, 128, 256)
            return 0
        lax.fori_loop(0, 2, again, 0)
        next(two_gen)
        lax.fori_loop(2, PACKS, again, 0)
        next(two_gen)
        for c in loads:
            c.wait()
        lax.fori_loop(0, 4, out_block, 0)
        run([two_gen])
        gen = ag_z_gen(w, me, shard, dm_full)
        next(gen)
        own = pltpu.make_async_copy(shard, dm_full.at[me.h, me.c, me.l], lsem.at[0])
        own.start()
        lax.fori_loop(4, 8, out_block, 0)

        def put_out(s, v):
            block_output[s] = middle[s] + v
        out_gen = rs_z_gen(w, me, out_part, put_out, sibs_a, t_a, r_a)
        next(gen)
        next(out_gen)
        run([gen])
        own.wait()
        w.finish()

        def one_pack(p):
            cosine, sine = waves[p, 0:32], waves[p, 32:64]
            mixed_grad = dot(pack_of(dm_full, p), front_full[:, :, :, 384:640].reshape(D, 256)).T.astype(bf16)
            value_rows = v_rows[p].astype(f32).T.astype(bf16)
            key_pre = qk_pre[p, 256:320]
            _n, k_inverse = head_norm(key_pre, gain_key)
            kr = turned[p, 256:320]
            dk = jnp.zeros((HD, SEQ), f32)
            dv = jnp.zeros((HD, SEQ), f32)
            heads = []
            terms_q = jnp.zeros((HD, SEQ), f32)
            for j in range(4):
                query_pre = qk_pre[p, 64 * j:64 * j + 64]
                _n, q_inverse = head_norm(query_pre, gain_query)
                qr = turned[p, 64 * j:64 * j + 64]
                probs = probs_at[p, j]
                do = mixed_grad[64 * j:64 * j + 64]
                dp = dot(value_rows, do)
                inner = jnp.sum(probs * dp, axis=0, keepdims=True)
                ds = (probs * (dp - inner)).astype(bf16)
                dqr = dot(kr, ds) * score_scale
                dk += dot(qr, ds, 1, 1)
                dv += dot(do, probs.astype(bf16), 1, 1)
                dq, terms = head_norm_back(query_pre, q_inverse, gain_query, turn_back(dqr, cosine, sine))
                terms_q += terms
                heads.append(dq)
            dk, terms_k = head_norm_back(key_pre, k_inverse, gain_key, turn_back(dk * score_scale, cosine, sine))
            q_acc[...] += terms_q
            k_acc[...] += terms_k
            grads = jnp.concatenate(heads + [dk, dv], axis=0).T.astype(bf16)
            dqkv[p] = grads
            out = dot(grads, front_full[:, :, :, 0:384].reshape(D, 384), 1, 1).astype(bf16)
            part[lax.div(p, 2), lax.rem(p, 2)] = out.reshape(2, 128, D)
        def grad_block(i):
            at = 512 * i
            a_rows = a_full[:, :, :, :, at:at + 512].reshape(ROWS, 512)
            dm_rows = dm_full[:, :, :, :, at:at + 512].reshape(ROWS, 512)
            g = jnp.concatenate([dot(a_rows, dqkv[...].reshape(ROWS, 384), 0, 0),
                                 dot(dm_rows, mixed[...].reshape(ROWS, 256), 0, 0)], axis=1)
            front_grad[i] = g.astype(bf16).reshape(4, 128, 640)

        def put_in(s, v):
            dz, terms = back(x[s].astype(f32), gain_one, v)
            input_grad[s] = mid_grad[s] + dz
            one_acc[...] += terms
        in_gen = rs_z_packs(w, me, part, put_in, sibs_b, t_b, r_b)
        next(out_gen)
        one_pack(pack_turn(me, 0))
        next(in_gen)
        next(out_gen)
        one_pack(pack_turn(me, 1))
        run([out_gen])
        next(in_gen)
        one_pack(pack_turn(me, 2))
        next(in_gen)
        one_pack(pack_turn(me, 3))
        next(in_gen)
        for i in range(4):
            grad_block(i)
        ga, gb = rs_xy_gens(w, me, front_grad, front_mine, t1, r1, t2, r2, mid)
        for g in (ga, gb, ga, gb, ga, gb, ga, gb):
            next(g)
        run([in_gen])
        run([ga, gb])
        w.finish()
        one = jnp.sum(one_acc[...], axis=0, keepdims=True)
        two = jnp.sum(two_acc[...], axis=0, keepdims=True)
        for i in range(16):
            gain_terms[i:i + 1, :] = one[:, 128 * i:128 * i + 128]
            gain_terms[16 + i:17 + i, :] = two[:, 128 * i:128 * i + 128]
        small = jnp.concatenate([q_acc[...], k_acc[...]], axis=0).T
        gain_terms[32:33, :] = jnp.sum(small, axis=0, keepdims=True)

    full = (2, 2, 2, 128, D)
    rows = jax.ShapeDtypeStruct((128, D), f32)
    return pl.pallas_call(
        kernel,
        out_shape=[rows, rows, jax.ShapeDtypeStruct((128, 640), bf16), jax.ShapeDtypeStruct((33, 128), f32)],
        in_specs=vm_specs(3) + any_specs(3) + vm_specs(8), out_specs=vm_specs(4),
        scratch_shapes=[VM((128, D), bf16), VM((ROWS, 1024), bf16), VM((D, 1024), bf16), VM(full, bf16),
                        VM(full, bf16), VM((128, D), f32), VM((PACKS, SEQ, 384), bf16),
                        VM(full, bf16), VM((4, 4, 128, 640), bf16), VM((HD, SEQ), f32), VM((HD, SEQ), f32),
                        VM((16, D), f32), VM((16, D), f32)]
        + [VM((PACKS, 4, SEQ, SEQ), f32), VM((PACKS, 320, SEQ), bf16), VM((PACKS, HD, SEQ), f32)]
        + rs_z_scratch(D) * 3 + rs_xy_scratch(640) + dma_sems(80) + [pltpu.SemaphoreType.DMA((4,))],
        compiler_params=params(cid, 60))(
            x, cot, middle, db_part, hidden, weights, a_full, front_full, qk_pre, v_rows, mixed, segs,
            gains, table)


def adam(weight, moment, square, gradient, rate, decay):
    momentum = beta_one * moment + (1.0 - beta_one) * gradient
    variance = beta_two * square + (1.0 - beta_two) * gradient * gradient
    ratio = momentum / (1.0 - beta_one**STEP) / (jnp.sqrt(variance / (1.0 - beta_two**STEP)) + adam_epsilon)
    return weight - rate * (ratio + decay * weight), momentum, variance


RATES = (0.04, 0.04, 0.04, 0.15, 0.04, 0.04, 0.02)
SPANS = (256, 64, 64, 256, 1024, 1024, 1024)


def return_gradients(front, rest, gain_terms, cid):
    def kernel(front, rest, terms, fbuf, rbuf, gain_sum, z_in, x_in, y_in, send, recv):
        me = Place()
        peers = swap_devs(me)
        mine = me.h * 2 + me.c
        zs = [me.at(z=m4(me.z + dz), c=lax.rem(me.c + dc, 2)) for dz in range(4) for dc in range(2) if dz or dc]
        xs = [me.step("x", d) for d in (1, 2, 3)]
        ys = [me.step("y", d) for d in (1, 2, 3)]
        meet(zs + xs + ys)
        w = Wire(send, recv)

        def total(buf, n):
            v = buf[0]
            for k in range(1, n):
                v = v + buf[k]
            return v

        def share(value, buf, slot, devs):
            buf[slot] = value
            return [w.go(buf.at[slot], buf.at[slot], d) for d in devs]
        gs = share(terms[...], z_in, me.z * 2 + me.c, zs)
        arrivals = []
        for j, dev in reversed(peers):
            arrivals.append(w.go(front.at[j], fbuf.at[mine], dev))
            arrivals.append(w.go(rest.at[j], rbuf.at[mine], dev))
        fbuf[mine] = front[mine]
        rbuf[mine] = rest[mine]
        for c in gs:
            c.wait_recv()
        gs = share(total(z_in, 8), x_in, me.x, xs)
        for c in gs:
            c.wait_recv()
        gs = share(total(x_in, 4), y_in, me.y, ys)
        for c in gs:
            c.wait_recv()
        gain_sum[...] = total(y_in, 4)
        for a in arrivals:
            a.wait_recv()
        w.finish()

    return pl.pallas_call(
        kernel, out_shape=[jax.ShapeDtypeStruct((4, 32, 640), bf16), jax.ShapeDtypeStruct((4, 32, 3072), bf16),
                           jax.ShapeDtypeStruct((33, 128), f32)],
        in_specs=vm_specs(3), out_specs=vm_specs(3),
        scratch_shapes=[VM((8, 33, 128), f32), VM((4, 33, 128), f32), VM((4, 33, 128), f32)] + dma_sems(19),
        compiler_params=params(cid))(front, rest, gain_terms)


def update(front, rest, gain_sum, gain_states, states, tokens):
    def kernel(*refs):
        front, rest, g_sum, g_w, g_m, g_v = refs[:6]
        ins, t_in, g_out, outs, t_out = refs[6:27], refs[27:29], refs[29:32], refs[32:53], refs[53:55]
        held, made, kept = refs[55:76], refs[76:97], refs[97:99]
        lsem, osem, tsem = refs[99:]
        loads = [pltpu.make_async_copy(a, b, lsem.at[i]) for i, (a, b) in enumerate(zip(ins, held))]
        coming = [pltpu.make_async_copy(a, b, tsem.at[i]) for i, (a, b) in enumerate(zip(t_in, kept))]
        for c in loads + coming:
            c.start()
        new = adam(g_w[...], g_m[...], g_v[...], g_sum[...], gain_rate, 0.0)
        for ref, v in zip(g_out, new):
            ref[...] = v
        stores = []
        at = {False: 0, True: 0}
        for i, (n, rate) in enumerate(zip(SPANS, RATES)):
            late = i >= 4
            buf = rest if late else front
            for k in range(3):
                loads[3 * i + k].wait()
            for j in range(4):
                here = pl.ds(n * j, n)
                grad = buf[j, :, at[late]:at[late] + n].astype(f32)
                new = adam(held[3 * i][:, here], held[3 * i + 1][:, here], held[3 * i + 2][:, here], grad, rate,
                           weight_decay)
                for k in range(3):
                    made[3 * i + k][:, here] = new[k]
            at[late] += n
            for k in range(3):
                c = pltpu.make_async_copy(made[3 * i + k], outs[3 * i + k], osem.at[3 * i + k])
                c.start()
                stores.append(c)
        for i in range(2):
            coming[i].wait()
            c = pltpu.make_async_copy(kept[i], t_out[i], tsem.at[2 + i])
            c.start()
            stores.append(c)
        for c in stores:
            c.wait()

    shapes = [jax.ShapeDtypeStruct(s.shape, f32) for s in states]
    gain_shape = jax.ShapeDtypeStruct((33, 128), f32)
    return pl.pallas_call(
        kernel, out_shape=[gain_shape] * 3 + shapes + [jax.ShapeDtypeStruct(t.shape, f32) for t in tokens],
        in_specs=vm_specs(6) + any_specs(23), out_specs=vm_specs(3) + any_specs(23),
        scratch_shapes=[VM(s.shape, f32) for s in states] * 2 + [VM(t.shape, f32) for t in tokens]
        + [pltpu.SemaphoreType.DMA((21,)), pltpu.SemaphoreType.DMA((21,)), pltpu.SemaphoreType.DMA((4,))],
        compiler_params=pltpu.CompilerParams(has_side_effects=True, vmem_limit_bytes=56 * 2**20))(
            front, rest, gain_sum, *gain_states, *states, *tokens)


from jax.sharding import PartitionSpec as P

PLANE = [[x * 16 + y * 4 + k for x in range(4) for y in range(4)] for k in range(4)]


def scatter_plane(whole):
    return lax.psum_scatter(whole, "dp", axis_index_groups=PLANE, scatter_dimension=0, tiled=True)


def local(block_input, output_grad, segment_ids, norm_gains, gain_moment, gain_square, *states):
    square = lambda v: v.reshape(33, 128)
    gains = square(norm_gains)
    table = jnp.asarray(rope_constants())
    one_full, cot_full, two_full, rest_full, front_full, segments, qk_pre, v_rows, mixed, middle = attention_forward(
        block_input, output_grad, states[::3], segment_ids, gains, table, 2)
    rest_full = rest_full.reshape(D, 3072)
    rest_grad, hidden, db_part = feed_forward(two_full, cot_full, output_grad, rest_full, 3)
    rest_mine = scatter_plane(rest_grad)
    input_grad, block_output, front_mine, gain_terms = attention_backward(
        block_input, output_grad, middle, db_part, hidden, rest_full, one_full, front_full, qk_pre, v_rows, mixed, segments,
        gains, table, 4)
    front_back, rest_back, gain_sum = return_gradients(
        front_mine.reshape(4, 32, 640), rest_mine.reshape(4, 32, 3072), gain_terms, 5)
    news = update(front_back, rest_back, gain_sum, [gains, square(gain_moment), square(gain_square)], states,
                  (block_output, input_grad))
    return tuple(news[-2:]) + tuple(v.reshape(-1) for v in news[:3]) + tuple(news[3:-2])


def solution(mesh):
    tokens, weight = P(("dp", "tensor"), None), P("dp", "tensor")
    in_specs = (tokens, tokens, P("dp", None), P(), P(), P()) + (weight,) * 21
    out_specs = (tokens, tokens, P(), P(), P()) + (weight,) * 21
    return jax.shard_map(local, mesh=mesh, in_specs=in_specs, out_specs=out_specs, check_vma=False)
```

```python
import jax
import jax.numpy as jnp
import numpy as np
from jax import lax
from jax.experimental import pallas as pl
from jax.experimental.pallas import tpu as pltpu

MESH = pl.DeviceIdType.MESH
VM = pltpu.VMEM
bf16 = jnp.bfloat16
f32 = jnp.float32


def m4(v):
    return lax.rem(v + 4, 4)


class Place:
    def __init__(self):
        dp = lax.axis_index("dp")
        self.l = lax.axis_index("tensor")
        self.x = lax.div(dp, 16)
        self.y = lax.rem(lax.div(dp, 4), 4)
        self.h = lax.rem(lax.div(dp, 2), 2)
        self.c = lax.rem(dp, 2)
        self.z = self.h * 2 + self.l

    def at(self, x=None, y=None, z=None, c=None):
        x = self.x if x is None else x
        y = self.y if y is None else y
        z = self.z if z is None else z
        c = self.c if c is None else c
        return (x * 16 + y * 4 + lax.div(z, 2) * 2 + c, lax.rem(z, 2))

    def pos(self, axis):
        return {"x": self.x, "y": self.y, "z": self.z}[axis]

    def step(self, axis, d):
        return self.at(**{axis: m4(self.pos(axis) + d)})

    def sibling(self):
        return self.at(c=1 - self.c)


class Wire:
    def __init__(self, send, recv, first=0):
        self.send, self.recv, self.n = send, recv, first
        self.pending = []

    def go(self, src, dst, dev):
        i = self.n
        self.n += 1
        c = pltpu.make_async_remote_copy(
            src_ref=src, dst_ref=dst, send_sem=self.send.at[i], recv_sem=self.recv.at[i],
            device_id=dev, device_id_type=MESH)
        c.start()
        self.pending.append(c)
        return c

    def finish(self):
        for c in self.pending:
            c.wait_send()
        self.pending = []


def meet(devs):
    b = pltpu.get_barrier_semaphore()
    for d in devs:
        pl.semaphore_signal(b, inc=1, device_id=d, device_id_type=MESH)
    pl.semaphore_wait(b, len(devs))


def ring_gather(w, me, axis, whole, lo, hi, first=None, arrived=None):
    p = me.pos(axis)
    up, down = me.step(axis, 1), me.step(axis, -1)
    own = whole(p) if first is None else first
    a = w.go(own, whole(p), up)
    b = w.go(own, whole(p), down)
    yield
    a.wait_recv()
    fa = w.go(lo(m4(p - 1)), lo(m4(p - 1)), up)
    if arrived:
        arrived(whole(m4(p - 1)))
    b.wait_recv()
    fb = w.go(hi(m4(p + 1)), hi(m4(p + 1)), down)
    if arrived:
        arrived(whole(m4(p + 1)))
    yield
    fa.wait_recv()
    if arrived:
        arrived(lo(m4(p - 2)))
    fb.wait_recv()
    if arrived:
        arrived(hi(m4(p - 2)))


def ring_scatter(w, me, axis, lo, hi, tlo, thi, rup, rdown, add):
    p = me.pos(axis)
    up, down = me.step(axis, 1), me.step(axis, -1)
    far, nu, nd = m4(p + 2), m4(p + 1), m4(p - 1)
    ta = w.go(lo(far), tlo, up)
    tb = w.go(hi(far), thi, down)
    da = w.go(hi(nu), rup[1], up)
    db = w.go(lo(nd), rdown[0], down)
    yield
    ta.wait_recv()
    add(tlo, lo(nu))
    sa = w.go(tlo, rup[0], up)
    tb.wait_recv()
    add(thi, hi(nd))
    sb = w.go(thi, rdown[1], down)
    yield
    da.wait_recv()
    db.wait_recv()
    sa.wait_recv()
    sb.wait_recv()


def loop_add(dst, a, b=None, rows=16):
    n = dst.shape[0]

    def body(i, _):
        def inner(j, _):
            s = pl.ds(pl.multiple_of(j * rows, rows), rows)
            v = dst[i, s].astype(f32) + a[i, s].astype(f32)
            if b is not None:
                v = v + b[i, s].astype(f32)
            dst[i, s] = v.astype(dst.dtype)
            return 0
        return lax.fori_loop(0, dst.shape[1] // rows, inner, 0)
    lax.fori_loop(0, n, body, 0)


def run(gens):
    gens = list(gens)
    while gens:
        for g in list(gens):
            try:
                next(g)
            except StopIteration:
                gens.remove(g)


def params(cid, mb=56):
    return pltpu.CompilerParams(collective_id=cid, has_side_effects=True, vmem_limit_bytes=mb * 2**20)


def ag_xy_gens(w, me, src, out):
    H = 64
    x, y = me.x, me.y

    def half_a():
        yield from ring_gather(w, me, "x", lambda i: out.at[i, y, pl.ds(0, 64)], lambda i: out.at[i, y, pl.ds(0, 32)],
                               lambda i: out.at[i, y, pl.ds(32, 32)], first=src.at[pl.ds(0, 64)])
        yield
        yield from ring_gather(w, me, "y", lambda i: out.at[:, i, pl.ds(0, 64)], lambda i: out.at[:, i, pl.ds(0, 32)],
                               lambda i: out.at[:, i, pl.ds(32, 32)])

    def half_b():
        yield from ring_gather(w, me, "y", lambda i: out.at[x, i, pl.ds(64, 64)], lambda i: out.at[x, i, pl.ds(64, 32)],
                               lambda i: out.at[x, i, pl.ds(96, 32)], first=src.at[pl.ds(64, 64)])
        yield
        yield from ring_gather(w, me, "x", lambda i: out.at[i, :, pl.ds(64, 64)], lambda i: out.at[i, :, pl.ds(64, 32)],
                               lambda i: out.at[i, :, pl.ds(96, 32)])
    return [half_a(), half_b()]


def ag_xy(shard, cid, space=pl.ANY):
    C = shard.shape[1]

    def kernel(src, out, send, recv, lsem):
        me = Place()
        meet([me.step("x", 1), me.step("x", -1), me.step("y", 1), me.step("y", -1)])
        w = Wire(send, recv)
        lc = pltpu.make_async_copy(src, out.at[me.x, me.y], lsem)
        lc.start()
        lc.wait()
        run(ag_xy_gens(w, me, src, out))
        w.finish()

    return pl.pallas_call(
        kernel, out_shape=jax.ShapeDtypeStruct((4, 4, 128, C), shard.dtype),
        in_specs=[pl.BlockSpec(memory_space=space)], out_specs=pl.BlockSpec(memory_space=space),
        scratch_shapes=[pltpu.SemaphoreType.DMA((16,)), pltpu.SemaphoreType.DMA((16,)), pltpu.SemaphoreType.DMA],
        compiler_params=params(cid))(shard)


def rs_xy_scratch(C):
    return [VM((2, 2, 4, 32, C), bf16), VM((2, 2, 2, 4, 32, C), bf16),
            VM((2, 2, 32, C), bf16), VM((2, 2, 2, 32, C), bf16), VM((2, 4, 64, C), bf16)]


def rs_xy_gens(w, me, g, out, t1, r1, t2, r2, mid):
    x, y = me.x, me.y

    def half(k, first, second):
        base = k * 64
        if first == "y":
            pick = lambda i, o: g.at[:, i, pl.ds(base + o, 32)]
        else:
            pick = lambda i, o: g.at[i, :, pl.ds(base + o, 32)]
        yield from ring_scatter(w, me, first, lambda i: pick(i, 0), lambda i: pick(i, 32), t1.at[k, 0], t1.at[k, 1],
                                (r1.at[k, 0, 0], r1.at[k, 0, 1]), (r1.at[k, 1, 0], r1.at[k, 1, 1]), loop_add)
        p = me.pos(first)
        m = mid.at[k]
        for hh in range(2):
            own = pick(p, 32 * hh)

            def body(i, _):
                def inner(j, _):
                    s = pl.ds(pl.multiple_of(j * 16, 16), 16)
                    d = pl.ds(pl.multiple_of(j * 16 + 32 * hh, 16), 16)
                    v = own[i, s].astype(f32) + r1[k, 0, hh, i, s].astype(f32) + r1[k, 1, hh, i, s].astype(f32)
                    m[i, d] = v.astype(bf16)
                    return 0
                return lax.fori_loop(0, 2, inner, 0)
            lax.fori_loop(0, 4, body, 0)
        yield
        q = me.pos(second)
        add1 = lambda dst, a: loop_add(dst, a)
        pick2 = lambda i, o: mid.at[k, i, pl.ds(o, 32)]

        def add2(dst, a):
            def inner(j, _):
                s = pl.ds(pl.multiple_of(j * 16, 16), 16)
                dst[s] = (dst[s].astype(f32) + a[s].astype(f32)).astype(bf16)
                return 0
            lax.fori_loop(0, 2, inner, 0)
        yield from ring_scatter(w, me, second, lambda i: pick2(i, 0), lambda i: pick2(i, 32), t2.at[k, 0], t2.at[k, 1],
                                (r2.at[k, 0, 0], r2.at[k, 0, 1]), (r2.at[k, 1, 0], r2.at[k, 1, 1]), add2)
        for hh in range(2):
            def inner(j, _):
                s = pl.ds(pl.multiple_of(j * 16, 16), 16)
                d = pl.ds(pl.multiple_of(j * 16 + 32 * hh, 16), 16)
                dd = pl.ds(pl.multiple_of(j * 16 + 32 * hh + base, 16), 16)
                v = m[q, d].astype(f32) + r2[k, 0, hh, s].astype(f32) + r2[k, 1, hh, s].astype(f32)
                out[dd] = v.astype(out.dtype)
                return 0
            lax.fori_loop(0, 2, inner, 0)
    return [half(0, "y", "x"), half(1, "x", "y")]


def rs_xy(g, cid, out_dtype=f32):
    C = g.shape[-1]

    def kernel(gin, out, send, recv, *scr):
        me = Place()
        meet([me.step("x", 1), me.step("x", -1), me.step("y", 1), me.step("y", -1)])
        w = Wire(send, recv)
        run(rs_xy_gens(w, me, gin, out, *scr))
        w.finish()

    return pl.pallas_call(
        kernel, out_shape=jax.ShapeDtypeStruct((128, C), out_dtype),
        in_specs=[pl.BlockSpec(memory_space=VM)], out_specs=pl.BlockSpec(memory_space=VM),
        scratch_shapes=[pltpu.SemaphoreType.DMA((24,)), pltpu.SemaphoreType.DMA((24,))] + rs_xy_scratch(C),
        compiler_params=params(cid, 60))(g)


def ag_z_gen(w, me, src, out, r0=0, n=128):
    sib = me.sibling()
    blk = lambda i, cc: out.at[lax.div(i, 2), cc, lax.rem(i, 2)]
    cs = []

    def to_sib(ref):
        cs.append(w.go(ref, ref, sib))
    whole = lambda i: blk(i, me.c).at[pl.ds(r0, n)]
    lo = lambda i: blk(i, me.c).at[pl.ds(r0, n // 2)]
    hi = lambda i: blk(i, me.c).at[pl.ds(r0 + n // 2, n // 2)]
    own = w.go(src, whole(me.z), sib)
    yield from ring_gather(w, me, "z", whole, lo, hi, first=src, arrived=to_sib)
    own.wait_recv()
    for c in cs:
        c.wait_recv()


def ag_z(shard, cid, space=VM):
    C = shard.shape[1]

    def kernel(src, out, send, recv, lsem):
        me = Place()
        meet([me.step("z", 1), me.step("z", -1), me.sibling()])
        w = Wire(send, recv)
        lc = pltpu.make_async_copy(src, out.at[me.h, me.c, me.l], lsem)
        lc.start()
        lc.wait()
        run([ag_z_gen(w, me, src, out)])
        w.finish()

    return pl.pallas_call(
        kernel, out_shape=jax.ShapeDtypeStruct((2, 2, 2, 128, C), shard.dtype),
        in_specs=[pl.BlockSpec(memory_space=space)], out_specs=pl.BlockSpec(memory_space=space),
        scratch_shapes=[pltpu.SemaphoreType.DMA((16,)), pltpu.SemaphoreType.DMA((16,)), pltpu.SemaphoreType.DMA],
        compiler_params=params(cid))(shard)


def rs_z_scratch(C):
    return [VM((4, 128, C), bf16), VM((2, 64, C), bf16), VM((2, 2, 64, C), bf16)]


def rs_z_gen(w, me, g, out, sibs, t, r):
    sib = me.sibling()
    oc = 1 - me.c
    order = [2, 1, 3, 0]
    blk = lambda i, cc: g.at[lax.div(i, 2), cc, lax.rem(i, 2)]
    z = me.z
    sc = {}
    for o in order:
        i = m4(z + o)
        sc[o] = w.go(blk(i, oc), sibs.at[i], sib)
    yield

    def fold(o, s0, n):
        i = m4(z + o)
        b = blk(i, me.c)

        def inner(j, _):
            s = pl.ds(pl.multiple_of(j * 16 + s0, 16), 16)
            sibs[i, s] = (sibs[i, s].astype(f32) + b[s].astype(f32)).astype(bf16)
            return 0
        lax.fori_loop(0, n // 16, inner, 0)
    up, down = me.step("z", 1), me.step("z", -1)
    half = lambda o, k: sibs.at[m4(z + o), pl.ds(64 * k, 64)]
    sc[2].wait_recv()
    fold(2, 0, 64)
    ta = w.go(half(2, 0), t.at[0], up)
    fold(2, 64, 64)
    tb = w.go(half(2, 1), t.at[1], down)
    sc[1].wait_recv()
    fold(1, 64, 64)
    da = w.go(half(1, 1), r.at[0, 1], up)
    sc[3].wait_recv()
    fold(3, 0, 64)
    db = w.go(half(3, 0), r.at[1, 0], down)
    fold(1, 0, 64)
    fold(3, 64, 64)
    yield

    def add(dst, a):
        def inner(j, _):
            s = pl.ds(pl.multiple_of(j * 16, 16), 16)
            dst[s] = (dst[s].astype(f32) + a[s].astype(f32)).astype(bf16)
            return 0
        lax.fori_loop(0, 4, inner, 0)
    ta.wait_recv()
    add(t.at[0], half(1, 0))
    sa = w.go(t.at[0], r.at[0, 0], up)
    tb.wait_recv()
    add(t.at[1], half(3, 1))
    sb = w.go(t.at[1], r.at[1, 1], down)
    sc[0].wait_recv()
    own = blk(z, me.c)
    yield

    def last(hh):
        def inner(j, _):
            s = pl.ds(pl.multiple_of(j * 16, 16), 16)
            d = pl.ds(pl.multiple_of(j * 16 + 64 * hh, 16), 16)
            v = own[d].astype(f32) + sibs[z, d].astype(f32) + r[0, hh, s].astype(f32) + r[1, hh, s].astype(f32)
            out(d, v)
            return 0
        lax.fori_loop(0, 4, inner, 0)
    da.wait_recv()
    sa.wait_recv()
    db.wait_recv()
    sb.wait_recv()
    last(0)
    last(1)


def rs_z(g, cid, out_dtype=f32):
    C = g.shape[-1]

    def kernel(gin, out, send, recv, *scr):
        me = Place()
        meet([me.step("z", 1), me.step("z", -1), me.sibling()])
        w = Wire(send, recv)

        def put(s, v):
            out[s] = v.astype(out.dtype)
        run([rs_z_gen(w, me, gin, put, *scr)])
        w.finish()

    return pl.pallas_call(
        kernel, out_shape=jax.ShapeDtypeStruct((128, C), out_dtype),
        in_specs=[pl.BlockSpec(memory_space=VM)], out_specs=pl.BlockSpec(memory_space=VM),
        scratch_shapes=[pltpu.SemaphoreType.DMA((16,)), pltpu.SemaphoreType.DMA((16,))] + rs_z_scratch(C),
        compiler_params=params(cid))(g)


def swap_devs(me):
    out = []
    for dh, dc in ((0, 1), (1, 0), (1, 1)):
        h = lax.rem(me.h + dh, 2)
        c = lax.rem(me.c + dc, 2)
        out.append((h * 2 + c, me.at(z=h * 2 + me.l, c=c)))
    return out


def swap_hc(parts, cid):
    n = len(parts)

    def kernel(*refs):
        ins, outs = refs[:n], refs[n:2 * n]
        send, recv, lsem = refs[2 * n:]
        me = Place()
        peers = swap_devs(me)
        meet([d for _, d in peers])
        w = Wire(send, recv)
        mine = me.h * 2 + me.c
        arrivals = []
        for j, d in reversed(peers):
            for a, b in zip(ins, outs):
                arrivals.append(w.go(a.at[j], b.at[mine], d))
        ls = []
        for k, (a, b) in enumerate(zip(ins, outs)):
            lc = pltpu.make_async_copy(a.at[mine], b.at[mine], lsem.at[k])
            lc.start()
            ls.append(lc)
        for lc in ls:
            lc.wait()
        for a in arrivals:
            a.wait_recv()
        w.finish()

    return pl.pallas_call(
        kernel, out_shape=[jax.ShapeDtypeStruct(p.shape, p.dtype) for p in parts],
        in_specs=[pl.BlockSpec(memory_space=VM)] * n, out_specs=[pl.BlockSpec(memory_space=VM)] * n,
        scratch_shapes=[pltpu.SemaphoreType.DMA((3 * n,)), pltpu.SemaphoreType.DMA((3 * n,)),
                        pltpu.SemaphoreType.DMA((n,))],
        compiler_params=params(cid))(*parts)


def sum_all(v, cid):
    R, C = v.shape

    def kernel(src, out, z_in, x_in, y_in, acc, send, recv):
        me = Place()
        zs = []
        for dz in range(4):
            for dc in range(2):
                if dz or dc:
                    z, c = m4(me.z + dz), lax.rem(me.c + dc, 2)
                    zs.append(me.at(z=z, c=c))
        xs = [me.step("x", d) for d in (1, 2, 3)]
        ys = [me.step("y", d) for d in (1, 2, 3)]
        meet(zs + xs + ys)
        w = Wire(send, recv)
        acc[...] = src[...]
        for buf, slot, devs, n in ((z_in, me.z * 2 + me.c, zs, 8), (x_in, me.x, xs, 4), (y_in, me.y, ys, 4)):
            buf[slot] = acc[...]
            cs = [w.go(buf.at[slot], buf.at[slot], d) for d in devs]
            for c in cs:
                c.wait_recv()
            total = buf[0]
            for k in range(1, n):
                total = total + buf[k]
            w.finish()
            acc[...] = total
        out[...] = acc[...]

    return pl.pallas_call(
        kernel, out_shape=jax.ShapeDtypeStruct((R, C), f32),
        in_specs=[pl.BlockSpec(memory_space=VM)], out_specs=pl.BlockSpec(memory_space=VM),
        scratch_shapes=[VM((8, R, C), f32), VM((4, R, C), f32), VM((4, R, C), f32), VM((R, C), f32),
                        pltpu.SemaphoreType.DMA((13,)), pltpu.SemaphoreType.DMA((13,))],
        compiler_params=params(cid))(v)


def rs_z_packs(w, me, g, put, sibs, t, r):
    sib, oc, z = me.sibling(), 1 - me.c, me.z
    blk = lambda i, cc: g.at[lax.div(i, 2), cc, lax.rem(i, 2)]
    far = m4(z + 2)
    flip = lambda i: i + 1 - 2 * lax.rem(i, 2)
    beside, partner = flip(far), flip(z)
    up, down = me.step("z", 1), me.step("z", -1)
    half = lambda i, k: sibs.at[i, pl.ds(64 * k, 64)]

    def fold(i, s0, n):
        b = blk(i, me.c)

        def inner(j, _):
            s = pl.ds(pl.multiple_of(j * 16 + s0, 16), 16)
            sibs[i, s] = (sibs[i, s].astype(f32) + b[s].astype(f32)).astype(bf16)
            return 0
        lax.fori_loop(0, n // 16, inner, 0)

    def add(dst, a):
        def inner(j, _):
            s = pl.ds(pl.multiple_of(j * 16, 16), 16)
            dst[s] = (dst[s].astype(f32) + a[s].astype(f32)).astype(bf16)
            return 0
        lax.fori_loop(0, 4, inner, 0)
    s_far = w.go(blk(far, oc), sibs.at[far], sib)
    s_beside = w.go(blk(beside, oc), sibs.at[beside], sib)
    yield
    s_far.wait_recv()
    fold(far, 0, 64)
    ta = w.go(half(far, 0), t.at[0], up)
    fold(far, 64, 64)
    tb = w.go(half(far, 1), t.at[1], down)
    s_beside.wait_recv()
    fold(beside, 0, 128)
    yield
    s_partner = w.go(blk(partner, oc), sibs.at[partner], sib)
    s_own = w.go(blk(z, oc), sibs.at[z], sib)
    yield
    s_partner.wait_recv()
    fold(partner, 0, 128)
    nu, nd = m4(z + 1), m4(z - 1)
    da = w.go(half(nu, 1), r.at[0, 1], up)
    db = w.go(half(nd, 0), r.at[1, 0], down)
    ta.wait_recv()
    add(t.at[0], half(nu, 0))
    sa = w.go(t.at[0], r.at[0, 0], up)
    tb.wait_recv()
    add(t.at[1], half(nd, 1))
    sb = w.go(t.at[1], r.at[1, 1], down)
    s_own.wait_recv()
    own = blk(z, me.c)
    yield

    def last(hh):
        def inner(j, _):
            s = pl.ds(pl.multiple_of(j * 16, 16), 16)
            d = pl.ds(pl.multiple_of(j * 16 + 64 * hh, 16), 16)
            put(d, own[d].astype(f32) + sibs[z, d].astype(f32) + r[0, hh, s].astype(f32) + r[1, hh, s].astype(f32))
            return 0
        lax.fori_loop(0, 4, inner, 0)
    da.wait_recv()
    sa.wait_recv()
    db.wait_recv()
    sb.wait_recv()
    last(0)
    last(1)


D = 2048
HD = 64
STEP = 10
SEQ = 256
PACKS = 4
ROWS = 1024
epsilon = 1e-06
rope_base = 1000000.0
beta_one = 0.9
beta_two = 0.999
adam_epsilon = 1e-08
weight_decay = 0.1
gain_rate = 0.3
masked_score = -1000000000.0
score_scale = HD ** (-0.5)
exact = lax.Precision.HIGHEST


def dot(a, b, ca=1, cb=0, precision=None):
    return lax.dot_general(a, b, (((ca,), (cb,)), ((), ())), precision=precision, preferred_element_type=f32)


def chunks(n, body, rows=16):
    def one(j, _):
        body(pl.ds(pl.multiple_of(j * rows, rows), rows))
        return 0
    lax.fori_loop(0, n // rows, one, 0)


def dma_sems(n):
    return [pltpu.SemaphoreType.DMA((n,)), pltpu.SemaphoreType.DMA((n,))]


def vm_specs(n):
    return [pl.BlockSpec(memory_space=VM)] * n


def any_specs(n):
    return [pl.BlockSpec(memory_space=pl.ANY)] * n


class Columns:
    def __init__(self, ref, n):
        self.ref, self.n = ref, n

    def __getitem__(self, j):
        return self.ref[:, pl.ds(pl.multiple_of(j * self.n, self.n), self.n)]


def gain_rows(gains):
    one = jnp.concatenate([gains[i:i + 1, :] for i in range(16)], axis=1)
    two = jnp.concatenate([gains[16 + i:17 + i, :] for i in range(16)], axis=1)
    small = jnp.broadcast_to(gains[32:33, :], (128, 128)).T
    return one, two, small[0:64, 0:1], small[64:128, 0:1]


def rope_constants():
    frequency = np.float32(rope_base) ** (np.float32(-2.0) * np.arange(HD // 2, dtype=np.float32) / np.float32(HD))
    angles = (np.arange(SEQ, dtype=np.float32)[None, :] * frequency[:, None].astype(np.float32)).astype(np.float64)
    return np.concatenate([np.cos(angles), np.sin(angles)], axis=0).astype(np.float32)


def pack_tables(segs, p, table):
    row = segs[p].astype(f32)[0:1, :]
    column = jnp.broadcast_to(row, (128, SEQ)).T[:, 0:1]
    key_at = lax.broadcasted_iota(jnp.int32, (SEQ, SEQ), 0)
    query_at = lax.broadcasted_iota(jnp.int32, (SEQ, SEQ), 1)
    allowed = (column == row) & (key_at <= query_at)
    start = jnp.sum(jnp.where(column < row, 1.0, 0.0), axis=0, keepdims=True)
    where = query_at.astype(f32) - start
    hot = jnp.where(key_at.astype(f32) == where, 1.0, 0.0)
    both = dot(table[...], hot, precision=exact)
    return allowed, both[0:32], both[32:64]


def head_norm(z, gain):
    inverse = lax.rsqrt(jnp.mean(z * z, axis=0, keepdims=True) + epsilon)
    return z * inverse * gain, inverse


def head_norm_back(z, inverse, gain, up):
    scaled = up * gain
    inner = jnp.mean(z * scaled, axis=0, keepdims=True)
    return inverse * (scaled - z * inverse * inverse * inner), up * z * inverse


def turn(u, cosine, sine):
    a, b = u[0:32], u[32:64]
    return jnp.concatenate([a * cosine - b * sine, b * cosine + a * sine], axis=0)


def turn_back(u, cosine, sine):
    a, b = u[0:32], u[32:64]
    return jnp.concatenate([a * cosine + b * sine, b * cosine - a * sine], axis=0)


def pack_probs(key_rows, query_rot, allowed):
    scores = jnp.where(allowed, dot(key_rows, query_rot) * score_scale, masked_score)
    exps = jnp.exp(scores - jnp.max(scores, axis=0, keepdims=True))
    return exps / jnp.sum(exps, axis=0, keepdims=True)


def pack_of(ref, p):
    v = ref[lax.div(p, 2), lax.rem(p, 2)]
    return v.reshape(SEQ, v.shape[-1])


def pack_turn(me, i):
    h = me.h if i >= 2 else 1 - me.h
    c = me.c if i % 2 else 1 - me.c
    return h * 2 + c


def attention_forward(x, cot, weights, seg, gains, table, cid):
    def kernel(x, cot, q_, k_, v_, o_, g_, u_, d_, seg, gains, table,
               a_full, cot_full, n_full, rest_full, front_full, segs, qk_pre, v_rows, mixed, middle,
               fbuf, rbuf, sbuf, kv, fshard, rshard, rest, shard, shard_two, a_buf, part, sibs, t, r,
               send, recv, lsem, ksem):
        me = Place()
        gain_one, gain_two, gain_query, gain_key = gain_rows(gains)
        peers = swap_devs(me)
        mine = me.h * 2 + me.c
        q, o = Columns(q_, 256), Columns(o_, 256)
        g, u, d = Columns(g_, 1024), Columns(u_, 1024), Columns(d_, 1024)
        for j in range(4):
            kv[j] = jnp.concatenate([k_[:, 64 * j:64 * j + 64], v_[:, 64 * j:64 * j + 64]], axis=1)
        sbuf[...] = jnp.broadcast_to(seg[...], (8, SEQ))
        here = pl.ds(pl.multiple_of(mine * 32, 32), 32)

        def round_front(j, dst):
            dst[:, 0:256] = q[j].astype(bf16)
            dst[:, 256:384] = kv[j].astype(bf16)
            dst[:, 384:640] = o[j].astype(bf16)

        def round_rest(j, dst):
            for i, w in enumerate((g, u, d)):
                dst[:, 1024 * i:1024 * i + 1024] = w[j].astype(bf16)
        meet([me.step("x", 1), me.step("x", -1), me.step("y", 1), me.step("y", -1),
              me.step("z", 1), me.step("z", -1)] + [dev for _, dev in peers])
        w = Wire(send, recv)
        first, second = [], []
        for j, dev in reversed(peers):
            round_front(j, fbuf.at[j])
            first.append(w.go(fbuf.at[j], fshard.at[here], dev))
            second.append(w.go(sbuf, segs.at[mine], dev))
        for j, dev in reversed(peers):
            round_rest(j, rbuf.at[j])
            second.append(w.go(rbuf.at[j], rshard.at[here], dev))
        round_front(mine, fshard.at[here])
        round_rest(mine, rshard.at[here])
        segs[mine] = sbuf[...]

        def norm_one(s):
            v = x[s].astype(f32)
            inverse = lax.rsqrt(jnp.mean(v * v, axis=-1, keepdims=True) + epsilon)
            shard[s] = (v * inverse * gain_one).astype(bf16)
        chunks(128, norm_one)
        for c in first:
            c.wait_recv()

        def both(gens):
            for g in gens:
                next(g)
        front_gens = ag_xy_gens(w, me, fshard, front_full)
        both(front_gens)
        gz = ag_z_gen(w, me, shard, a_buf)
        next(gz)
        locals_ = [pltpu.make_async_copy(fshard, front_full.at[me.x, me.y], lsem.at[0]),
                   pltpu.make_async_copy(shard, a_buf.at[me.h, me.c, me.l], lsem.at[1]),
                   pltpu.make_async_copy(cot, cot_full.at[me.h, me.c, me.l], lsem.at[2])]
        for c in locals_:
            c.start()
        both(front_gens)
        for c in locals_:
            c.wait()
        both(front_gens)
        both(front_gens)
        for c in second:
            c.wait_recv()
        rest_gens = ag_xy_gens(w, me, rshard, rest)
        both(rest_gens)
        own = pltpu.make_async_copy(rshard, rest.at[me.x, me.y], lsem.at[3])
        own.start()
        both(front_gens)
        both(rest_gens)
        own.wait()
        run(front_gens)
        both(rest_gens)
        both(rest_gens)
        next(gz)
        run([gz])
        cot_gen = ag_z_gen(w, me, cot.at[pl.ds(0, 64)], cot_full, 0, 64)
        next(cot_gen)
        keep = pltpu.make_async_copy(a_buf, a_full, lsem.at[4])
        keep.start()

        def one_pack(p):
            allowed, cosine, sine = pack_tables(segs, p, table)
            qkv = dot(pack_of(a_buf, p), front_full[:, :, :, 0:384].reshape(D, 384)).T
            qk_pre[p] = qkv[0:320]
            value = qkv[320:384].astype(bf16)
            v_rows[p] = value
            kn, _i = head_norm(qkv[256:320], gain_key)
            key_rows = turn(kn, cosine, sine).T.astype(bf16)
            heads = []
            for j in range(4):
                qn, _i = head_norm(qkv[64 * j:64 * j + 64], gain_query)
                probs = pack_probs(key_rows, turn(qn, cosine, sine).astype(bf16), allowed)
                heads.append(dot(value, probs.astype(bf16)))
            o = jnp.concatenate(heads, axis=0).T.astype(bf16)
            mixed[p] = o
            out = dot(o, front_full[:, :, :, 384:640].reshape(D, 256), 1, 1).astype(bf16)
            part[lax.div(p, 2), lax.rem(p, 2)] = out.reshape(2, 128, D)

        def residual(s, v):
            middle[s] = x[s].astype(f32) + v
        sum_gen = rs_z_packs(w, me, part, residual, sibs, t, r)
        for i in range(4):
            one_pack(pack_turn(me, i))
            next(sum_gen)
            if i == 2:
                next(cot_gen)
        both(rest_gens)
        run([sum_gen])

        def norm_two(s):
            v = middle[s]
            inverse = lax.rsqrt(jnp.mean(v * v, axis=-1, keepdims=True) + epsilon)
            shard_two[s] = (v * inverse * gain_two).astype(bf16)
        chunks(128, norm_two)
        n_gen = ag_z_gen(w, me, shard_two, n_full)
        next(n_gen)
        own = pltpu.make_async_copy(shard_two, n_full.at[me.h, me.c, me.l], lsem.at[3])
        own.start()
        run([cot_gen])
        stores = []

        def store(k, a, b, at):
            here = pl.ds(at, 64)
            c = pltpu.make_async_copy(rest.at[a, b, here], rest_full.at[a, b, here], ksem.at[k])
            c.start()
            stores.append(c)
        every = slice(None)
        for k in (0, 1, 3):
            store(k, every, m4(me.y + k), 0)
            store(4 + k, m4(me.x + k), every, 64)
        next(n_gen)
        cot_gen = ag_z_gen(w, me, cot.at[pl.ds(64, 64)], cot_full, 64, 64)
        next(cot_gen)
        run([n_gen])
        run(rest_gens)
        store(2, every, m4(me.y + 2), 0)
        store(6, m4(me.x + 2), every, 64)
        run([cot_gen])
        own.wait()
        keep.wait()
        for c in stores:
            c.wait()
        w.finish()

    full = jax.ShapeDtypeStruct((2, 2, 2, 128, D), bf16)
    return pl.pallas_call(
        kernel,
        out_shape=[full, full, full, jax.ShapeDtypeStruct((4, 4, 128, 3072), bf16),
                   jax.ShapeDtypeStruct((4, 4, 128, 640), bf16), jax.ShapeDtypeStruct((4, 8, SEQ), jnp.int32),
                   jax.ShapeDtypeStruct((PACKS, 320, SEQ), f32), jax.ShapeDtypeStruct((PACKS, HD, SEQ), bf16),
                   jax.ShapeDtypeStruct((PACKS, SEQ, 256), bf16), jax.ShapeDtypeStruct((128, D), f32)],
        in_specs=vm_specs(12), out_specs=any_specs(4) + vm_specs(6),
        scratch_shapes=[VM((4, 32, 640), bf16), VM((4, 32, 3072), bf16), VM((8, SEQ), jnp.int32), VM((4, 32, 128), f32),
                        VM((128, 640), bf16), VM((128, 3072), bf16), VM((4, 4, 128, 3072), bf16)]
        + [VM((128, D), bf16)] * 2 + [VM((2, 2, 2, 128, D), bf16)] * 2 + rs_z_scratch(D)
        + dma_sems(96) + [pltpu.SemaphoreType.DMA((5,)), pltpu.SemaphoreType.DMA((8,))],
        compiler_params=params(cid, 58))(x, cot, *weights, seg, gains, table)


def sigmoid(v):
    return 1.0 / (1.0 + jnp.exp(-v))


def feed_forward(n_full, cot_full, weights):
    def kernel(n_hbm, cot_hbm, w_hbm, grad_hbm, hidden_hbm, gate_up_hbm,
               n, cot, w, hidden, gate_up, grad, lsem, wsem, gsem):
        loads = [pltpu.make_async_copy(n_hbm, n, lsem.at[0]), pltpu.make_async_copy(cot_hbm, cot, lsem.at[1])]
        loads[0].start()

        def piece(i, k):
            here = pl.ds(pl.multiple_of(i * 256 + 1024 * k, 256), 256)
            return pltpu.make_async_copy(w_hbm.at[:, here], w.at[:, here], wsem.at[i, k])
        for i in range(4):
            for k in range(3):
                piece(i, k).start()
            if i == 0:
                loads[1].start()
        for c in loads:
            c.wait()

        def hidden_block(i, _):
            at = pl.multiple_of(i * 256, 256)
            for k in range(3):
                piece(i, k).wait()
            rows = n[...].reshape(ROWS, D)
            g = dot(rows, w[:, pl.ds(at, 256)])
            u = dot(rows, w[:, pl.ds(at + 1024, 256)])
            dh = dot(cot[...].reshape(ROWS, D), w[:, pl.ds(at + 2048, 256)])
            s = sigmoid(g)
            silu = g * s
            hidden[:, pl.ds(at, 256)] = (silu * u).astype(bf16)
            gate_up[:, pl.ds(at, 256)] = (dh * u * (s + silu * (1.0 - s))).astype(bf16)
            gate_up[:, pl.ds(at + 1024, 256)] = (dh * silu).astype(bf16)
            return 0
        lax.fori_loop(0, 4, hidden_block, 0)
        keep = [pltpu.make_async_copy(hidden, hidden_hbm, lsem.at[2]),
                pltpu.make_async_copy(gate_up, gate_up_hbm, lsem.at[3])]
        for c in keep:
            c.start()
        stores = []
        for i in range(4):
            at = 512 * i
            slot = i % 2
            if i >= 2:
                stores[i - 2].wait()
            grad[slot, :, 0:2048] = dot(n[:, :, :, :, at:at + 512].reshape(ROWS, 512), gate_up[...], 0, 0).astype(bf16)
            grad[slot, :, 2048:3072] = dot(cot[:, :, :, :, at:at + 512].reshape(ROWS, 512), hidden[...], 0, 0).astype(bf16)
            c = pltpu.make_async_copy(grad.at[slot], grad_hbm.at[pl.ds(at, 512)], gsem.at[i])
            c.start()
            stores.append(c)
        for c in stores[2:] + keep:
            c.wait()

    full = (2, 2, 2, 128, D)
    return pl.pallas_call(
        kernel,
        out_shape=[jax.ShapeDtypeStruct((D, 3072), bf16), jax.ShapeDtypeStruct((ROWS, 1024), bf16),
                   jax.ShapeDtypeStruct((ROWS, 2048), bf16)],
        in_specs=any_specs(3), out_specs=any_specs(3),
        scratch_shapes=[VM(full, bf16), VM(full, bf16), VM((D, 3072), bf16), VM((ROWS, 1024), bf16),
                        VM((ROWS, 2048), bf16), VM((2, 512, 3072), bf16), pltpu.SemaphoreType.DMA((4,)),
                        pltpu.SemaphoreType.DMA((4, 3)), pltpu.SemaphoreType.DMA((4,))],
        compiler_params=pltpu.CompilerParams(has_side_effects=True, vmem_limit_bytes=60 * 2**20))(
            n_full, cot_full, weights)


def attention_backward(x, cot, middle, gate_up, hidden, weights, a_full, front_full, qk_pre, v_rows, mixed, segs,
                       gains, table, cid):
    def kernel(x, cot, middle, gate_up_hbm, hidden_hbm, w_hbm, a_hbm, front_full, qk_pre, v_rows, mixed, segs,
               gains, table, input_grad, block_output, front_mine, gain_terms,
               shard, hidden, wd, out_part, dm_full, mid_grad, dqkv, part, front_grad, q_acc, k_acc, one_acc, two_acc,
               gate_up, wgu, db_sum,
               sibs_a, t_a, r_a, sibs_b, t_b, r_b, t1, r1, t2, r2, mid, send, recv, lsem, wsem):
        me = Place()
        gain_one, gain_two, gain_query, gain_key = gain_rows(gains)
        loads = [pltpu.make_async_copy(hidden_hbm, hidden, lsem.at[1]),
                 pltpu.make_async_copy(w_hbm.at[:, pl.ds(2048, 1024)], wd, lsem.at[2])]
        unit_load = pltpu.make_async_copy(gate_up_hbm, gate_up, lsem.at[3])
        unit_load.start()

        def piece(i):
            here = pl.ds(pl.multiple_of(i * 256, 256), 256)
            return pltpu.make_async_copy(w_hbm.at[here, pl.ds(0, 2048)], wgu.at[here], wsem.at[i])
        for i in range(8):
            piece(i).start()
        for c in loads:
            c.start()
        two_acc[...] = jnp.zeros_like(two_acc)
        one_acc[...] = jnp.zeros_like(one_acc)
        q_acc[...] = jnp.zeros_like(q_acc)
        k_acc[...] = jnp.zeros_like(k_acc)

        def back(z, gain, up):
            inverse = lax.rsqrt(jnp.mean(z * z, axis=-1, keepdims=True) + epsilon)
            scaled = up * gain
            inner = jnp.mean(z * scaled, axis=-1, keepdims=True)
            return inverse * (scaled - z * inverse * inverse * inner), up * z * inverse

        meet([me.step("x", 1), me.step("x", -1), me.step("y", 1), me.step("y", -1),
              me.step("z", 1), me.step("z", -1), me.sibling()])
        w, w_db = Wire(send, recv), Wire(send, recv, 60)

        def put_a(s, v):
            db_sum[s, 0:1024] = v

        def put_b(s, v):
            db_sum[s, 1024:2048] = v

        def back_block(i, _):
            at = pl.multiple_of(i * 256, 256)
            piece(i).wait()
            v = dot(gate_up[...], wgu[pl.ds(at, 256)], 1, 1).astype(bf16)
            part[:, :, :, :, pl.ds(at, 256)] = v.reshape(2, 2, 2, 128, 256)
            return 0

        def out_block(i, _):
            at = pl.multiple_of(i * 256, 256)
            v = dot(hidden[...], wd[pl.ds(at, 256)], 1, 1).astype(bf16)
            out_part[:, :, :, :, pl.ds(at, 256)] = v.reshape(2, 2, 2, 128, 256)
            return 0

        def columns(k):
            c = pl.ds(1024 * k, 1024)
            return part.at[:, :, :, :, c], (put_a, put_b)[k], sibs_b.at[:, :, c], t_b.at[:, :, c], r_b.at[:, :, :, c]
        unit_load.wait()
        gen_a, gen_b = [rs_z_gen(w_db, me, *columns(k)) for k in range(2)]
        lax.fori_loop(0, 4, back_block, 0)
        next(gen_a)
        lax.fori_loop(4, 8, back_block, 0)
        a_load = pltpu.make_async_copy(a_hbm, gate_up, lsem.at[4])
        a_load.start()
        next(gen_b)
        next(gen_a)
        for c in loads:
            c.wait()
        lax.fori_loop(0, 2, out_block, 0)
        next(gen_b)
        lax.fori_loop(2, 6, out_block, 0)
        next(gen_a)
        lax.fori_loop(6, 8, out_block, 0)
        next(gen_b)
        run([gen_a])
        run([gen_b])
        w_db.finish()

        def norm_two(s):
            dz, terms = back(middle[s], gain_two, db_sum[s])
            v = cot[s].astype(f32) + dz
            mid_grad[s] = v
            shard[s] = v.astype(bf16)
            two_acc[...] += terms
        chunks(128, norm_two)
        gen = ag_z_gen(w, me, shard, dm_full)
        next(gen)
        own = pltpu.make_async_copy(shard, dm_full.at[me.h, me.c, me.l], lsem.at[0])
        own.start()

        def put_out(s, v):
            block_output[s] = middle[s] + v
        out_gen = rs_z_gen(w, me, out_part, put_out, sibs_a, t_a, r_a)
        next(gen)
        next(out_gen)
        run([gen])
        own.wait()

        def one_pack(p):
            allowed, cosine, sine = pack_tables(segs, p, table)
            mixed_grad = dot(pack_of(dm_full, p), front_full[:, :, :, 384:640].reshape(D, 256)).T.astype(bf16)
            value_rows = v_rows[p].astype(f32).T.astype(bf16)
            key_pre = qk_pre[p, 256:320]
            kn, k_inverse = head_norm(key_pre, gain_key)
            kr = turn(kn, cosine, sine)
            key_rows = kr.T.astype(bf16)
            kr = kr.astype(bf16)
            dk = jnp.zeros((HD, SEQ), f32)
            dv = jnp.zeros((HD, SEQ), f32)
            heads = []
            terms_q = jnp.zeros((HD, SEQ), f32)
            for j in range(4):
                query_pre = qk_pre[p, 64 * j:64 * j + 64]
                qn, q_inverse = head_norm(query_pre, gain_query)
                qr = turn(qn, cosine, sine).astype(bf16)
                probs = pack_probs(key_rows, qr, allowed)
                do = mixed_grad[64 * j:64 * j + 64]
                dp = dot(value_rows, do)
                inner = jnp.sum(probs * dp, axis=0, keepdims=True)
                ds = (probs * (dp - inner)).astype(bf16)
                dqr = dot(kr, ds) * score_scale
                dk += dot(qr, ds, 1, 1)
                dv += dot(do, probs.astype(bf16), 1, 1)
                dq, terms = head_norm_back(query_pre, q_inverse, gain_query, turn_back(dqr, cosine, sine))
                terms_q += terms
                heads.append(dq)
            dk, terms_k = head_norm_back(key_pre, k_inverse, gain_key, turn_back(dk * score_scale, cosine, sine))
            q_acc[...] += terms_q
            k_acc[...] += terms_k
            grads = jnp.concatenate(heads + [dk, dv], axis=0).T.astype(bf16)
            dqkv[p] = grads
            out = dot(grads, front_full[:, :, :, 0:384].reshape(D, 384), 1, 1).astype(bf16)
            part[lax.div(p, 2), lax.rem(p, 2)] = out.reshape(2, 128, D)
        def grad_block(i):
            at = 512 * i
            a_rows = gate_up[:, at:at + 512]
            dm_rows = dm_full[:, :, :, :, at:at + 512].reshape(ROWS, 512)
            g = jnp.concatenate([dot(a_rows, dqkv[...].reshape(ROWS, 384), 0, 0),
                                 dot(dm_rows, mixed[...].reshape(ROWS, 256), 0, 0)], axis=1)
            front_grad[i] = g.astype(bf16).reshape(4, 128, 640)

        def put_in(s, v):
            dz, terms = back(x[s].astype(f32), gain_one, v)
            input_grad[s] = mid_grad[s] + dz
            one_acc[...] += terms
        in_gen = rs_z_packs(w, me, part, put_in, sibs_b, t_b, r_b)
        next(out_gen)
        one_pack(pack_turn(me, 0))
        next(in_gen)
        one_pack(pack_turn(me, 1))
        next(out_gen)
        next(in_gen)
        one_pack(pack_turn(me, 2))
        next(in_gen)
        one_pack(pack_turn(me, 3))
        next(in_gen)
        a_load.wait()
        for i in range(4):
            grad_block(i)
        ga, gb = rs_xy_gens(w, me, front_grad, front_mine, t1, r1, t2, r2, mid)
        for g in (ga, gb, ga, gb, ga, gb, ga, gb):
            next(g)
        run([out_gen])
        run([in_gen])
        run([ga, gb])
        w.finish()
        one = jnp.sum(one_acc[...], axis=0, keepdims=True)
        two = jnp.sum(two_acc[...], axis=0, keepdims=True)
        for i in range(16):
            gain_terms[i:i + 1, :] = one[:, 128 * i:128 * i + 128]
            gain_terms[16 + i:17 + i, :] = two[:, 128 * i:128 * i + 128]
        small = jnp.concatenate([q_acc[...], k_acc[...]], axis=0).T
        gain_terms[32:33, :] = jnp.sum(small, axis=0, keepdims=True)

    full = (2, 2, 2, 128, D)
    rows = jax.ShapeDtypeStruct((128, D), f32)
    return pl.pallas_call(
        kernel,
        out_shape=[rows, rows, jax.ShapeDtypeStruct((128, 640), bf16), jax.ShapeDtypeStruct((33, 128), f32)],
        in_specs=vm_specs(3) + any_specs(4) + vm_specs(7), out_specs=vm_specs(4),
        scratch_shapes=[VM((128, D), bf16), VM((ROWS, 1024), bf16), VM((D, 1024), bf16), VM(full, bf16),
                        VM(full, bf16), VM((128, D), f32), VM((PACKS, SEQ, 384), bf16),
                        VM(full, bf16), VM((4, 4, 128, 640), bf16), VM((HD, SEQ), f32), VM((HD, SEQ), f32),
                        VM((16, D), f32), VM((16, D), f32)]
        + [VM((ROWS, D), bf16), VM((D, D), bf16), VM((128, D), f32)]
        + rs_z_scratch(D) * 2 + rs_xy_scratch(640) + dma_sems(84)
        + [pltpu.SemaphoreType.DMA((5,)), pltpu.SemaphoreType.DMA((8,))],
        compiler_params=params(cid, 60))(
            x, cot, middle, gate_up, hidden, weights, a_full.reshape(ROWS, D), front_full, qk_pre, v_rows, mixed, segs,
            gains, table)


def adam(weight, moment, square, gradient, rate, decay):
    momentum = beta_one * moment + (1.0 - beta_one) * gradient
    variance = beta_two * square + (1.0 - beta_two) * gradient * gradient
    ratio = momentum / (1.0 - beta_one**STEP) / (jnp.sqrt(variance / (1.0 - beta_two**STEP)) + adam_epsilon)
    return weight - rate * (ratio + decay * weight), momentum, variance


RATES = (0.04, 0.04, 0.04, 0.15, 0.04, 0.04, 0.02)
SPANS = (256, 64, 64, 256, 1024, 1024, 1024)


def return_gradients(front, rest, gain_terms, cid):
    def kernel(front, rest, terms, fbuf, rbuf, gain_sum, z_in, x_in, y_in, send, recv):
        me = Place()
        peers = swap_devs(me)
        mine = me.h * 2 + me.c
        zs = [me.at(z=m4(me.z + dz), c=lax.rem(me.c + dc, 2)) for dz in range(4) for dc in range(2) if dz or dc]
        xs = [me.step("x", d) for d in (1, 2, 3)]
        ys = [me.step("y", d) for d in (1, 2, 3)]
        meet(zs + xs + ys)
        w = Wire(send, recv)

        def total(buf, n):
            v = buf[0]
            for k in range(1, n):
                v = v + buf[k]
            return v

        def share(value, buf, slot, devs):
            buf[slot] = value
            return [w.go(buf.at[slot], buf.at[slot], d) for d in devs]
        gs = share(terms[...], z_in, me.z * 2 + me.c, zs)
        arrivals = []
        for j, dev in reversed(peers):
            arrivals.append(w.go(front.at[j], fbuf.at[mine], dev))
            arrivals.append(w.go(rest.at[j], rbuf.at[mine], dev))
        fbuf[mine] = front[mine]
        rbuf[mine] = rest[mine]
        for c in gs:
            c.wait_recv()
        gs = share(total(z_in, 8), x_in, me.x, xs)
        for c in gs:
            c.wait_recv()
        gs = share(total(x_in, 4), y_in, me.y, ys)
        for c in gs:
            c.wait_recv()
        gain_sum[...] = total(y_in, 4)
        for a in arrivals:
            a.wait_recv()
        w.finish()

    return pl.pallas_call(
        kernel, out_shape=[jax.ShapeDtypeStruct((4, 32, 640), bf16), jax.ShapeDtypeStruct((4, 32, 3072), bf16),
                           jax.ShapeDtypeStruct((33, 128), f32)],
        in_specs=vm_specs(3), out_specs=vm_specs(3),
        scratch_shapes=[VM((8, 33, 128), f32), VM((4, 33, 128), f32), VM((4, 33, 128), f32)] + dma_sems(19),
        compiler_params=params(cid))(front, rest, gain_terms)


def update(front, rest, gain_sum, gain_states, states, tokens):
    def kernel(*refs):
        front, rest, g_sum, g_w, g_m, g_v = refs[:6]
        ins, t_in, g_out, outs, t_out = refs[6:27], refs[27:29], refs[29:32], refs[32:53], refs[53:55]
        held, made, kept = refs[55:76], refs[76:97], refs[97:99]
        lsem, osem, tsem = refs[99:]
        loads = [pltpu.make_async_copy(a, b, lsem.at[i]) for i, (a, b) in enumerate(zip(ins, held))]
        coming = [pltpu.make_async_copy(a, b, tsem.at[i]) for i, (a, b) in enumerate(zip(t_in, kept))]
        for c in loads + coming:
            c.start()
        new = adam(g_w[...], g_m[...], g_v[...], g_sum[...], gain_rate, 0.0)
        for ref, v in zip(g_out, new):
            ref[...] = v
        stores = []
        at = {False: 0, True: 0}
        for i, (n, rate) in enumerate(zip(SPANS, RATES)):
            late = i >= 4
            buf = rest if late else front
            for k in range(3):
                loads[3 * i + k].wait()
            for j in range(4):
                here = pl.ds(n * j, n)
                grad = buf[j, :, at[late]:at[late] + n].astype(f32)
                new = adam(held[3 * i][:, here], held[3 * i + 1][:, here], held[3 * i + 2][:, here], grad, rate,
                           weight_decay)
                for k in range(3):
                    made[3 * i + k][:, here] = new[k]
            at[late] += n
            for k in range(3):
                c = pltpu.make_async_copy(made[3 * i + k], outs[3 * i + k], osem.at[3 * i + k])
                c.start()
                stores.append(c)
        for i in range(2):
            coming[i].wait()
            c = pltpu.make_async_copy(kept[i], t_out[i], tsem.at[2 + i])
            c.start()
            stores.append(c)
        for c in stores:
            c.wait()

    shapes = [jax.ShapeDtypeStruct(s.shape, f32) for s in states]
    gain_shape = jax.ShapeDtypeStruct((33, 128), f32)
    return pl.pallas_call(
        kernel, out_shape=[gain_shape] * 3 + shapes + [jax.ShapeDtypeStruct(t.shape, f32) for t in tokens],
        in_specs=vm_specs(6) + any_specs(23), out_specs=vm_specs(3) + any_specs(23),
        scratch_shapes=[VM(s.shape, f32) for s in states] * 2 + [VM(t.shape, f32) for t in tokens]
        + [pltpu.SemaphoreType.DMA((21,)), pltpu.SemaphoreType.DMA((21,)), pltpu.SemaphoreType.DMA((4,))],
        compiler_params=pltpu.CompilerParams(has_side_effects=True, vmem_limit_bytes=56 * 2**20))(
            front, rest, gain_sum, *gain_states, *states, *tokens)


from jax.sharding import PartitionSpec as P

PLANE = [[x * 16 + y * 4 + k for x in range(4) for y in range(4)] for k in range(4)]


def scatter_plane(whole):
    return lax.psum_scatter(whole, "dp", axis_index_groups=PLANE, scatter_dimension=0, tiled=True)


def local(block_input, output_grad, segment_ids, norm_gains, gain_moment, gain_square, *states):
    square = lambda v: v.reshape(33, 128)
    gains = square(norm_gains)
    table = jnp.asarray(rope_constants())
    one_full, cot_full, two_full, rest_full, front_full, segments, qk_pre, v_rows, mixed, middle = attention_forward(
        block_input, output_grad, states[::3], segment_ids, gains, table, 2)
    rest_full = rest_full.reshape(D, 3072)
    rest_grad, hidden, gate_up = feed_forward(two_full, cot_full, rest_full)
    rest_mine = scatter_plane(rest_grad)
    input_grad, block_output, front_mine, gain_terms = attention_backward(
        block_input, output_grad, middle, gate_up, hidden, rest_full, one_full, front_full, qk_pre, v_rows, mixed, segments,
        gains, table, 4)
    front_back, rest_back, gain_sum = return_gradients(
        front_mine.reshape(4, 32, 640), rest_mine.reshape(4, 32, 3072), gain_terms, 5)
    news = update(front_back, rest_back, gain_sum, [gains, square(gain_moment), square(gain_square)], states,
                  (block_output, input_grad))
    return tuple(news[-2:]) + tuple(v.reshape(-1) for v in news[:3]) + tuple(news[3:-2])


def solution(mesh):
    tokens, weight = P(("dp", "tensor"), None), P("dp", "tensor")
    in_specs = (tokens, tokens, P("dp", None), P(), P(), P()) + (weight,) * 21
    out_specs = (tokens, tokens, P(), P(), P()) + (weight,) * 21
    return jax.shard_map(local, mesh=mesh, in_specs=in_specs, out_specs=out_specs, check_vma=False)
```

```python
import jax
import jax.numpy as jnp
import numpy as np
from jax import lax
from jax.experimental import pallas as pl
from jax.experimental.pallas import tpu as pltpu

MESH = pl.DeviceIdType.MESH
VM = pltpu.VMEM
bf16 = jnp.bfloat16
f32 = jnp.float32


def m4(v):
    return lax.rem(v + 4, 4)


class Place:
    def __init__(self):
        dp = lax.axis_index("dp")
        self.l = lax.axis_index("tensor")
        self.x = lax.div(dp, 16)
        self.y = lax.rem(lax.div(dp, 4), 4)
        self.h = lax.rem(lax.div(dp, 2), 2)
        self.c = lax.rem(dp, 2)
        self.z = self.h * 2 + self.l

    def at(self, x=None, y=None, z=None, c=None):
        x = self.x if x is None else x
        y = self.y if y is None else y
        z = self.z if z is None else z
        c = self.c if c is None else c
        return (x * 16 + y * 4 + lax.div(z, 2) * 2 + c, lax.rem(z, 2))

    def pos(self, axis):
        return {"x": self.x, "y": self.y, "z": self.z}[axis]

    def step(self, axis, d):
        return self.at(**{axis: m4(self.pos(axis) + d)})

    def sibling(self):
        return self.at(c=1 - self.c)


class Wire:
    def __init__(self, send, recv, first=0):
        self.send, self.recv, self.n = send, recv, first
        self.pending = []

    def go(self, src, dst, dev):
        i = self.n
        self.n += 1
        c = pltpu.make_async_remote_copy(
            src_ref=src, dst_ref=dst, send_sem=self.send.at[i], recv_sem=self.recv.at[i],
            device_id=dev, device_id_type=MESH)
        c.start()
        self.pending.append(c)
        return c

    def finish(self):
        for c in self.pending:
            c.wait_send()
        self.pending = []


def meet(devs):
    b = pltpu.get_barrier_semaphore()
    for d in devs:
        pl.semaphore_signal(b, inc=1, device_id=d, device_id_type=MESH)
    pl.semaphore_wait(b, len(devs))


def ring_gather(w, me, axis, whole, lo, hi, first=None, arrived=None):
    p = me.pos(axis)
    up, down = me.step(axis, 1), me.step(axis, -1)
    own = whole(p) if first is None else first
    a = w.go(own, whole(p), up)
    b = w.go(own, whole(p), down)
    yield
    a.wait_recv()
    fa = w.go(lo(m4(p - 1)), lo(m4(p - 1)), up)
    if arrived:
        arrived(whole(m4(p - 1)))
    b.wait_recv()
    fb = w.go(hi(m4(p + 1)), hi(m4(p + 1)), down)
    if arrived:
        arrived(whole(m4(p + 1)))
    yield
    fa.wait_recv()
    if arrived:
        arrived(lo(m4(p - 2)))
    fb.wait_recv()
    if arrived:
        arrived(hi(m4(p - 2)))


def ring_scatter(w, me, axis, lo, hi, tlo, thi, rup, rdown, add):
    p = me.pos(axis)
    up, down = me.step(axis, 1), me.step(axis, -1)
    far, nu, nd = m4(p + 2), m4(p + 1), m4(p - 1)
    ta = w.go(lo(far), tlo, up)
    tb = w.go(hi(far), thi, down)
    da = w.go(hi(nu), rup[1], up)
    db = w.go(lo(nd), rdown[0], down)
    yield
    ta.wait_recv()
    add(tlo, lo(nu))
    sa = w.go(tlo, rup[0], up)
    tb.wait_recv()
    add(thi, hi(nd))
    sb = w.go(thi, rdown[1], down)
    yield
    da.wait_recv()
    db.wait_recv()
    sa.wait_recv()
    sb.wait_recv()


def loop_add(dst, a, b=None, rows=16):
    n = dst.shape[0]

    def body(i, _):
        def inner(j, _):
            s = pl.ds(pl.multiple_of(j * rows, rows), rows)
            v = dst[i, s].astype(f32) + a[i, s].astype(f32)
            if b is not None:
                v = v + b[i, s].astype(f32)
            dst[i, s] = v.astype(dst.dtype)
            return 0
        return lax.fori_loop(0, dst.shape[1] // rows, inner, 0)
    lax.fori_loop(0, n, body, 0)


def run(gens):
    gens = list(gens)
    while gens:
        for g in list(gens):
            try:
                next(g)
            except StopIteration:
                gens.remove(g)


def params(cid, mb=56):
    return pltpu.CompilerParams(collective_id=cid, has_side_effects=True, vmem_limit_bytes=mb * 2**20)


def ag_xy_gens(w, me, src, out):
    H = 64
    x, y = me.x, me.y

    def half_a():
        yield from ring_gather(w, me, "x", lambda i: out.at[i, y, pl.ds(0, 64)], lambda i: out.at[i, y, pl.ds(0, 32)],
                               lambda i: out.at[i, y, pl.ds(32, 32)], first=src.at[pl.ds(0, 64)])
        yield
        yield from ring_gather(w, me, "y", lambda i: out.at[:, i, pl.ds(0, 64)], lambda i: out.at[:, i, pl.ds(0, 32)],
                               lambda i: out.at[:, i, pl.ds(32, 32)])

    def half_b():
        yield from ring_gather(w, me, "y", lambda i: out.at[x, i, pl.ds(64, 64)], lambda i: out.at[x, i, pl.ds(64, 32)],
                               lambda i: out.at[x, i, pl.ds(96, 32)], first=src.at[pl.ds(64, 64)])
        yield
        yield from ring_gather(w, me, "x", lambda i: out.at[i, :, pl.ds(64, 64)], lambda i: out.at[i, :, pl.ds(64, 32)],
                               lambda i: out.at[i, :, pl.ds(96, 32)])
    return [half_a(), half_b()]


def ag_xy(shard, cid, space=pl.ANY):
    C = shard.shape[1]

    def kernel(src, out, send, recv, lsem):
        me = Place()
        meet([me.step("x", 1), me.step("x", -1), me.step("y", 1), me.step("y", -1)])
        w = Wire(send, recv)
        lc = pltpu.make_async_copy(src, out.at[me.x, me.y], lsem)
        lc.start()
        lc.wait()
        run(ag_xy_gens(w, me, src, out))
        w.finish()

    return pl.pallas_call(
        kernel, out_shape=jax.ShapeDtypeStruct((4, 4, 128, C), shard.dtype),
        in_specs=[pl.BlockSpec(memory_space=space)], out_specs=pl.BlockSpec(memory_space=space),
        scratch_shapes=[pltpu.SemaphoreType.DMA((16,)), pltpu.SemaphoreType.DMA((16,)), pltpu.SemaphoreType.DMA],
        compiler_params=params(cid))(shard)


def rs_xy_scratch(C):
    return [VM((2, 2, 4, 32, C), bf16), VM((2, 2, 2, 4, 32, C), bf16),
            VM((2, 2, 32, C), bf16), VM((2, 2, 2, 32, C), bf16), VM((2, 4, 64, C), bf16)]


def rs_xy_gens(w, me, g, out, t1, r1, t2, r2, mid):
    x, y = me.x, me.y

    def half(k, first, second):
        base = k * 64
        if first == "y":
            pick = lambda i, o: g.at[:, i, pl.ds(base + o, 32)]
        else:
            pick = lambda i, o: g.at[i, :, pl.ds(base + o, 32)]
        yield from ring_scatter(w, me, first, lambda i: pick(i, 0), lambda i: pick(i, 32), t1.at[k, 0], t1.at[k, 1],
                                (r1.at[k, 0, 0], r1.at[k, 0, 1]), (r1.at[k, 1, 0], r1.at[k, 1, 1]), loop_add)
        p = me.pos(first)
        m = mid.at[k]
        for hh in range(2):
            own = pick(p, 32 * hh)

            def body(i, _):
                def inner(j, _):
                    s = pl.ds(pl.multiple_of(j * 16, 16), 16)
                    d = pl.ds(pl.multiple_of(j * 16 + 32 * hh, 16), 16)
                    v = own[i, s].astype(f32) + r1[k, 0, hh, i, s].astype(f32) + r1[k, 1, hh, i, s].astype(f32)
                    m[i, d] = v.astype(bf16)
                    return 0
                return lax.fori_loop(0, 2, inner, 0)
            lax.fori_loop(0, 4, body, 0)
        yield
        q = me.pos(second)
        add1 = lambda dst, a: loop_add(dst, a)
        pick2 = lambda i, o: mid.at[k, i, pl.ds(o, 32)]

        def add2(dst, a):
            def inner(j, _):
                s = pl.ds(pl.multiple_of(j * 16, 16), 16)
                dst[s] = (dst[s].astype(f32) + a[s].astype(f32)).astype(bf16)
                return 0
            lax.fori_loop(0, 2, inner, 0)
        yield from ring_scatter(w, me, second, lambda i: pick2(i, 0), lambda i: pick2(i, 32), t2.at[k, 0], t2.at[k, 1],
                                (r2.at[k, 0, 0], r2.at[k, 0, 1]), (r2.at[k, 1, 0], r2.at[k, 1, 1]), add2)
        for hh in range(2):
            def inner(j, _):
                s = pl.ds(pl.multiple_of(j * 16, 16), 16)
                d = pl.ds(pl.multiple_of(j * 16 + 32 * hh, 16), 16)
                dd = pl.ds(pl.multiple_of(j * 16 + 32 * hh + base, 16), 16)
                v = m[q, d].astype(f32) + r2[k, 0, hh, s].astype(f32) + r2[k, 1, hh, s].astype(f32)
                out[dd] = v.astype(out.dtype)
                return 0
            lax.fori_loop(0, 2, inner, 0)
    return [half(0, "y", "x"), half(1, "x", "y")]


def rs_xy(g, cid, out_dtype=f32):
    C = g.shape[-1]

    def kernel(gin, out, send, recv, *scr):
        me = Place()
        meet([me.step("x", 1), me.step("x", -1), me.step("y", 1), me.step("y", -1)])
        w = Wire(send, recv)
        run(rs_xy_gens(w, me, gin, out, *scr))
        w.finish()

    return pl.pallas_call(
        kernel, out_shape=jax.ShapeDtypeStruct((128, C), out_dtype),
        in_specs=[pl.BlockSpec(memory_space=VM)], out_specs=pl.BlockSpec(memory_space=VM),
        scratch_shapes=[pltpu.SemaphoreType.DMA((24,)), pltpu.SemaphoreType.DMA((24,))] + rs_xy_scratch(C),
        compiler_params=params(cid, 60))(g)


def ag_z_gen(w, me, src, out, r0=0, n=128):
    sib = me.sibling()
    blk = lambda i, cc: out.at[lax.div(i, 2), cc, lax.rem(i, 2)]
    cs = []

    def to_sib(ref):
        cs.append(w.go(ref, ref, sib))
    whole = lambda i: blk(i, me.c).at[pl.ds(r0, n)]
    lo = lambda i: blk(i, me.c).at[pl.ds(r0, n // 2)]
    hi = lambda i: blk(i, me.c).at[pl.ds(r0 + n // 2, n // 2)]
    own = w.go(src, whole(me.z), sib)
    yield from ring_gather(w, me, "z", whole, lo, hi, first=src, arrived=to_sib)
    own.wait_recv()
    for c in cs:
        c.wait_recv()


def ag_z(shard, cid, space=VM):
    C = shard.shape[1]

    def kernel(src, out, send, recv, lsem):
        me = Place()
        meet([me.step("z", 1), me.step("z", -1), me.sibling()])
        w = Wire(send, recv)
        lc = pltpu.make_async_copy(src, out.at[me.h, me.c, me.l], lsem)
        lc.start()
        lc.wait()
        run([ag_z_gen(w, me, src, out)])
        w.finish()

    return pl.pallas_call(
        kernel, out_shape=jax.ShapeDtypeStruct((2, 2, 2, 128, C), shard.dtype),
        in_specs=[pl.BlockSpec(memory_space=space)], out_specs=pl.BlockSpec(memory_space=space),
        scratch_shapes=[pltpu.SemaphoreType.DMA((16,)), pltpu.SemaphoreType.DMA((16,)), pltpu.SemaphoreType.DMA],
        compiler_params=params(cid))(shard)


def rs_z_scratch(C):
    return [VM((4, 128, C), bf16), VM((2, 64, C), bf16), VM((2, 2, 64, C), bf16)]


def rs_z_gen(w, me, g, out, sibs, t, r):
    sib = me.sibling()
    oc = 1 - me.c
    order = [2, 1, 3, 0]
    blk = lambda i, cc: g.at[lax.div(i, 2), cc, lax.rem(i, 2)]
    z = me.z
    sc = {}
    for o in order:
        i = m4(z + o)
        sc[o] = w.go(blk(i, oc), sibs.at[i], sib)
    yield

    def fold(o, s0, n):
        i = m4(z + o)
        b = blk(i, me.c)

        def inner(j, _):
            s = pl.ds(pl.multiple_of(j * 16 + s0, 16), 16)
            sibs[i, s] = (sibs[i, s].astype(f32) + b[s].astype(f32)).astype(bf16)
            return 0
        lax.fori_loop(0, n // 16, inner, 0)
    up, down = me.step("z", 1), me.step("z", -1)
    half = lambda o, k: sibs.at[m4(z + o), pl.ds(64 * k, 64)]
    sc[2].wait_recv()
    fold(2, 0, 64)
    ta = w.go(half(2, 0), t.at[0], up)
    fold(2, 64, 64)
    tb = w.go(half(2, 1), t.at[1], down)
    sc[1].wait_recv()
    fold(1, 64, 64)
    da = w.go(half(1, 1), r.at[0, 1], up)
    sc[3].wait_recv()
    fold(3, 0, 64)
    db = w.go(half(3, 0), r.at[1, 0], down)
    fold(1, 0, 64)
    fold(3, 64, 64)
    yield

    def add(dst, a):
        def inner(j, _):
            s = pl.ds(pl.multiple_of(j * 16, 16), 16)
            dst[s] = (dst[s].astype(f32) + a[s].astype(f32)).astype(bf16)
            return 0
        lax.fori_loop(0, 4, inner, 0)
    ta.wait_recv()
    add(t.at[0], half(1, 0))
    sa = w.go(t.at[0], r.at[0, 0], up)
    tb.wait_recv()
    add(t.at[1], half(3, 1))
    sb = w.go(t.at[1], r.at[1, 1], down)
    sc[0].wait_recv()
    own = blk(z, me.c)
    yield

    def last(hh):
        def inner(j, _):
            s = pl.ds(pl.multiple_of(j * 16, 16), 16)
            d = pl.ds(pl.multiple_of(j * 16 + 64 * hh, 16), 16)
            v = own[d].astype(f32) + sibs[z, d].astype(f32) + r[0, hh, s].astype(f32) + r[1, hh, s].astype(f32)
            out(d, v)
            return 0
        lax.fori_loop(0, 4, inner, 0)
    da.wait_recv()
    sa.wait_recv()
    db.wait_recv()
    sb.wait_recv()
    last(0)
    last(1)


def rs_z(g, cid, out_dtype=f32):
    C = g.shape[-1]

    def kernel(gin, out, send, recv, *scr):
        me = Place()
        meet([me.step("z", 1), me.step("z", -1), me.sibling()])
        w = Wire(send, recv)

        def put(s, v):
            out[s] = v.astype(out.dtype)
        run([rs_z_gen(w, me, gin, put, *scr)])
        w.finish()

    return pl.pallas_call(
        kernel, out_shape=jax.ShapeDtypeStruct((128, C), out_dtype),
        in_specs=[pl.BlockSpec(memory_space=VM)], out_specs=pl.BlockSpec(memory_space=VM),
        scratch_shapes=[pltpu.SemaphoreType.DMA((16,)), pltpu.SemaphoreType.DMA((16,))] + rs_z_scratch(C),
        compiler_params=params(cid))(g)


def swap_devs(me):
    out = []
    for dh, dc in ((0, 1), (1, 0), (1, 1)):
        h = lax.rem(me.h + dh, 2)
        c = lax.rem(me.c + dc, 2)
        out.append((h * 2 + c, me.at(z=h * 2 + me.l, c=c)))
    return out


def swap_hc(parts, cid):
    n = len(parts)

    def kernel(*refs):
        ins, outs = refs[:n], refs[n:2 * n]
        send, recv, lsem = refs[2 * n:]
        me = Place()
        peers = swap_devs(me)
        meet([d for _, d in peers])
        w = Wire(send, recv)
        mine = me.h * 2 + me.c
        arrivals = []
        for j, d in reversed(peers):
            for a, b in zip(ins, outs):
                arrivals.append(w.go(a.at[j], b.at[mine], d))
        ls = []
        for k, (a, b) in enumerate(zip(ins, outs)):
            lc = pltpu.make_async_copy(a.at[mine], b.at[mine], lsem.at[k])
            lc.start()
            ls.append(lc)
        for lc in ls:
            lc.wait()
        for a in arrivals:
            a.wait_recv()
        w.finish()

    return pl.pallas_call(
        kernel, out_shape=[jax.ShapeDtypeStruct(p.shape, p.dtype) for p in parts],
        in_specs=[pl.BlockSpec(memory_space=VM)] * n, out_specs=[pl.BlockSpec(memory_space=VM)] * n,
        scratch_shapes=[pltpu.SemaphoreType.DMA((3 * n,)), pltpu.SemaphoreType.DMA((3 * n,)),
                        pltpu.SemaphoreType.DMA((n,))],
        compiler_params=params(cid))(*parts)


def sum_all(v, cid):
    R, C = v.shape

    def kernel(src, out, z_in, x_in, y_in, acc, send, recv):
        me = Place()
        zs = []
        for dz in range(4):
            for dc in range(2):
                if dz or dc:
                    z, c = m4(me.z + dz), lax.rem(me.c + dc, 2)
                    zs.append(me.at(z=z, c=c))
        xs = [me.step("x", d) for d in (1, 2, 3)]
        ys = [me.step("y", d) for d in (1, 2, 3)]
        meet(zs + xs + ys)
        w = Wire(send, recv)
        acc[...] = src[...]
        for buf, slot, devs, n in ((z_in, me.z * 2 + me.c, zs, 8), (x_in, me.x, xs, 4), (y_in, me.y, ys, 4)):
            buf[slot] = acc[...]
            cs = [w.go(buf.at[slot], buf.at[slot], d) for d in devs]
            for c in cs:
                c.wait_recv()
            total = buf[0]
            for k in range(1, n):
                total = total + buf[k]
            w.finish()
            acc[...] = total
        out[...] = acc[...]

    return pl.pallas_call(
        kernel, out_shape=jax.ShapeDtypeStruct((R, C), f32),
        in_specs=[pl.BlockSpec(memory_space=VM)], out_specs=pl.BlockSpec(memory_space=VM),
        scratch_shapes=[VM((8, R, C), f32), VM((4, R, C), f32), VM((4, R, C), f32), VM((R, C), f32),
                        pltpu.SemaphoreType.DMA((13,)), pltpu.SemaphoreType.DMA((13,))],
        compiler_params=params(cid))(v)


def rs_z_packs(w, me, g, put, sibs, t, r):
    sib, oc, z = me.sibling(), 1 - me.c, me.z
    blk = lambda i, cc: g.at[lax.div(i, 2), cc, lax.rem(i, 2)]
    far = m4(z + 2)
    flip = lambda i: i + 1 - 2 * lax.rem(i, 2)
    beside, partner = flip(far), flip(z)
    up, down = me.step("z", 1), me.step("z", -1)
    half = lambda i, k: sibs.at[i, pl.ds(64 * k, 64)]

    def fold(i, s0, n):
        b = blk(i, me.c)

        def inner(j, _):
            s = pl.ds(pl.multiple_of(j * 16 + s0, 16), 16)
            sibs[i, s] = (sibs[i, s].astype(f32) + b[s].astype(f32)).astype(bf16)
            return 0
        lax.fori_loop(0, n // 16, inner, 0)

    def add(dst, a):
        def inner(j, _):
            s = pl.ds(pl.multiple_of(j * 16, 16), 16)
            dst[s] = (dst[s].astype(f32) + a[s].astype(f32)).astype(bf16)
            return 0
        lax.fori_loop(0, 4, inner, 0)
    s_far = w.go(blk(far, oc), sibs.at[far], sib)
    s_beside = w.go(blk(beside, oc), sibs.at[beside], sib)
    yield
    s_far.wait_recv()
    fold(far, 0, 64)
    ta = w.go(half(far, 0), t.at[0], up)
    fold(far, 64, 64)
    tb = w.go(half(far, 1), t.at[1], down)
    s_beside.wait_recv()
    fold(beside, 0, 128)
    yield
    s_partner = w.go(blk(partner, oc), sibs.at[partner], sib)
    s_own = w.go(blk(z, oc), sibs.at[z], sib)
    yield
    s_partner.wait_recv()
    fold(partner, 0, 128)
    nu, nd = m4(z + 1), m4(z - 1)
    da = w.go(half(nu, 1), r.at[0, 1], up)
    db = w.go(half(nd, 0), r.at[1, 0], down)
    yield
    ta.wait_recv()
    add(t.at[0], half(nu, 0))
    sa = w.go(t.at[0], r.at[0, 0], up)
    tb.wait_recv()
    add(t.at[1], half(nd, 1))
    sb = w.go(t.at[1], r.at[1, 1], down)
    s_own.wait_recv()
    own = blk(z, me.c)
    yield

    def last(hh):
        def inner(j, _):
            s = pl.ds(pl.multiple_of(j * 16, 16), 16)
            d = pl.ds(pl.multiple_of(j * 16 + 64 * hh, 16), 16)
            put(d, own[d].astype(f32) + sibs[z, d].astype(f32) + r[0, hh, s].astype(f32) + r[1, hh, s].astype(f32))
            return 0
        lax.fori_loop(0, 4, inner, 0)
    da.wait_recv()
    sa.wait_recv()
    db.wait_recv()
    sb.wait_recv()
    last(0)
    last(1)


D = 2048
HD = 64
STEP = 10
SEQ = 256
PACKS = 4
ROWS = 1024
epsilon = 1e-06
rope_base = 1000000.0
beta_one = 0.9
beta_two = 0.999
adam_epsilon = 1e-08
weight_decay = 0.1
gain_rate = 0.3
masked_score = -1000000000.0
score_scale = HD ** (-0.5)
exact = lax.Precision.HIGHEST


def dot(a, b, ca=1, cb=0, precision=None):
    return lax.dot_general(a, b, (((ca,), (cb,)), ((), ())), precision=precision, preferred_element_type=f32)


def chunks(n, body, rows=16):
    def one(j, _):
        body(pl.ds(pl.multiple_of(j * rows, rows), rows))
        return 0
    lax.fori_loop(0, n // rows, one, 0)


def dma_sems(n):
    return [pltpu.SemaphoreType.DMA((n,)), pltpu.SemaphoreType.DMA((n,))]


def vm_specs(n):
    return [pl.BlockSpec(memory_space=VM)] * n


def any_specs(n):
    return [pl.BlockSpec(memory_space=pl.ANY)] * n


class Columns:
    def __init__(self, ref, n):
        self.ref, self.n = ref, n

    def __getitem__(self, j):
        return self.ref[:, pl.ds(pl.multiple_of(j * self.n, self.n), self.n)]


def gain_rows(gains):
    one = jnp.concatenate([gains[i:i + 1, :] for i in range(16)], axis=1)
    two = jnp.concatenate([gains[16 + i:17 + i, :] for i in range(16)], axis=1)
    small = jnp.broadcast_to(gains[32:33, :], (128, 128)).T
    return one, two, small[0:64, 0:1], small[64:128, 0:1]


def rope_constants():
    frequency = np.float32(rope_base) ** (np.float32(-2.0) * np.arange(HD // 2, dtype=np.float32) / np.float32(HD))
    angles = (np.arange(SEQ, dtype=np.float32)[None, :] * frequency[:, None].astype(np.float32)).astype(np.float64)
    return np.concatenate([np.cos(angles), np.sin(angles)], axis=0).astype(np.float32)


def pack_tables(segs, p, table):
    row = segs[p].astype(f32)[0:1, :]
    column = jnp.broadcast_to(row, (128, SEQ)).T[:, 0:1]
    key_at = lax.broadcasted_iota(jnp.int32, (SEQ, SEQ), 0)
    query_at = lax.broadcasted_iota(jnp.int32, (SEQ, SEQ), 1)
    allowed = (column == row) & (key_at <= query_at)
    start = jnp.sum(jnp.where(column < row, 1.0, 0.0), axis=0, keepdims=True)
    where = query_at.astype(f32) - start
    hot = jnp.where(key_at.astype(f32) == where, 1.0, 0.0)
    both = dot(table[...], hot, precision=exact)
    return allowed, both[0:32], both[32:64]


def head_norm(z, gain):
    inverse = lax.rsqrt(jnp.mean(z * z, axis=0, keepdims=True) + epsilon)
    return z * inverse * gain, inverse


def head_norm_back(z, inverse, gain, up):
    scaled = up * gain
    inner = jnp.mean(z * scaled, axis=0, keepdims=True)
    return inverse * (scaled - z * inverse * inverse * inner), up * z * inverse


def turn(u, cosine, sine):
    a, b = u[0:32], u[32:64]
    return jnp.concatenate([a * cosine - b * sine, b * cosine + a * sine], axis=0)


def turn_back(u, cosine, sine):
    a, b = u[0:32], u[32:64]
    return jnp.concatenate([a * cosine + b * sine, b * cosine - a * sine], axis=0)


def pack_probs(key_rows, query_rot, allowed):
    scores = jnp.where(allowed, dot(key_rows, query_rot) * score_scale, masked_score)
    exps = jnp.exp(scores - jnp.max(scores, axis=0, keepdims=True))
    return exps / jnp.sum(exps, axis=0, keepdims=True)


def pack_of(ref, p):
    v = ref[lax.div(p, 2), lax.rem(p, 2)]
    return v.reshape(SEQ, v.shape[-1])


def pack_turn(me, i):
    h = me.h if i >= 2 else 1 - me.h
    c = me.c if i % 2 else 1 - me.c
    return h * 2 + c


def attention_forward(x, weights, seg, gains, table, cid):
    def kernel(x, q_, k_, v_, o_, g_, u_, d_, seg, gains, table,
               a_full, n_full, rest_full, front_full, segs, qk_pre, v_rows, mixed, middle,
               fbuf, rbuf, sbuf, kv, fshard, rshard, rest, shard, shard_two, a_buf, part, sibs, t, r,
               send, recv, lsem, ksem):
        me = Place()
        gain_one, gain_two, gain_query, gain_key = gain_rows(gains)
        peers = swap_devs(me)
        mine = me.h * 2 + me.c
        q, o = Columns(q_, 256), Columns(o_, 256)
        g, u, d = Columns(g_, 1024), Columns(u_, 1024), Columns(d_, 1024)
        for j in range(4):
            kv[j] = jnp.concatenate([k_[:, 64 * j:64 * j + 64], v_[:, 64 * j:64 * j + 64]], axis=1)
        sbuf[...] = jnp.broadcast_to(seg[...], (8, SEQ))
        here = pl.ds(pl.multiple_of(mine * 32, 32), 32)

        def round_front(j, dst):
            dst[:, 0:256] = q[j].astype(bf16)
            dst[:, 256:384] = kv[j].astype(bf16)
            dst[:, 384:640] = o[j].astype(bf16)

        def round_rest(j, dst):
            for i, w in enumerate((g, u, d)):
                dst[:, 1024 * i:1024 * i + 1024] = w[j].astype(bf16)
        meet([me.step("x", 1), me.step("x", -1), me.step("y", 1), me.step("y", -1),
              me.step("z", 1), me.step("z", -1)] + [dev for _, dev in peers])
        w = Wire(send, recv)
        first, second = [], []
        for j, dev in reversed(peers):
            round_front(j, fbuf.at[j])
            first.append(w.go(fbuf.at[j], fshard.at[here], dev))
            second.append(w.go(sbuf, segs.at[mine], dev))
        for j, dev in reversed(peers):
            round_rest(j, rbuf.at[j])
            second.append(w.go(rbuf.at[j], rshard.at[here], dev))
        round_front(mine, fshard.at[here])
        round_rest(mine, rshard.at[here])
        segs[mine] = sbuf[...]

        def norm_one(s):
            v = x[s].astype(f32)
            inverse = lax.rsqrt(jnp.mean(v * v, axis=-1, keepdims=True) + epsilon)
            shard[s] = (v * inverse * gain_one).astype(bf16)
        chunks(128, norm_one)
        for c in first:
            c.wait_recv()

        def both(gens):
            for g in gens:
                next(g)
        front_gens = ag_xy_gens(w, me, fshard, front_full)
        both(front_gens)
        gz = ag_z_gen(w, me, shard, a_buf)
        next(gz)
        locals_ = [pltpu.make_async_copy(fshard, front_full.at[me.x, me.y], lsem.at[0]),
                   pltpu.make_async_copy(shard, a_buf.at[me.h, me.c, me.l], lsem.at[1])]
        for c in locals_:
            c.start()
        both(front_gens)
        for c in locals_:
            c.wait()
        both(front_gens)
        both(front_gens)
        for c in second:
            c.wait_recv()
        rest_gens = ag_xy_gens(w, me, rshard, rest)
        both(rest_gens)
        own = pltpu.make_async_copy(rshard, rest.at[me.x, me.y], lsem.at[3])
        own.start()
        both(front_gens)
        both(rest_gens)
        own.wait()
        run(front_gens)
        both(rest_gens)
        both(rest_gens)
        next(gz)
        run([gz])
        keep = pltpu.make_async_copy(a_buf, a_full, lsem.at[4])
        keep.start()

        def one_pack(p):
            allowed, cosine, sine = pack_tables(segs, p, table)
            qkv = dot(pack_of(a_buf, p), front_full[:, :, :, 0:384].reshape(D, 384)).T
            qk_pre[p] = qkv[0:320]
            value = qkv[320:384].astype(bf16)
            v_rows[p] = value
            kn, _i = head_norm(qkv[256:320], gain_key)
            key_rows = turn(kn, cosine, sine).T.astype(bf16)
            heads = []
            for j in range(4):
                qn, _i = head_norm(qkv[64 * j:64 * j + 64], gain_query)
                probs = pack_probs(key_rows, turn(qn, cosine, sine).astype(bf16), allowed)
                heads.append(dot(value, probs.astype(bf16)))
            o = jnp.concatenate(heads, axis=0).T.astype(bf16)
            mixed[p] = o
            out = dot(o, front_full[:, :, :, 384:640].reshape(D, 256), 1, 1).astype(bf16)
            part[lax.div(p, 2), lax.rem(p, 2)] = out.reshape(2, 128, D)

        def residual(s, v):
            middle[s] = x[s].astype(f32) + v
        sum_gen = rs_z_packs(w, me, part, residual, sibs, t, r)
        for i in range(4):
            one_pack(pack_turn(me, i))
            next(sum_gen)
        both(rest_gens)
        run([sum_gen])

        def norm_two(s):
            v = middle[s]
            inverse = lax.rsqrt(jnp.mean(v * v, axis=-1, keepdims=True) + epsilon)
            shard_two[s] = (v * inverse * gain_two).astype(bf16)
        chunks(128, norm_two)
        n_gen = ag_z_gen(w, me, shard_two, n_full)
        next(n_gen)
        own = pltpu.make_async_copy(shard_two, n_full.at[me.h, me.c, me.l], lsem.at[3])
        own.start()
        stores = []

        def store(k, a, b, at):
            here = pl.ds(at, 64)
            c = pltpu.make_async_copy(rest.at[a, b, here], rest_full.at[a, b, here], ksem.at[k])
            c.start()
            stores.append(c)
        every = slice(None)
        for k in (0, 1, 3):
            store(k, every, m4(me.y + k), 0)
            store(4 + k, m4(me.x + k), every, 64)
        next(n_gen)
        run([n_gen])
        run(rest_gens)
        store(2, every, m4(me.y + 2), 0)
        store(6, m4(me.x + 2), every, 64)
        own.wait()
        keep.wait()
        for c in stores:
            c.wait()
        w.finish()

    full = jax.ShapeDtypeStruct((2, 2, 2, 128, D), bf16)
    return pl.pallas_call(
        kernel,
        out_shape=[full, full, jax.ShapeDtypeStruct((4, 4, 128, 3072), bf16),
                   jax.ShapeDtypeStruct((4, 4, 128, 640), bf16), jax.ShapeDtypeStruct((4, 8, SEQ), jnp.int32),
                   jax.ShapeDtypeStruct((PACKS, 320, SEQ), f32), jax.ShapeDtypeStruct((PACKS, HD, SEQ), bf16),
                   jax.ShapeDtypeStruct((PACKS, SEQ, 256), bf16), jax.ShapeDtypeStruct((128, D), f32)],
        in_specs=vm_specs(11), out_specs=any_specs(3) + vm_specs(6),
        scratch_shapes=[VM((4, 32, 640), bf16), VM((4, 32, 3072), bf16), VM((8, SEQ), jnp.int32), VM((4, 32, 128), f32),
                        VM((128, 640), bf16), VM((128, 3072), bf16), VM((4, 4, 128, 3072), bf16)]
        + [VM((128, D), bf16)] * 2 + [VM((2, 2, 2, 128, D), bf16)] * 2 + rs_z_scratch(D)
        + dma_sems(96) + [pltpu.SemaphoreType.DMA((5,)), pltpu.SemaphoreType.DMA((8,))],
        compiler_params=params(cid, 58))(x, *weights, seg, gains, table)


def sigmoid(v):
    return 1.0 / (1.0 + jnp.exp(-v))


def feed_forward(n_full, cot_full, weights, cid):
    def kernel(n_hbm, cot_hbm, w_hbm, grad_hbm, hidden_hbm, rest_part, db_sum,
               n, cot, w, hidden, gate_up, part, grad, sibs_a, t_a, r_a, send, recv, lsem, wsem, gsem):
        me = Place()
        loads = [pltpu.make_async_copy(n_hbm, n, lsem.at[0]), pltpu.make_async_copy(cot_hbm, cot, lsem.at[1])]
        loads[0].start()

        def piece(i, k):
            here = pl.ds(pl.multiple_of(i * 256 + 1024 * k, 256), 256)
            return pltpu.make_async_copy(w_hbm.at[:, here], w.at[:, here], wsem.at[i, k])
        for i in range(4):
            for k in range(3):
                piece(i, k).start()
            if i == 0:
                loads[1].start()
        meet([me.step("z", 1), me.step("z", -1), me.sibling()])
        for c in loads:
            c.wait()

        def hidden_block(i, _):
            at = pl.multiple_of(i * 256, 256)
            for k in range(3):
                piece(i, k).wait()
            rows = n[...].reshape(ROWS, D)
            g = dot(rows, w[:, pl.ds(at, 256)])
            u = dot(rows, w[:, pl.ds(at + 1024, 256)])
            dh = dot(cot[...].reshape(ROWS, D), w[:, pl.ds(at + 2048, 256)])
            s = sigmoid(g)
            silu = g * s
            hidden[:, pl.ds(at, 256)] = (silu * u).astype(bf16)
            gate_up[:, pl.ds(at, 256)] = (dh * u * (s + silu * (1.0 - s))).astype(bf16)
            gate_up[:, pl.ds(at + 1024, 256)] = (dh * silu).astype(bf16)
            return 0
        lax.fori_loop(0, 4, hidden_block, 0)
        keep = pltpu.make_async_copy(hidden, hidden_hbm, lsem.at[2])
        keep.start()

        def back_block(i, _):
            at = pl.multiple_of(i * 256, 256)
            v = dot(gate_up[...], w[pl.ds(at, 256), 0:2048], 1, 1).astype(bf16)
            part[:, :, :, :, pl.ds(at, 256)] = v.reshape(2, 2, 2, 128, 256)
            return 0
        wire = Wire(send, recv)

        def put_a(s, v):
            db_sum[s] = v
        stores = []

        def grad_block(i):
            at = 512 * i
            slot = i % 2
            if i >= 2:
                stores[i - 2].wait()
            grad[slot, :, 0:2048] = dot(n[:, :, :, :, at:at + 512].reshape(ROWS, 512), gate_up[...], 0, 0).astype(bf16)
            grad[slot, :, 2048:3072] = dot(cot[:, :, :, :, at:at + 512].reshape(ROWS, 512), hidden[...], 0, 0).astype(bf16)
            c = pltpu.make_async_copy(grad.at[slot], grad_hbm.at[pl.ds(at, 512)], gsem.at[i])
            c.start()
            stores.append(c)
        lax.fori_loop(0, 4, back_block, 0)
        gen_a = rs_z_gen(wire, me, part.at[:, :, :, :, pl.ds(0, 1024)], put_a, sibs_a, t_a, r_a)
        next(gen_a)
        lax.fori_loop(4, 8, back_block, 0)
        keep_part = pltpu.make_async_copy(part.at[:, :, :, :, pl.ds(1024, 1024)], rest_part, lsem.at[3])
        keep_part.start()
        next(gen_a)
        grad_block(0)
        grad_block(1)
        next(gen_a)
        grad_block(2)
        grad_block(3)
        run([gen_a])
        for c in stores[2:] + [keep, keep_part]:
            c.wait()
        wire.finish()

    full = (2, 2, 2, 128, D)
    return pl.pallas_call(
        kernel,
        out_shape=[jax.ShapeDtypeStruct((D, 3072), bf16), jax.ShapeDtypeStruct((ROWS, 1024), bf16),
                   jax.ShapeDtypeStruct((2, 2, 2, 128, 1024), bf16), jax.ShapeDtypeStruct((128, 1024), f32)],
        in_specs=any_specs(3), out_specs=any_specs(3) + vm_specs(1),
        scratch_shapes=[VM(full, bf16), VM(full, bf16), VM((D, 3072), bf16), VM((ROWS, 1024), bf16),
                        VM((ROWS, 2048), bf16), VM(full, bf16), VM((2, 512, 3072), bf16)]
        + rs_z_scratch(1024) + dma_sems(16) + [pltpu.SemaphoreType.DMA((4,)), pltpu.SemaphoreType.DMA((4, 3)),
                                                   pltpu.SemaphoreType.DMA((4,))],
        compiler_params=params(cid, 60))(n_full, cot_full, weights)


def attention_backward(x, cot, middle, db_front, rest_part, hidden, weights, a_full, front_full, qk_pre, v_rows, mixed, segs,
                       gains, table, cid):
    def kernel(x, cot, middle, db_front, part_hbm, hidden_hbm, w_hbm, a_hbm, front_full, qk_pre, v_rows, mixed, segs,
               gains, table, input_grad, block_output, front_mine, gain_terms,
               shard, hidden, wd, out_part, dm_full, mid_grad, dqkv, part, front_grad, q_acc, k_acc, one_acc, two_acc,
               a_rows, rest_term, db_rest, o_grad, o_mine, qkv_mine, sibs_c, t_c, r_c,
               sibs_a, t_a, r_a, sibs_b, t_b, r_b, t1, r1, t2, r2, mid, u1, s1, u2, s2, mid_o, send, recv, lsem):
        me = Place()
        gain_one, gain_two, gain_query, gain_key = gain_rows(gains)
        loads = [pltpu.make_async_copy(hidden_hbm, hidden, lsem.at[1]),
                 pltpu.make_async_copy(w_hbm.at[:, pl.ds(2048, 1024)], wd, lsem.at[2])]
        unit_load = pltpu.make_async_copy(part_hbm, rest_term, lsem.at[3])
        a_load = pltpu.make_async_copy(a_hbm, a_rows, lsem.at[4])
        for c in [unit_load] + loads + [a_load]:
            c.start()
        two_acc[...] = jnp.zeros_like(two_acc)
        one_acc[...] = jnp.zeros_like(one_acc)
        q_acc[...] = jnp.zeros_like(q_acc)
        k_acc[...] = jnp.zeros_like(k_acc)

        def back(z, gain, up):
            inverse = lax.rsqrt(jnp.mean(z * z, axis=-1, keepdims=True) + epsilon)
            scaled = up * gain
            inner = jnp.mean(z * scaled, axis=-1, keepdims=True)
            return inverse * (scaled - z * inverse * inverse * inner), up * z * inverse

        meet([me.step("x", 1), me.step("x", -1), me.step("y", 1), me.step("y", -1),
              me.step("z", 1), me.step("z", -1), me.sibling()])
        w = Wire(send, recv)

        def put_rest(s, v):
            db_rest[s] = v

        def out_block(i, _):
            at = pl.multiple_of(i * 256, 256)
            v = dot(hidden[...], wd[pl.ds(at, 256)], 1, 1).astype(bf16)
            out_part[:, :, :, :, pl.ds(at, 256)] = v.reshape(2, 2, 2, 128, 256)
            return 0
        unit_load.wait()
        rest_gen = rs_z_gen(w, me, rest_term, put_rest, sibs_c, t_c, r_c)
        next(rest_gen)
        for c in loads:
            c.wait()
        lax.fori_loop(0, 2, out_block, 0)
        next(rest_gen)
        lax.fori_loop(2, 6, out_block, 0)
        next(rest_gen)
        lax.fori_loop(6, 8, out_block, 0)
        run([rest_gen])

        def norm_two(s):
            up = jnp.concatenate([db_front[s], db_rest[s]], axis=1)
            dz, terms = back(middle[s], gain_two, up)
            v = cot[s].astype(f32) + dz
            mid_grad[s] = v
            shard[s] = v.astype(bf16)
            two_acc[...] += terms
        chunks(128, norm_two)
        gen = ag_z_gen(w, me, shard, dm_full)
        next(gen)
        own = pltpu.make_async_copy(shard, dm_full.at[me.h, me.c, me.l], lsem.at[0])
        own.start()

        def put_out(s, v):
            block_output[s] = middle[s] + v
        out_gen = rs_z_gen(w, me, out_part, put_out, sibs_a, t_a, r_a)
        next(gen)
        next(out_gen)
        run([gen])
        own.wait()

        def one_pack(p):
            allowed, cosine, sine = pack_tables(segs, p, table)
            mixed_grad = dot(pack_of(dm_full, p), front_full[:, :, :, 384:640].reshape(D, 256)).T.astype(bf16)
            value_rows = v_rows[p].astype(f32).T.astype(bf16)
            key_pre = qk_pre[p, 256:320]
            kn, k_inverse = head_norm(key_pre, gain_key)
            kr = turn(kn, cosine, sine)
            key_rows = kr.T.astype(bf16)
            kr = kr.astype(bf16)
            dk = jnp.zeros((HD, SEQ), f32)
            dv = jnp.zeros((HD, SEQ), f32)
            heads = []
            terms_q = jnp.zeros((HD, SEQ), f32)
            for j in range(4):
                query_pre = qk_pre[p, 64 * j:64 * j + 64]
                qn, q_inverse = head_norm(query_pre, gain_query)
                qr = turn(qn, cosine, sine).astype(bf16)
                probs = pack_probs(key_rows, qr, allowed)
                do = mixed_grad[64 * j:64 * j + 64]
                dp = dot(value_rows, do)
                inner = jnp.sum(probs * dp, axis=0, keepdims=True)
                ds = (probs * (dp - inner)).astype(bf16)
                dqr = dot(kr, ds) * score_scale
                dk += dot(qr, ds, 1, 1)
                dv += dot(do, probs.astype(bf16), 1, 1)
                dq, terms = head_norm_back(query_pre, q_inverse, gain_query, turn_back(dqr, cosine, sine))
                terms_q += terms
                heads.append(dq)
            dk, terms_k = head_norm_back(key_pre, k_inverse, gain_key, turn_back(dk * score_scale, cosine, sine))
            q_acc[...] += terms_q
            k_acc[...] += terms_k
            grads = jnp.concatenate(heads + [dk, dv], axis=0).T.astype(bf16)
            dqkv[p] = grads
            out = dot(grads, front_full[:, :, :, 0:384].reshape(D, 384), 1, 1).astype(bf16)
            part[lax.div(p, 2), lax.rem(p, 2)] = out.reshape(2, 128, D)
        def put_in(s, v):
            dz, terms = back(x[s].astype(f32), gain_one, v)
            input_grad[s] = mid_grad[s] + dz
            one_acc[...] += terms
        in_gen = rs_z_packs(w, me, part, put_in, sibs_b, t_b, r_b)
        next(out_gen)
        for i in range(4):
            dm_rows = dm_full[:, :, :, :, 512 * i:512 * i + 512].reshape(ROWS, 512)
            o_grad[i] = dot(dm_rows, mixed[...].reshape(ROWS, 256), 0, 0).astype(bf16).reshape(4, 128, 256)
        o_gens = rs_xy_gens(w, me, o_grad, o_mine, u1, s1, u2, s2, mid_o)

        def both(gens):
            for g in gens:
                next(g)
        both(o_gens)
        one_pack(pack_turn(me, 0))
        next(in_gen)
        both(o_gens)
        one_pack(pack_turn(me, 1))
        next(out_gen)
        next(in_gen)
        both(o_gens)
        both(o_gens)
        one_pack(pack_turn(me, 2))
        next(in_gen)
        both(o_gens)
        one_pack(pack_turn(me, 3))
        next(in_gen)
        a_load.wait()
        for i in range(4):
            g = dot(a_rows[:, 512 * i:512 * i + 512], dqkv[...].reshape(ROWS, 384), 0, 0)
            front_grad[i] = g.astype(bf16).reshape(4, 128, 384)
        qkv_gens = rs_xy_gens(w, me, front_grad, qkv_mine, t1, r1, t2, r2, mid)
        both(qkv_gens)
        run(o_gens)
        next(in_gen)
        both(qkv_gens)
        both(qkv_gens)
        both(qkv_gens)
        run([out_gen])
        both(qkv_gens)
        run([in_gen])
        run(qkv_gens)
        front_mine[:, 0:384] = qkv_mine[...]
        front_mine[:, 384:640] = o_mine[...]
        w.finish()
        one = jnp.sum(one_acc[...], axis=0, keepdims=True)
        two = jnp.sum(two_acc[...], axis=0, keepdims=True)
        for i in range(16):
            gain_terms[i:i + 1, :] = one[:, 128 * i:128 * i + 128]
            gain_terms[16 + i:17 + i, :] = two[:, 128 * i:128 * i + 128]
        small = jnp.concatenate([q_acc[...], k_acc[...]], axis=0).T
        gain_terms[32:33, :] = jnp.sum(small, axis=0, keepdims=True)

    full = (2, 2, 2, 128, D)
    rows = jax.ShapeDtypeStruct((128, D), f32)
    return pl.pallas_call(
        kernel,
        out_shape=[rows, rows, jax.ShapeDtypeStruct((128, 640), bf16), jax.ShapeDtypeStruct((33, 128), f32)],
        in_specs=vm_specs(4) + any_specs(4) + vm_specs(7), out_specs=vm_specs(4),
        scratch_shapes=[VM((128, D), bf16), VM((ROWS, 1024), bf16), VM((D, 1024), bf16), VM(full, bf16),
                        VM(full, bf16), VM((128, D), f32), VM((PACKS, SEQ, 384), bf16),
                        VM(full, bf16), VM((4, 4, 128, 384), bf16), VM((HD, SEQ), f32), VM((HD, SEQ), f32),
                        VM((16, D), f32), VM((16, D), f32)]
        + [VM((ROWS, D), bf16), VM((2, 2, 2, 128, 1024), bf16), VM((128, 1024), f32), VM((4, 4, 128, 256), bf16),
           VM((128, 256), bf16), VM((128, 384), bf16)]
        + rs_z_scratch(1024) + rs_z_scratch(D) * 2 + rs_xy_scratch(384) + rs_xy_scratch(256) + dma_sems(100)
        + [pltpu.SemaphoreType.DMA((5,))],
        compiler_params=params(cid, 60))(
            x, cot, middle, db_front, rest_part, hidden, weights, a_full.reshape(ROWS, D), front_full, qk_pre, v_rows, mixed, segs,
            gains, table)


def adam(weight, moment, square, gradient, rate, decay):
    momentum = beta_one * moment + (1.0 - beta_one) * gradient
    variance = beta_two * square + (1.0 - beta_two) * gradient * gradient
    ratio = momentum / (1.0 - beta_one**STEP) / (jnp.sqrt(variance / (1.0 - beta_two**STEP)) + adam_epsilon)
    return weight - rate * (ratio + decay * weight), momentum, variance


RATES = (0.04, 0.04, 0.04, 0.15, 0.04, 0.04, 0.02)
SPANS = (256, 64, 64, 256, 1024, 1024, 1024)


def return_gradients(front, rest, gain_terms, cid):
    def kernel(front, rest, terms, fbuf, rbuf, gain_sum, z_in, x_in, y_in, send, recv):
        me = Place()
        peers = swap_devs(me)
        mine = me.h * 2 + me.c
        zs = [me.at(z=m4(me.z + dz), c=lax.rem(me.c + dc, 2)) for dz in range(4) for dc in range(2) if dz or dc]
        xs = [me.step("x", d) for d in (1, 2, 3)]
        ys = [me.step("y", d) for d in (1, 2, 3)]
        meet(zs + xs + ys)
        w = Wire(send, recv)

        def total(buf, n):
            v = buf[0]
            for k in range(1, n):
                v = v + buf[k]
            return v

        def share(value, buf, slot, devs):
            buf[slot] = value
            return [w.go(buf.at[slot], buf.at[slot], d) for d in devs]
        gs = share(terms[...], z_in, me.z * 2 + me.c, zs)
        arrivals = []
        for j, dev in reversed(peers):
            arrivals.append(w.go(front.at[j], fbuf.at[mine], dev))
            arrivals.append(w.go(rest.at[j], rbuf.at[mine], dev))
        fbuf[mine] = front[mine]
        rbuf[mine] = rest[mine]
        for c in gs:
            c.wait_recv()
        gs = share(total(z_in, 8), x_in, me.x, xs)
        for c in gs:
            c.wait_recv()
        gs = share(total(x_in, 4), y_in, me.y, ys)
        for c in gs:
            c.wait_recv()
        gain_sum[...] = total(y_in, 4)
        for a in arrivals:
            a.wait_recv()
        w.finish()

    return pl.pallas_call(
        kernel, out_shape=[jax.ShapeDtypeStruct((4, 32, 640), bf16), jax.ShapeDtypeStruct((4, 32, 3072), bf16),
                           jax.ShapeDtypeStruct((33, 128), f32)],
        in_specs=vm_specs(3), out_specs=vm_specs(3),
        scratch_shapes=[VM((8, 33, 128), f32), VM((4, 33, 128), f32), VM((4, 33, 128), f32)] + dma_sems(19),
        compiler_params=params(cid))(front, rest, gain_terms)


def update(front, rest, gain_sum, gain_states, states, tokens):
    def kernel(*refs):
        front, rest, g_sum, g_w, g_m, g_v = refs[:6]
        ins, t_in, g_out, outs, t_out = refs[6:27], refs[27:29], refs[29:32], refs[32:53], refs[53:55]
        held, made, kept = refs[55:76], refs[76:97], refs[97:99]
        lsem, osem, tsem = refs[99:]
        loads = [pltpu.make_async_copy(a, b, lsem.at[i]) for i, (a, b) in enumerate(zip(ins, held))]
        coming = [pltpu.make_async_copy(a, b, tsem.at[i]) for i, (a, b) in enumerate(zip(t_in, kept))]
        for c in loads + coming:
            c.start()
        new = adam(g_w[...], g_m[...], g_v[...], g_sum[...], gain_rate, 0.0)
        for ref, v in zip(g_out, new):
            ref[...] = v
        stores = []
        at = {False: 0, True: 0}
        for i, (n, rate) in enumerate(zip(SPANS, RATES)):
            late = i >= 4
            buf = rest if late else front
            for k in range(3):
                loads[3 * i + k].wait()
            for j in range(4):
                here = pl.ds(n * j, n)
                grad = buf[j, :, at[late]:at[late] + n].astype(f32)
                new = adam(held[3 * i][:, here], held[3 * i + 1][:, here], held[3 * i + 2][:, here], grad, rate,
                           weight_decay)
                for k in range(3):
                    made[3 * i + k][:, here] = new[k]
            at[late] += n
            for k in range(3):
                c = pltpu.make_async_copy(made[3 * i + k], outs[3 * i + k], osem.at[3 * i + k])
                c.start()
                stores.append(c)
        for i in range(2):
            coming[i].wait()
            c = pltpu.make_async_copy(kept[i], t_out[i], tsem.at[2 + i])
            c.start()
            stores.append(c)
        for c in stores:
            c.wait()

    shapes = [jax.ShapeDtypeStruct(s.shape, f32) for s in states]
    gain_shape = jax.ShapeDtypeStruct((33, 128), f32)
    return pl.pallas_call(
        kernel, out_shape=[gain_shape] * 3 + shapes + [jax.ShapeDtypeStruct(t.shape, f32) for t in tokens],
        in_specs=vm_specs(6) + any_specs(23), out_specs=vm_specs(3) + any_specs(23),
        scratch_shapes=[VM(s.shape, f32) for s in states] * 2 + [VM(t.shape, f32) for t in tokens]
        + [pltpu.SemaphoreType.DMA((21,)), pltpu.SemaphoreType.DMA((21,)), pltpu.SemaphoreType.DMA((4,))],
        compiler_params=pltpu.CompilerParams(has_side_effects=True, vmem_limit_bytes=56 * 2**20))(
            front, rest, gain_sum, *gain_states, *states, *tokens)


from jax.sharding import PartitionSpec as P

PLANE = [[x * 16 + y * 4 + k for x in range(4) for y in range(4)] for k in range(4)]
COLUMNS = [[8 * k + j for j in range(8)] for k in range(16)]


def scatter_plane(whole):
    return lax.psum_scatter(whole, "dp", axis_index_groups=PLANE, scatter_dimension=0, tiled=True)


def local(block_input, output_grad, segment_ids, norm_gains, gain_moment, gain_square, *states):
    square = lambda v: v.reshape(33, 128)
    gains = square(norm_gains)
    table = jnp.asarray(rope_constants())
    cot_full = lax.all_gather(output_grad, ("dp", "tensor"), axis_index_groups=COLUMNS, axis=0, tiled=True)
    one_full, two_full, rest_full, front_full, segments, qk_pre, v_rows, mixed, middle = attention_forward(
        block_input, states[::3], segment_ids, gains, table, 2)
    rest_full = rest_full.reshape(D, 3072)
    rest_grad, hidden, rest_part, db_front = feed_forward(
        two_full, cot_full.reshape(2, 2, 2, 128, D), rest_full, 3)
    rest_mine = scatter_plane(rest_grad)
    input_grad, block_output, front_mine, gain_terms = attention_backward(
        block_input, output_grad, middle, db_front, rest_part, hidden, rest_full, one_full, front_full, qk_pre, v_rows, mixed, segments,
        gains, table, 4)
    front_back, rest_back, gain_sum = return_gradients(
        front_mine.reshape(4, 32, 640), rest_mine.reshape(4, 32, 3072), gain_terms, 5)
    news = update(front_back, rest_back, gain_sum, [gains, square(gain_moment), square(gain_square)], states,
                  (block_output, input_grad))
    return tuple(news[-2:]) + tuple(v.reshape(-1) for v in news[:3]) + tuple(news[3:-2])


def solution(mesh):
    tokens, weight = P(("dp", "tensor"), None), P("dp", "tensor")
    in_specs = (tokens, tokens, P("dp", None), P(), P(), P()) + (weight,) * 21
    out_specs = (tokens, tokens, P(), P(), P()) + (weight,) * 21
    return jax.shard_map(local, mesh=mesh, in_specs=in_specs, out_specs=out_specs, check_vma=False)
```

```python
import jax
import jax.numpy as jnp
import numpy as np
from jax import lax
from jax.experimental import pallas as pl
from jax.experimental.pallas import tpu as pltpu

MESH = pl.DeviceIdType.MESH
VM = pltpu.VMEM
bf16 = jnp.bfloat16
f32 = jnp.float32


def m4(v):
    return lax.rem(v + 4, 4)


class Place:
    def __init__(self):
        dp = lax.axis_index("dp")
        self.l = lax.axis_index("tensor")
        self.x = lax.div(dp, 16)
        self.y = lax.rem(lax.div(dp, 4), 4)
        self.h = lax.rem(lax.div(dp, 2), 2)
        self.c = lax.rem(dp, 2)
        self.z = self.h * 2 + self.l

    def at(self, x=None, y=None, z=None, c=None):
        x = self.x if x is None else x
        y = self.y if y is None else y
        z = self.z if z is None else z
        c = self.c if c is None else c
        return (x * 16 + y * 4 + lax.div(z, 2) * 2 + c, lax.rem(z, 2))

    def pos(self, axis):
        return {"x": self.x, "y": self.y, "z": self.z}[axis]

    def step(self, axis, d):
        return self.at(**{axis: m4(self.pos(axis) + d)})

    def sibling(self):
        return self.at(c=1 - self.c)


class Wire:
    def __init__(self, send, recv, first=0):
        self.send, self.recv, self.n = send, recv, first
        self.pending = []

    def go(self, src, dst, dev):
        i = self.n
        self.n += 1
        c = pltpu.make_async_remote_copy(
            src_ref=src, dst_ref=dst, send_sem=self.send.at[i], recv_sem=self.recv.at[i],
            device_id=dev, device_id_type=MESH)
        c.start()
        self.pending.append(c)
        return c

    def finish(self):
        for c in self.pending:
            c.wait_send()
        self.pending = []


def meet(devs):
    b = pltpu.get_barrier_semaphore()
    for d in devs:
        pl.semaphore_signal(b, inc=1, device_id=d, device_id_type=MESH)
    pl.semaphore_wait(b, len(devs))


def ring_gather(w, me, axis, whole, lo, hi, first=None, arrived=None):
    p = me.pos(axis)
    up, down = me.step(axis, 1), me.step(axis, -1)
    own = whole(p) if first is None else first
    a = w.go(own, whole(p), up)
    b = w.go(own, whole(p), down)
    yield
    a.wait_recv()
    fa = w.go(lo(m4(p - 1)), lo(m4(p - 1)), up)
    if arrived:
        arrived(whole(m4(p - 1)))
    b.wait_recv()
    fb = w.go(hi(m4(p + 1)), hi(m4(p + 1)), down)
    if arrived:
        arrived(whole(m4(p + 1)))
    yield
    fa.wait_recv()
    if arrived:
        arrived(lo(m4(p - 2)))
    fb.wait_recv()
    if arrived:
        arrived(hi(m4(p - 2)))


def ring_scatter(w, me, axis, lo, hi, tlo, thi, rup, rdown, add):
    p = me.pos(axis)
    up, down = me.step(axis, 1), me.step(axis, -1)
    far, nu, nd = m4(p + 2), m4(p + 1), m4(p - 1)
    ta = w.go(lo(far), tlo, up)
    tb = w.go(hi(far), thi, down)
    da = w.go(hi(nu), rup[1], up)
    db = w.go(lo(nd), rdown[0], down)
    yield
    ta.wait_recv()
    add(tlo, lo(nu))
    sa = w.go(tlo, rup[0], up)
    tb.wait_recv()
    add(thi, hi(nd))
    sb = w.go(thi, rdown[1], down)
    yield
    da.wait_recv()
    db.wait_recv()
    sa.wait_recv()
    sb.wait_recv()


def loop_add(dst, a, b=None, rows=16):
    n = dst.shape[0]

    def body(i, _):
        def inner(j, _):
            s = pl.ds(pl.multiple_of(j * rows, rows), rows)
            v = dst[i, s].astype(f32) + a[i, s].astype(f32)
            if b is not None:
                v = v + b[i, s].astype(f32)
            dst[i, s] = v.astype(dst.dtype)
            return 0
        return lax.fori_loop(0, dst.shape[1] // rows, inner, 0)
    lax.fori_loop(0, n, body, 0)


def run(gens):
    gens = list(gens)
    while gens:
        for g in list(gens):
            try:
                next(g)
            except StopIteration:
                gens.remove(g)


def params(cid, mb=56):
    return pltpu.CompilerParams(collective_id=cid, has_side_effects=True, vmem_limit_bytes=mb * 2**20)


def ag_xy_gens(w, me, src, out):
    H = 64
    x, y = me.x, me.y

    def half_a():
        yield from ring_gather(w, me, "x", lambda i: out.at[i, y, pl.ds(0, 64)], lambda i: out.at[i, y, pl.ds(0, 32)],
                               lambda i: out.at[i, y, pl.ds(32, 32)], first=src.at[pl.ds(0, 64)])
        yield
        yield from ring_gather(w, me, "y", lambda i: out.at[:, i, pl.ds(0, 64)], lambda i: out.at[:, i, pl.ds(0, 32)],
                               lambda i: out.at[:, i, pl.ds(32, 32)])

    def half_b():
        yield from ring_gather(w, me, "y", lambda i: out.at[x, i, pl.ds(64, 64)], lambda i: out.at[x, i, pl.ds(64, 32)],
                               lambda i: out.at[x, i, pl.ds(96, 32)], first=src.at[pl.ds(64, 64)])
        yield
        yield from ring_gather(w, me, "x", lambda i: out.at[i, :, pl.ds(64, 64)], lambda i: out.at[i, :, pl.ds(64, 32)],
                               lambda i: out.at[i, :, pl.ds(96, 32)])
    return [half_a(), half_b()]


def ag_xy(shard, cid, space=pl.ANY):
    C = shard.shape[1]

    def kernel(src, out, send, recv, lsem):
        me = Place()
        meet([me.step("x", 1), me.step("x", -1), me.step("y", 1), me.step("y", -1)])
        w = Wire(send, recv)
        lc = pltpu.make_async_copy(src, out.at[me.x, me.y], lsem)
        lc.start()
        lc.wait()
        run(ag_xy_gens(w, me, src, out))
        w.finish()

    return pl.pallas_call(
        kernel, out_shape=jax.ShapeDtypeStruct((4, 4, 128, C), shard.dtype),
        in_specs=[pl.BlockSpec(memory_space=space)], out_specs=pl.BlockSpec(memory_space=space),
        scratch_shapes=[pltpu.SemaphoreType.DMA((16,)), pltpu.SemaphoreType.DMA((16,)), pltpu.SemaphoreType.DMA],
        compiler_params=params(cid))(shard)


def rs_xy_scratch(C):
    return [VM((2, 2, 4, 32, C), bf16), VM((2, 2, 2, 4, 32, C), bf16),
            VM((2, 2, 32, C), bf16), VM((2, 2, 2, 32, C), bf16), VM((2, 4, 64, C), bf16)]


def rs_xy_gens(w, me, g, out, t1, r1, t2, r2, mid):
    x, y = me.x, me.y

    def half(k, first, second):
        base = k * 64
        if first == "y":
            pick = lambda i, o: g.at[:, i, pl.ds(base + o, 32)]
        else:
            pick = lambda i, o: g.at[i, :, pl.ds(base + o, 32)]
        yield from ring_scatter(w, me, first, lambda i: pick(i, 0), lambda i: pick(i, 32), t1.at[k, 0], t1.at[k, 1],
                                (r1.at[k, 0, 0], r1.at[k, 0, 1]), (r1.at[k, 1, 0], r1.at[k, 1, 1]), loop_add)
        p = me.pos(first)
        m = mid.at[k]
        for hh in range(2):
            own = pick(p, 32 * hh)

            def body(i, _):
                def inner(j, _):
                    s = pl.ds(pl.multiple_of(j * 16, 16), 16)
                    d = pl.ds(pl.multiple_of(j * 16 + 32 * hh, 16), 16)
                    v = own[i, s].astype(f32) + r1[k, 0, hh, i, s].astype(f32) + r1[k, 1, hh, i, s].astype(f32)
                    m[i, d] = v.astype(bf16)
                    return 0
                return lax.fori_loop(0, 2, inner, 0)
            lax.fori_loop(0, 4, body, 0)
        yield
        q = me.pos(second)
        add1 = lambda dst, a: loop_add(dst, a)
        pick2 = lambda i, o: mid.at[k, i, pl.ds(o, 32)]

        def add2(dst, a):
            def inner(j, _):
                s = pl.ds(pl.multiple_of(j * 16, 16), 16)
                dst[s] = (dst[s].astype(f32) + a[s].astype(f32)).astype(bf16)
                return 0
            lax.fori_loop(0, 2, inner, 0)
        yield from ring_scatter(w, me, second, lambda i: pick2(i, 0), lambda i: pick2(i, 32), t2.at[k, 0], t2.at[k, 1],
                                (r2.at[k, 0, 0], r2.at[k, 0, 1]), (r2.at[k, 1, 0], r2.at[k, 1, 1]), add2)
        for hh in range(2):
            def inner(j, _):
                s = pl.ds(pl.multiple_of(j * 16, 16), 16)
                d = pl.ds(pl.multiple_of(j * 16 + 32 * hh, 16), 16)
                dd = pl.ds(pl.multiple_of(j * 16 + 32 * hh + base, 16), 16)
                v = m[q, d].astype(f32) + r2[k, 0, hh, s].astype(f32) + r2[k, 1, hh, s].astype(f32)
                out[dd] = v.astype(out.dtype)
                return 0
            lax.fori_loop(0, 2, inner, 0)
    return [half(0, "y", "x"), half(1, "x", "y")]


def rs_xy(g, cid, out_dtype=f32):
    C = g.shape[-1]

    def kernel(gin, out, send, recv, *scr):
        me = Place()
        meet([me.step("x", 1), me.step("x", -1), me.step("y", 1), me.step("y", -1)])
        w = Wire(send, recv)
        run(rs_xy_gens(w, me, gin, out, *scr))
        w.finish()

    return pl.pallas_call(
        kernel, out_shape=jax.ShapeDtypeStruct((128, C), out_dtype),
        in_specs=[pl.BlockSpec(memory_space=VM)], out_specs=pl.BlockSpec(memory_space=VM),
        scratch_shapes=[pltpu.SemaphoreType.DMA((24,)), pltpu.SemaphoreType.DMA((24,))] + rs_xy_scratch(C),
        compiler_params=params(cid, 60))(g)


def ag_z_gen(w, me, src, out, r0=0, n=128):
    sib = me.sibling()
    blk = lambda i, cc: out.at[lax.div(i, 2), cc, lax.rem(i, 2)]
    cs = []

    def to_sib(ref):
        cs.append(w.go(ref, ref, sib))
    whole = lambda i: blk(i, me.c).at[pl.ds(r0, n)]
    lo = lambda i: blk(i, me.c).at[pl.ds(r0, n // 2)]
    hi = lambda i: blk(i, me.c).at[pl.ds(r0 + n // 2, n // 2)]
    own = w.go(src, whole(me.z), sib)
    yield from ring_gather(w, me, "z", whole, lo, hi, first=src, arrived=to_sib)
    own.wait_recv()
    for c in cs:
        c.wait_recv()


def ag_z(shard, cid, space=VM):
    C = shard.shape[1]

    def kernel(src, out, send, recv, lsem):
        me = Place()
        meet([me.step("z", 1), me.step("z", -1), me.sibling()])
        w = Wire(send, recv)
        lc = pltpu.make_async_copy(src, out.at[me.h, me.c, me.l], lsem)
        lc.start()
        lc.wait()
        run([ag_z_gen(w, me, src, out)])
        w.finish()

    return pl.pallas_call(
        kernel, out_shape=jax.ShapeDtypeStruct((2, 2, 2, 128, C), shard.dtype),
        in_specs=[pl.BlockSpec(memory_space=space)], out_specs=pl.BlockSpec(memory_space=space),
        scratch_shapes=[pltpu.SemaphoreType.DMA((16,)), pltpu.SemaphoreType.DMA((16,)), pltpu.SemaphoreType.DMA],
        compiler_params=params(cid))(shard)


def rs_z_scratch(C):
    return [VM((4, 128, C), bf16), VM((2, 64, C), bf16), VM((2, 2, 64, C), bf16)]


def rs_z_gen(w, me, g, out, sibs, t, r):
    sib = me.sibling()
    oc = 1 - me.c
    order = [2, 1, 3, 0]
    blk = lambda i, cc: g.at[lax.div(i, 2), cc, lax.rem(i, 2)]
    z = me.z
    sc = {}
    for o in order:
        i = m4(z + o)
        sc[o] = w.go(blk(i, oc), sibs.at[i], sib)
    yield

    def fold(o, s0, n):
        i = m4(z + o)
        b = blk(i, me.c)

        def inner(j, _):
            s = pl.ds(pl.multiple_of(j * 16 + s0, 16), 16)
            sibs[i, s] = (sibs[i, s].astype(f32) + b[s].astype(f32)).astype(bf16)
            return 0
        lax.fori_loop(0, n // 16, inner, 0)
    up, down = me.step("z", 1), me.step("z", -1)
    half = lambda o, k: sibs.at[m4(z + o), pl.ds(64 * k, 64)]
    sc[2].wait_recv()
    fold(2, 0, 64)
    ta = w.go(half(2, 0), t.at[0], up)
    fold(2, 64, 64)
    tb = w.go(half(2, 1), t.at[1], down)
    sc[1].wait_recv()
    fold(1, 64, 64)
    da = w.go(half(1, 1), r.at[0, 1], up)
    sc[3].wait_recv()
    fold(3, 0, 64)
    db = w.go(half(3, 0), r.at[1, 0], down)
    fold(1, 0, 64)
    fold(3, 64, 64)
    yield

    def add(dst, a):
        def inner(j, _):
            s = pl.ds(pl.multiple_of(j * 16, 16), 16)
            dst[s] = (dst[s].astype(f32) + a[s].astype(f32)).astype(bf16)
            return 0
        lax.fori_loop(0, 4, inner, 0)
    ta.wait_recv()
    add(t.at[0], half(1, 0))
    sa = w.go(t.at[0], r.at[0, 0], up)
    tb.wait_recv()
    add(t.at[1], half(3, 1))
    sb = w.go(t.at[1], r.at[1, 1], down)
    sc[0].wait_recv()
    own = blk(z, me.c)
    yield

    def last(hh):
        def inner(j, _):
            s = pl.ds(pl.multiple_of(j * 16, 16), 16)
            d = pl.ds(pl.multiple_of(j * 16 + 64 * hh, 16), 16)
            v = own[d].astype(f32) + sibs[z, d].astype(f32) + r[0, hh, s].astype(f32) + r[1, hh, s].astype(f32)
            out(d, v)
            return 0
        lax.fori_loop(0, 4, inner, 0)
    da.wait_recv()
    sa.wait_recv()
    db.wait_recv()
    sb.wait_recv()
    last(0)
    last(1)


def rs_z(g, cid, out_dtype=f32):
    C = g.shape[-1]

    def kernel(gin, out, send, recv, *scr):
        me = Place()
        meet([me.step("z", 1), me.step("z", -1), me.sibling()])
        w = Wire(send, recv)

        def put(s, v):
            out[s] = v.astype(out.dtype)
        run([rs_z_gen(w, me, gin, put, *scr)])
        w.finish()

    return pl.pallas_call(
        kernel, out_shape=jax.ShapeDtypeStruct((128, C), out_dtype),
        in_specs=[pl.BlockSpec(memory_space=VM)], out_specs=pl.BlockSpec(memory_space=VM),
        scratch_shapes=[pltpu.SemaphoreType.DMA((16,)), pltpu.SemaphoreType.DMA((16,))] + rs_z_scratch(C),
        compiler_params=params(cid))(g)


def swap_devs(me):
    out = []
    for dh, dc in ((0, 1), (1, 0), (1, 1)):
        h = lax.rem(me.h + dh, 2)
        c = lax.rem(me.c + dc, 2)
        out.append((h * 2 + c, me.at(z=h * 2 + me.l, c=c)))
    return out


def swap_hc(parts, cid):
    n = len(parts)

    def kernel(*refs):
        ins, outs = refs[:n], refs[n:2 * n]
        send, recv, lsem = refs[2 * n:]
        me = Place()
        peers = swap_devs(me)
        meet([d for _, d in peers])
        w = Wire(send, recv)
        mine = me.h * 2 + me.c
        arrivals = []
        for j, d in reversed(peers):
            for a, b in zip(ins, outs):
                arrivals.append(w.go(a.at[j], b.at[mine], d))
        ls = []
        for k, (a, b) in enumerate(zip(ins, outs)):
            lc = pltpu.make_async_copy(a.at[mine], b.at[mine], lsem.at[k])
            lc.start()
            ls.append(lc)
        for lc in ls:
            lc.wait()
        for a in arrivals:
            a.wait_recv()
        w.finish()

    return pl.pallas_call(
        kernel, out_shape=[jax.ShapeDtypeStruct(p.shape, p.dtype) for p in parts],
        in_specs=[pl.BlockSpec(memory_space=VM)] * n, out_specs=[pl.BlockSpec(memory_space=VM)] * n,
        scratch_shapes=[pltpu.SemaphoreType.DMA((3 * n,)), pltpu.SemaphoreType.DMA((3 * n,)),
                        pltpu.SemaphoreType.DMA((n,))],
        compiler_params=params(cid))(*parts)


def sum_all(v, cid):
    R, C = v.shape

    def kernel(src, out, z_in, x_in, y_in, acc, send, recv):
        me = Place()
        zs = []
        for dz in range(4):
            for dc in range(2):
                if dz or dc:
                    z, c = m4(me.z + dz), lax.rem(me.c + dc, 2)
                    zs.append(me.at(z=z, c=c))
        xs = [me.step("x", d) for d in (1, 2, 3)]
        ys = [me.step("y", d) for d in (1, 2, 3)]
        meet(zs + xs + ys)
        w = Wire(send, recv)
        acc[...] = src[...]
        for buf, slot, devs, n in ((z_in, me.z * 2 + me.c, zs, 8), (x_in, me.x, xs, 4), (y_in, me.y, ys, 4)):
            buf[slot] = acc[...]
            cs = [w.go(buf.at[slot], buf.at[slot], d) for d in devs]
            for c in cs:
                c.wait_recv()
            total = buf[0]
            for k in range(1, n):
                total = total + buf[k]
            w.finish()
            acc[...] = total
        out[...] = acc[...]

    return pl.pallas_call(
        kernel, out_shape=jax.ShapeDtypeStruct((R, C), f32),
        in_specs=[pl.BlockSpec(memory_space=VM)], out_specs=pl.BlockSpec(memory_space=VM),
        scratch_shapes=[VM((8, R, C), f32), VM((4, R, C), f32), VM((4, R, C), f32), VM((R, C), f32),
                        pltpu.SemaphoreType.DMA((13,)), pltpu.SemaphoreType.DMA((13,))],
        compiler_params=params(cid))(v)


def rs_z_packs(w, me, g, put, sibs, t, r):
    sib, oc, z = me.sibling(), 1 - me.c, me.z
    blk = lambda i, cc: g.at[lax.div(i, 2), cc, lax.rem(i, 2)]
    far = m4(z + 2)
    flip = lambda i: i + 1 - 2 * lax.rem(i, 2)
    beside, partner = flip(far), flip(z)
    up, down = me.step("z", 1), me.step("z", -1)
    half = lambda i, k: sibs.at[i, pl.ds(64 * k, 64)]

    def fold(i, s0, n):
        b = blk(i, me.c)

        def inner(j, _):
            s = pl.ds(pl.multiple_of(j * 16 + s0, 16), 16)
            sibs[i, s] = (sibs[i, s].astype(f32) + b[s].astype(f32)).astype(bf16)
            return 0
        lax.fori_loop(0, n // 16, inner, 0)

    def add(dst, a):
        def inner(j, _):
            s = pl.ds(pl.multiple_of(j * 16, 16), 16)
            dst[s] = (dst[s].astype(f32) + a[s].astype(f32)).astype(bf16)
            return 0
        lax.fori_loop(0, 4, inner, 0)
    s_far = w.go(blk(far, oc), sibs.at[far], sib)
    s_beside = w.go(blk(beside, oc), sibs.at[beside], sib)
    yield
    s_far.wait_recv()
    fold(far, 0, 64)
    ta = w.go(half(far, 0), t.at[0], up)
    fold(far, 64, 64)
    tb = w.go(half(far, 1), t.at[1], down)
    s_beside.wait_recv()
    fold(beside, 0, 128)
    yield
    s_partner = w.go(blk(partner, oc), sibs.at[partner], sib)
    s_own = w.go(blk(z, oc), sibs.at[z], sib)
    yield
    s_partner.wait_recv()
    fold(partner, 0, 128)
    nu, nd = m4(z + 1), m4(z - 1)
    da = w.go(half(nu, 1), r.at[0, 1], up)
    db = w.go(half(nd, 0), r.at[1, 0], down)
    yield
    ta.wait_recv()
    add(t.at[0], half(nu, 0))
    sa = w.go(t.at[0], r.at[0, 0], up)
    tb.wait_recv()
    add(t.at[1], half(nd, 1))
    sb = w.go(t.at[1], r.at[1, 1], down)
    s_own.wait_recv()
    own = blk(z, me.c)
    yield

    def last(hh):
        def inner(j, _):
            s = pl.ds(pl.multiple_of(j * 16, 16), 16)
            d = pl.ds(pl.multiple_of(j * 16 + 64 * hh, 16), 16)
            put(d, own[d].astype(f32) + sibs[z, d].astype(f32) + r[0, hh, s].astype(f32) + r[1, hh, s].astype(f32))
            return 0
        lax.fori_loop(0, 4, inner, 0)
    da.wait_recv()
    sa.wait_recv()
    db.wait_recv()
    sb.wait_recv()
    last(0)
    last(1)


D = 2048
HD = 64
STEP = 10
SEQ = 256
PACKS = 4
ROWS = 1024
epsilon = 1e-06
rope_base = 1000000.0
beta_one = 0.9
beta_two = 0.999
adam_epsilon = 1e-08
weight_decay = 0.1
gain_rate = 0.3
masked_score = -1000000000.0
score_scale = HD ** (-0.5)
exact = lax.Precision.HIGHEST


def dot(a, b, ca=1, cb=0, precision=None):
    return lax.dot_general(a, b, (((ca,), (cb,)), ((), ())), precision=precision, preferred_element_type=f32)


def chunks(n, body, rows=16):
    def one(j, _):
        body(pl.ds(pl.multiple_of(j * rows, rows), rows))
        return 0
    lax.fori_loop(0, n // rows, one, 0)


def dma_sems(n):
    return [pltpu.SemaphoreType.DMA((n,)), pltpu.SemaphoreType.DMA((n,))]


def vm_specs(n):
    return [pl.BlockSpec(memory_space=VM)] * n


def any_specs(n):
    return [pl.BlockSpec(memory_space=pl.ANY)] * n


class Columns:
    def __init__(self, ref, n):
        self.ref, self.n = ref, n

    def __getitem__(self, j):
        return self.ref[:, pl.ds(pl.multiple_of(j * self.n, self.n), self.n)]


def gain_rows(gains):
    one = jnp.concatenate([gains[i:i + 1, :] for i in range(16)], axis=1)
    two = jnp.concatenate([gains[16 + i:17 + i, :] for i in range(16)], axis=1)
    small = jnp.broadcast_to(gains[32:33, :], (128, 128)).T
    return one, two, small[0:64, 0:1], small[64:128, 0:1]


def rope_constants():
    frequency = np.float32(rope_base) ** (np.float32(-2.0) * np.arange(HD // 2, dtype=np.float32) / np.float32(HD))
    angles = (np.arange(SEQ, dtype=np.float32)[None, :] * frequency[:, None].astype(np.float32)).astype(np.float64)
    return np.concatenate([np.cos(angles), np.sin(angles)], axis=0).astype(np.float32)


def pack_tables(segs, p, table):
    row = segs[p].astype(f32)[0:1, :]
    column = jnp.broadcast_to(row, (128, SEQ)).T[:, 0:1]
    key_at = lax.broadcasted_iota(jnp.int32, (SEQ, SEQ), 0)
    query_at = lax.broadcasted_iota(jnp.int32, (SEQ, SEQ), 1)
    allowed = (column == row) & (key_at <= query_at)
    start = jnp.sum(jnp.where(column < row, 1.0, 0.0), axis=0, keepdims=True)
    where = query_at.astype(f32) - start
    hot = jnp.where(key_at.astype(f32) == where, 1.0, 0.0)
    both = dot(table[...], hot, precision=exact)
    return allowed, both[0:32], both[32:64]


def head_norm(z, gain):
    inverse = lax.rsqrt(jnp.mean(z * z, axis=0, keepdims=True) + epsilon)
    return z * inverse * gain, inverse


def head_norm_back(z, inverse, gain, up):
    scaled = up * gain
    inner = jnp.mean(z * scaled, axis=0, keepdims=True)
    return inverse * (scaled - z * inverse * inverse * inner), up * z * inverse


def turn(u, cosine, sine):
    a, b = u[0:32], u[32:64]
    return jnp.concatenate([a * cosine - b * sine, b * cosine + a * sine], axis=0)


def turn_back(u, cosine, sine):
    a, b = u[0:32], u[32:64]
    return jnp.concatenate([a * cosine + b * sine, b * cosine - a * sine], axis=0)


def pack_probs(key_rows, query_rot, allowed):
    scores = jnp.where(allowed, dot(key_rows, query_rot) * score_scale, masked_score)
    exps = jnp.exp(scores - jnp.max(scores, axis=0, keepdims=True))
    return exps / jnp.sum(exps, axis=0, keepdims=True)


def pack_of(ref, p):
    v = ref[lax.div(p, 2), lax.rem(p, 2)]
    return v.reshape(SEQ, v.shape[-1])


def pack_turn(me, i):
    h = me.h if i >= 2 else 1 - me.h
    c = me.c if i % 2 else 1 - me.c
    return h * 2 + c


def attention_forward(x, cot, weights, seg, gains, table, cid):
    def kernel(x, cot, q_, k_, v_, o_, g_, u_, d_, seg, gains, table,
               a_full, cot_full, n_full, rest_full, front_full, segs, qk_pre, v_rows, mixed, middle,
               fbuf, rbuf, sbuf, kv, fshard, rshard, rest, shard, shard_two, a_buf, part, sibs, t, r,
               send, recv, lsem, ksem):
        me = Place()
        gain_one, gain_two, gain_query, gain_key = gain_rows(gains)
        peers = swap_devs(me)
        mine = me.h * 2 + me.c
        q, o = Columns(q_, 256), Columns(o_, 256)
        g, u, d = Columns(g_, 1024), Columns(u_, 1024), Columns(d_, 1024)
        for j in range(4):
            kv[j] = jnp.concatenate([k_[:, 64 * j:64 * j + 64], v_[:, 64 * j:64 * j + 64]], axis=1)
        sbuf[...] = jnp.broadcast_to(seg[...], (8, SEQ))
        here = pl.ds(pl.multiple_of(mine * 32, 32), 32)

        def round_front(j, dst):
            dst[:, 0:256] = q[j].astype(bf16)
            dst[:, 256:384] = kv[j].astype(bf16)
            dst[:, 384:640] = o[j].astype(bf16)

        def round_rest(j, dst):
            for i, w in enumerate((g, u, d)):
                dst[:, 1024 * i:1024 * i + 1024] = w[j].astype(bf16)
        meet([me.step("x", 1), me.step("x", -1), me.step("y", 1), me.step("y", -1),
              me.step("z", 1), me.step("z", -1)] + [dev for _, dev in peers])
        w = Wire(send, recv)
        first, second = [], []
        for j, dev in reversed(peers):
            round_front(j, fbuf.at[j])
            first.append(w.go(fbuf.at[j], fshard.at[here], dev))
            second.append(w.go(sbuf, segs.at[mine], dev))
        for j, dev in reversed(peers):
            round_rest(j, rbuf.at[j])
            second.append(w.go(rbuf.at[j], rshard.at[here], dev))
        round_front(mine, fshard.at[here])
        round_rest(mine, rshard.at[here])
        segs[mine] = sbuf[...]

        def norm_one(s):
            v = x[s].astype(f32)
            inverse = lax.rsqrt(jnp.mean(v * v, axis=-1, keepdims=True) + epsilon)
            shard[s] = (v * inverse * gain_one).astype(bf16)
        chunks(128, norm_one)
        for c in first:
            c.wait_recv()

        def both(gens):
            for g in gens:
                next(g)
        front_gens = ag_xy_gens(w, me, fshard, front_full)
        both(front_gens)
        gz = ag_z_gen(w, me, shard, a_buf)
        next(gz)
        locals_ = [pltpu.make_async_copy(fshard, front_full.at[me.x, me.y], lsem.at[0]),
                   pltpu.make_async_copy(shard, a_buf.at[me.h, me.c, me.l], lsem.at[1]),
                   pltpu.make_async_copy(cot, cot_full.at[me.h, me.c, me.l], lsem.at[2])]
        for c in locals_:
            c.start()
        both(front_gens)
        for c in locals_:
            c.wait()
        both(front_gens)
        both(front_gens)
        for c in second:
            c.wait_recv()
        rest_gens = ag_xy_gens(w, me, rshard, rest)
        both(rest_gens)
        own = pltpu.make_async_copy(rshard, rest.at[me.x, me.y], lsem.at[3])
        own.start()
        both(front_gens)
        both(rest_gens)
        own.wait()
        run(front_gens)
        both(rest_gens)
        both(rest_gens)
        next(gz)
        run([gz])
        cot_gen = ag_z_gen(w, me, cot.at[pl.ds(0, 64)], cot_full, 0, 64)
        next(cot_gen)
        keep = pltpu.make_async_copy(a_buf, a_full, lsem.at[4])
        keep.start()

        def one_pack(p):
            allowed, cosine, sine = pack_tables(segs, p, table)
            qkv = dot(pack_of(a_buf, p), front_full[:, :, :, 0:384].reshape(D, 384)).T
            qk_pre[p] = qkv[0:320]
            value = qkv[320:384].astype(bf16)
            v_rows[p] = value
            kn, _i = head_norm(qkv[256:320], gain_key)
            key_rows = turn(kn, cosine, sine).T.astype(bf16)
            heads = []
            for j in range(4):
                qn, _i = head_norm(qkv[64 * j:64 * j + 64], gain_query)
                probs = pack_probs(key_rows, turn(qn, cosine, sine).astype(bf16), allowed)
                heads.append(dot(value, probs.astype(bf16)))
            o = jnp.concatenate(heads, axis=0).T.astype(bf16)
            mixed[p] = o
            out = dot(o, front_full[:, :, :, 384:640].reshape(D, 256), 1, 1).astype(bf16)
            part[lax.div(p, 2), lax.rem(p, 2)] = out.reshape(2, 128, D)

        def residual(s, v):
            middle[s] = x[s].astype(f32) + v
        sum_gen = rs_z_packs(w, me, part, residual, sibs, t, r)
        for i in range(4):
            one_pack(pack_turn(me, i))
            next(sum_gen)
            if i == 2:
                next(cot_gen)
        both(rest_gens)
        run([sum_gen])

        def norm_two(s):
            v = middle[s]
            inverse = lax.rsqrt(jnp.mean(v * v, axis=-1, keepdims=True) + epsilon)
            shard_two[s] = (v * inverse * gain_two).astype(bf16)
        chunks(128, norm_two)
        n_gen = ag_z_gen(w, me, shard_two, n_full)
        next(n_gen)
        own = pltpu.make_async_copy(shard_two, n_full.at[me.h, me.c, me.l], lsem.at[3])
        own.start()
        run([cot_gen])
        stores = []

        def store(k, a, b, at):
            here = pl.ds(at, 64)
            c = pltpu.make_async_copy(rest.at[a, b, here], rest_full.at[a, b, here], ksem.at[k])
            c.start()
            stores.append(c)
        every = slice(None)
        for k in (0, 1, 3):
            store(k, every, m4(me.y + k), 0)
            store(4 + k, m4(me.x + k), every, 64)
        next(n_gen)
        cot_gen = ag_z_gen(w, me, cot.at[pl.ds(64, 64)], cot_full, 64, 64)
        next(cot_gen)
        run([n_gen])
        run(rest_gens)
        store(2, every, m4(me.y + 2), 0)
        store(6, m4(me.x + 2), every, 64)
        run([cot_gen])
        own.wait()
        keep.wait()
        for c in stores:
            c.wait()
        w.finish()

    full = jax.ShapeDtypeStruct((2, 2, 2, 128, D), bf16)
    return pl.pallas_call(
        kernel,
        out_shape=[full, full, full, jax.ShapeDtypeStruct((4, 4, 128, 3072), bf16),
                   jax.ShapeDtypeStruct((4, 4, 128, 640), bf16), jax.ShapeDtypeStruct((4, 8, SEQ), jnp.int32),
                   jax.ShapeDtypeStruct((PACKS, 320, SEQ), f32), jax.ShapeDtypeStruct((PACKS, HD, SEQ), bf16),
                   jax.ShapeDtypeStruct((PACKS, SEQ, 256), bf16), jax.ShapeDtypeStruct((128, D), f32)],
        in_specs=vm_specs(12), out_specs=any_specs(4) + vm_specs(6),
        scratch_shapes=[VM((4, 32, 640), bf16), VM((4, 32, 3072), bf16), VM((8, SEQ), jnp.int32), VM((4, 32, 128), f32),
                        VM((128, 640), bf16), VM((128, 3072), bf16), VM((4, 4, 128, 3072), bf16)]
        + [VM((128, D), bf16)] * 2 + [VM((2, 2, 2, 128, D), bf16)] * 2 + rs_z_scratch(D)
        + dma_sems(96) + [pltpu.SemaphoreType.DMA((5,)), pltpu.SemaphoreType.DMA((8,))],
        compiler_params=params(cid, 58))(x, cot, *weights, seg, gains, table)


def sigmoid(v):
    return 1.0 / (1.0 + jnp.exp(-v))


def feed_forward(n_full, cot_full, weights):
    def kernel(n_hbm, cot_hbm, w_hbm, grad_hbm, hidden_hbm, part_hbm,
               n, cot, w, hidden, gate_up, part, grad, lsem, wsem, gsem):
        loads = [pltpu.make_async_copy(n_hbm, n, lsem.at[0]), pltpu.make_async_copy(cot_hbm, cot, lsem.at[1])]
        loads[0].start()

        def piece(i, k):
            here = pl.ds(pl.multiple_of(i * 256 + 1024 * k, 256), 256)
            return pltpu.make_async_copy(w_hbm.at[:, here], w.at[:, here], wsem.at[i, k])
        for i in range(4):
            for k in range(3):
                piece(i, k).start()
            if i == 0:
                loads[1].start()
        for c in loads:
            c.wait()

        def hidden_block(i, _):
            at = pl.multiple_of(i * 256, 256)
            for k in range(3):
                piece(i, k).wait()
            rows = n[...].reshape(ROWS, D)
            g = dot(rows, w[:, pl.ds(at, 256)])
            u = dot(rows, w[:, pl.ds(at + 1024, 256)])
            dh = dot(cot[...].reshape(ROWS, D), w[:, pl.ds(at + 2048, 256)])
            s = sigmoid(g)
            silu = g * s
            hidden[:, pl.ds(at, 256)] = (silu * u).astype(bf16)
            gate_up[:, pl.ds(at, 256)] = (dh * u * (s + silu * (1.0 - s))).astype(bf16)
            gate_up[:, pl.ds(at + 1024, 256)] = (dh * silu).astype(bf16)
            return 0
        lax.fori_loop(0, 4, hidden_block, 0)
        keep = [pltpu.make_async_copy(hidden, hidden_hbm, lsem.at[2]), pltpu.make_async_copy(part, part_hbm, lsem.at[3])]
        keep[0].start()

        def back_block(i, _):
            at = pl.multiple_of(i * 256, 256)
            v = dot(gate_up[...], w[pl.ds(at, 256), 0:2048], 1, 1).astype(bf16)
            part[:, :, :, :, pl.ds(at, 256)] = v.reshape(2, 2, 2, 128, 256)
            return 0
        lax.fori_loop(0, 8, back_block, 0)
        keep[1].start()
        stores = []
        for i in range(4):
            at = 512 * i
            slot = i % 2
            if i >= 2:
                stores[i - 2].wait()
            grad[slot, :, 0:2048] = dot(n[:, :, :, :, at:at + 512].reshape(ROWS, 512), gate_up[...], 0, 0).astype(bf16)
            grad[slot, :, 2048:3072] = dot(cot[:, :, :, :, at:at + 512].reshape(ROWS, 512), hidden[...], 0, 0).astype(bf16)
            c = pltpu.make_async_copy(grad.at[slot], grad_hbm.at[pl.ds(at, 512)], gsem.at[i])
            c.start()
            stores.append(c)
        for c in stores[2:] + keep:
            c.wait()

    full = (2, 2, 2, 128, D)
    return pl.pallas_call(
        kernel,
        out_shape=[jax.ShapeDtypeStruct((D, 3072), bf16), jax.ShapeDtypeStruct((ROWS, 1024), bf16),
                   jax.ShapeDtypeStruct(full, bf16)],
        in_specs=any_specs(3), out_specs=any_specs(3),
        scratch_shapes=[VM(full, bf16), VM(full, bf16), VM((D, 3072), bf16), VM((ROWS, 1024), bf16),
                        VM((ROWS, 2048), bf16), VM(full, bf16), VM((2, 512, 3072), bf16), pltpu.SemaphoreType.DMA((4,)),
                        pltpu.SemaphoreType.DMA((4, 3)), pltpu.SemaphoreType.DMA((4,))],
        compiler_params=pltpu.CompilerParams(has_side_effects=True, vmem_limit_bytes=60 * 2**20))(
            n_full, cot_full, weights)


def attention_backward(x, cot, middle, db_part, hidden, weights, a_full, front_full, qk_pre, v_rows, mixed, segs,
                       gains, table, cid):
    def kernel(x, cot, middle, part_hbm, hidden_hbm, w_hbm, a_hbm, front_full, qk_pre, v_rows, mixed, segs,
               gains, table, input_grad, block_output, front_mine, gain_terms,
               shard, hidden, wd, out_part, dm_full, mid_grad, dqkv, part, front_grad, q_acc, k_acc, one_acc, two_acc,
               a_rows, db_term, db_sum, o_grad, o_mine, qkv_mine, sibs_c, t_c, r_c,
               sibs_a, t_a, r_a, sibs_b, t_b, r_b, t1, r1, t2, r2, mid, u1, s1, u2, s2, mid_o, send, recv, lsem):
        me = Place()
        gain_one, gain_two, gain_query, gain_key = gain_rows(gains)
        loads = [pltpu.make_async_copy(hidden_hbm, hidden, lsem.at[1]),
                 pltpu.make_async_copy(w_hbm.at[:, pl.ds(2048, 1024)], wd, lsem.at[2])]
        unit_load = pltpu.make_async_copy(part_hbm, db_term, lsem.at[3])
        a_load = pltpu.make_async_copy(a_hbm, a_rows, lsem.at[4])
        for c in [unit_load] + loads + [a_load]:
            c.start()
        two_acc[...] = jnp.zeros_like(two_acc)
        one_acc[...] = jnp.zeros_like(one_acc)
        q_acc[...] = jnp.zeros_like(q_acc)
        k_acc[...] = jnp.zeros_like(k_acc)

        def back(z, gain, up):
            inverse = lax.rsqrt(jnp.mean(z * z, axis=-1, keepdims=True) + epsilon)
            scaled = up * gain
            inner = jnp.mean(z * scaled, axis=-1, keepdims=True)
            return inverse * (scaled - z * inverse * inverse * inner), up * z * inverse

        meet([me.step("x", 1), me.step("x", -1), me.step("y", 1), me.step("y", -1),
              me.step("z", 1), me.step("z", -1), me.sibling()])
        w = Wire(send, recv)

        def put_a(s, v):
            db_sum[s, 0:1024] = v

        def put_b(s, v):
            db_sum[s, 1024:2048] = v

        def columns(k):
            c = pl.ds(1024 * k, 1024)
            return db_term.at[:, :, :, :, c], (put_a, put_b)[k], sibs_c.at[:, :, c], t_c.at[:, :, c], r_c.at[:, :, :, c]

        def out_block(i, _):
            at = pl.multiple_of(i * 256, 256)
            v = dot(hidden[...], wd[pl.ds(at, 256)], 1, 1).astype(bf16)
            out_part[:, :, :, :, pl.ds(at, 256)] = v.reshape(2, 2, 2, 128, 256)
            return 0
        unit_load.wait()
        gen_a, gen_b = [rs_z_gen(w, me, *columns(k)) for k in range(2)]
        next(gen_a)
        next(gen_b)
        next(gen_a)
        for c in loads:
            c.wait()
        lax.fori_loop(0, 1, out_block, 0)
        next(gen_b)
        lax.fori_loop(1, 4, out_block, 0)
        next(gen_a)
        lax.fori_loop(4, 6, out_block, 0)
        next(gen_b)
        lax.fori_loop(6, 8, out_block, 0)
        run([gen_a])
        run([gen_b])

        def norm_two(s):
            dz, terms = back(middle[s], gain_two, db_sum[s])
            v = cot[s].astype(f32) + dz
            mid_grad[s] = v
            shard[s] = v.astype(bf16)
            two_acc[...] += terms
        chunks(128, norm_two)
        gen = ag_z_gen(w, me, shard, dm_full)
        next(gen)
        own = pltpu.make_async_copy(shard, dm_full.at[me.h, me.c, me.l], lsem.at[0])
        own.start()

        def put_out(s, v):
            block_output[s] = middle[s] + v
        out_gen = rs_z_gen(w, me, out_part, put_out, sibs_a, t_a, r_a)
        next(gen)
        next(out_gen)
        run([gen])
        own.wait()

        def one_pack(p):
            allowed, cosine, sine = pack_tables(segs, p, table)
            mixed_grad = dot(pack_of(dm_full, p), front_full[:, :, :, 384:640].reshape(D, 256)).T.astype(bf16)
            value_rows = v_rows[p].astype(f32).T.astype(bf16)
            key_pre = qk_pre[p, 256:320]
            kn, k_inverse = head_norm(key_pre, gain_key)
            kr = turn(kn, cosine, sine)
            key_rows = kr.T.astype(bf16)
            kr = kr.astype(bf16)
            dk = jnp.zeros((HD, SEQ), f32)
            dv = jnp.zeros((HD, SEQ), f32)
            heads = []
            terms_q = jnp.zeros((HD, SEQ), f32)
            for j in range(4):
                query_pre = qk_pre[p, 64 * j:64 * j + 64]
                qn, q_inverse = head_norm(query_pre, gain_query)
                qr = turn(qn, cosine, sine).astype(bf16)
                probs = pack_probs(key_rows, qr, allowed)
                do = mixed_grad[64 * j:64 * j + 64]
                dp = dot(value_rows, do)
                inner = jnp.sum(probs * dp, axis=0, keepdims=True)
                ds = (probs * (dp - inner)).astype(bf16)
                dqr = dot(kr, ds) * score_scale
                dk += dot(qr, ds, 1, 1)
                dv += dot(do, probs.astype(bf16), 1, 1)
                dq, terms = head_norm_back(query_pre, q_inverse, gain_query, turn_back(dqr, cosine, sine))
                terms_q += terms
                heads.append(dq)
            dk, terms_k = head_norm_back(key_pre, k_inverse, gain_key, turn_back(dk * score_scale, cosine, sine))
            q_acc[...] += terms_q
            k_acc[...] += terms_k
            grads = jnp.concatenate(heads + [dk, dv], axis=0).T.astype(bf16)
            dqkv[p] = grads
            out = dot(grads, front_full[:, :, :, 0:384].reshape(D, 384), 1, 1).astype(bf16)
            part[lax.div(p, 2), lax.rem(p, 2)] = out.reshape(2, 128, D)
        def put_in(s, v):
            dz, terms = back(x[s].astype(f32), gain_one, v)
            input_grad[s] = mid_grad[s] + dz
            one_acc[...] += terms
        in_gen = rs_z_packs(w, me, part, put_in, sibs_b, t_b, r_b)
        next(out_gen)
        for i in range(4):
            dm_rows = dm_full[:, :, :, :, 512 * i:512 * i + 512].reshape(ROWS, 512)
            o_grad[i] = dot(dm_rows, mixed[...].reshape(ROWS, 256), 0, 0).astype(bf16).reshape(4, 128, 256)
        o_gens = rs_xy_gens(w, me, o_grad, o_mine, u1, s1, u2, s2, mid_o)

        def both(gens):
            for g in gens:
                next(g)
        both(o_gens)
        one_pack(pack_turn(me, 0))
        next(in_gen)
        both(o_gens)
        one_pack(pack_turn(me, 1))
        next(out_gen)
        next(in_gen)
        both(o_gens)
        both(o_gens)
        one_pack(pack_turn(me, 2))
        next(in_gen)
        both(o_gens)
        one_pack(pack_turn(me, 3))
        next(in_gen)
        a_load.wait()
        for i in range(4):
            g = dot(a_rows[:, 512 * i:512 * i + 512], dqkv[...].reshape(ROWS, 384), 0, 0)
            front_grad[i] = g.astype(bf16).reshape(4, 128, 384)
        qkv_gens = rs_xy_gens(w, me, front_grad, qkv_mine, t1, r1, t2, r2, mid)
        both(qkv_gens)
        run(o_gens)
        next(in_gen)
        both(qkv_gens)
        both(qkv_gens)
        both(qkv_gens)
        run([out_gen])
        both(qkv_gens)
        run([in_gen])
        run(qkv_gens)
        front_mine[:, 0:384] = qkv_mine[...]
        front_mine[:, 384:640] = o_mine[...]
        w.finish()
        one = jnp.sum(one_acc[...], axis=0, keepdims=True)
        two = jnp.sum(two_acc[...], axis=0, keepdims=True)
        for i in range(16):
            gain_terms[i:i + 1, :] = one[:, 128 * i:128 * i + 128]
            gain_terms[16 + i:17 + i, :] = two[:, 128 * i:128 * i + 128]
        small = jnp.concatenate([q_acc[...], k_acc[...]], axis=0).T
        gain_terms[32:33, :] = jnp.sum(small, axis=0, keepdims=True)

    full = (2, 2, 2, 128, D)
    rows = jax.ShapeDtypeStruct((128, D), f32)
    return pl.pallas_call(
        kernel,
        out_shape=[rows, rows, jax.ShapeDtypeStruct((128, 640), bf16), jax.ShapeDtypeStruct((33, 128), f32)],
        in_specs=vm_specs(3) + any_specs(4) + vm_specs(7), out_specs=vm_specs(4),
        scratch_shapes=[VM((128, D), bf16), VM((ROWS, 1024), bf16), VM((D, 1024), bf16), VM(full, bf16),
                        VM(full, bf16), VM((128, D), f32), VM((PACKS, SEQ, 384), bf16),
                        VM(full, bf16), VM((4, 4, 128, 384), bf16), VM((HD, SEQ), f32), VM((HD, SEQ), f32),
                        VM((16, D), f32), VM((16, D), f32)]
        + [VM((ROWS, D), bf16), VM(full, bf16), VM((128, D), f32), VM((4, 4, 128, 256), bf16),
           VM((128, 256), bf16), VM((128, 384), bf16)]
        + rs_z_scratch(D) * 3 + rs_xy_scratch(384) + rs_xy_scratch(256) + dma_sems(112)
        + [pltpu.SemaphoreType.DMA((5,))],
        compiler_params=params(cid, 60))(
            x, cot, middle, db_part, hidden, weights, a_full.reshape(ROWS, D), front_full, qk_pre, v_rows, mixed, segs,
            gains, table)


def adam(weight, moment, square, gradient, rate, decay):
    momentum = beta_one * moment + (1.0 - beta_one) * gradient
    variance = beta_two * square + (1.0 - beta_two) * gradient * gradient
    ratio = momentum / (1.0 - beta_one**STEP) / (jnp.sqrt(variance / (1.0 - beta_two**STEP)) + adam_epsilon)
    return weight - rate * (ratio + decay * weight), momentum, variance


RATES = (0.04, 0.04, 0.04, 0.15, 0.04, 0.04, 0.02)
SPANS = (256, 64, 64, 256, 1024, 1024, 1024)


def return_gradients(front, rest, gain_terms, cid):
    def kernel(front, rest, terms, fbuf, rbuf, gain_sum, z_in, x_in, y_in, send, recv):
        me = Place()
        peers = swap_devs(me)
        mine = me.h * 2 + me.c
        zs = [me.at(z=m4(me.z + dz), c=lax.rem(me.c + dc, 2)) for dz in range(4) for dc in range(2) if dz or dc]
        xs = [me.step("x", d) for d in (1, 2, 3)]
        ys = [me.step("y", d) for d in (1, 2, 3)]
        meet(zs + xs + ys)
        w = Wire(send, recv)

        def total(buf, n):
            v = buf[0]
            for k in range(1, n):
                v = v + buf[k]
            return v

        def share(value, buf, slot, devs):
            buf[slot] = value
            return [w.go(buf.at[slot], buf.at[slot], d) for d in devs]
        gs = share(terms[...], z_in, me.z * 2 + me.c, zs)
        arrivals = []
        for j, dev in reversed(peers):
            arrivals.append(w.go(front.at[j], fbuf.at[mine], dev))
            arrivals.append(w.go(rest.at[j], rbuf.at[mine], dev))
        fbuf[mine] = front[mine]
        rbuf[mine] = rest[mine]
        for c in gs:
            c.wait_recv()
        gs = share(total(z_in, 8), x_in, me.x, xs)
        for c in gs:
            c.wait_recv()
        gs = share(total(x_in, 4), y_in, me.y, ys)
        for c in gs:
            c.wait_recv()
        gain_sum[...] = total(y_in, 4)
        for a in arrivals:
            a.wait_recv()
        w.finish()

    return pl.pallas_call(
        kernel, out_shape=[jax.ShapeDtypeStruct((4, 32, 640), bf16), jax.ShapeDtypeStruct((4, 32, 3072), bf16),
                           jax.ShapeDtypeStruct((33, 128), f32)],
        in_specs=vm_specs(3), out_specs=vm_specs(3),
        scratch_shapes=[VM((8, 33, 128), f32), VM((4, 33, 128), f32), VM((4, 33, 128), f32)] + dma_sems(19),
        compiler_params=params(cid))(front, rest, gain_terms)


def update(front, rest, gain_sum, gain_states, states, tokens):
    def kernel(*refs):
        front, rest, g_sum, g_w, g_m, g_v = refs[:6]
        ins, t_in, g_out, outs, t_out = refs[6:27], refs[27:29], refs[29:32], refs[32:53], refs[53:55]
        held, made, kept = refs[55:76], refs[76:97], refs[97:99]
        lsem, osem, tsem = refs[99:]
        loads = [pltpu.make_async_copy(a, b, lsem.at[i]) for i, (a, b) in enumerate(zip(ins, held))]
        coming = [pltpu.make_async_copy(a, b, tsem.at[i]) for i, (a, b) in enumerate(zip(t_in, kept))]
        for c in loads + coming:
            c.start()
        new = adam(g_w[...], g_m[...], g_v[...], g_sum[...], gain_rate, 0.0)
        for ref, v in zip(g_out, new):
            ref[...] = v
        stores = []
        at = {False: 0, True: 0}
        for i, (n, rate) in enumerate(zip(SPANS, RATES)):
            late = i >= 4
            buf = rest if late else front
            for k in range(3):
                loads[3 * i + k].wait()
            for j in range(4):
                here = pl.ds(n * j, n)
                grad = buf[j, :, at[late]:at[late] + n].astype(f32)
                new = adam(held[3 * i][:, here], held[3 * i + 1][:, here], held[3 * i + 2][:, here], grad, rate,
                           weight_decay)
                for k in range(3):
                    made[3 * i + k][:, here] = new[k]
            at[late] += n
            for k in range(3):
                c = pltpu.make_async_copy(made[3 * i + k], outs[3 * i + k], osem.at[3 * i + k])
                c.start()
                stores.append(c)
        for i in range(2):
            coming[i].wait()
            c = pltpu.make_async_copy(kept[i], t_out[i], tsem.at[2 + i])
            c.start()
            stores.append(c)
        for c in stores:
            c.wait()

    shapes = [jax.ShapeDtypeStruct(s.shape, f32) for s in states]
    gain_shape = jax.ShapeDtypeStruct((33, 128), f32)
    return pl.pallas_call(
        kernel, out_shape=[gain_shape] * 3 + shapes + [jax.ShapeDtypeStruct(t.shape, f32) for t in tokens],
        in_specs=vm_specs(6) + any_specs(23), out_specs=vm_specs(3) + any_specs(23),
        scratch_shapes=[VM(s.shape, f32) for s in states] * 2 + [VM(t.shape, f32) for t in tokens]
        + [pltpu.SemaphoreType.DMA((21,)), pltpu.SemaphoreType.DMA((21,)), pltpu.SemaphoreType.DMA((4,))],
        compiler_params=pltpu.CompilerParams(has_side_effects=True, vmem_limit_bytes=56 * 2**20))(
            front, rest, gain_sum, *gain_states, *states, *tokens)


from jax.sharding import PartitionSpec as P

PLANE = [[x * 16 + y * 4 + k for x in range(4) for y in range(4)] for k in range(4)]


def scatter_plane(whole):
    return lax.psum_scatter(whole, "dp", axis_index_groups=PLANE, scatter_dimension=0, tiled=True)


def local(block_input, output_grad, segment_ids, norm_gains, gain_moment, gain_square, *states):
    square = lambda v: v.reshape(33, 128)
    gains = square(norm_gains)
    table = jnp.asarray(rope_constants())
    one_full, cot_full, two_full, rest_full, front_full, segments, qk_pre, v_rows, mixed, middle = attention_forward(
        block_input, output_grad, states[::3], segment_ids, gains, table, 2)
    rest_full = rest_full.reshape(D, 3072)
    rest_grad, hidden, db_part = feed_forward(two_full, cot_full, rest_full)
    rest_mine = scatter_plane(rest_grad)
    input_grad, block_output, front_mine, gain_terms = attention_backward(
        block_input, output_grad, middle, db_part, hidden, rest_full, one_full, front_full, qk_pre, v_rows, mixed, segments,
        gains, table, 4)
    front_back, rest_back, gain_sum = return_gradients(
        front_mine.reshape(4, 32, 640), rest_mine.reshape(4, 32, 3072), gain_terms, 5)
    news = update(front_back, rest_back, gain_sum, [gains, square(gain_moment), square(gain_square)], states,
                  (block_output, input_grad))
    return tuple(news[-2:]) + tuple(v.reshape(-1) for v in news[:3]) + tuple(news[3:-2])


def solution(mesh):
    tokens, weight = P(("dp", "tensor"), None), P("dp", "tensor")
    in_specs = (tokens, tokens, P("dp", None), P(), P(), P()) + (weight,) * 21
    out_specs = (tokens, tokens, P(), P(), P()) + (weight,) * 21
    return jax.shard_map(local, mesh=mesh, in_specs=in_specs, out_specs=out_specs, check_vma=False)
```

```python
import jax
import jax.numpy as jnp
import numpy as np
from jax import lax
from jax.experimental import pallas as pl
from jax.experimental.pallas import tpu as pltpu

MESH = pl.DeviceIdType.MESH
VM = pltpu.VMEM
bf16 = jnp.bfloat16
f32 = jnp.float32


def m4(v):
    return lax.rem(v + 4, 4)


class Place:
    def __init__(self):
        dp = lax.axis_index("dp")
        self.l = lax.axis_index("tensor")
        self.x = lax.div(dp, 16)
        self.y = lax.rem(lax.div(dp, 4), 4)
        self.h = lax.rem(lax.div(dp, 2), 2)
        self.c = lax.rem(dp, 2)
        self.z = self.h * 2 + self.l

    def at(self, x=None, y=None, z=None, c=None):
        x = self.x if x is None else x
        y = self.y if y is None else y
        z = self.z if z is None else z
        c = self.c if c is None else c
        return (x * 16 + y * 4 + lax.div(z, 2) * 2 + c, lax.rem(z, 2))

    def pos(self, axis):
        return {"x": self.x, "y": self.y, "z": self.z}[axis]

    def step(self, axis, d):
        return self.at(**{axis: m4(self.pos(axis) + d)})

    def sibling(self):
        return self.at(c=1 - self.c)


class Wire:
    def __init__(self, send, recv, first=0):
        self.send, self.recv, self.n = send, recv, first
        self.pending = []

    def go(self, src, dst, dev):
        i = self.n
        self.n += 1
        c = pltpu.make_async_remote_copy(
            src_ref=src, dst_ref=dst, send_sem=self.send.at[i], recv_sem=self.recv.at[i],
            device_id=dev, device_id_type=MESH)
        c.start()
        self.pending.append(c)
        return c

    def finish(self):
        for c in self.pending:
            c.wait_send()
        self.pending = []


def meet(devs):
    b = pltpu.get_barrier_semaphore()
    for d in devs:
        pl.semaphore_signal(b, inc=1, device_id=d, device_id_type=MESH)
    pl.semaphore_wait(b, len(devs))


def ring_gather(w, me, axis, whole, lo, hi, first=None, arrived=None):
    p = me.pos(axis)
    up, down = me.step(axis, 1), me.step(axis, -1)
    own = whole(p) if first is None else first
    a = w.go(own, whole(p), up)
    b = w.go(own, whole(p), down)
    yield
    a.wait_recv()
    fa = w.go(lo(m4(p - 1)), lo(m4(p - 1)), up)
    if arrived:
        arrived(whole(m4(p - 1)))
    b.wait_recv()
    fb = w.go(hi(m4(p + 1)), hi(m4(p + 1)), down)
    if arrived:
        arrived(whole(m4(p + 1)))
    yield
    fa.wait_recv()
    if arrived:
        arrived(lo(m4(p - 2)))
    fb.wait_recv()
    if arrived:
        arrived(hi(m4(p - 2)))


def ring_scatter(w, me, axis, lo, hi, tlo, thi, rup, rdown, add):
    p = me.pos(axis)
    up, down = me.step(axis, 1), me.step(axis, -1)
    far, nu, nd = m4(p + 2), m4(p + 1), m4(p - 1)
    ta = w.go(lo(far), tlo, up)
    tb = w.go(hi(far), thi, down)
    da = w.go(hi(nu), rup[1], up)
    db = w.go(lo(nd), rdown[0], down)
    yield
    ta.wait_recv()
    add(tlo, lo(nu))
    sa = w.go(tlo, rup[0], up)
    tb.wait_recv()
    add(thi, hi(nd))
    sb = w.go(thi, rdown[1], down)
    yield
    da.wait_recv()
    db.wait_recv()
    sa.wait_recv()
    sb.wait_recv()


def loop_add(dst, a, b=None, rows=16):
    n = dst.shape[0]

    def body(i, _):
        def inner(j, _):
            s = pl.ds(pl.multiple_of(j * rows, rows), rows)
            v = dst[i, s].astype(f32) + a[i, s].astype(f32)
            if b is not None:
                v = v + b[i, s].astype(f32)
            dst[i, s] = v.astype(dst.dtype)
            return 0
        return lax.fori_loop(0, dst.shape[1] // rows, inner, 0)
    lax.fori_loop(0, n, body, 0)


def run(gens):
    gens = list(gens)
    while gens:
        for g in list(gens):
            try:
                next(g)
            except StopIteration:
                gens.remove(g)


def params(cid, mb=56):
    return pltpu.CompilerParams(collective_id=cid, has_side_effects=True, vmem_limit_bytes=mb * 2**20)


def ag_xy_gens(w, me, src, out):
    H = 64
    x, y = me.x, me.y

    def half_a():
        yield from ring_gather(w, me, "x", lambda i: out.at[i, y, pl.ds(0, 64)], lambda i: out.at[i, y, pl.ds(0, 32)],
                               lambda i: out.at[i, y, pl.ds(32, 32)], first=src.at[pl.ds(0, 64)])
        yield
        yield from ring_gather(w, me, "y", lambda i: out.at[:, i, pl.ds(0, 64)], lambda i: out.at[:, i, pl.ds(0, 32)],
                               lambda i: out.at[:, i, pl.ds(32, 32)])

    def half_b():
        yield from ring_gather(w, me, "y", lambda i: out.at[x, i, pl.ds(64, 64)], lambda i: out.at[x, i, pl.ds(64, 32)],
                               lambda i: out.at[x, i, pl.ds(96, 32)], first=src.at[pl.ds(64, 64)])
        yield
        yield from ring_gather(w, me, "x", lambda i: out.at[i, :, pl.ds(64, 64)], lambda i: out.at[i, :, pl.ds(64, 32)],
                               lambda i: out.at[i, :, pl.ds(96, 32)])
    return [half_a(), half_b()]


def ag_xy(shard, cid, space=pl.ANY):
    C = shard.shape[1]

    def kernel(src, out, send, recv, lsem):
        me = Place()
        meet([me.step("x", 1), me.step("x", -1), me.step("y", 1), me.step("y", -1)])
        w = Wire(send, recv)
        lc = pltpu.make_async_copy(src, out.at[me.x, me.y], lsem)
        lc.start()
        lc.wait()
        run(ag_xy_gens(w, me, src, out))
        w.finish()

    return pl.pallas_call(
        kernel, out_shape=jax.ShapeDtypeStruct((4, 4, 128, C), shard.dtype),
        in_specs=[pl.BlockSpec(memory_space=space)], out_specs=pl.BlockSpec(memory_space=space),
        scratch_shapes=[pltpu.SemaphoreType.DMA((16,)), pltpu.SemaphoreType.DMA((16,)), pltpu.SemaphoreType.DMA],
        compiler_params=params(cid))(shard)


def rs_xy_scratch(C):
    return [VM((2, 2, 4, 32, C), bf16), VM((2, 2, 2, 4, 32, C), bf16),
            VM((2, 2, 32, C), bf16), VM((2, 2, 2, 32, C), bf16), VM((2, 4, 64, C), bf16)]


def rs_xy_gens(w, me, g, out, t1, r1, t2, r2, mid):
    x, y = me.x, me.y

    def half(k, first, second):
        base = k * 64
        if first == "y":
            pick = lambda i, o: g.at[:, i, pl.ds(base + o, 32)]
        else:
            pick = lambda i, o: g.at[i, :, pl.ds(base + o, 32)]
        yield from ring_scatter(w, me, first, lambda i: pick(i, 0), lambda i: pick(i, 32), t1.at[k, 0], t1.at[k, 1],
                                (r1.at[k, 0, 0], r1.at[k, 0, 1]), (r1.at[k, 1, 0], r1.at[k, 1, 1]), loop_add)
        p = me.pos(first)
        m = mid.at[k]
        for hh in range(2):
            own = pick(p, 32 * hh)

            def body(i, _):
                def inner(j, _):
                    s = pl.ds(pl.multiple_of(j * 16, 16), 16)
                    d = pl.ds(pl.multiple_of(j * 16 + 32 * hh, 16), 16)
                    v = own[i, s].astype(f32) + r1[k, 0, hh, i, s].astype(f32) + r1[k, 1, hh, i, s].astype(f32)
                    m[i, d] = v.astype(bf16)
                    return 0
                return lax.fori_loop(0, 2, inner, 0)
            lax.fori_loop(0, 4, body, 0)
        yield
        q = me.pos(second)
        add1 = lambda dst, a: loop_add(dst, a)
        pick2 = lambda i, o: mid.at[k, i, pl.ds(o, 32)]

        def add2(dst, a):
            def inner(j, _):
                s = pl.ds(pl.multiple_of(j * 16, 16), 16)
                dst[s] = (dst[s].astype(f32) + a[s].astype(f32)).astype(bf16)
                return 0
            lax.fori_loop(0, 2, inner, 0)
        yield from ring_scatter(w, me, second, lambda i: pick2(i, 0), lambda i: pick2(i, 32), t2.at[k, 0], t2.at[k, 1],
                                (r2.at[k, 0, 0], r2.at[k, 0, 1]), (r2.at[k, 1, 0], r2.at[k, 1, 1]), add2)
        for hh in range(2):
            def inner(j, _):
                s = pl.ds(pl.multiple_of(j * 16, 16), 16)
                d = pl.ds(pl.multiple_of(j * 16 + 32 * hh, 16), 16)
                dd = pl.ds(pl.multiple_of(j * 16 + 32 * hh + base, 16), 16)
                v = m[q, d].astype(f32) + r2[k, 0, hh, s].astype(f32) + r2[k, 1, hh, s].astype(f32)
                out[dd] = v.astype(out.dtype)
                return 0
            lax.fori_loop(0, 2, inner, 0)
    return [half(0, "y", "x"), half(1, "x", "y")]


def rs_xy(g, cid, out_dtype=f32):
    C = g.shape[-1]

    def kernel(gin, out, send, recv, *scr):
        me = Place()
        meet([me.step("x", 1), me.step("x", -1), me.step("y", 1), me.step("y", -1)])
        w = Wire(send, recv)
        run(rs_xy_gens(w, me, gin, out, *scr))
        w.finish()

    return pl.pallas_call(
        kernel, out_shape=jax.ShapeDtypeStruct((128, C), out_dtype),
        in_specs=[pl.BlockSpec(memory_space=VM)], out_specs=pl.BlockSpec(memory_space=VM),
        scratch_shapes=[pltpu.SemaphoreType.DMA((24,)), pltpu.SemaphoreType.DMA((24,))] + rs_xy_scratch(C),
        compiler_params=params(cid, 60))(g)


def ag_z_gen(w, me, src, out, r0=0, n=128):
    sib = me.sibling()
    blk = lambda i, cc: out.at[lax.div(i, 2), cc, lax.rem(i, 2)]
    cs = []

    def to_sib(ref):
        cs.append(w.go(ref, ref, sib))
    whole = lambda i: blk(i, me.c).at[pl.ds(r0, n)]
    lo = lambda i: blk(i, me.c).at[pl.ds(r0, n // 2)]
    hi = lambda i: blk(i, me.c).at[pl.ds(r0 + n // 2, n // 2)]
    own = w.go(src, whole(me.z), sib)
    yield from ring_gather(w, me, "z", whole, lo, hi, first=src, arrived=to_sib)
    own.wait_recv()
    for c in cs:
        c.wait_recv()


def ag_z(shard, cid, space=VM):
    C = shard.shape[1]

    def kernel(src, out, send, recv, lsem):
        me = Place()
        meet([me.step("z", 1), me.step("z", -1), me.sibling()])
        w = Wire(send, recv)
        lc = pltpu.make_async_copy(src, out.at[me.h, me.c, me.l], lsem)
        lc.start()
        lc.wait()
        run([ag_z_gen(w, me, src, out)])
        w.finish()

    return pl.pallas_call(
        kernel, out_shape=jax.ShapeDtypeStruct((2, 2, 2, 128, C), shard.dtype),
        in_specs=[pl.BlockSpec(memory_space=space)], out_specs=pl.BlockSpec(memory_space=space),
        scratch_shapes=[pltpu.SemaphoreType.DMA((16,)), pltpu.SemaphoreType.DMA((16,)), pltpu.SemaphoreType.DMA],
        compiler_params=params(cid))(shard)


def rs_z_scratch(C):
    return [VM((4, 128, C), bf16), VM((2, 64, C), bf16), VM((2, 2, 64, C), bf16)]


def rs_z_gen(w, me, g, out, sibs, t, r):
    sib = me.sibling()
    oc = 1 - me.c
    order = [2, 1, 3, 0]
    blk = lambda i, cc: g.at[lax.div(i, 2), cc, lax.rem(i, 2)]
    z = me.z
    sc = {}
    for o in order:
        i = m4(z + o)
        sc[o] = w.go(blk(i, oc), sibs.at[i], sib)
    yield

    def fold(o, s0, n):
        i = m4(z + o)
        b = blk(i, me.c)

        def inner(j, _):
            s = pl.ds(pl.multiple_of(j * 16 + s0, 16), 16)
            sibs[i, s] = (sibs[i, s].astype(f32) + b[s].astype(f32)).astype(bf16)
            return 0
        lax.fori_loop(0, n // 16, inner, 0)
    up, down = me.step("z", 1), me.step("z", -1)
    half = lambda o, k: sibs.at[m4(z + o), pl.ds(64 * k, 64)]
    sc[2].wait_recv()
    fold(2, 0, 64)
    ta = w.go(half(2, 0), t.at[0], up)
    fold(2, 64, 64)
    tb = w.go(half(2, 1), t.at[1], down)
    sc[1].wait_recv()
    fold(1, 64, 64)
    da = w.go(half(1, 1), r.at[0, 1], up)
    sc[3].wait_recv()
    fold(3, 0, 64)
    db = w.go(half(3, 0), r.at[1, 0], down)
    fold(1, 0, 64)
    fold(3, 64, 64)
    yield

    def add(dst, a):
        def inner(j, _):
            s = pl.ds(pl.multiple_of(j * 16, 16), 16)
            dst[s] = (dst[s].astype(f32) + a[s].astype(f32)).astype(bf16)
            return 0
        lax.fori_loop(0, 4, inner, 0)
    ta.wait_recv()
    add(t.at[0], half(1, 0))
    sa = w.go(t.at[0], r.at[0, 0], up)
    tb.wait_recv()
    add(t.at[1], half(3, 1))
    sb = w.go(t.at[1], r.at[1, 1], down)
    sc[0].wait_recv()
    own = blk(z, me.c)
    yield

    def last(hh):
        def inner(j, _):
            s = pl.ds(pl.multiple_of(j * 16, 16), 16)
            d = pl.ds(pl.multiple_of(j * 16 + 64 * hh, 16), 16)
            v = own[d].astype(f32) + sibs[z, d].astype(f32) + r[0, hh, s].astype(f32) + r[1, hh, s].astype(f32)
            out(d, v)
            return 0
        lax.fori_loop(0, 4, inner, 0)
    da.wait_recv()
    sa.wait_recv()
    db.wait_recv()
    sb.wait_recv()
    last(0)
    last(1)


def rs_z(g, cid, out_dtype=f32):
    C = g.shape[-1]

    def kernel(gin, out, send, recv, *scr):
        me = Place()
        meet([me.step("z", 1), me.step("z", -1), me.sibling()])
        w = Wire(send, recv)

        def put(s, v):
            out[s] = v.astype(out.dtype)
        run([rs_z_gen(w, me, gin, put, *scr)])
        w.finish()

    return pl.pallas_call(
        kernel, out_shape=jax.ShapeDtypeStruct((128, C), out_dtype),
        in_specs=[pl.BlockSpec(memory_space=VM)], out_specs=pl.BlockSpec(memory_space=VM),
        scratch_shapes=[pltpu.SemaphoreType.DMA((16,)), pltpu.SemaphoreType.DMA((16,))] + rs_z_scratch(C),
        compiler_params=params(cid))(g)


def swap_devs(me):
    out = []
    for dh, dc in ((0, 1), (1, 0), (1, 1)):
        h = lax.rem(me.h + dh, 2)
        c = lax.rem(me.c + dc, 2)
        out.append((h * 2 + c, me.at(z=h * 2 + me.l, c=c)))
    return out


def swap_hc(parts, cid):
    n = len(parts)

    def kernel(*refs):
        ins, outs = refs[:n], refs[n:2 * n]
        send, recv, lsem = refs[2 * n:]
        me = Place()
        peers = swap_devs(me)
        meet([d for _, d in peers])
        w = Wire(send, recv)
        mine = me.h * 2 + me.c
        arrivals = []
        for j, d in reversed(peers):
            for a, b in zip(ins, outs):
                arrivals.append(w.go(a.at[j], b.at[mine], d))
        ls = []
        for k, (a, b) in enumerate(zip(ins, outs)):
            lc = pltpu.make_async_copy(a.at[mine], b.at[mine], lsem.at[k])
            lc.start()
            ls.append(lc)
        for lc in ls:
            lc.wait()
        for a in arrivals:
            a.wait_recv()
        w.finish()

    return pl.pallas_call(
        kernel, out_shape=[jax.ShapeDtypeStruct(p.shape, p.dtype) for p in parts],
        in_specs=[pl.BlockSpec(memory_space=VM)] * n, out_specs=[pl.BlockSpec(memory_space=VM)] * n,
        scratch_shapes=[pltpu.SemaphoreType.DMA((3 * n,)), pltpu.SemaphoreType.DMA((3 * n,)),
                        pltpu.SemaphoreType.DMA((n,))],
        compiler_params=params(cid))(*parts)


def sum_all(v, cid):
    R, C = v.shape

    def kernel(src, out, z_in, x_in, y_in, acc, send, recv):
        me = Place()
        zs = []
        for dz in range(4):
            for dc in range(2):
                if dz or dc:
                    z, c = m4(me.z + dz), lax.rem(me.c + dc, 2)
                    zs.append(me.at(z=z, c=c))
        xs = [me.step("x", d) for d in (1, 2, 3)]
        ys = [me.step("y", d) for d in (1, 2, 3)]
        meet(zs + xs + ys)
        w = Wire(send, recv)
        acc[...] = src[...]
        for buf, slot, devs, n in ((z_in, me.z * 2 + me.c, zs, 8), (x_in, me.x, xs, 4), (y_in, me.y, ys, 4)):
            buf[slot] = acc[...]
            cs = [w.go(buf.at[slot], buf.at[slot], d) for d in devs]
            for c in cs:
                c.wait_recv()
            total = buf[0]
            for k in range(1, n):
                total = total + buf[k]
            w.finish()
            acc[...] = total
        out[...] = acc[...]

    return pl.pallas_call(
        kernel, out_shape=jax.ShapeDtypeStruct((R, C), f32),
        in_specs=[pl.BlockSpec(memory_space=VM)], out_specs=pl.BlockSpec(memory_space=VM),
        scratch_shapes=[VM((8, R, C), f32), VM((4, R, C), f32), VM((4, R, C), f32), VM((R, C), f32),
                        pltpu.SemaphoreType.DMA((13,)), pltpu.SemaphoreType.DMA((13,))],
        compiler_params=params(cid))(v)


def rs_z_packs(w, me, g, put, sibs, t, r):
    sib, oc, z = me.sibling(), 1 - me.c, me.z
    blk = lambda i, cc: g.at[lax.div(i, 2), cc, lax.rem(i, 2)]
    far = m4(z + 2)
    flip = lambda i: i + 1 - 2 * lax.rem(i, 2)
    beside, partner = flip(far), flip(z)
    up, down = me.step("z", 1), me.step("z", -1)
    half = lambda i, k: sibs.at[i, pl.ds(64 * k, 64)]

    def fold(i, s0, n):
        b = blk(i, me.c)

        def inner(j, _):
            s = pl.ds(pl.multiple_of(j * 16 + s0, 16), 16)
            sibs[i, s] = (sibs[i, s].astype(f32) + b[s].astype(f32)).astype(bf16)
            return 0
        lax.fori_loop(0, n // 16, inner, 0)

    def add(dst, a):
        def inner(j, _):
            s = pl.ds(pl.multiple_of(j * 16, 16), 16)
            dst[s] = (dst[s].astype(f32) + a[s].astype(f32)).astype(bf16)
            return 0
        lax.fori_loop(0, 4, inner, 0)
    s_far = w.go(blk(far, oc), sibs.at[far], sib)
    s_beside = w.go(blk(beside, oc), sibs.at[beside], sib)
    yield
    s_far.wait_recv()
    fold(far, 0, 64)
    ta = w.go(half(far, 0), t.at[0], up)
    fold(far, 64, 64)
    tb = w.go(half(far, 1), t.at[1], down)
    s_beside.wait_recv()
    fold(beside, 0, 128)
    yield
    s_partner = w.go(blk(partner, oc), sibs.at[partner], sib)
    s_own = w.go(blk(z, oc), sibs.at[z], sib)
    yield
    s_partner.wait_recv()
    fold(partner, 0, 128)
    nu, nd = m4(z + 1), m4(z - 1)
    da = w.go(half(nu, 1), r.at[0, 1], up)
    db = w.go(half(nd, 0), r.at[1, 0], down)
    yield
    ta.wait_recv()
    add(t.at[0], half(nu, 0))
    sa = w.go(t.at[0], r.at[0, 0], up)
    tb.wait_recv()
    add(t.at[1], half(nd, 1))
    sb = w.go(t.at[1], r.at[1, 1], down)
    s_own.wait_recv()
    own = blk(z, me.c)
    yield

    def last(hh):
        def inner(j, _):
            s = pl.ds(pl.multiple_of(j * 16, 16), 16)
            d = pl.ds(pl.multiple_of(j * 16 + 64 * hh, 16), 16)
            put(d, own[d].astype(f32) + sibs[z, d].astype(f32) + r[0, hh, s].astype(f32) + r[1, hh, s].astype(f32))
            return 0
        lax.fori_loop(0, 4, inner, 0)
    da.wait_recv()
    sa.wait_recv()
    db.wait_recv()
    sb.wait_recv()
    last(0)
    last(1)


D = 2048
HD = 64
STEP = 10
SEQ = 256
PACKS = 4
ROWS = 1024
epsilon = 1e-06
rope_base = 1000000.0
beta_one = 0.9
beta_two = 0.999
adam_epsilon = 1e-08
weight_decay = 0.1
gain_rate = 0.3
masked_score = -1000000000.0
score_scale = HD ** (-0.5)
exact = lax.Precision.HIGHEST


def dot(a, b, ca=1, cb=0, precision=None):
    return lax.dot_general(a, b, (((ca,), (cb,)), ((), ())), precision=precision, preferred_element_type=f32)


def chunks(n, body, rows=16):
    def one(j, _):
        body(pl.ds(pl.multiple_of(j * rows, rows), rows))
        return 0
    lax.fori_loop(0, n // rows, one, 0)


def dma_sems(n):
    return [pltpu.SemaphoreType.DMA((n,)), pltpu.SemaphoreType.DMA((n,))]


def vm_specs(n):
    return [pl.BlockSpec(memory_space=VM)] * n


def any_specs(n):
    return [pl.BlockSpec(memory_space=pl.ANY)] * n


class Columns:
    def __init__(self, ref, n):
        self.ref, self.n = ref, n

    def __getitem__(self, j):
        return self.ref[:, pl.ds(pl.multiple_of(j * self.n, self.n), self.n)]


def gain_rows(gains):
    one = jnp.concatenate([gains[i:i + 1, :] for i in range(16)], axis=1)
    two = jnp.concatenate([gains[16 + i:17 + i, :] for i in range(16)], axis=1)
    small = jnp.broadcast_to(gains[32:33, :], (128, 128)).T
    return one, two, small[0:64, 0:1], small[64:128, 0:1]


def rope_constants():
    frequency = np.float32(rope_base) ** (np.float32(-2.0) * np.arange(HD // 2, dtype=np.float32) / np.float32(HD))
    angles = (np.arange(SEQ, dtype=np.float32)[None, :] * frequency[:, None].astype(np.float32)).astype(np.float64)
    return np.concatenate([np.cos(angles), np.sin(angles)], axis=0).astype(np.float32)


def pack_tables(segs, p, table):
    row = segs[p].astype(f32)[0:1, :]
    column = jnp.broadcast_to(row, (128, SEQ)).T[:, 0:1]
    key_at = lax.broadcasted_iota(jnp.int32, (SEQ, SEQ), 0)
    query_at = lax.broadcasted_iota(jnp.int32, (SEQ, SEQ), 1)
    allowed = (column == row) & (key_at <= query_at)
    start = jnp.sum(jnp.where(column < row, 1.0, 0.0), axis=0, keepdims=True)
    where = query_at.astype(f32) - start
    hot = jnp.where(key_at.astype(f32) == where, 1.0, 0.0)
    both = dot(table[...], hot, precision=exact)
    return allowed, both[0:32], both[32:64]


def head_norm(z, gain):
    inverse = lax.rsqrt(jnp.mean(z * z, axis=0, keepdims=True) + epsilon)
    return z * inverse * gain, inverse


def head_norm_back(z, inverse, gain, up):
    scaled = up * gain
    inner = jnp.mean(z * scaled, axis=0, keepdims=True)
    return inverse * (scaled - z * inverse * inverse * inner), up * z * inverse


def turn(u, cosine, sine):
    a, b = u[0:32], u[32:64]
    return jnp.concatenate([a * cosine - b * sine, b * cosine + a * sine], axis=0)


def turn_back(u, cosine, sine):
    a, b = u[0:32], u[32:64]
    return jnp.concatenate([a * cosine + b * sine, b * cosine - a * sine], axis=0)


def pack_probs(key_rows, query_rot, allowed):
    scores = jnp.where(allowed, dot(key_rows, query_rot) * score_scale, masked_score)
    exps = jnp.exp(scores - jnp.max(scores, axis=0, keepdims=True))
    return exps / jnp.sum(exps, axis=0, keepdims=True)


def pack_of(ref, p):
    v = ref[lax.div(p, 2), lax.rem(p, 2)]
    return v.reshape(SEQ, v.shape[-1])


def pack_turn(me, i):
    h = me.h if i >= 2 else 1 - me.h
    c = me.c if i % 2 else 1 - me.c
    return h * 2 + c


def attention_forward(x, cot, weights, seg, gains, table, cid):
    def kernel(x, cot, q_, k_, v_, o_, g_, u_, d_, seg, gains, table,
               a_full, cot_full, n_full, rest_full, front_full, segs, qk_pre, v_rows, mixed, middle,
               fbuf, rbuf, sbuf, kv, fshard, rshard, rest, shard, shard_two, a_buf, part, sibs, t, r,
               send, recv, lsem, ksem):
        me = Place()
        gain_one, gain_two, gain_query, gain_key = gain_rows(gains)
        peers = swap_devs(me)
        mine = me.h * 2 + me.c
        q, o = Columns(q_, 256), Columns(o_, 256)
        g, u, d = Columns(g_, 1024), Columns(u_, 1024), Columns(d_, 1024)
        for j in range(4):
            kv[j] = jnp.concatenate([k_[:, 64 * j:64 * j + 64], v_[:, 64 * j:64 * j + 64]], axis=1)
        sbuf[...] = jnp.broadcast_to(seg[...], (8, SEQ))
        here = pl.ds(pl.multiple_of(mine * 32, 32), 32)

        def round_front(j, dst):
            dst[:, 0:256] = q[j].astype(bf16)
            dst[:, 256:384] = kv[j].astype(bf16)
            dst[:, 384:640] = o[j].astype(bf16)

        def round_rest(j, dst):
            for i, w in enumerate((g, u, d)):
                dst[:, 1024 * i:1024 * i + 1024] = w[j].astype(bf16)
        meet([me.step("x", 1), me.step("x", -1), me.step("y", 1), me.step("y", -1),
              me.step("z", 1), me.step("z", -1)] + [dev for _, dev in peers])
        w = Wire(send, recv)
        first, second = [], []
        for j, dev in reversed(peers):
            round_front(j, fbuf.at[j])
            first.append(w.go(fbuf.at[j], fshard.at[here], dev))
            second.append(w.go(sbuf, segs.at[mine], dev))
        for j, dev in reversed(peers):
            round_rest(j, rbuf.at[j])
            second.append(w.go(rbuf.at[j], rshard.at[here], dev))
        round_front(mine, fshard.at[here])
        round_rest(mine, rshard.at[here])
        segs[mine] = sbuf[...]

        def norm_one(s):
            v = x[s].astype(f32)
            inverse = lax.rsqrt(jnp.mean(v * v, axis=-1, keepdims=True) + epsilon)
            shard[s] = (v * inverse * gain_one).astype(bf16)
        chunks(128, norm_one)
        for c in first:
            c.wait_recv()

        def both(gens):
            for g in gens:
                next(g)
        front_gens = ag_xy_gens(w, me, fshard, front_full)
        both(front_gens)
        gz = ag_z_gen(w, me, shard, a_buf)
        next(gz)
        locals_ = [pltpu.make_async_copy(fshard, front_full.at[me.x, me.y], lsem.at[0]),
                   pltpu.make_async_copy(shard, a_buf.at[me.h, me.c, me.l], lsem.at[1]),
                   pltpu.make_async_copy(cot, cot_full.at[me.h, me.c, me.l], lsem.at[2])]
        for c in locals_:
            c.start()
        both(front_gens)
        for c in locals_:
            c.wait()
        both(front_gens)
        both(front_gens)
        for c in second:
            c.wait_recv()
        rest_gens = ag_xy_gens(w, me, rshard, rest)
        both(rest_gens)
        own = pltpu.make_async_copy(rshard, rest.at[me.x, me.y], lsem.at[3])
        own.start()
        both(front_gens)
        both(rest_gens)
        own.wait()
        run(front_gens)
        both(rest_gens)
        both(rest_gens)
        next(gz)
        run([gz])
        cot_gen = ag_z_gen(w, me, cot.at[pl.ds(0, 64)], cot_full, 0, 64)
        next(cot_gen)
        keep = pltpu.make_async_copy(a_buf, a_full, lsem.at[4])
        keep.start()

        def one_pack(p):
            allowed, cosine, sine = pack_tables(segs, p, table)
            qkv = dot(pack_of(a_buf, p), front_full[:, :, :, 0:384].reshape(D, 384)).T
            qk_pre[p] = qkv[0:320]
            value = qkv[320:384].astype(bf16)
            v_rows[p] = value
            kn, _i = head_norm(qkv[256:320], gain_key)
            key_rows = turn(kn, cosine, sine).T.astype(bf16)
            heads = []
            for j in range(4):
                qn, _i = head_norm(qkv[64 * j:64 * j + 64], gain_query)
                probs = pack_probs(key_rows, turn(qn, cosine, sine).astype(bf16), allowed)
                heads.append(dot(value, probs.astype(bf16)))
            o = jnp.concatenate(heads, axis=0).T.astype(bf16)
            mixed[p] = o
            out = dot(o, front_full[:, :, :, 384:640].reshape(D, 256), 1, 1).astype(bf16)
            part[lax.div(p, 2), lax.rem(p, 2)] = out.reshape(2, 128, D)

        def residual(s, v):
            middle[s] = x[s].astype(f32) + v
        sum_gen = rs_z_packs(w, me, part, residual, sibs, t, r)
        for i in range(4):
            one_pack(pack_turn(me, i))
            next(sum_gen)
            if i == 2:
                next(cot_gen)
        both(rest_gens)
        run([sum_gen])

        def norm_two(s):
            v = middle[s]
            inverse = lax.rsqrt(jnp.mean(v * v, axis=-1, keepdims=True) + epsilon)
            shard_two[s] = (v * inverse * gain_two).astype(bf16)
        chunks(128, norm_two)
        n_gen = ag_z_gen(w, me, shard_two, n_full)
        next(n_gen)
        own = pltpu.make_async_copy(shard_two, n_full.at[me.h, me.c, me.l], lsem.at[3])
        own.start()
        run([cot_gen])
        stores = []

        def store(k, a, b, at):
            here = pl.ds(at, 64)
            c = pltpu.make_async_copy(rest.at[a, b, here], rest_full.at[a, b, here], ksem.at[k])
            c.start()
            stores.append(c)
        every = slice(None)
        for k in (0, 1, 3):
            store(k, every, m4(me.y + k), 0)
            store(4 + k, m4(me.x + k), every, 64)
        next(n_gen)
        cot_gen = ag_z_gen(w, me, cot.at[pl.ds(64, 64)], cot_full, 64, 64)
        next(cot_gen)
        run([n_gen])
        run(rest_gens)
        store(2, every, m4(me.y + 2), 0)
        store(6, m4(me.x + 2), every, 64)
        run([cot_gen])
        own.wait()
        keep.wait()
        for c in stores:
            c.wait()
        w.finish()

    full = jax.ShapeDtypeStruct((2, 2, 2, 128, D), bf16)
    return pl.pallas_call(
        kernel,
        out_shape=[full, full, full, jax.ShapeDtypeStruct((4, 4, 128, 3072), bf16),
                   jax.ShapeDtypeStruct((4, 4, 128, 640), bf16), jax.ShapeDtypeStruct((4, 8, SEQ), jnp.int32),
                   jax.ShapeDtypeStruct((PACKS, 320, SEQ), f32), jax.ShapeDtypeStruct((PACKS, HD, SEQ), bf16),
                   jax.ShapeDtypeStruct((PACKS, SEQ, 256), bf16), jax.ShapeDtypeStruct((128, D), f32)],
        in_specs=vm_specs(12), out_specs=any_specs(4) + vm_specs(6),
        scratch_shapes=[VM((4, 32, 640), bf16), VM((4, 32, 3072), bf16), VM((8, SEQ), jnp.int32), VM((4, 32, 128), f32),
                        VM((128, 640), bf16), VM((128, 3072), bf16), VM((4, 4, 128, 3072), bf16)]
        + [VM((128, D), bf16)] * 2 + [VM((2, 2, 2, 128, D), bf16)] * 2 + rs_z_scratch(D)
        + dma_sems(96) + [pltpu.SemaphoreType.DMA((5,)), pltpu.SemaphoreType.DMA((8,))],
        compiler_params=params(cid, 58))(x, cot, *weights, seg, gains, table)


def sigmoid(v):
    return 1.0 / (1.0 + jnp.exp(-v))


def feed_forward(n_full, cot_full, weights):
    def kernel(n_hbm, cot_hbm, w_hbm, grad_hbm, hidden_hbm, part_hbm,
               n, cot, w, hidden, gate_up, part, grad, lsem, wsem, gsem):
        loads = [pltpu.make_async_copy(n_hbm, n, lsem.at[0]), pltpu.make_async_copy(cot_hbm, cot, lsem.at[1])]
        loads[0].start()

        def piece(i, k):
            here = pl.ds(pl.multiple_of(i * 256 + 1024 * k, 256), 256)
            return pltpu.make_async_copy(w_hbm.at[:, here], w.at[:, here], wsem.at[i, k])
        for i in range(4):
            for k in range(3):
                piece(i, k).start()
            if i == 0:
                loads[1].start()
        for c in loads:
            c.wait()

        def hidden_block(i, _):
            at = pl.multiple_of(i * 256, 256)
            for k in range(3):
                piece(i, k).wait()
            rows = n[...].reshape(ROWS, D)
            g = dot(rows, w[:, pl.ds(at, 256)])
            u = dot(rows, w[:, pl.ds(at + 1024, 256)])
            dh = dot(cot[...].reshape(ROWS, D), w[:, pl.ds(at + 2048, 256)])
            s = sigmoid(g)
            silu = g * s
            hidden[:, pl.ds(at, 256)] = (silu * u).astype(bf16)
            gate_up[:, pl.ds(at, 256)] = (dh * u * (s + silu * (1.0 - s))).astype(bf16)
            gate_up[:, pl.ds(at + 1024, 256)] = (dh * silu).astype(bf16)
            return 0
        lax.fori_loop(0, 4, hidden_block, 0)
        keep = [pltpu.make_async_copy(hidden, hidden_hbm, lsem.at[2]), pltpu.make_async_copy(part, part_hbm, lsem.at[3])]
        keep[0].start()

        def back_block(i, _):
            at = pl.multiple_of(i * 256, 256)
            v = dot(gate_up[...], w[pl.ds(at, 256), 0:2048], 1, 1).astype(bf16)
            part[:, :, :, :, pl.ds(at, 256)] = v.reshape(2, 2, 2, 128, 256)
            return 0
        lax.fori_loop(0, 8, back_block, 0)
        keep[1].start()
        stores = []
        for i in range(4):
            at = 512 * i
            slot = i % 2
            if i >= 2:
                stores[i - 2].wait()
            grad[slot, :, 0:2048] = dot(n[:, :, :, :, at:at + 512].reshape(ROWS, 512), gate_up[...], 0, 0).astype(bf16)
            grad[slot, :, 2048:3072] = dot(cot[:, :, :, :, at:at + 512].reshape(ROWS, 512), hidden[...], 0, 0).astype(bf16)
            c = pltpu.make_async_copy(grad.at[slot], grad_hbm.at[pl.ds(at, 512)], gsem.at[i])
            c.start()
            stores.append(c)
        for c in stores[2:] + keep:
            c.wait()

    full = (2, 2, 2, 128, D)
    return pl.pallas_call(
        kernel,
        out_shape=[jax.ShapeDtypeStruct((D, 3072), bf16), jax.ShapeDtypeStruct((ROWS, 1024), bf16),
                   jax.ShapeDtypeStruct(full, bf16)],
        in_specs=any_specs(3), out_specs=any_specs(3),
        scratch_shapes=[VM(full, bf16), VM(full, bf16), VM((D, 3072), bf16), VM((ROWS, 1024), bf16),
                        VM((ROWS, 2048), bf16), VM(full, bf16), VM((2, 512, 3072), bf16), pltpu.SemaphoreType.DMA((4,)),
                        pltpu.SemaphoreType.DMA((4, 3)), pltpu.SemaphoreType.DMA((4,))],
        compiler_params=pltpu.CompilerParams(has_side_effects=True, vmem_limit_bytes=60 * 2**20))(
            n_full, cot_full, weights)


def attention_backward(x, cot, middle, db_part, hidden, weights, a_full, front_full, qk_pre, v_rows, mixed, segs,
                       gains, table, cid):
    def kernel(x, cot, middle, part_hbm, hidden_hbm, w_hbm, a_hbm, front_full, qk_pre, v_rows, mixed, segs,
               gains, table, input_grad, block_output, front_mine, gain_terms,
               shard, hidden, wd, out_part, dm_full, mid_grad, dqkv, part, front_grad, q_acc, k_acc, one_acc, two_acc,
               a_rows, db_term, db_sum, o_grad, o_mine, qkv_mine, sibs_c, t_c, r_c,
               sibs_a, t_a, r_a, sibs_b, t_b, r_b, t1, r1, t2, r2, mid, u1, s1, u2, s2, mid_o, send, recv, lsem):
        me = Place()
        gain_one, gain_two, gain_query, gain_key = gain_rows(gains)
        loads = [pltpu.make_async_copy(hidden_hbm, hidden, lsem.at[1]),
                 pltpu.make_async_copy(w_hbm.at[:, pl.ds(2048, 1024)], wd, lsem.at[2])]
        unit_load = pltpu.make_async_copy(part_hbm, db_term, lsem.at[3])
        a_load = pltpu.make_async_copy(a_hbm, a_rows, lsem.at[4])
        for c in [unit_load] + loads + [a_load]:
            c.start()
        two_acc[...] = jnp.zeros_like(two_acc)
        one_acc[...] = jnp.zeros_like(one_acc)
        q_acc[...] = jnp.zeros_like(q_acc)
        k_acc[...] = jnp.zeros_like(k_acc)

        def back(z, gain, up):
            inverse = lax.rsqrt(jnp.mean(z * z, axis=-1, keepdims=True) + epsilon)
            scaled = up * gain
            inner = jnp.mean(z * scaled, axis=-1, keepdims=True)
            return inverse * (scaled - z * inverse * inverse * inner), up * z * inverse

        meet([me.step("x", 1), me.step("x", -1), me.step("y", 1), me.step("y", -1),
              me.step("z", 1), me.step("z", -1), me.sibling()])
        w = Wire(send, recv)

        def put_a(s, v):
            db_sum[s, 0:1024] = v

        def put_b(s, v):
            db_sum[s, 1024:2048] = v

        def columns(k):
            c = pl.ds(1024 * k, 1024)
            return db_term.at[:, :, :, :, c], (put_a, put_b)[k], sibs_c.at[:, :, c], t_c.at[:, :, c], r_c.at[:, :, :, c]

        def out_block(i, _):
            at = pl.multiple_of(i * 256, 256)
            v = dot(hidden[...], wd[pl.ds(at, 256)], 1, 1).astype(bf16)
            out_part[:, :, :, :, pl.ds(at, 256)] = v.reshape(2, 2, 2, 128, 256)
            return 0
        unit_load.wait()
        gen_a, gen_b = [rs_z_gen(w, me, *columns(k)) for k in range(2)]
        next(gen_a)
        next(gen_b)
        next(gen_a)
        for c in loads:
            c.wait()
        lax.fori_loop(0, 1, out_block, 0)
        next(gen_b)
        lax.fori_loop(1, 4, out_block, 0)
        next(gen_a)
        lax.fori_loop(4, 6, out_block, 0)
        next(gen_b)
        lax.fori_loop(6, 8, out_block, 0)
        run([gen_a])
        run([gen_b])

        def norm_two(s):
            dz, terms = back(middle[s], gain_two, db_sum[s])
            v = cot[s].astype(f32) + dz
            mid_grad[s] = v
            shard[s] = v.astype(bf16)
            two_acc[...] += terms
        chunks(128, norm_two)
        gen = ag_z_gen(w, me, shard, dm_full)
        next(gen)
        own = pltpu.make_async_copy(shard, dm_full.at[me.h, me.c, me.l], lsem.at[0])
        own.start()

        def put_out(s, v):
            block_output[s] = middle[s] + v
        out_gen = rs_z_gen(w, me, out_part, put_out, sibs_a, t_a, r_a)
        next(gen)
        next(out_gen)
        run([gen])
        own.wait()

        def one_pack(p):
            allowed, cosine, sine = pack_tables(segs, p, table)
            mixed_grad = dot(pack_of(dm_full, p), front_full[:, :, :, 384:640].reshape(D, 256)).T.astype(bf16)
            value_rows = v_rows[p].astype(f32).T.astype(bf16)
            key_pre = qk_pre[p, 256:320]
            kn, k_inverse = head_norm(key_pre, gain_key)
            kr = turn(kn, cosine, sine)
            key_rows = kr.T.astype(bf16)
            kr = kr.astype(bf16)
            dk = jnp.zeros((HD, SEQ), f32)
            dv = jnp.zeros((HD, SEQ), f32)
            heads = []
            terms_q = jnp.zeros((HD, SEQ), f32)
            for j in range(4):
                query_pre = qk_pre[p, 64 * j:64 * j + 64]
                qn, q_inverse = head_norm(query_pre, gain_query)
                qr = turn(qn, cosine, sine).astype(bf16)
                probs = pack_probs(key_rows, qr, allowed)
                do = mixed_grad[64 * j:64 * j + 64]
                dp = dot(value_rows, do)
                inner = jnp.sum(probs * dp, axis=0, keepdims=True)
                ds = (probs * (dp - inner)).astype(bf16)
                dqr = dot(kr, ds) * score_scale
                dk += dot(qr, ds, 1, 1)
                dv += dot(do, probs.astype(bf16), 1, 1)
                dq, terms = head_norm_back(query_pre, q_inverse, gain_query, turn_back(dqr, cosine, sine))
                terms_q += terms
                heads.append(dq)
            dk, terms_k = head_norm_back(key_pre, k_inverse, gain_key, turn_back(dk * score_scale, cosine, sine))
            q_acc[...] += terms_q
            k_acc[...] += terms_k
            grads = jnp.concatenate(heads + [dk, dv], axis=0).T.astype(bf16)
            dqkv[p] = grads
            out = dot(grads, front_full[:, :, :, 0:384].reshape(D, 384), 1, 1).astype(bf16)
            part[lax.div(p, 2), lax.rem(p, 2)] = out.reshape(2, 128, D)
        def put_in(s, v):
            dz, terms = back(x[s].astype(f32), gain_one, v)
            input_grad[s] = mid_grad[s] + dz
            one_acc[...] += terms
        in_gen = rs_z_packs(w, me, part, put_in, sibs_b, t_b, r_b)
        next(out_gen)
        for i in range(4):
            dm_rows = dm_full[:, :, :, :, 512 * i:512 * i + 512].reshape(ROWS, 512)
            o_grad[i] = dot(dm_rows, mixed[...].reshape(ROWS, 256), 0, 0).astype(bf16).reshape(4, 128, 256)
        o_gens = rs_xy_gens(w, me, o_grad, o_mine, u1, s1, u2, s2, mid_o)

        def both(gens):
            for g in gens:
                next(g)
        both(o_gens)
        one_pack(pack_turn(me, 0))
        next(in_gen)
        both(o_gens)
        one_pack(pack_turn(me, 1))
        next(out_gen)
        next(in_gen)
        both(o_gens)
        both(o_gens)
        one_pack(pack_turn(me, 2))
        next(in_gen)
        both(o_gens)
        one_pack(pack_turn(me, 3))
        next(in_gen)
        a_load.wait()
        for i in range(4):
            g = dot(a_rows[:, 512 * i:512 * i + 512], dqkv[...].reshape(ROWS, 384), 0, 0)
            front_grad[i] = g.astype(bf16).reshape(4, 128, 384)
        qkv_gens = rs_xy_gens(w, me, front_grad, qkv_mine, t1, r1, t2, r2, mid)
        both(qkv_gens)
        run(o_gens)
        next(in_gen)
        both(qkv_gens)
        both(qkv_gens)
        both(qkv_gens)
        run([out_gen])
        both(qkv_gens)
        run([in_gen])
        run(qkv_gens)
        front_mine[:, 0:384] = qkv_mine[...]
        front_mine[:, 384:640] = o_mine[...]
        w.finish()
        one = jnp.sum(one_acc[...], axis=0, keepdims=True)
        two = jnp.sum(two_acc[...], axis=0, keepdims=True)
        for i in range(16):
            gain_terms[i:i + 1, :] = one[:, 128 * i:128 * i + 128]
            gain_terms[16 + i:17 + i, :] = two[:, 128 * i:128 * i + 128]
        small = jnp.concatenate([q_acc[...], k_acc[...]], axis=0).T
        gain_terms[32:33, :] = jnp.sum(small, axis=0, keepdims=True)

    full = (2, 2, 2, 128, D)
    rows = jax.ShapeDtypeStruct((128, D), f32)
    return pl.pallas_call(
        kernel,
        out_shape=[rows, rows, jax.ShapeDtypeStruct((128, 640), bf16), jax.ShapeDtypeStruct((33, 128), f32)],
        in_specs=vm_specs(3) + any_specs(4) + vm_specs(7), out_specs=vm_specs(4),
        scratch_shapes=[VM((128, D), bf16), VM((ROWS, 1024), bf16), VM((D, 1024), bf16), VM(full, bf16),
                        VM(full, bf16), VM((128, D), f32), VM((PACKS, SEQ, 384), bf16),
                        VM(full, bf16), VM((4, 4, 128, 384), bf16), VM((HD, SEQ), f32), VM((HD, SEQ), f32),
                        VM((16, D), f32), VM((16, D), f32)]
        + [VM((ROWS, D), bf16), VM(full, bf16), VM((128, D), f32), VM((4, 4, 128, 256), bf16),
           VM((128, 256), bf16), VM((128, 384), bf16)]
        + rs_z_scratch(D) * 3 + rs_xy_scratch(384) + rs_xy_scratch(256) + dma_sems(112)
        + [pltpu.SemaphoreType.DMA((5,))],
        compiler_params=params(cid, 60))(
            x, cot, middle, db_part, hidden, weights, a_full.reshape(ROWS, D), front_full, qk_pre, v_rows, mixed, segs,
            gains, table)


def adam(weight, moment, square, gradient, rate, decay):
    momentum = beta_one * moment + (1.0 - beta_one) * gradient
    variance = beta_two * square + (1.0 - beta_two) * gradient * gradient
    ratio = momentum / (1.0 - beta_one**STEP) / (jnp.sqrt(variance / (1.0 - beta_two**STEP)) + adam_epsilon)
    return weight - rate * (ratio + decay * weight), momentum, variance


RATES = (0.04, 0.04, 0.04, 0.15, 0.04, 0.04, 0.02)
SPANS = (256, 64, 64, 256, 1024, 1024, 1024)


def return_gradients(front, rest, gain_terms, cid):
    def kernel(front, rest, terms, fbuf, rbuf, gain_sum, z_in, x_in, y_in, send, recv):
        me = Place()
        peers = swap_devs(me)
        mine = me.h * 2 + me.c
        zs = [me.at(z=m4(me.z + dz), c=lax.rem(me.c + dc, 2)) for dz in range(4) for dc in range(2) if dz or dc]
        xs = [me.step("x", d) for d in (1, 2, 3)]
        ys = [me.step("y", d) for d in (1, 2, 3)]
        meet(zs + xs + ys)
        w = Wire(send, recv)

        def total(buf, n):
            v = buf[0]
            for k in range(1, n):
                v = v + buf[k]
            return v

        def share(value, buf, slot, devs):
            buf[slot] = value
            return [w.go(buf.at[slot], buf.at[slot], d) for d in devs]
        gs = share(terms[...], x_in, me.x, xs)
        arrivals = []
        for j, dev in reversed(peers):
            arrivals.append(w.go(front.at[j], fbuf.at[mine], dev))
            arrivals.append(w.go(rest.at[j], rbuf.at[mine], dev))
        fbuf[mine] = front[mine]
        rbuf[mine] = rest[mine]
        for c in gs:
            c.wait_recv()
        gs = share(total(x_in, 4), y_in, me.y, ys)
        for c in gs:
            c.wait_recv()
        gs = share(total(y_in, 4), z_in, me.z * 2 + me.c, zs)
        for c in gs:
            c.wait_recv()
        gain_sum[...] = total(z_in, 8)
        for a in arrivals:
            a.wait_recv()
        w.finish()

    return pl.pallas_call(
        kernel, out_shape=[jax.ShapeDtypeStruct((4, 32, 640), bf16), jax.ShapeDtypeStruct((4, 32, 3072), bf16),
                           jax.ShapeDtypeStruct((33, 128), f32)],
        in_specs=vm_specs(3), out_specs=vm_specs(3),
        scratch_shapes=[VM((8, 33, 128), f32), VM((4, 33, 128), f32), VM((4, 33, 128), f32)] + dma_sems(19),
        compiler_params=params(cid))(front, rest, gain_terms)


def update(front, rest, gain_sum, gain_states, states, tokens):
    def kernel(*refs):
        front, rest, g_sum, g_w, g_m, g_v = refs[:6]
        ins, t_in, g_out, outs, t_out = refs[6:27], refs[27:29], refs[29:32], refs[32:53], refs[53:55]
        held, made, kept = refs[55:76], refs[76:97], refs[97:99]
        lsem, osem, tsem = refs[99:]
        loads = [pltpu.make_async_copy(a, b, lsem.at[i]) for i, (a, b) in enumerate(zip(ins, held))]
        coming = [pltpu.make_async_copy(a, b, tsem.at[i]) for i, (a, b) in enumerate(zip(t_in, kept))]
        for c in loads + coming:
            c.start()
        new = adam(g_w[...], g_m[...], g_v[...], g_sum[...], gain_rate, 0.0)
        for ref, v in zip(g_out, new):
            ref[...] = v
        stores = []
        at = {False: 0, True: 0}
        for i, (n, rate) in enumerate(zip(SPANS, RATES)):
            late = i >= 4
            buf = rest if late else front
            for k in range(3):
                loads[3 * i + k].wait()
            for j in range(4):
                here = pl.ds(n * j, n)
                grad = buf[j, :, at[late]:at[late] + n].astype(f32)
                new = adam(held[3 * i][:, here], held[3 * i + 1][:, here], held[3 * i + 2][:, here], grad, rate,
                           weight_decay)
                for k in range(3):
                    made[3 * i + k][:, here] = new[k]
            at[late] += n
            for k in range(3):
                c = pltpu.make_async_copy(made[3 * i + k], outs[3 * i + k], osem.at[3 * i + k])
                c.start()
                stores.append(c)
        for i in range(2):
            coming[i].wait()
            c = pltpu.make_async_copy(kept[i], t_out[i], tsem.at[2 + i])
            c.start()
            stores.append(c)
        for c in stores:
            c.wait()

    shapes = [jax.ShapeDtypeStruct(s.shape, f32) for s in states]
    gain_shape = jax.ShapeDtypeStruct((33, 128), f32)
    return pl.pallas_call(
        kernel, out_shape=[gain_shape] * 3 + shapes + [jax.ShapeDtypeStruct(t.shape, f32) for t in tokens],
        in_specs=vm_specs(6) + any_specs(23), out_specs=vm_specs(3) + any_specs(23),
        scratch_shapes=[VM(s.shape, f32) for s in states] * 2 + [VM(t.shape, f32) for t in tokens]
        + [pltpu.SemaphoreType.DMA((21,)), pltpu.SemaphoreType.DMA((21,)), pltpu.SemaphoreType.DMA((4,))],
        compiler_params=pltpu.CompilerParams(has_side_effects=True, vmem_limit_bytes=56 * 2**20))(
            front, rest, gain_sum, *gain_states, *states, *tokens)


from jax.sharding import PartitionSpec as P

PLANE = [[x * 16 + y * 4 + k for x in range(4) for y in range(4)] for k in range(4)]


def scatter_plane(whole):
    return lax.psum_scatter(whole, "dp", axis_index_groups=PLANE, scatter_dimension=0, tiled=True)


def local(block_input, output_grad, segment_ids, norm_gains, gain_moment, gain_square, *states):
    square = lambda v: v.reshape(33, 128)
    gains = square(norm_gains)
    table = jnp.asarray(rope_constants())
    one_full, cot_full, two_full, rest_full, front_full, segments, qk_pre, v_rows, mixed, middle = attention_forward(
        block_input, output_grad, states[::3], segment_ids, gains, table, 2)
    rest_full = rest_full.reshape(D, 3072)
    rest_grad, hidden, db_part = feed_forward(two_full, cot_full, rest_full)
    rest_mine = scatter_plane(rest_grad)
    input_grad, block_output, front_mine, gain_terms = attention_backward(
        block_input, output_grad, middle, db_part, hidden, rest_full, one_full, front_full, qk_pre, v_rows, mixed, segments,
        gains, table, 4)
    front_back, rest_back, gain_sum = return_gradients(
        front_mine.reshape(4, 32, 640), rest_mine.reshape(4, 32, 3072), gain_terms, 5)
    news = update(front_back, rest_back, gain_sum, [gains, square(gain_moment), square(gain_square)], states,
                  (block_output, input_grad))
    return tuple(news[-2:]) + tuple(v.reshape(-1) for v in news[:3]) + tuple(news[3:-2])


def solution(mesh):
    tokens, weight = P(("dp", "tensor"), None), P("dp", "tensor")
    in_specs = (tokens, tokens, P("dp", None), P(), P(), P()) + (weight,) * 21
    out_specs = (tokens, tokens, P(), P(), P()) + (weight,) * 21
    return jax.shard_map(local, mesh=mesh, in_specs=in_specs, out_specs=out_specs, check_vma=False)
```
